32 devices in a mesh: gz: 4 (over x, core), gx: 8 (over z, y).
Axes of the slice: x: 2, y: 2, z: 4, core: 2. Of those that a mesh axis runs over, the one named last changes fastest.
Arguments:
- clean_field: float32 [3, 8, 4, 512], P(None, 'gx', None, 'gz'), may hold values from -64 to 64
- noise_field: float32 [3, 8, 4, 512], P(None, 'gx', None, 'gz'), may hold values from -6 to 6
- timestep: int32 [1], replicated, may hold values from 0 to 499
- dilations: int32 [2], replicated, may hold values from 1 to 256, as said below
- w_in: float32 [3, 128], replicated, may hold values from -3.5 to 3.5
- w_time: float32 [128, 128], replicated, may hold values from -0.5 to 0.5
- w_z: bfloat16 [2, 3, 128, 128], replicated, may hold values from -0.15625 to 0.15625
- w_xy: bfloat16 [2, 8, 128, 128], replicated, may hold values from -0.15625 to 0.15625
- w_point: bfloat16 [2, 128, 128], replicated, may hold values from -0.5 to 0.5
- biases: float32 [2, 128], replicated, may hold values from -3 to 3
- norm_gains: float32 [3, 128], replicated, may hold values from 0.25 to 1.75
- w_out: bfloat16 [3, 128], replicated, may hold values from -0.5 to 0.5
Outputs:
- prediction: float32 [3, 8, 4, 512], P(None, 'gx', None, 'gz')
- field_grad: float32 [3, 8, 4, 512], P(None, 'gx', None, 'gz')
- grad_w_in: float32 [3, 128], replicated
- grad_w_time: float32 [128, 128], replicated
- grad_w_z: float32 [2, 3, 128, 128], replicated
- grad_w_xy: float32 [2, 8, 128, 128], replicated
- grad_w_point: float32 [2, 128, 128], replicated
- grad_biases: float32 [2, 128], replicated
- grad_norm_gains: float32 [3, 128], replicated
- grad_w_out: float32 [3, 128], replicated
The draws below stay inside these ranges and needn't reach their ends.
Inputs may be any that keep to these rules, and one draw needn't show every extreme that they name: `dilations`: every layer's dilation is a power of two no larger than 256; one layer's dilation equals 256 and every other layer's is at most 128.
All inputs are finite; a program needn't handle non-finite values.
Results may differ from the reference program's by a relative error of at most 0.0043.
Values may be sent and summed in bfloat16 or wider, within the bound.
No kernel may reach another device: no remote copies, remote signals or barrier semaphores. Data moves between devices by JAX's collectives and lax.ppermute only.
A program may use at most 64 MiB of HBM per device.

```python
import math
import jax
import jax.numpy as jnp
from jax import lax

C = 128
LAYERS = 2
STEPS = 1000
YW = 4
CZ = 128
NX = 8
NZ = 512


def draw_clean_field(key, part):
    key = jax.random.fold_in(key, 11)
    across = jnp.arange(NX, dtype=jnp.float32) / NX
    along_z = jnp.arange(NZ, dtype=jnp.float32) / NZ
    rough_part = jnp.clip(jax.random.normal(key, (3, NX, YW, NZ), jnp.float32), -6.0, 6.0)
    growth = 3.0
    envelope = jnp.exp(jnp.log(growth) * (across[:, None, None] + along_z[None, None, :]))
    return rough_part * envelope[None]


def draw_dilations(key, part):
    key = jax.random.fold_in(key, 23)
    power_key, pick_key = jax.random.split(key)
    top_power = (2 * CZ).bit_length() - 1
    exponents = jax.random.randint(power_key, (LAYERS,), 0, top_power).astype(jnp.int32)
    powers = jnp.left_shift(jnp.ones((LAYERS,), jnp.int32), exponents)
    chosen = jax.random.randint(pick_key, (), 0, LAYERS)
    return jnp.where(jnp.arange(LAYERS) == chosen, 2 * CZ, powers).astype(jnp.int32)


def block_levels(own_key, extent, cuts, low, high):
    gain, own = 1.0, jax.random.fold_in(own_key, 6)
    for axis_at, blocks in cuts:
        steps = jnp.exp(jax.random.uniform(jax.random.fold_in(own, axis_at), (blocks,), jnp.float32, low / len(cuts), high / len(cuts)))
        gain = gain * jnp.repeat(steps, extent[axis_at] // blocks).reshape([-1 if axis == axis_at else 1 for axis in range(len(extent))])
    return gain


def normal_values(own_key, dims, width, bound, shards=(), held_as=jnp.bfloat16):
    level = block_levels(own_key, dims, shards, -0.22, 0.18) if shards else 1.0
    drawn = jax.random.normal(own_key, dims, jnp.float32) * width * level
    return jnp.minimum(jnp.maximum(drawn, -bound), bound).astype(held_as)


def setup_inputs(seed: int = 0) -> dict:
    streams_of = jax.random.split(jax.random.key(seed), 13)
    return {
        "clean_field": draw_clean_field(jax.random.fold_in(streams_of[12], 71), 0),
        "noise_field": normal_values(streams_of[1], (3, NX, YW, NZ), 1.0, 6.0, ((1, 8), (3, 4)), jnp.float32),
        "timestep": jax.random.randint(streams_of[2], (1,), 0, STEPS // 2).astype(jnp.int32),
        "dilations": draw_dilations(jax.random.fold_in(streams_of[12], 71), 0),
        "w_in": normal_values(streams_of[4], (3, C), 3 ** -0.5, 3.5, (), jnp.float32),
        "w_time": normal_values(streams_of[5], (C, C), C ** -0.5, 0.5, (), jnp.float32),
        "w_z": normal_values(streams_of[6], (LAYERS, 3, C, C), (11 * C) ** -0.5, 0.15625),
        "w_xy": normal_values(streams_of[7], (LAYERS, 8, C, C), (11 * C) ** -0.5, 0.15625),
        "w_point": normal_values(streams_of[8], (LAYERS, C, C), C ** -0.5, 0.5),
        "biases": normal_values(streams_of[9], (LAYERS, C), 0.5, 3.0, (), jnp.float32),
        "norm_gains": jnp.clip(1.0 + 0.15 * jax.random.normal(streams_of[10], (LAYERS + 1, C), jnp.float32), 0.25, 1.75),
        "w_out": normal_values(streams_of[11], (3, C), C ** -0.5, 0.5),
    }


eps_norm = 1e-05
highest = lax.Precision.HIGHEST
plane_offsets = ((-1, -1), (-1, 0), (-1, 1), (0, -1), (0, 1), (1, -1), (1, 0), (1, 1))

def time_terms(timestep, w_time):
    moment = timestep[0].astype(jnp.float32)
    half_width = w_time.shape[0] // 2
    alpha_bar = jnp.cos(0.5 * math.pi * (moment + 0.5) / STEPS) ** 2
    ladder = jnp.exp(-math.log(10000.0) * jnp.arange(half_width, dtype=jnp.float32) / half_width)
    angles = moment * ladder
    features = jnp.concatenate([jnp.sin(angles), jnp.cos(angles)])
    time_raw = jnp.dot(features, w_time, precision=highest)
    return (alpha_bar, features, time_raw, jax.nn.silu(time_raw))

def shift_z(source, offset):
    length = source.shape[2]
    doubled = jnp.concatenate([source, source], axis=2)
    anchor = (offset % length).astype(jnp.int32)
    return lax.dynamic_slice_in_dim(doubled, anchor, length, 2)

def pad_plane(source):
    wrapped = jnp.concatenate([source[-1:], source, source[:1]], axis=0)
    return jnp.pad(wrapped, ((0, 0), (1, 1), (0, 0), (0, 0)))

def plane_tap(padded, shift_x, shift_y, rows_x, rows_y):
    return padded[1 + shift_x:1 + shift_x + rows_x, 1 + shift_y:1 + shift_y + rows_y]

def flat_dot(left, right):
    result = jnp.dot(left.reshape(-1, right.shape[0]), right, preferred_element_type=jnp.float32)
    return result.reshape(left.shape[:-1] + (right.shape[1],))

def cell_product(left, right):
    return jnp.dot(left.reshape(-1, left.shape[-1]).T, right.reshape(-1, right.shape[-1]), preferred_element_type=jnp.float32)

def norm_forward(hidden, gains):
    cell_count = hidden.shape[0] * hidden.shape[1] * hidden.shape[2]
    average = lax.optimization_barrier(jnp.sum(hidden, axis=(0, 1, 2))) / cell_count
    centered = hidden - average
    spread = lax.optimization_barrier(jnp.sum(centered * centered, axis=(0, 1, 2))) / cell_count
    inverse_std = lax.rsqrt(spread + eps_norm)
    whitened = centered * inverse_std
    return ((whitened * gains).astype(jnp.bfloat16), whitened, inverse_std)

def norm_backward(d_normed, whitened, inverse_std, gains):
    cell_count = d_normed.shape[0] * d_normed.shape[1] * d_normed.shape[2]
    scaled = d_normed * gains
    mean_grad = lax.optimization_barrier(jnp.sum(scaled, axis=(0, 1, 2))) / cell_count
    mean_cross = lax.optimization_barrier(jnp.sum(scaled * whitened, axis=(0, 1, 2))) / cell_count
    d_hidden = inverse_std * (scaled - mean_grad - whitened * mean_cross)
    return (d_hidden, lax.optimization_barrier(jnp.sum(d_normed * whitened, axis=(0, 1, 2))))

def conv_forward(normed, dilation, weights_z, weights_xy):
    rows_x, rows_y = (normed.shape[0], normed.shape[1])
    summed = flat_dot(shift_z(normed, -dilation), weights_z[0])
    summed = summed + flat_dot(normed, weights_z[1]) + flat_dot(shift_z(normed, dilation), weights_z[2])
    padded = pad_plane(normed)
    for tap_number, (shift_x, shift_y) in enumerate(plane_offsets):
        summed = summed + flat_dot(plane_tap(padded, shift_x, shift_y, rows_x, rows_y), weights_xy[tap_number])
    return summed

def conv_backward(pre_cot, normed, dilation, weights_z, weights_xy):
    rows_x, rows_y = (normed.shape[0], normed.shape[1])
    d_normed = flat_dot(shift_z(pre_cot, dilation), weights_z[0].T)
    d_normed = d_normed + flat_dot(pre_cot, weights_z[1].T) + flat_dot(shift_z(pre_cot, -dilation), weights_z[2].T)
    padded_cot = pad_plane(pre_cot)
    padded = pad_plane(normed)
    xy_terms = []
    for tap_number, (shift_x, shift_y) in enumerate(plane_offsets):
        d_normed = d_normed + flat_dot(plane_tap(padded_cot, -shift_x, -shift_y, rows_x, rows_y), weights_xy[tap_number].T)
        xy_terms.append(cell_product(plane_tap(padded, shift_x, shift_y, rows_x, rows_y), pre_cot))
    z_terms = jnp.stack([cell_product(shift_z(normed, -dilation), pre_cot), cell_product(normed, pre_cot), cell_product(shift_z(normed, dilation), pre_cot)])
    return (d_normed, z_terms, jnp.stack(xy_terms))

def reference(clean_field, noise_field, timestep, dilations, w_in, w_time, w_z, w_xy, w_point, biases, norm_gains, w_out):
    inv_area = 1.0 / (NX * NZ)
    alpha_bar, features, time_raw, time_code = time_terms(timestep, w_time)
    noisy = jnp.sqrt(alpha_bar) * clean_field + jnp.sqrt(1.0 - alpha_bar) * noise_field
    stream = jnp.einsum('kxyz,kc->xyzc', noisy, w_in, precision=highest)
    saved_streams = []
    saved_pre = []
    for which_layer in range(LAYERS):
        normed, unused_white, unused_inverse = norm_forward(stream, norm_gains[which_layer])
        pre_act = conv_forward(normed, dilations[which_layer], w_z[which_layer], w_xy[which_layer])
        pre_act = pre_act + biases[which_layer] + time_code
        activated = jax.nn.gelu(pre_act).astype(jnp.bfloat16)
        saved_streams.append(stream)
        saved_pre.append(pre_act)
        stream = stream + flat_dot(activated, w_point[which_layer])
    out_normed, out_white, out_inverse = norm_forward(stream, norm_gains[LAYERS])
    prediction = jnp.einsum('xyzc,kc->kxyz', out_normed.astype(jnp.float32), w_out.astype(jnp.float32), precision=highest)
    misfit = prediction - noise_field
    d_out = jnp.einsum('kxyz,kc->xyzc', misfit, w_out.astype(jnp.float32), precision=highest)
    grad_w_out = inv_area * jnp.einsum('kxyz,xyzc->kc', misfit, out_normed.astype(jnp.float32), precision=highest)
    d_stream, out_gain_raw = norm_backward(d_out, out_white, out_inverse, norm_gains[LAYERS])
    z_list, xy_list, point_list, bias_list, gain_list = ([], [], [], [], [])
    for which_layer in reversed(range(LAYERS)):
        normed, whitened, inverse_std = norm_forward(saved_streams[which_layer], norm_gains[which_layer])
        pre_act = saved_pre[which_layer]
        activated = jax.nn.gelu(pre_act).astype(jnp.bfloat16)
        stream_cot = d_stream.astype(jnp.bfloat16)
        point_raw = cell_product(activated, stream_cot)
        d_act = flat_dot(stream_cot, w_point[which_layer].T)
        gelu_back = jax.vjp(jax.nn.gelu, pre_act)[1]
        pre_cot = gelu_back(d_act)[0].astype(jnp.bfloat16)
        bias_raw = lax.optimization_barrier(jnp.sum(pre_cot.astype(jnp.float32), axis=(0, 1, 2)))
        d_normed, z_raw, xy_raw = conv_backward(pre_cot, normed, dilations[which_layer], w_z[which_layer], w_xy[which_layer])
        d_back, gain_raw = norm_backward(d_normed, whitened, inverse_std, norm_gains[which_layer])
        d_stream = d_stream + d_back
        z_list.insert(0, z_raw)
        xy_list.insert(0, xy_raw)
        point_list.insert(0, point_raw)
        bias_list.insert(0, bias_raw)
        gain_list.insert(0, gain_raw)
    field_grad = jnp.einsum('xyzc,kc->kxyz', d_stream, w_in, precision=highest)
    grad_w_in = inv_area * jnp.einsum('kxyz,xyzc->kc', noisy, d_stream, precision=highest)
    bias_all = jnp.stack(bias_list)
    time_back = jax.vjp(jax.nn.silu, time_raw)[1](lax.optimization_barrier(jnp.sum(bias_all, axis=0)))[0]
    grad_w_time = inv_area * jnp.outer(features, time_back)
    return (prediction, field_grad, grad_w_in, grad_w_time, inv_area * jnp.stack(z_list), inv_area * jnp.stack(xy_list), inv_area * jnp.stack(point_list), inv_area * bias_all, inv_area * jnp.stack(gain_list + [out_gain_raw]), grad_w_out)
```

```python
import functools
import math

import jax
import jax.numpy as jnp
from jax import lax
from jax.experimental import pallas as pl
from jax.experimental.pallas import tpu as pltpu
from jax.sharding import PartitionSpec as P

STEPS = 1000
REACH = 256
RIM = 4

eps_norm = 1e-05
highest = lax.Precision.HIGHEST
bf16 = jnp.bfloat16
f32 = jnp.float32
plane_offsets = ((-1, -1), (-1, 0), (-1, 1), (0, -1), (0, 1), (1, -1), (1, 0), (1, 1))


def time_terms(timestep, w_time):
    moment = timestep[0].astype(jnp.float32)
    half_width = w_time.shape[0] // 2
    alpha_bar = jnp.cos(0.5 * math.pi * (moment + 0.5) / STEPS) ** 2
    ladder = jnp.exp(-math.log(10000.0) * jnp.arange(half_width, dtype=jnp.float32) / half_width)
    angles = moment * ladder
    features = jnp.concatenate([jnp.sin(angles), jnp.cos(angles)])
    time_raw = jnp.dot(features, w_time, precision=highest)
    return (alpha_bar, features, time_raw, jax.nn.silu(time_raw))


def mm(left, right):
    return lax.dot_general(left, right, (((1,), (0,)), ((), ())), preferred_element_type=f32)


def mm_nt(left, right):
    return lax.dot_general(left, right, (((1,), (1,)), ((), ())), preferred_element_type=f32)


def mm_tn(left, right):
    return lax.dot_general(left, right, (((0,), (0,)), ((), ())), preferred_element_type=f32)


def halves(value):
    high = value.astype(bf16)
    return high, (value - high.astype(f32)).astype(bf16)


def wide(vector):
    return jnp.concatenate([vector] * 4, axis=1)


def folded(vector):
    channels = vector.shape[1] // 4
    return sum(vector[:, y * channels : (y + 1) * channels] for y in range(4))


def own_rows(sc, shape, span):
    row = lax.broadcasted_iota(jnp.int32, shape, 0)
    in_span = lax.rem(row, span)
    near = (in_span >= RIM) & (in_span < span - RIM)
    wide_step = (sc[1] >= sc[6]).astype(jnp.int32)
    far = row < sc[2]
    flag = jnp.where(wide_step == 1, far.astype(jnp.int32), near.astype(jnp.int32))
    return flag == 1


def z_of_rows(sc, shape, span, cells_z):
    row = lax.broadcasted_iota(jnp.int32, shape, 0)
    members, reach_own = sc[6], span - 2 * RIM
    residues = jnp.minimum(sc[1], members)
    member = sc[0]
    step_far = row * members + member
    part = member // residues
    start = lax.rem(member, residues)
    period = row // span
    inside = row - period * span - RIM + part * reach_own
    step_near = start + residues * inside + period * REACH
    wide_step = (sc[1] >= members).astype(jnp.int32)
    z = jnp.where(wide_step == 1, step_far, step_near)
    return lax.rem(z + 2 * cells_z, cells_z)


def pick_z(sc, rows, span, cells_z):
    z = z_of_rows(sc, (rows, cells_z), span, cells_z)
    return (z == lax.broadcasted_iota(jnp.int32, (rows, cells_z), 1)).astype(f32).astype(bf16)


def shifts(rows, length, step):
    row = lax.broadcasted_iota(jnp.int32, (rows, rows), 0)
    col = lax.broadcasted_iota(jnp.int32, (rows, rows), 1)
    down = row - step
    down = jnp.where(down < 0, down + length, down)
    up = row + step
    up = jnp.where(up >= length, up - length, up)
    return jnp.concatenate(
        [(down == col).astype(f32).astype(bf16), (up == col).astype(f32).astype(bf16)], axis=0
    )


def build_taps(w, taps, taps_z):
    channels = w.shape[-1]
    zero = jnp.zeros((channels, channels), bf16)
    for q in range(2):
        for i in range(3):
            for y_in in range(4):
                for side in range(2):
                    j = y_in - (2 * q + side)
                    block = w[i * 3 + j + 1] if abs(j) <= 1 else zero
                    taps[
                        q,
                        i,
                        y_in * channels : (y_in + 1) * channels,
                        side * channels : (side + 1) * channels,
                    ] = block
    for m in range(2):
        build_pair(w[9 + m], taps_z, m)


def build_pair(block, target, m):
    channels = block.shape[-1]
    zero = jnp.zeros((channels, channels), bf16)
    target[m, :channels, :channels] = block
    target[m, channels:, channels:] = block
    target[m, :channels, channels:] = zero
    target[m, channels:, :channels] = zero


def fill_rims(padded, planes):
    padded[0] = padded[planes]
    padded[planes + 1] = padded[1]


def fill_shifted(padded, shifted, both, planes):
    rows = padded.shape[1]

    def body(x, carry):
        moved = mm(both, padded[x + 1]).astype(bf16)
        shifted[0, x] = moved[:rows]
        shifted[1, x] = moved[rows:]
        return carry

    lax.fori_loop(0, planes, body, 0)


def conv_half(padded, shifted, taps, taps_z, x0, count, q):
    rows, lanes = padded.shape[1:]
    half = lanes // 2
    total = None
    for i in range(3):
        part = mm(padded[pl.ds(x0 + i, count)].reshape(count * rows, lanes), taps[q, i])
        total = part if total is None else total + part
    for m in range(2):
        source = shifted[m, pl.ds(x0, count), :, q * half : (q + 1) * half]
        total = total + mm(source.reshape(count * rows, half), taps_z[m])
    return total


def gelu_pair(value):
    scale = math.sqrt(2.0 / math.pi)
    square = value * value
    bent = jnp.tanh(scale * value * (1.0 + 0.044715 * square))
    half = 0.5 + 0.5 * bent
    slope = half + 0.5 * value * (1.0 - bent * bent) * (
        scale * (1.0 + 3.0 * 0.044715 * square)
    )
    return value * half, slope


def merged_stats(parts, per_member):
    found = []
    for part in parts:
        for at in range(0, part.shape[0], 8):
            found.append((part[at : at + 1], part[at + 1 : at + 2]))
    total = sum(one[0] for one in found)
    mean = total / (per_member * len(found))
    spread = sum(one[1] for one in found)
    for one in found:
        gap = one[0] / per_member - mean
        spread = spread + per_member * gap * gap
    return mean, lax.rsqrt(spread / (per_member * len(found)) + eps_norm)


def merged_sums(parts):
    found = []
    for part in parts:
        for at in range(0, part.shape[0], 8):
            found.append(part[at : at + 8])
    return sum(found)


def put_rows(ref, *vectors):
    rows = list(vectors)
    rows += [jnp.zeros((1, ref.shape[1]), f32)] * (ref.shape[0] - len(rows))
    ref[...] = jnp.concatenate(rows, axis=0)


def layer_forward(sc, which, padded, shifted, taps, taps_z, pair, w, wp, shift_bias, old, stream,
                  act, slope, stats, acc, span, per_member):
    planes, rows, lanes = stream.shape
    half = lanes // 2
    count = 2
    build_taps(w, taps, taps_z)
    build_pair(wp[...], pair, 0)
    fill_rims(padded, planes)
    fill_shifted(padded, shifted, shifts(rows, sc[2], sc[3 + which]), planes)
    acc[...] = jnp.zeros_like(acc)
    bias = wide(shift_bias)[:, :half]

    def body(step, carry):
        x0 = step * count
        for q in range(2):
            side = slice(q * half, (q + 1) * half)
            pre = conv_half(padded, shifted, taps, taps_z, x0, count, q) + bias
            value, grad = gelu_pair(pre)
            value = value.astype(bf16)
            act[pl.ds(x0, count), :, side] = value.reshape(count, rows, half)
            slope[pl.ds(x0, count), :, side] = grad.astype(bf16).reshape(count, rows, half)
            branch = mm(value, pair[0]).reshape(count, rows, half)
            new = old[pl.ds(x0, count), :, side] + branch
            stream[pl.ds(x0, count), :, side] = new
            acc[:, side] += jnp.sum(new, axis=0)
        return carry

    lax.fori_loop(0, planes // count, body, 0)
    mask = own_rows(sc, (rows, lanes), span)
    total = folded(jnp.sum(jnp.where(mask, acc[...], 0.0), axis=0, keepdims=True))
    mean = wide(total / per_member)
    spread = jnp.zeros((rows, lanes), f32)
    for x in range(planes):
        gap = stream[x] - mean
        spread = spread + gap * gap
    spread = folded(jnp.sum(jnp.where(mask, spread, 0.0), axis=0, keepdims=True))
    put_rows(stats, total, spread)


def kernel_first(span, cells_z, per_member, sc, fields, lift_hi, lift_lo, w_in, gain, shift_bias, w, wp,
                 stream, normed, act, slope, gathered, stats, consts,
                 padded, shifted, taps, taps_z, pair, acc, old, staged):
    planes, rows, lanes = stream.shape
    channels = lanes // 4
    slabs = cells_z // fields.shape[2]
    cell_count = float(planes * 4 * cells_z)
    comps = [fields[:, 4 * k : 4 * k + 4, :] for k in range(3)]

    def all_sum(value):
        value = jnp.sum(jnp.sum(value, axis=0), axis=0, keepdims=True)
        return jnp.sum(value, axis=1, keepdims=True)

    means = [all_sum(comp) / cell_count for comp in comps]
    gaps = [comp - mean[None] for comp, mean in zip(comps, means)]
    covs = {}
    for j in range(3):
        for k in range(j, 3):
            covs[j, k] = all_sum(gaps[j] * gaps[k]) / cell_count
    rows_in = [w_in[k : k + 1, :] for k in range(3)]
    mean_c = sum(means[k] * rows_in[k] for k in range(3))
    var_c = jnp.zeros((1, channels), f32)
    for (j, k), cov in covs.items():
        var_c = var_c + (1.0 if j == k else 2.0) * cov * (rows_in[j] * rows_in[k])
    inv_c = lax.rsqrt(jnp.maximum(var_c, 0.0) + eps_norm)
    flat = [jnp.broadcast_to(value, (1, channels)) for value in means + list(covs.values())]
    put_rows(consts, mean_c, inv_c, *flat)
    pick = pick_z(sc, rows, span, cells_z)
    depth = fields.shape[2]
    got = [jnp.zeros((rows, planes * 32), f32) for _ in range(2)]
    staged[:, 24:, :] = jnp.zeros((planes, 8, depth), f32)
    for s in range(slabs):
        staged[:, :24, :] = fields[s * planes : (s + 1) * planes]
        both = halves(staged[...].reshape(planes * 32, depth))
        for at in range(2):
            got[at] = got[at] + mm_nt(pick[:, s * depth : (s + 1) * depth], both[at])
    high, low = got[0].astype(bf16), got[1].astype(bf16)
    gathered[:, : planes * 32] = high
    gathered[:, planes * 32 :] = low
    scale = wide(inv_c * gain[...])
    mean_w = wide(mean_c)
    for x in range(planes):
        at = slice((planes - 1 - x) * 32, (planes - 1 - x) * 32 + planes * 32)
        value = mm(high, lift_hi[at]) + mm(low, lift_hi[at]) + mm(high, lift_lo[at])
        old[x] = value
        unit = ((value - mean_w) * scale).astype(bf16)
        padded[x + 1] = unit
        normed[x] = unit
    layer_forward(sc, 0, padded, shifted, taps, taps_z, pair, w, wp, shift_bias[...], old, stream, act,
                  slope, stats, acc, span, per_member)


def kernel_second(span, per_member, sc, *refs):
    parts, refs = refs[:3], refs[3:]
    (old, gain, shift_bias, w, wp, stream, normed, act, slope, stats, consts,
     padded, shifted, taps, taps_z, pair, acc) = refs
    planes = stream.shape[0]
    mean, inverse = merged_stats(parts, per_member)
    put_rows(consts, mean, inverse)
    mean_w, scale = wide(mean), wide(inverse * gain[...])
    for x in range(planes):
        unit = ((old[x] - mean_w) * scale).astype(bf16)
        padded[x + 1] = unit
        normed[x] = unit
    layer_forward(sc, 1, padded, shifted, taps, taps_z, pair, w, wp, shift_bias[...], old, stream, act,
                  slope, stats, acc, span, per_member)


def kernel_out(span, per_member, sc, *refs):
    parts, refs = refs[:3], refs[3:]
    stream, gain, gathered, lift_out, prediction, misfit, sums, w_out_raw, consts, acc = refs
    planes, rows, lanes = stream.shape
    half = planes * 32
    mean, inverse = merged_stats(parts, per_member)
    put_rows(consts, mean, inverse)
    mean_w, inv_w, gain_w = wide(mean), wide(inverse), wide(gain[...])
    total = jnp.zeros((rows, half), f32)

    def place(x):
        return slice((planes - 1 - x) * 32, (planes - 1 - x) * 32 + half)

    for x in range(planes):
        unit = ((stream[x] - mean_w) * (inv_w * gain_w)).astype(bf16)
        total = total + mm_nt(unit, lift_out[place(x)])
    slot = lax.rem(lax.broadcasted_iota(jnp.int32, (rows, half), 1), 32)
    noise = gathered[:, :half].astype(f32) + gathered[:, half:].astype(f32)
    gap = jnp.where((slot >= 12) & (slot < 24), total - noise, 0.0)
    prediction[...] = total
    high, low = halves(gap)
    misfit[:, :half] = high
    misfit[:, half:] = low
    mask = own_rows(sc, (rows, half), span)
    high_own = jnp.where(mask, gap, 0.0).astype(bf16)
    low_own = jnp.where(mask, low.astype(f32), 0.0).astype(bf16)
    plain = jnp.zeros((rows, lanes), f32)
    cross = jnp.zeros((rows, lanes), f32)
    raw = jnp.zeros((32, lanes), f32)
    for x in range(planes):
        white = (stream[x] - mean_w) * inv_w
        unit = (white * gain_w).astype(bf16)
        d_out = mm(high, lift_out[place(x)]) + mm(low, lift_out[place(x)])
        plain = plain + d_out
        cross = cross + d_out * white
        got = mm_tn(high_own, unit) + mm_tn(low_own, unit)
        raw = raw + got[x * 32 : x * 32 + 32]
    mask = own_rows(sc, (rows, lanes), span)
    s_plain = folded(jnp.sum(jnp.where(mask, plain, 0.0), axis=0, keepdims=True))
    s_cross = folded(jnp.sum(jnp.where(mask, cross, 0.0), axis=0, keepdims=True))
    put_rows(sums, s_plain, s_cross)
    put_rows(w_out_raw, *by_component(raw, 3))


def by_component(raw, first):
    channels = raw.shape[1] // 4
    found = []
    for k in range(first, first + 3):
        found.append(
            sum(raw[k * 4 + y : k * 4 + y + 1, y * channels : (y + 1) * channels] for y in range(4))
        )
    return found


def branch_backward(sc, planes, d_stream_of, pair, act, slope, normed, padded, scot, span, bias_acc):
    rows, lanes = padded.shape[1:]
    half = lanes // 2

    def body(x, carry):
        cot = d_stream_of(x).astype(bf16)
        scot[x] = cot
        for q in range(2):
            side = slice(q * half, (q + 1) * half)
            d_act = mm(cot[:, side], pair[0])
            pre = (d_act * slope[x, :, side].astype(f32)).astype(bf16)
            padded[x + 1, :, side] = pre
            bias_acc[:, side] += pre.astype(f32)
        return carry

    lax.fori_loop(0, planes, body, 0)


def weight_grads(sc, which, planes, padded, scot, normed, act, grads, picked, wide_left, own_pre, span, share):
    rows, lanes = padded.shape[1:]
    channels = lanes // 4
    wide_share = 4 * share
    row = lax.broadcasted_iota(jnp.int32, (lanes, wide_share), 0)
    col = lax.broadcasted_iota(jnp.int32, (lanes, wide_share), 1)
    hit = (row // channels == col // share) & (
        lax.rem(row, channels) == lax.rem(col, share) + sc[5] * share
    )
    choose = hit.astype(f32).astype(bf16)
    both = shifts(rows, sc[2], sc[3 + which])
    mask = own_rows(sc, (rows, lanes), span)

    def gather(x, carry):
        picked[x] = mm(normed[x], choose).astype(bf16)
        return carry

    lax.fori_loop(0, planes, gather, 0)
    raw = jnp.zeros((5 * wide_share, lanes), f32)
    raw_point = jnp.zeros((wide_share, lanes), f32)
    for x in range(planes):
        here = picked[x]
        moved = mm(both, here).astype(bf16)
        left = jnp.concatenate(
            [picked[(x - 1) % planes], here, picked[(x + 1) % planes], moved[:rows], moved[rows:]],
            axis=1,
        )
        wide_left[x] = left
        own_pre[x] = jnp.where(mask, padded[x + 1].astype(f32), 0.0).astype(bf16)
    raw = mm_tn(
        wide_left[...].reshape(planes * rows, 5 * wide_share), own_pre[...].reshape(planes * rows, lanes)
    )

    def gather_act(x, carry):
        picked[x] = mm(act[x], choose).astype(bf16)
        own_pre[x] = jnp.where(mask, scot[x].astype(f32), 0.0).astype(bf16)
        return carry

    lax.fori_loop(0, planes, gather_act, 0)
    raw_point = mm_tn(
        picked[...].reshape(planes * rows, wide_share), own_pre[...].reshape(planes * rows, lanes)
    )

    def block(source, part, y_in, y_out):
        at = part * wide_share + y_in * share
        return source[at : at + share, y_out * channels : (y_out + 1) * channels]

    for i in range(3):
        for j in range(-1, 2):
            grads[i * 3 + j + 1] = sum(
                block(raw, i, y + j, y) for y in range(4) if 0 <= y + j < 4
            )
    for m in range(2):
        grads[9 + m] = sum(block(raw, 3 + m, y, y) for y in range(4))
    grads[11] = sum(block(raw_point, 0, y, y) for y in range(4))


def conv_backward(sc, which, planes, padded, shifted, taps, taps_z, w, emit):
    rows, lanes = padded.shape[1:]
    half = lanes // 2
    build_taps(w, taps, taps_z)
    fill_rims(padded, planes)
    fill_shifted(padded, shifted, shifts(rows, sc[2], sc[3 + which]), planes)
    count = 2

    def body(step, carry):
        x0 = step * count
        for q in range(2):
            emit(x0, count, q, conv_half(padded, shifted, taps, taps_z, x0, count, q))
        return carry

    lax.fori_loop(0, planes // count, body, 0)


def masked_total(sc, value, span):
    mask = own_rows(sc, value.shape, span)
    return folded(jnp.sum(jnp.where(mask, value, 0.0), axis=0, keepdims=True))


def kernel_back_second(span, share, cell_count, sc, *refs):
    parts, refs = refs[:3], refs[3:]
    (stream, out_consts, gain_out, gain, misfit, lift_out, act, slope, normed, w, wp,
     d_stream, d_normed, sums, grads,
     padded, shifted, taps, taps_z, pair, acc, acc2, scot, picked, wide_left, own_pre) = refs
    planes, rows, lanes = stream.shape
    half = lanes // 2
    sums_out = merged_sums(parts)
    gain_w = wide(gain_out[...])
    mean_w, inv_w = wide(out_consts[0:1]), wide(out_consts[1:2])
    m_plain = gain_w * wide(sums_out[0:1]) / cell_count
    m_cross = gain_w * wide(sums_out[1:2]) / cell_count
    high, low = misfit[:, : planes * 32], misfit[:, planes * 32 :]
    build_pair(wp[...], pair, 0)
    acc[...] = jnp.zeros_like(acc)

    def d_stream_of(x):
        at = pl.ds(pl.multiple_of((planes - 1 - x) * 32, 32), planes * 32)
        d_out = mm(high, lift_out[at]) + mm(low, lift_out[at])
        white = (stream[x] - mean_w) * inv_w
        value = inv_w * (gain_w * d_out - m_plain - white * m_cross)
        d_stream[x] = value
        return value

    branch_backward(sc, planes, d_stream_of, pair, act, slope, normed, padded, scot, span, acc)
    s_bias = masked_total(sc, acc[...], span)
    acc[...] = jnp.zeros_like(acc)
    acc2[...] = jnp.zeros_like(acc2)

    def emit(x0, count, q, value):
        side = slice(q * half, (q + 1) * half)
        value = value.reshape(count, rows, half)
        d_normed[pl.ds(x0, count), :, side] = value
        acc[:, side] += jnp.sum(value, axis=0)
        acc2[:, side] += jnp.sum(value * normed[pl.ds(x0, count), :, side].astype(f32), axis=0)

    conv_backward(sc, 1, planes, padded, shifted, taps, taps_z, w, emit)
    s_plain = masked_total(sc, acc[...], span)
    s_cross = masked_total(sc, acc2[...], span) / gain[...]
    put_rows(sums, s_plain, s_cross, s_bias)
    weight_grads(sc, 1, planes, padded, scot, normed, act, grads, picked, wide_left, own_pre, span, share)


def kernel_back_first(span, share, cell_count, sc, *refs):
    parts, refs = refs[:3], refs[3:]
    (consts, d_next, d_normed, normed_next, gain_next, act, slope, normed, wp,
     d_stream, pre_cot, sums, grads,
     padded, pair, acc, scot, picked, wide_left, own_pre) = refs
    planes, rows, lanes = d_next.shape
    sums_in = merged_sums(parts)
    gain_w = wide(gain_next[...])
    inv_w = wide(consts[1:2])
    m_plain = gain_w * wide(sums_in[0:1]) / cell_count
    m_cross = wide(sums_in[1:2]) / cell_count
    build_pair(wp[...], pair, 0)
    acc[...] = jnp.zeros_like(acc)

    def d_stream_of(x):
        back = gain_w * d_normed[x] - m_plain - normed_next[x].astype(f32) * m_cross
        value = d_next[x] + inv_w * back
        d_stream[x] = value
        return value

    branch_backward(sc, planes, d_stream_of, pair, act, slope, normed, padded, scot, span, acc)
    put_rows(sums, masked_total(sc, acc[...], span))

    def hand_on(x, carry):
        pre_cot[x] = padded[x + 1]
        return carry

    lax.fori_loop(0, planes, hand_on, 0)
    weight_grads(sc, 0, planes, padded, scot, normed, act, grads, picked, wide_left, own_pre, span, share)


def kernel_last(span, cells_z, sc, pre_cot, d_stream, normed, gain, consts, gathered, lift_hi, lift_lo, w,
                prediction, slab, sums, in_raw,
                padded, shifted, taps, taps_z, acc, acc2, field, raw, turned):
    planes, rows, lanes = d_stream.shape
    half = lanes // 2
    wide_in = planes * 32

    def take(x, carry):
        padded[x + 1] = pre_cot[x]
        return carry

    lax.fori_loop(0, planes, take, 0)
    acc[...] = jnp.zeros_like(acc)
    acc2[...] = jnp.zeros_like(acc2)
    slot = lax.rem(lax.broadcasted_iota(jnp.int32, (rows, wide_in), 1), 32)
    field[...] = jnp.where((slot >= 12) & (slot < 24), prediction[...], 0.0)
    raw[...] = jnp.zeros_like(raw)
    mask = own_rows(sc, (rows, wide_in), span)
    keep = lambda value: jnp.where(mask, value.astype(f32), 0.0).astype(bf16)
    high_own = keep(gathered[:, :wide_in])
    low_own = keep(gathered[:, wide_in:])
    scale = wide(consts[1:2] * gain[...])

    def emit(x0, count, q, value):
        side = slice(q * half, (q + 1) * half)
        value = value.reshape(count, rows, half)
        acc[:, side] += jnp.sum(value, axis=0)
        acc2[:, side] += jnp.sum(value * normed[pl.ds(x0, count), :, side].astype(f32), axis=0)
        full = d_stream[pl.ds(x0, count), :, side] + value * scale[:, side]
        for t in range(count):
            high, low = halves(full[t])
            at = pl.ds(pl.multiple_of((planes - 1 - x0 - t) * 32, 32), wide_in)
            l_hi, l_lo = lift_hi[at, side], lift_lo[at, side]
            field[...] += mm_nt(high, l_hi) + mm_nt(low, l_hi) + mm_nt(high, l_lo)
            got = mm_tn(high_own, high) + mm_tn(high_own, low) + mm_tn(low_own, high)
            turned[:, :half] = got
            raw[:, side] += turned[pl.ds(pl.multiple_of((x0 + t) * 32, 32), 32), :half]

    conv_backward(sc, 0, planes, padded, shifted, taps, taps_z, w, emit)
    s_plain = masked_total(sc, acc[...], span)
    s_cross = masked_total(sc, acc2[...], span) / gain[...]
    put_rows(sums, s_plain, s_cross)
    put_rows(in_raw, *by_component(raw[...], 0))
    pick = pick_z(sc, rows, span, cells_z)
    pick = jnp.where(own_rows(sc, pick.shape, span), pick.astype(f32), 0.0).astype(bf16)
    high, low = halves(field[...])
    turned[...] = mm_tn(high, pick) + mm_tn(low, pick)
    slab[...] = turned[pl.ds(pl.multiple_of(sc[7] * 32, 32), 32)]


def call(kernel, outs, scratch, scalars, *args):
    spec = pl.BlockSpec(memory_space=pltpu.VMEM)
    return pl.pallas_call(
        kernel,
        out_shape=[jax.ShapeDtypeStruct(shape, dtype) for shape, dtype in outs],
        in_specs=[pl.BlockSpec(memory_space=pltpu.SMEM)] + [spec] * len(args),
        out_specs=[spec] * len(outs),
        scratch_shapes=[pltpu.VMEM(shape, dtype) for shape, dtype in scratch],
        compiler_params=pltpu.CompilerParams(vmem_limit_bytes=56 * 2**20),
    )(scalars, *args)


def swapped(value, axis, bit):
    count = lax.axis_size(axis)
    return lax.ppermute(value, axis, [(i, i ^ bit) for i in range(count)])


def group_parts(value):
    beside = swapped(value, "gz", 1)
    pair = jnp.concatenate([value, beside], axis=0)
    return (value, beside, swapped(pair, "gz", 2))


def group_sum(value):
    value = value + swapped(value, "gz", 1)
    return value + swapped(value, "gz", 2)


def shared_grads(grads):
    members = lax.axis_size("gz")
    taps, share, channels = grads.shape
    pieces = grads.reshape(members, (taps // members) * share, channels)
    mine = jnp.sum(lax.all_to_all(pieces, "gz", 0, 0), axis=0).astype(bf16)
    total = members * lax.axis_size("gx")
    every = lax.all_to_all(
        jnp.broadcast_to(mine[None], (total,) + mine.shape), ("gz", "gx"), 0, 0
    )
    every = every.reshape(members, total // members, taps // members, share, channels)
    return every.transpose(0, 2, 1, 3, 4).reshape(taps, channels, channels)


def per_device_grouped(clean_field, noise_field, timestep, dilations, w_in, w_time, w_z, w_xy, w_point,
                       biases, norm_gains, w_out):
    members, groups = lax.axis_size("gz"), lax.axis_size("gx")
    depth = clean_field.shape[3]
    planes, cells_z = groups, depth * members
    channels = w_in.shape[1]
    lanes = 4 * channels
    periods = cells_z // REACH
    span = REACH // members + 2 * RIM
    rows = periods * span
    share = channels // groups
    per_member = float(planes * 4 * depth)
    cell_count = per_member * members
    inv_area = 4.0 / cell_count

    alpha_bar, features, time_raw, time_code = time_terms(timestep, w_time)
    noisy = jnp.sqrt(alpha_bar) * clean_field + jnp.sqrt(1.0 - alpha_bar) * noise_field
    block = jnp.concatenate([noisy, noise_field], axis=0).reshape(24, depth)
    total = members * groups
    fields = lax.all_to_all(
        jnp.broadcast_to(block[None], (total, 24, depth)), ("gz", "gx"), 0, 0
    )

    small = jnp.min(dilations)
    coarse = small >= members
    length = jnp.where(coarse, depth, rows)
    step_small = jnp.where(coarse, small // members, 1)
    step_far = jnp.where(coarse, REACH // members, span)
    steps = jnp.where(dilations == REACH, step_far, step_small)
    scalars = jnp.stack(
        [
            lax.axis_index("gz"),
            small,
            length,
            steps[0],
            steps[1],
            lax.axis_index("gx"),
            jnp.int32(members),
            lax.axis_index("gx"),
        ]
    ).astype(jnp.int32)

    eye = jnp.eye(4, dtype=f32)

    def lifted(weights, first):
        spread = (eye[None, :, :, None] * weights[:, None, None, :]).reshape(12, lanes)
        spread = jnp.pad(spread, ((first * 4, 20 - first * 4), (0, 0)))
        return jnp.pad(spread, (((planes - 1) * 32, (planes - 1) * 32), (0, 0)))

    in_hi = lax.reduce_precision(w_in, 8, 7)
    lift_hi, lift_lo = (lifted(part, 0).astype(bf16) for part in (in_hi, w_in - in_hi))
    lift_out = lifted(w_out.astype(f32), 3).astype(bf16)
    taps_f = jnp.concatenate([w_xy[:, :4], w_z[:, 1:2], w_xy[:, 4:], w_z[:, 0:1], w_z[:, 2:3]], axis=1)
    turned = taps_f.swapaxes(-1, -2)
    taps_b = jnp.concatenate([turned[:, 8::-1], turned[:, 10:11], turned[:, 9:10]], axis=1)
    point_t = w_point.swapaxes(-1, -2)
    shift_bias = biases + time_code
    gains = [norm_gains[l : l + 1] for l in range(3)]

    big = (planes, rows, lanes)
    vec = ((8, channels), f32)
    conv_scratch = [
        ((planes + 2, rows, lanes), bf16),
        ((2,) + big, bf16),
        ((2, 3, lanes, lanes // 2), bf16),
        ((2, lanes // 2, lanes // 2), bf16),
    ]
    pair = ((1, lanes // 2, lanes // 2), bf16)
    flat = ((rows, lanes), f32)
    wide_share = 4 * share
    grad_scratch = [
        (big, bf16),
        ((planes, rows, wide_share), bf16),
        ((planes, rows, 5 * wide_share), bf16),
        (big, bf16),
    ]

    stream1, normed0, act0, slope0, gathered, stats1, consts0 = call(
        functools.partial(kernel_first, span, cells_z, per_member),
        [(big, f32), (big, bf16), (big, bf16), (big, bf16), ((rows, 2 * planes * 32), bf16), vec,
         ((16, channels), f32)],
        conv_scratch + [pair, flat, (big, f32), ((planes, 32, depth), f32)],
        scalars, fields, lift_hi, lift_lo, w_in, gains[0], shift_bias[0:1], taps_f[0], w_point[0],
    )
    stream2, normed1, act1, slope1, stats2, consts1 = call(
        functools.partial(kernel_second, span, per_member),
        [(big, f32), (big, bf16), (big, bf16), (big, bf16), vec, vec],
        conv_scratch + [pair, flat],
        scalars, *group_parts(stats1), stream1, gains[1], shift_bias[1:2], taps_f[1], w_point[1],
    )
    prediction, misfit, sums2, out_raw, consts2 = call(
        functools.partial(kernel_out, span, per_member),
        [((rows, planes * 32), f32), ((rows, 2 * planes * 32), bf16), vec, vec, vec],
        [flat],
        scalars, *group_parts(stats2), stream2, gains[2], gathered, lift_out,
    )
    parts2 = group_parts(sums2)
    d_stream2, d_normed1, sums1, grads1 = call(
        functools.partial(kernel_back_second, span, share, cell_count),
        [(big, f32), (big, f32), vec, ((12, share, channels), f32)],
        conv_scratch + [pair, flat, flat] + grad_scratch,
        scalars, *parts2, stream2, consts2, gains[2], gains[1], misfit, lift_out, act1, slope1, normed1,
        taps_b[1], point_t[1],
    )
    parts1 = group_parts(sums1)
    d_stream1, pre_cot0, sums_b0, grads0 = call(
        functools.partial(kernel_back_first, span, share, cell_count),
        [(big, f32), (big, bf16), vec, ((12, share, channels), f32)],
        [conv_scratch[0], pair, flat] + grad_scratch,
        scalars, *parts1, consts1, d_stream2, d_normed1, normed1, gains[1], act0, slope0, normed0,
        point_t[0],
    )
    slab, sums0, in_part = call(
        functools.partial(kernel_last, span, cells_z),
        [((32, cells_z), f32), vec, vec],
        conv_scratch + [flat, flat, ((rows, planes * 32), f32), ((32, lanes), f32),
                        ((planes * 32, cells_z), f32)],
        scalars, pre_cot0, d_stream1, normed0, gains[0], consts0, gathered, lift_hi, lift_lo, taps_b[0],
        prediction,
    )
    all1 = shared_grads(grads1)
    all0 = shared_grads(grads0)

    tails = group_sum(jnp.concatenate([sums0, in_part, sums_b0, out_raw], axis=0))
    s_plain, s_cross, in_sum = tails[0], tails[1], tails[8:11]
    bias0, out_sum = tails[16], tails[24:27]
    s1 = sum(part[at : at + 8] for part in parts1 for at in range(0, part.shape[0], 8))
    s2 = sum(part[at : at + 8] for part in parts2 for at in range(0, part.shape[0], 8))
    inverse = consts0[1]
    m_plain = norm_gains[0] * s_plain / cell_count
    m_cross = norm_gains[0] * s_cross / cell_count
    mean_k = consts0[2:5, 0]
    c00, c01, c02, c11, c12, c22 = (consts0[5 + at, 0] for at in range(6))
    cov = jnp.stack([jnp.stack([c00, c01, c02]), jnp.stack([c01, c11, c12]), jnp.stack([c02, c12, c22])])
    offset = jnp.sum(w_in * (inverse * m_plain), axis=1)
    mix = jnp.sum(w_in[:, None, :] * (inverse * inverse * m_cross) * w_in[None, :, :], axis=2)
    pieces = slab.reshape(32, members, depth)[:24].transpose(1, 0, 2)
    landed = jnp.sum(lax.all_to_all(pieces, "gz", 0, 0), axis=0)
    landed = landed.reshape(6, 1, 4, depth)
    centered = noisy - mean_k[:, None, None, None]
    field_grad = landed[:3] - offset[:, None, None, None] - sum(
        mix[:, j, None, None, None] * centered[j][None] for j in range(3)
    )
    prediction_out = landed[3:]
    cross_in = jnp.sum(cov[:, :, None] * w_in[None, :, :], axis=1)
    in_raw = in_sum - cell_count * (
        mean_k[:, None] * (inverse * m_plain) + (inverse * inverse * m_cross) * cross_in
    )
    bias_all = jnp.stack([bias0, s1[2]])
    gain_all = jnp.stack([s_cross, s1[1], s2[1]])
    weights = jnp.stack([all0, all1]).astype(f32) * inv_area
    z_all = jnp.stack([weights[:, 9], weights[:, 4], weights[:, 10]], axis=1)
    xy_all = jnp.concatenate([weights[:, :4], weights[:, 5:9]], axis=1)
    time_back = jax.vjp(jax.nn.silu, time_raw)[1](jnp.sum(bias_all, axis=0))[0]
    grad_w_time = inv_area * jnp.outer(features, time_back)
    return (
        prediction_out,
        field_grad,
        inv_area * in_raw,
        grad_w_time,
        z_all,
        xy_all,
        weights[:, 11],
        inv_area * bias_all,
        inv_area * gain_all,
        inv_area * out_sum,
    )


def padded_2(cells, sides, width):
    for axis, dim in sides:
        count = lax.axis_size(axis)
        head = lax.slice_in_dim(cells, 0, width, axis=dim)
        tail = lax.slice_in_dim(cells, cells.shape[dim] - width, cells.shape[dim], axis=dim)
        cells = jnp.concatenate(
            [
                lax.ppermute(tail, axis, [(i, (i + 1) % count) for i in range(count)]),
                cells,
                lax.ppermute(head, axis, [((i + 1) % count, i) for i in range(count)]),
            ],
            axis=dim,
        )
    return cells


def passed_along(value, axis, steps):
    count = lax.axis_size(axis)
    pairs = [(source, (source + steps) % count) for source in range(count)]
    return lax.ppermute(value, axis, pairs)


def contract_cells(left, right):
    return lax.dot_general(
        left, right, (((0, 1, 2), (0, 1, 2)), ((), ())), preferred_element_type=jnp.float32
    )


def plane_tap(padded, shift_x, shift_y, rows_x, rows_y):
    return padded[1 + shift_x : 1 + shift_x + rows_x, 1 + shift_y : 1 + shift_y + rows_y]


def plane_pad(source):
    rimmed = padded_2(source, (("gx", 0),), 1)
    return jnp.pad(rimmed, ((0, 0), (1, 1), (0, 0), (0, 0)))


def slab_windows(source, dilation):
    slab_depth = source.shape[2]
    above = passed_along(source, "gz", -1)
    above_far = passed_along(source, "gz", -2)
    below = passed_along(source, "gz", 1)
    below_far = passed_along(source, "gz", 2)
    ahead_rows = jnp.concatenate([source, above, above_far], axis=2)
    behind_rows = jnp.concatenate([below_far, below, source], axis=2)
    upper = lax.dynamic_slice_in_dim(ahead_rows, dilation, slab_depth, 2)
    lower = lax.dynamic_slice_in_dim(behind_rows, 2 * slab_depth - dilation, slab_depth, 2)
    return (lower, upper)


def normalize(hidden, gains, cell_count):
    average = lax.psum(jnp.sum(hidden, axis=(0, 1, 2)), ("gz", "gx")) / cell_count
    centered = hidden - average
    spread = lax.psum(jnp.sum(centered * centered, axis=(0, 1, 2)), ("gz", "gx")) / cell_count
    inverse_std = lax.rsqrt(spread + eps_norm)
    whitened = (hidden - average) * inverse_std
    return ((whitened * gains).astype(jnp.bfloat16), whitened, inverse_std)


def norm_back(d_normed, whitened, inverse_std, gains, cell_count):
    scaled = d_normed * gains
    sum_grad, sum_cross = lax.psum(
        (jnp.sum(scaled, axis=(0, 1, 2)), jnp.sum(scaled * whitened, axis=(0, 1, 2))), ("gz", "gx")
    )
    d_hidden = inverse_std * (scaled - sum_grad / cell_count - whitened * (sum_cross / cell_count))
    return (d_hidden, jnp.sum(d_normed * whitened, axis=(0, 1, 2)))


def conv_forward(normed, dilation, weights_z, weights_xy):
    rows_x, rows_y = (normed.shape[0], normed.shape[1])
    lower, upper = slab_windows(normed, dilation)
    padded = plane_pad(normed)
    summed = jnp.dot(lower, weights_z[0], preferred_element_type=jnp.float32)
    summed = summed + jnp.dot(normed, weights_z[1], preferred_element_type=jnp.float32)
    summed = summed + jnp.dot(upper, weights_z[2], preferred_element_type=jnp.float32)
    for tap_number, (shift_x, shift_y) in enumerate(plane_offsets):
        summed = summed + jnp.dot(
            plane_tap(padded, shift_x, shift_y, rows_x, rows_y),
            weights_xy[tap_number],
            preferred_element_type=jnp.float32,
        )
    return summed


def conv_backward_split(pre_cot, normed, dilation, weights_z, weights_xy):
    rows_x, rows_y = (normed.shape[0], normed.shape[1])
    lower_cot, upper_cot = slab_windows(pre_cot, dilation)
    padded_cot = plane_pad(pre_cot)
    d_normed = jnp.dot(upper_cot, weights_z[0].T, preferred_element_type=jnp.float32)
    d_normed = d_normed + jnp.dot(pre_cot, weights_z[1].T, preferred_element_type=jnp.float32)
    d_normed = d_normed + jnp.dot(lower_cot, weights_z[2].T, preferred_element_type=jnp.float32)
    xy_terms = []
    for tap_number, (shift_x, shift_y) in enumerate(plane_offsets):
        shifted = plane_tap(padded_cot, -shift_x, -shift_y, rows_x, rows_y)
        d_normed = d_normed + jnp.dot(
            shifted, weights_xy[tap_number].T, preferred_element_type=jnp.float32
        )
        xy_terms.append(contract_cells(normed, shifted))
    z_terms = jnp.stack(
        [
            contract_cells(normed, upper_cot),
            contract_cells(normed, pre_cot),
            contract_cells(normed, lower_cot),
        ]
    )
    return (d_normed, z_terms, jnp.stack(xy_terms))


def per_device_split(
    clean_field,
    noise_field,
    timestep,
    dilations,
    w_in,
    w_time,
    w_z,
    w_xy,
    w_point,
    biases,
    norm_gains,
    w_out,
):
    layer_total = w_z.shape[0]
    rows_x, rows_y, slab_depth = (clean_field.shape[1], clean_field.shape[2], clean_field.shape[3])
    plane_cells = rows_x * lax.axis_size("gx") * slab_depth * lax.axis_size("gz")
    cell_count = float(plane_cells * rows_y)
    inv_area = 1.0 / plane_cells
    alpha_bar, features, time_raw, time_code = time_terms(timestep, w_time)
    noisy = jnp.sqrt(alpha_bar) * clean_field + jnp.sqrt(1.0 - alpha_bar) * noise_field
    stream = jnp.einsum("kxyz,kc->xyzc", noisy, w_in, precision=highest)
    saved = []
    for which_layer in range(layer_total):
        normed, whitened, inverse_std = normalize(stream, norm_gains[which_layer], cell_count)
        pre_act = conv_forward(normed, dilations[which_layer], w_z[which_layer], w_xy[which_layer])
        pre_act = pre_act + biases[which_layer] + time_code
        activated = jax.nn.gelu(pre_act).astype(jnp.bfloat16)
        saved.append((normed, whitened, inverse_std, pre_act, activated))
        stream = stream + jnp.dot(
            activated, w_point[which_layer], preferred_element_type=jnp.float32
        )
    out_normed, out_white, out_inverse = normalize(stream, norm_gains[layer_total], cell_count)
    prediction = jnp.einsum("xyzc,kc->kxyz", out_normed, w_out, preferred_element_type=jnp.float32)
    misfit = prediction - noise_field
    d_out = jnp.einsum("kxyz,kc->xyzc", misfit, w_out.astype(jnp.float32), precision=highest)
    out_raw = jnp.einsum(
        "kxyz,xyzc->kc", misfit, out_normed, precision=highest, preferred_element_type=jnp.float32
    )
    d_stream, out_gain_raw = norm_back(
        d_out, out_white, out_inverse, norm_gains[layer_total], cell_count
    )
    z_list, xy_list, point_list, bias_list, gain_list = ([], [], [], [], [])
    for which_layer in reversed(range(layer_total)):
        normed, whitened, inverse_std, pre_act, activated = saved[which_layer]
        stream_cot = d_stream.astype(jnp.bfloat16)
        point_raw = contract_cells(activated, stream_cot)
        d_act = jnp.dot(stream_cot, w_point[which_layer].T, preferred_element_type=jnp.float32)
        gelu_back = jax.vjp(jax.nn.gelu, pre_act)[1]
        pre_cot = gelu_back(d_act)[0].astype(jnp.bfloat16)
        bias_raw = jnp.sum(pre_cot, axis=(0, 1, 2), dtype=jnp.float32)
        d_normed, z_raw, xy_raw = conv_backward_split(
            pre_cot, normed, dilations[which_layer], w_z[which_layer], w_xy[which_layer]
        )
        d_back, gain_raw = norm_back(
            d_normed, whitened, inverse_std, norm_gains[which_layer], cell_count
        )
        d_stream = d_stream + d_back
        z_list.insert(0, z_raw)
        xy_list.insert(0, xy_raw)
        point_list.insert(0, point_raw)
        bias_list.insert(0, bias_raw)
        gain_list.insert(0, gain_raw)
    field_grad = jnp.einsum("xyzc,kc->kxyz", d_stream, w_in, precision=highest)
    in_raw = jnp.einsum("kxyz,xyzc->kc", noisy, d_stream, precision=highest)
    z_all, xy_all, point_all, bias_all, gain_all, in_raw, out_raw = lax.psum(
        (
            jnp.stack(z_list),
            jnp.stack(xy_list),
            jnp.stack(point_list),
            jnp.stack(bias_list),
            jnp.stack(gain_list + [out_gain_raw]),
            in_raw,
            out_raw,
        ),
        ("gz", "gx"),
    )
    time_back = jax.vjp(jax.nn.silu, time_raw)[1](jnp.sum(bias_all, axis=0))[0]
    grad_w_time = inv_area * jnp.outer(features, time_back)
    return (
        prediction,
        field_grad,
        inv_area * in_raw,
        grad_w_time,
        inv_area * z_all,
        inv_area * xy_all,
        inv_area * point_all,
        inv_area * bias_all,
        inv_area * gain_all,
        inv_area * out_raw,
    )


def per_device(*args):
    members, groups = lax.axis_size("gz"), lax.axis_size("gx")
    _, rows_x, rows_y, depth = args[0].shape
    small = rows_x == 1 and rows_y == 4 and members == 4 and groups == 8 and depth * members == 2 * REACH
    return per_device_grouped(*args) if small else per_device_split(*args)


def solution(mesh):
    return jax.shard_map(
        per_device,
        mesh=mesh,
        in_specs=(
            P(None, "gx", None, "gz"),
            P(None, "gx", None, "gz"),
            P(),
            P(),
            P(),
            P(),
            P(),
            P(),
            P(),
            P(),
            P(),
            P(),
        ),
        out_specs=(
            P(None, "gx", None, "gz"),
            P(None, "gx", None, "gz"),
            P(),
            P(),
            P(),
            P(),
            P(),
            P(),
            P(),
            P(),
        ),
        check_vma=False,
    )
```

```python
import functools
import math

import jax
import jax.numpy as jnp
from jax import lax
from jax.experimental import pallas as pl
from jax.experimental.pallas import tpu as pltpu
from jax.sharding import PartitionSpec as P

STEPS = 1000
REACH = 256
RIM = 4
TILE = 16
LIMITS = (8, 24, 24, 16, 28, 28, 28)

eps_norm = 1e-05
highest = lax.Precision.HIGHEST
bf16 = jnp.bfloat16
f32 = jnp.float32
plane_offsets = ((-1, -1), (-1, 0), (-1, 1), (0, -1), (0, 1), (1, -1), (1, 0), (1, 1))


def time_terms(timestep, w_time):
    moment = timestep[0].astype(jnp.float32)
    half_width = w_time.shape[0] // 2
    alpha_bar = jnp.cos(0.5 * math.pi * (moment + 0.5) / STEPS) ** 2
    ladder = jnp.exp(-math.log(10000.0) * jnp.arange(half_width, dtype=jnp.float32) / half_width)
    angles = moment * ladder
    features = jnp.concatenate([jnp.sin(angles), jnp.cos(angles)])
    time_raw = jnp.dot(features, w_time, precision=highest)
    return (alpha_bar, features, time_raw, jax.nn.silu(time_raw))


def mm(left, right):
    return lax.dot_general(left, right, (((1,), (0,)), ((), ())), preferred_element_type=f32)


def mm_nt(left, right):
    return lax.dot_general(left, right, (((1,), (1,)), ((), ())), preferred_element_type=f32)


def mm_tn(left, right):
    return lax.dot_general(left, right, (((0,), (0,)), ((), ())), preferred_element_type=f32)


def halves(value):
    high = value.astype(bf16)
    return high, (value - high.astype(f32)).astype(bf16)


def wide(vector):
    return jnp.concatenate([vector] * 4, axis=1)


def folded(vector):
    channels = vector.shape[1] // 4
    return sum(vector[:, y * channels : (y + 1) * channels] for y in range(4))


class Place:
    def __init__(self, sc, rows):
        self.rows = rows
        self.members = lax.axis_size("gz")
        self.member = lax.axis_index("gz")
        self.small = jnp.minimum(sc[0], sc[1])
        self.coarse = self.small >= self.members
        tiles = rows // TILE
        self.tiles = tiles
        self.stride = jnp.where(self.coarse, tiles - 1, tiles)
        self.span = REACH // self.members + 2 * RIM
        far = jnp.where(self.coarse, REACH // self.members, self.span)
        near = jnp.where(self.coarse, self.small // self.members, 1)
        self.steps = [jnp.where(sc[l] == REACH, far, near) for l in range(2)]

    def index(self, shape):
        row = lax.broadcasted_iota(jnp.int32, shape, 0)
        return lax.rem(row, TILE) * self.stride + row // TILE, row // TILE

    def own(self, shape):
        place, tile = self.index(shape)
        inside = lax.rem(place, self.span)
        near = ((inside >= RIM) & (inside < self.span - RIM)).astype(jnp.int32)
        far = (tile < self.tiles - 1).astype(jnp.int32)
        return jnp.where(self.coarse, far, near) == 1

    def pick(self, cells_z):
        shape = (self.rows, cells_z)
        place, _ = self.index(shape)
        residues = jnp.minimum(self.small, self.members)
        part, start = self.member // residues, lax.rem(self.member, residues)
        period = place // self.span
        inside = place - period * self.span - RIM + part * (REACH // self.members)
        near = start + residues * inside + period * REACH
        z = jnp.where(self.coarse, place * self.members + self.member, near)
        z = lax.rem(z + 2 * cells_z, cells_z)
        return z == lax.broadcasted_iota(jnp.int32, shape, 1)


def build_taps(block_of, taps, taps_z):
    channels = taps_z.shape[-1] // 2
    zero = jnp.zeros((channels, channels), bf16)
    for i in range(3):
        for j in range(3):
            block = block_of(i, j)
            for q in range(2):
                for side in range(2):
                    y_in = 2 * q + side + j - 1
                    if 0 <= y_in < 4:
                        taps[
                            q,
                            i,
                            y_in * channels : (y_in + 1) * channels,
                            side * channels : (side + 1) * channels,
                        ] = block
        for q in range(2):
            for side in range(2):
                for y_in in range(4):
                    if abs(y_in - 2 * q - side) > 1:
                        taps[
                            q,
                            i,
                            y_in * channels : (y_in + 1) * channels,
                            side * channels : (side + 1) * channels,
                        ] = zero
    for m in range(2):
        build_pair(block_of(3, m), taps_z, m)


def build_pair(block, target, m):
    channels = block.shape[-1]
    zero = jnp.zeros((channels, channels), bf16)
    target[m, :channels, :channels] = block
    target[m, channels:, channels:] = block
    target[m, :channels, channels:] = zero
    target[m, channels:, :channels] = zero


def forward_blocks(w_z, w_xy, layer):
    def block_of(i, j):
        if i == 3:
            return w_z[layer, 2 * j]
        at = i * 3 + j
        return w_z[layer, 1] if at == 4 else w_xy[layer, at - (at > 4)]

    return block_of


def backward_blocks(w_back, layer):
    return lambda i, j: w_back[layer, i * 3 + j]


def kernel_prepare(w_z, w_xy, w_point, w_in, w_out, w_back, point_back, lift_in, lift_out):
    for layer in range(2):
        forward = forward_blocks(w_z, w_xy, layer)
        for i in range(3):
            for j in range(3):
                w_back[layer, i * 3 + j] = forward(2 - i, 2 - j).T
        for m in range(2):
            w_back[layer, 9 + m] = forward(3, 1 - m).T
        point_back[layer] = w_point[layer].T
    whole = spread_rows(w_in[...], 0)
    high, low = halves(whole)
    lift_in[0:32] = high
    lift_in[32:64] = high
    lift_in[64:96] = low
    lift_in[96:128] = jnp.zeros_like(low)
    high = spread_rows(w_out[...].astype(f32), 3).astype(bf16)
    lift_out[0:32] = high
    lift_out[32:64] = high
    lift_out[64:96] = jnp.zeros_like(high)
    lift_out[96:128] = jnp.zeros_like(high)


def spread_rows(weights, first):
    channels = weights.shape[1]
    zero = jnp.zeros((1, channels), f32)
    rows = [jnp.zeros((1, 4 * channels), f32)] * 32
    for k in range(3):
        for y in range(4):
            parts = [weights[k : k + 1] if at == y else zero for at in range(4)]
            rows[(first + k) * 4 + y] = jnp.concatenate(parts, axis=1)
    return jnp.concatenate(rows, axis=0)


def fill_rims(padded, planes):
    padded[0] = padded[planes]
    padded[planes + 1] = padded[1]


def fill_shifted(place, layer, padded, shifted, planes):
    step, stride = place.steps[layer], place.stride
    for tile in range(place.tiles):
        for way in range(2):
            at = tile - step if way == 0 else tile + step
            moved = at + TILE * stride
            source = lax.rem(moved, stride)
            turn = lax.rem(2 * TILE - moved // stride, TILE)
            rows = padded[1 : planes + 1, pl.ds(pl.multiple_of(source * TILE, TILE), TILE), :]
            rows = pltpu.roll(rows.astype(f32), turn, 1)
            shifted[way, :, tile * TILE : (tile + 1) * TILE, :] = rows.astype(bf16)


def conv_half(padded, shifted, taps, taps_z, x0, count, q):
    rows, lanes = padded.shape[1:]
    half = lanes // 2
    total = None
    for i in range(3):
        part = mm(padded[pl.ds(x0 + i, count)].reshape(count * rows, lanes), taps[q, i])
        total = part if total is None else total + part
    for m in range(2):
        source = shifted[m, pl.ds(x0, count), :, q * half : (q + 1) * half]
        total = total + mm(source.reshape(count * rows, half), taps_z[m])
    return total


def gelu_pair(value):
    scale = math.sqrt(2.0 / math.pi)
    square = value * value
    bent = jnp.tanh(value * (scale + (scale * 0.044715) * square))
    half = 0.5 + 0.5 * bent
    slope = half + value * (0.5 - 0.5 * (bent * bent)) * (scale + (3.0 * 0.044715 * scale) * square)
    return value * half, slope


def members_of(parts):
    found = []
    for part in parts:
        for at in range(0, part.shape[0], 8):
            found.append(part[at : at + 8])
    return found


def merged_stats(parts, per_member):
    found = members_of(parts)
    mean = sum(one[0:1] for one in found) / (per_member * len(found))
    spread = sum(one[1:2] for one in found)
    for one in found:
        gap = one[0:1] / per_member - mean
        spread = spread + per_member * gap * gap
    return mean, lax.rsqrt(spread / (per_member * len(found)) + eps_norm)


def put_rows(ref, *vectors):
    rows = list(vectors)
    rows += [jnp.zeros((1, ref.shape[1]), f32)] * (ref.shape[0] - len(rows))
    ref[...] = jnp.concatenate(rows, axis=0)


def masked_total(mask, value):
    return folded(jnp.sum(jnp.where(mask, value, 0.0), axis=0, keepdims=True))


def layer_forward(place, layer, padded, shifted, taps, taps_z, pair, w_z, w_xy, wp, shift_bias, old,
                  stream, act, slope, stats, acc, per_member):
    planes, rows, lanes = stream.shape
    half = lanes // 2
    count = planes // 2
    build_taps(forward_blocks(w_z, w_xy, layer), taps, taps_z)
    build_pair(wp[layer], pair, 0)
    fill_rims(padded, planes)
    fill_shifted(place, layer, padded, shifted, planes)
    acc[...] = jnp.zeros_like(acc)
    bias = wide(shift_bias[layer : layer + 1, :])[:, :half]

    def body(step, carry):
        x0 = step * count
        for q in range(2):
            side = slice(q * half, (q + 1) * half)
            pre = conv_half(padded, shifted, taps, taps_z, x0, count, q) + bias
            value, grad = gelu_pair(pre)
            value = value.astype(bf16)
            act[pl.ds(x0, count), :, side] = value.reshape(count, rows, half)
            slope[pl.ds(x0, count), :, side] = grad.astype(bf16).reshape(count, rows, half)
            branch = mm(value, pair[0]).reshape(count, rows, half)
            new = old[pl.ds(x0, count), :, side] + branch
            stream[pl.ds(x0, count), :, side] = new
            acc[:, side] += jnp.sum(new, axis=0)
        return carry

    lax.fori_loop(0, planes // count, body, 0)
    mask = place.own((rows, lanes))
    total = masked_total(mask, acc[...])
    mean = wide(total / per_member)
    spread = jnp.zeros((rows, lanes), f32)
    for x in range(planes):
        gap = stream[x] - mean
        spread = spread + gap * gap
    put_rows(stats, total, masked_total(mask, spread))


def kernel_first(cells_z, per_member, sc, fields, lift_in, w_in, gains, shift_bias, w_z, w_xy, wp,
                 stream, normed, act, slope, gathered, stats, consts,
                 padded, shifted, taps, taps_z, pair, acc, old, source):
    planes, rows, lanes = stream.shape
    channels = lanes // 4
    depth = fields.shape[2]
    place = Place(sc, rows)
    cell_count = float(planes * 4 * cells_z)
    comps = [fields[:, 4 * k : 4 * k + 4, :] for k in range(3)]

    def all_sum(value):
        value = jnp.sum(jnp.sum(value, axis=0), axis=0, keepdims=True)
        return jnp.sum(value, axis=1, keepdims=True)

    means = [all_sum(comp) / cell_count for comp in comps]
    gaps = [comp - mean[None] for comp, mean in zip(comps, means)]
    covs = {}
    for j in range(3):
        for k in range(j, 3):
            covs[j, k] = all_sum(gaps[j] * gaps[k]) / cell_count
    rows_in = [w_in[k : k + 1, :] for k in range(3)]
    mean_c = sum(means[k] * rows_in[k] for k in range(3))
    var_c = jnp.zeros((1, channels), f32)
    for (j, k), cov in covs.items():
        var_c = var_c + (1.0 if j == k else 2.0) * cov * (rows_in[j] * rows_in[k])
    inv_c = lax.rsqrt(jnp.maximum(var_c, 0.0) + eps_norm)
    flat = [jnp.broadcast_to(value, (1, channels)) for value in means + list(covs.values())]
    put_rows(consts, mean_c, inv_c, *flat)
    blank = jnp.zeros((8, depth), f32)
    for slab in range(cells_z // depth):
        at = slice(slab * depth, (slab + 1) * depth)
        for x in range(planes):
            high, low = halves(jnp.concatenate([fields[slab * planes + x], blank], axis=0))
            source[x, 0:32, at] = high
            source[x, 32:64, at] = low
            source[x, 64:96, at] = high
            source[x, 96:128, at] = jnp.zeros_like(high)
    pick = place.pick(cells_z).astype(f32).astype(bf16)
    scale = wide(inv_c * gains[0:1, :])
    mean_w = wide(mean_c)
    for x in range(planes):
        gathered[x] = mm_nt(pick, source[x]).astype(bf16)
    for x0 in range(0, planes, planes // 2):
        part = slice(x0, x0 + planes // 2)
        value = mm(gathered[part].reshape(planes // 2 * rows, 128), lift_in[...])
        unit = ((value - mean_w) * scale).astype(bf16).reshape(planes // 2, rows, lanes)
        old[part] = value.reshape(planes // 2, rows, lanes)
        padded[x0 + 1 : x0 + 1 + planes // 2] = unit
        normed[part] = unit
    layer_forward(place, 0, padded, shifted, taps, taps_z, pair, w_z, w_xy, wp, shift_bias, old, stream,
                  act, slope, stats, acc, per_member)


def kernel_second(per_member, sc, *refs):
    parts, refs = refs[:3], refs[3:]
    (old, gains, shift_bias, w_z, w_xy, wp, stream, normed, act, slope, stats, consts,
     padded, shifted, taps, taps_z, pair, acc) = refs
    planes, rows, _ = stream.shape
    place = Place(sc, rows)
    mean, inverse = merged_stats(parts, per_member)
    put_rows(consts, mean, inverse)
    mean_w, scale = wide(mean), wide(inverse * gains[1:2, :])
    for x in range(planes):
        unit = ((old[x] - mean_w) * scale).astype(bf16)
        padded[x + 1] = unit
        normed[x] = unit
    layer_forward(place, 1, padded, shifted, taps, taps_z, pair, w_z, w_xy, wp, shift_bias, old, stream,
                  act, slope, stats, acc, per_member)


def kernel_out(per_member, sc, *refs):
    parts, refs = refs[:3], refs[3:]
    stream, gains, gathered, lift_out, prediction, misfit, sums, w_out_raw, consts, unit = refs
    planes, rows, lanes = stream.shape
    place = Place(sc, rows)
    mean, inverse = merged_stats(parts, per_member)
    put_rows(consts, mean, inverse)
    mean_w, inv_w, gain_w = wide(mean), wide(inverse), wide(gains[2:3, :])
    scale = inv_w * gain_w
    for x in range(planes):
        unit[x] = ((stream[x] - mean_w) * scale).astype(bf16)
    row = lax.broadcasted_iota(jnp.int32, (128, 128), 0)
    col = lax.broadcasted_iota(jnp.int32, (128, 128), 1)
    slot = lax.rem(col, 32)
    used = (col < 64) & (slot >= 12) & (slot < 24)
    take = (used & ((row == slot) | (row == slot + 32))).astype(f32).astype(bf16)
    total = mm_nt(unit[...].reshape(planes * rows, lanes), lift_out[...])
    noise = mm(gathered[...].reshape(planes * rows, 128), take)
    gap = total - noise
    high, low = halves(gap)
    lane = lax.broadcasted_iota(jnp.int32, gap.shape, 1)
    both = jnp.where(lane < 32, high.astype(f32), low.astype(f32)).astype(bf16)
    misfit[...] = both.reshape(planes, rows, 128)
    for x in range(planes):
        @pl.when(lax.axis_index("gx") == x)
        def _(x=x):
            prediction[...] = total[x * rows : (x + 1) * rows]
    plain = jnp.zeros((rows, lanes), f32)
    cross = jnp.zeros((rows, lanes), f32)
    for x0 in range(0, planes, planes // 2):
        part = slice(x0 * rows, (x0 + planes // 2) * rows)
        d_out = mm(both[part], lift_out[...]).reshape(planes // 2, rows, lanes)
        for x in range(planes // 2):
            plain = plain + d_out[x]
            cross = cross + d_out[x] * ((stream[x0 + x] - mean_w) * inv_w)
    own = place.own((rows, 128))
    kept = jnp.concatenate([jnp.where(own, misfit[x].astype(f32), 0.0) for x in range(planes)], axis=0)
    raw = mm_tn(kept.astype(bf16), unit[...].reshape(planes * rows, lanes))
    mask = place.own((rows, lanes))
    put_rows(sums, masked_total(mask, plain), masked_total(mask, cross))
    put_rows(w_out_raw, *by_component(raw[0:32] + raw[32:64], 3))


def by_component(raw, first):
    channels = raw.shape[1] // 4
    found = []
    for k in range(first, first + 3):
        found.append(
            sum(raw[k * 4 + y : k * 4 + y + 1, y * channels : (y + 1) * channels] for y in range(4))
        )
    return found


def branch_backward(planes, d_stream_of, pair, slope, padded, scot, bias_acc):
    rows, lanes = padded.shape[1:]
    half = lanes // 2
    count = planes // 2

    def body(step, carry):
        x0 = step * count
        for t in range(count):
            scot[x0 + t] = d_stream_of(x0 + t).astype(bf16)
        for q in range(2):
            side = slice(q * half, (q + 1) * half)
            cot = scot[pl.ds(x0, count), :, side].reshape(count * rows, half)
            d_act = mm(cot, pair[0]).reshape(count, rows, half)
            pre = (d_act * slope[pl.ds(x0, count), :, side].astype(f32)).astype(bf16)
            padded[pl.ds(x0 + 1, count), :, side] = pre
            bias_acc[:, side] += jnp.sum(pre.astype(f32), axis=0)
        return carry

    lax.fori_loop(0, planes // count, body, 0)


def weight_grads(place, planes, padded, shifted, scot, normed, act, grads, picked, share):
    rows, lanes = padded.shape[1:]
    channels = lanes // 4
    wide_share = 4 * share
    row = lax.broadcasted_iota(jnp.int32, (lanes, wide_share), 0)
    col = lax.broadcasted_iota(jnp.int32, (lanes, wide_share), 1)
    hit = (row // channels == col // share) & (
        lax.rem(row, channels) == lax.rem(col, share) + lax.axis_index("gx") * share
    )
    choose = hit.astype(f32).astype(bf16)
    mask = jnp.concatenate([place.own((rows, wide_share))] * planes, axis=0)

    def turned(source):
        got = mm(source[...].reshape(planes * rows, lanes), choose)
        return jnp.where(mask, got, 0.0).astype(bf16)

    def add_blocks(raw, j):
        return sum(
            raw[(y + j) * share : (y + j + 1) * share, y * channels : (y + 1) * channels]
            for y in range(4)
            if 0 <= y + j < 4
        )

    left = turned(normed)
    for i in range(3):
        raw = mm_tn(left, padded[2 - i : 2 - i + planes].reshape(planes * rows, lanes))
        for j in range(3):
            grads[i * 3 + j] = add_blocks(raw, j - 1)
    for m in range(2):
        raw = mm_tn(left, shifted[1 - m].reshape(planes * rows, lanes))
        grads[9 + m] = add_blocks(raw, 0)
    raw = mm_tn(turned(act), scot[...].reshape(planes * rows, lanes))
    grads[11] = add_blocks(raw, 0)


def conv_backward(planes, padded, shifted, taps, taps_z, emit):
    rows, lanes = padded.shape[1:]
    count = planes // 2

    def body(step, carry):
        x0 = step * count
        for q in range(2):
            emit(x0, count, q, conv_half(padded, shifted, taps, taps_z, x0, count, q))
        return carry

    lax.fori_loop(0, planes // count, body, 0)


def kernel_back_second(share, cell_count, sc, *refs):
    parts, refs = refs[:3], refs[3:]
    (stream, out_consts, gains, misfit, lift_out, act, slope, normed, w_back, point_back,
     d_stream, d_normed, sums, grads,
     padded, shifted, taps, taps_z, pair, acc, acc2, scot) = refs
    planes, rows, lanes = stream.shape
    half = lanes // 2
    place = Place(sc, rows)
    sums_out = sum(members_of(parts))
    gain_w = wide(gains[2:3, :])
    mean_w, inv_w = wide(out_consts[0:1]), wide(out_consts[1:2])
    m_plain = gain_w * wide(sums_out[0:1]) / cell_count
    m_cross = gain_w * wide(sums_out[1:2]) / cell_count
    build_pair(point_back[1], pair, 0)
    build_taps(backward_blocks(w_back, 1), taps, taps_z)
    acc[...] = jnp.zeros_like(acc)

    def d_stream_of(x):
        d_out = mm(misfit[x], lift_out[...])
        white = (stream[x] - mean_w) * inv_w
        value = inv_w * (gain_w * d_out - m_plain - white * m_cross)
        d_stream[x] = value
        return value

    branch_backward(planes, d_stream_of, pair, slope, padded, scot, acc)
    mask = place.own((rows, lanes))
    s_bias = masked_total(mask, acc[...])
    acc[...] = jnp.zeros_like(acc)
    acc2[...] = jnp.zeros_like(acc2)
    fill_rims(padded, planes)
    fill_shifted(place, 1, padded, shifted, planes)

    def emit(x0, count, q, value):
        side = slice(q * half, (q + 1) * half)
        value = value.reshape(count, rows, half)
        d_normed[pl.ds(x0, count), :, side] = value
        acc[:, side] += jnp.sum(value, axis=0)
        acc2[:, side] += jnp.sum(value * normed[pl.ds(x0, count), :, side].astype(f32), axis=0)

    conv_backward(planes, padded, shifted, taps, taps_z, emit)
    s_plain = masked_total(mask, acc[...])
    s_cross = masked_total(mask, acc2[...]) / gains[1:2, :]
    put_rows(sums, s_plain, s_cross, s_bias)
    weight_grads(place, planes, padded, shifted, scot, normed, act, grads, None, share)


def kernel_back_first(share, cell_count, sc, *refs):
    parts, refs = refs[:3], refs[3:]
    (consts, d_next, d_normed, normed_next, gains, act, slope, normed, point_back,
     d_stream, pre_cot, sums, grads,
     padded, shifted, pair, acc, scot) = refs
    planes, rows, lanes = d_next.shape
    place = Place(sc, rows)
    sums_in = sum(members_of(parts))
    gain_w = wide(gains[1:2, :])
    inv_w = wide(consts[1:2])
    m_plain = gain_w * wide(sums_in[0:1]) / cell_count
    m_cross = wide(sums_in[1:2]) / cell_count
    build_pair(point_back[0], pair, 0)
    acc[...] = jnp.zeros_like(acc)

    def d_stream_of(x):
        back = gain_w * d_normed[x] - m_plain - normed_next[x].astype(f32) * m_cross
        value = d_next[x] + inv_w * back
        d_stream[x] = value
        return value

    branch_backward(planes, d_stream_of, pair, slope, padded, scot, acc)
    put_rows(sums, masked_total(place.own((rows, lanes)), acc[...]))
    fill_rims(padded, planes)
    fill_shifted(place, 0, padded, shifted, planes)
    for x in range(planes):
        pre_cot[x] = padded[x + 1]
    weight_grads(place, planes, padded, shifted, scot, normed, act, grads, None, share)


def kernel_last(cells_z, sc, pre_cot, d_stream, normed, gains, consts, gathered, lift_in, w_back,
                prediction, ready, slab, sums, in_raw,
                padded, shifted, taps, taps_z, acc, acc2, high, low):
    planes, rows, lanes = d_stream.shape
    half = lanes // 2
    place = Place(sc, rows)
    for x in range(planes):
        padded[x + 1] = pre_cot[x]
    fill_rims(padded, planes)
    fill_shifted(place, 0, padded, shifted, planes)
    build_taps(backward_blocks(w_back, 0), taps, taps_z)
    acc[...] = jnp.zeros_like(acc)
    acc2[...] = jnp.zeros_like(acc2)
    scale = wide(consts[1:2] * gains[0:1, :])

    def emit(x0, count, q, value):
        side = slice(q * half, (q + 1) * half)
        part = pl.ds(x0, count)
        value = value.reshape(count, rows, half)
        acc[:, side] += jnp.sum(value, axis=0)
        acc2[:, side] += jnp.sum(value * normed[part, :, side].astype(f32), axis=0)
        full = d_stream[part, :, side] + value * scale[:, side]
        first, second = halves(full)
        high[part, :, side] = first
        low[part, :, side] = second

    conv_backward(planes, padded, shifted, taps, taps_z, emit)
    mask = place.own((rows, lanes))
    s_plain = masked_total(mask, acc[...])
    s_cross = masked_total(mask, acc2[...]) / gains[0:1, :]
    put_rows(sums, s_plain, s_cross)
    own = place.own((rows, 128))
    kept = jnp.concatenate([jnp.where(own, gathered[x].astype(f32), 0.0) for x in range(planes)], axis=0)
    kept = kept.astype(bf16)
    raw = mm_tn(kept, high[...].reshape(planes * rows, lanes))
    raw_low = mm_tn(kept, low[...].reshape(planes * rows, lanes))
    put_rows(in_raw, *by_component(raw[0:32] + raw[32:64] + raw_low[0:32], 0))
    here = lax.axis_index("gx")
    lane = lax.broadcasted_iota(jnp.int32, (rows, 128), 1)
    field = mm_nt(high[here], lift_in[...]) + jnp.where(lane < 32, mm_nt(low[here], lift_in[...]), 0.0)
    field = jnp.where((lane >= 32) & (lane < 64), 0.0, field)
    field = field + jnp.where((lane >= 12) & (lane < 24), prediction[...], 0.0)
    pick = (place.pick(cells_z) & place.own((rows, cells_z))).astype(f32).astype(bf16)
    first, second = halves(field)
    out = mm_tn(first, pick) + mm_tn(second, pick)
    slab[...] = out[0:32] + out[64:96]


def call(kernel, outs, scratch, flops, limit, *args, scalars=True, loose=()):
    spec = pl.BlockSpec(memory_space=pltpu.VMEM)
    specs = [pl.BlockSpec(memory_space=pltpu.SMEM)] * scalars + [spec] * (len(args) - scalars)
    for at in loose:
        specs[at] = pl.BlockSpec(memory_space=pl.ANY)
    return pl.pallas_call(
        kernel,
        out_shape=[jax.ShapeDtypeStruct(shape, dtype) for shape, dtype in outs],
        in_specs=specs,
        out_specs=[spec] * len(outs),
        scratch_shapes=[pltpu.VMEM(shape, dtype) for shape, dtype in scratch],
        compiler_params=pltpu.CompilerParams(vmem_limit_bytes=limit * 2**20),
        cost_estimate=pl.CostEstimate(flops=flops, bytes_accessed=2**23, transcendentals=0),
    )(*args)


def swapped(value, axis, bit):
    count = lax.axis_size(axis)
    return lax.ppermute(value, axis, [(i, i ^ bit) for i in range(count)])


def group_parts(value):
    beside = swapped(value, "gz", 1)
    pair = jnp.concatenate([value, beside], axis=0)
    return (value, beside, swapped(pair, "gz", 2))


def group_sum(value):
    value = value + swapped(value, "gz", 1)
    return value + swapped(value, "gz", 2)


def group_grads(grads):
    members = lax.axis_size("gz")
    taps, share, channels = grads.shape
    pieces = grads.reshape(members, (taps // members) * share, channels)
    return jnp.sum(lax.all_to_all(pieces, "gz", 0, 0), axis=0).astype(bf16)


def all_grads(mine, share):
    members = lax.axis_size("gz")
    total = members * lax.axis_size("gx")
    every = lax.all_to_all(
        jnp.broadcast_to(mine[None], (total,) + mine.shape), ("gz", "gx"), 0, 0
    )
    return every.reshape(members, total // members, mine.shape[0] // share, share, mine.shape[1])


def laid_out(every):
    members, groups, taps, share, channels = every.shape
    return every.transpose(0, 2, 1, 3, 4).reshape(members * taps, groups * share, channels)


def per_device_grouped(clean_field, noise_field, timestep, dilations, w_in, w_time, w_z, w_xy, w_point,
                       biases, norm_gains, w_out):
    members, groups = lax.axis_size("gz"), lax.axis_size("gx")
    depth = clean_field.shape[3]
    planes, cells_z = groups, depth * members
    channels = w_in.shape[1]
    lanes = 4 * channels
    rows = (cells_z // REACH) * (REACH // members + 2 * RIM)
    share = channels // groups
    per_member = float(planes * 4 * depth)
    cell_count = per_member * members
    inv_area = 4.0 / cell_count

    alpha_bar, features, time_raw, time_code = time_terms(timestep, w_time)
    noisy = jnp.sqrt(alpha_bar) * clean_field + jnp.sqrt(1.0 - alpha_bar) * noise_field
    block = jnp.concatenate([noisy, noise_field], axis=0).reshape(24, depth)
    total = members * groups
    fields = lax.all_to_all(
        jnp.broadcast_to(block[None], (total, 24, depth)), ("gz", "gx"), 0, 0
    )
    shift_bias = biases + time_code

    big = (planes, rows, lanes)
    vec = ((8, channels), f32)
    thin = ((planes, rows, 128), bf16)
    lift = ((128, lanes), bf16)
    conv_scratch = [
        ((planes + 2, rows, lanes), bf16),
        ((2,) + big, bf16),
        ((2, 3, lanes, lanes // 2), bf16),
        ((2, lanes // 2, lanes // 2), bf16),
    ]
    pair = ((1, lanes // 2, lanes // 2), bf16)
    flat = ((rows, lanes), f32)
    grad_out = ((12, share, channels), f32)

    w_back, point_back, lift_in, lift_out = call(
        kernel_prepare,
        [((2, 11, channels, channels), bf16), ((2, channels, channels), bf16), lift, lift],
        [], 10**8, LIMITS[0], w_z, w_xy, w_point, w_in, w_out, scalars=False,
    )
    stream1, normed0, act0, slope0, gathered, stats1, consts0 = call(
        functools.partial(kernel_first, cells_z, per_member),
        [(big, f32), (big, bf16), (big, bf16), (big, bf16), thin, vec, ((16, channels), f32)],
        conv_scratch + [pair, flat, (big, f32), ((planes, 128, cells_z), bf16)],
        4 * 10**9, LIMITS[1],
        dilations, fields, lift_in, w_in, norm_gains, shift_bias, w_z, w_xy, w_point,
    )
    stream2, normed1, act1, slope1, stats2, consts1 = call(
        functools.partial(kernel_second, per_member),
        [(big, f32), (big, bf16), (big, bf16), (big, bf16), vec, vec],
        conv_scratch + [pair, flat],
        4 * 10**9, LIMITS[2],
        dilations, *group_parts(stats1), stream1, norm_gains, shift_bias, w_z, w_xy, w_point,
    )
    prediction, misfit, sums2, out_raw, consts2 = call(
        functools.partial(kernel_out, per_member),
        [((rows, 128), f32), thin, vec, vec, vec],
        [(big, bf16)],
        10**9, LIMITS[3],
        dilations, *group_parts(stats2), stream2, norm_gains, gathered, lift_out,
    )
    parts2 = group_parts(sums2)
    d_stream2, d_normed1, sums1, grads1 = call(
        functools.partial(kernel_back_second, share, cell_count),
        [(big, f32), (big, f32), vec, grad_out],
        conv_scratch + [pair, flat, flat, (big, bf16)],
        6 * 10**9, LIMITS[4],
        dilations, *parts2, stream2, consts2, norm_gains, misfit, lift_out, act1, slope1, normed1,
        w_back, point_back,
    )
    parts1 = group_parts(sums1)
    d_stream1, pre_cot0, sums_b0, grads0 = call(
        functools.partial(kernel_back_first, share, cell_count),
        [(big, f32), (big, bf16), vec, grad_out],
        conv_scratch[:2] + [pair, flat, (big, bf16)],
        4 * 10**9, LIMITS[5],
        dilations, *parts1, consts1, d_stream2, d_normed1, normed1, norm_gains, act0, slope0, normed0,
        point_back,
    )
    mine1 = group_grads(grads1)
    slab, sums0, in_part = call(
        functools.partial(kernel_last, cells_z),
        [((32, cells_z), f32), vec, vec],
        conv_scratch + [flat, flat, (big, bf16), (big, bf16)],
        4 * 10**9, LIMITS[6],
        dilations, pre_cot0, d_stream1, normed0, norm_gains, consts0, gathered, lift_in, w_back, prediction,
        mine1, loose=(10,),
    )
    all1 = laid_out(all_grads(mine1, share))
    all0 = laid_out(all_grads(group_grads(grads0), share))

    tails = group_sum(jnp.concatenate([sums0, in_part, sums_b0, out_raw], axis=0))
    s_plain, s_cross, in_sum = tails[0], tails[1], tails[8:11]
    bias0, out_sum = tails[16], tails[24:27]
    s1 = sum(members_of(parts1))
    s2 = sum(members_of(parts2))
    inverse = consts0[1]
    m_plain = norm_gains[0] * s_plain / cell_count
    m_cross = norm_gains[0] * s_cross / cell_count
    mean_k = consts0[2:5, 0]
    c00, c01, c02, c11, c12, c22 = (consts0[5 + at, 0] for at in range(6))
    cov = jnp.stack([jnp.stack([c00, c01, c02]), jnp.stack([c01, c11, c12]), jnp.stack([c02, c12, c22])])
    offset = jnp.sum(w_in * (inverse * m_plain), axis=1)
    mix = jnp.sum(w_in[:, None, :] * (inverse * inverse * m_cross) * w_in[None, :, :], axis=2)
    pieces = slab.reshape(32, members, depth)[:24].transpose(1, 0, 2)
    landed = jnp.sum(lax.all_to_all(pieces, "gz", 0, 0), axis=0)
    landed = landed.reshape(6, 1, 4, depth)
    centered = noisy - mean_k[:, None, None, None]
    field_grad = landed[:3] - offset[:, None, None, None] - sum(
        mix[:, j, None, None, None] * centered[j][None] for j in range(3)
    )
    prediction_out = landed[3:]
    cross_in = jnp.sum(cov[:, :, None] * w_in[None, :, :], axis=1)
    in_raw = in_sum - cell_count * (
        mean_k[:, None] * (inverse * m_plain) + (inverse * inverse * m_cross) * cross_in
    )
    bias_all = jnp.stack([bias0, s1[2]])
    gain_all = jnp.stack([s_cross, s1[1], s2[1]])
    weights = jnp.stack([all0, all1]).astype(f32) * inv_area
    z_all = jnp.stack([weights[:, 9], weights[:, 4], weights[:, 10]], axis=1)
    xy_all = jnp.concatenate([weights[:, :4], weights[:, 5:9]], axis=1)
    time_back = jax.vjp(jax.nn.silu, time_raw)[1](jnp.sum(bias_all, axis=0))[0]
    grad_w_time = inv_area * jnp.outer(features, time_back)
    return (
        prediction_out,
        field_grad,
        inv_area * in_raw,
        grad_w_time,
        z_all,
        xy_all,
        weights[:, 11],
        inv_area * bias_all,
        inv_area * gain_all,
        inv_area * out_sum,
    )


def padded_2(cells, sides, width):
    for axis, dim in sides:
        count = lax.axis_size(axis)
        head = lax.slice_in_dim(cells, 0, width, axis=dim)
        tail = lax.slice_in_dim(cells, cells.shape[dim] - width, cells.shape[dim], axis=dim)
        cells = jnp.concatenate(
            [
                lax.ppermute(tail, axis, [(i, (i + 1) % count) for i in range(count)]),
                cells,
                lax.ppermute(head, axis, [((i + 1) % count, i) for i in range(count)]),
            ],
            axis=dim,
        )
    return cells


def passed_along(value, axis, steps):
    count = lax.axis_size(axis)
    pairs = [(source, (source + steps) % count) for source in range(count)]
    return lax.ppermute(value, axis, pairs)


def contract_cells(left, right):
    return lax.dot_general(
        left, right, (((0, 1, 2), (0, 1, 2)), ((), ())), preferred_element_type=jnp.float32
    )


def plane_tap(padded, shift_x, shift_y, rows_x, rows_y):
    return padded[1 + shift_x : 1 + shift_x + rows_x, 1 + shift_y : 1 + shift_y + rows_y]


def plane_pad(source):
    rimmed = padded_2(source, (("gx", 0),), 1)
    return jnp.pad(rimmed, ((0, 0), (1, 1), (0, 0), (0, 0)))


def slab_windows(source, dilation):
    slab_depth = source.shape[2]
    above = passed_along(source, "gz", -1)
    above_far = passed_along(source, "gz", -2)
    below = passed_along(source, "gz", 1)
    below_far = passed_along(source, "gz", 2)
    ahead_rows = jnp.concatenate([source, above, above_far], axis=2)
    behind_rows = jnp.concatenate([below_far, below, source], axis=2)
    upper = lax.dynamic_slice_in_dim(ahead_rows, dilation, slab_depth, 2)
    lower = lax.dynamic_slice_in_dim(behind_rows, 2 * slab_depth - dilation, slab_depth, 2)
    return (lower, upper)


def normalize(hidden, gains, cell_count):
    average = lax.psum(jnp.sum(hidden, axis=(0, 1, 2)), ("gz", "gx")) / cell_count
    centered = hidden - average
    spread = lax.psum(jnp.sum(centered * centered, axis=(0, 1, 2)), ("gz", "gx")) / cell_count
    inverse_std = lax.rsqrt(spread + eps_norm)
    whitened = (hidden - average) * inverse_std
    return ((whitened * gains).astype(jnp.bfloat16), whitened, inverse_std)


def norm_back(d_normed, whitened, inverse_std, gains, cell_count):
    scaled = d_normed * gains
    sum_grad, sum_cross = lax.psum(
        (jnp.sum(scaled, axis=(0, 1, 2)), jnp.sum(scaled * whitened, axis=(0, 1, 2))), ("gz", "gx")
    )
    d_hidden = inverse_std * (scaled - sum_grad / cell_count - whitened * (sum_cross / cell_count))
    return (d_hidden, jnp.sum(d_normed * whitened, axis=(0, 1, 2)))


def conv_forward(normed, dilation, weights_z, weights_xy):
    rows_x, rows_y = (normed.shape[0], normed.shape[1])
    lower, upper = slab_windows(normed, dilation)
    padded = plane_pad(normed)
    summed = jnp.dot(lower, weights_z[0], preferred_element_type=jnp.float32)
    summed = summed + jnp.dot(normed, weights_z[1], preferred_element_type=jnp.float32)
    summed = summed + jnp.dot(upper, weights_z[2], preferred_element_type=jnp.float32)
    for tap_number, (shift_x, shift_y) in enumerate(plane_offsets):
        summed = summed + jnp.dot(
            plane_tap(padded, shift_x, shift_y, rows_x, rows_y),
            weights_xy[tap_number],
            preferred_element_type=jnp.float32,
        )
    return summed


def conv_backward_split(pre_cot, normed, dilation, weights_z, weights_xy):
    rows_x, rows_y = (normed.shape[0], normed.shape[1])
    lower_cot, upper_cot = slab_windows(pre_cot, dilation)
    padded_cot = plane_pad(pre_cot)
    d_normed = jnp.dot(upper_cot, weights_z[0].T, preferred_element_type=jnp.float32)
    d_normed = d_normed + jnp.dot(pre_cot, weights_z[1].T, preferred_element_type=jnp.float32)
    d_normed = d_normed + jnp.dot(lower_cot, weights_z[2].T, preferred_element_type=jnp.float32)
    xy_terms = []
    for tap_number, (shift_x, shift_y) in enumerate(plane_offsets):
        shifted = plane_tap(padded_cot, -shift_x, -shift_y, rows_x, rows_y)
        d_normed = d_normed + jnp.dot(
            shifted, weights_xy[tap_number].T, preferred_element_type=jnp.float32
        )
        xy_terms.append(contract_cells(normed, shifted))
    z_terms = jnp.stack(
        [
            contract_cells(normed, upper_cot),
            contract_cells(normed, pre_cot),
            contract_cells(normed, lower_cot),
        ]
    )
    return (d_normed, z_terms, jnp.stack(xy_terms))


def per_device_split(
    clean_field,
    noise_field,
    timestep,
    dilations,
    w_in,
    w_time,
    w_z,
    w_xy,
    w_point,
    biases,
    norm_gains,
    w_out,
):
    layer_total = w_z.shape[0]
    rows_x, rows_y, slab_depth = (clean_field.shape[1], clean_field.shape[2], clean_field.shape[3])
    plane_cells = rows_x * lax.axis_size("gx") * slab_depth * lax.axis_size("gz")
    cell_count = float(plane_cells * rows_y)
    inv_area = 1.0 / plane_cells
    alpha_bar, features, time_raw, time_code = time_terms(timestep, w_time)
    noisy = jnp.sqrt(alpha_bar) * clean_field + jnp.sqrt(1.0 - alpha_bar) * noise_field
    stream = jnp.einsum("kxyz,kc->xyzc", noisy, w_in, precision=highest)
    saved = []
    for which_layer in range(layer_total):
        normed, whitened, inverse_std = normalize(stream, norm_gains[which_layer], cell_count)
        pre_act = conv_forward(normed, dilations[which_layer], w_z[which_layer], w_xy[which_layer])
        pre_act = pre_act + biases[which_layer] + time_code
        activated = jax.nn.gelu(pre_act).astype(jnp.bfloat16)
        saved.append((normed, whitened, inverse_std, pre_act, activated))
        stream = stream + jnp.dot(
            activated, w_point[which_layer], preferred_element_type=jnp.float32
        )
    out_normed, out_white, out_inverse = normalize(stream, norm_gains[layer_total], cell_count)
    prediction = jnp.einsum("xyzc,kc->kxyz", out_normed, w_out, preferred_element_type=jnp.float32)
    misfit = prediction - noise_field
    d_out = jnp.einsum("kxyz,kc->xyzc", misfit, w_out.astype(jnp.float32), precision=highest)
    out_raw = jnp.einsum(
        "kxyz,xyzc->kc", misfit, out_normed, precision=highest, preferred_element_type=jnp.float32
    )
    d_stream, out_gain_raw = norm_back(
        d_out, out_white, out_inverse, norm_gains[layer_total], cell_count
    )
    z_list, xy_list, point_list, bias_list, gain_list = ([], [], [], [], [])
    for which_layer in reversed(range(layer_total)):
        normed, whitened, inverse_std, pre_act, activated = saved[which_layer]
        stream_cot = d_stream.astype(jnp.bfloat16)
        point_raw = contract_cells(activated, stream_cot)
        d_act = jnp.dot(stream_cot, w_point[which_layer].T, preferred_element_type=jnp.float32)
        gelu_back = jax.vjp(jax.nn.gelu, pre_act)[1]
        pre_cot = gelu_back(d_act)[0].astype(jnp.bfloat16)
        bias_raw = jnp.sum(pre_cot, axis=(0, 1, 2), dtype=jnp.float32)
        d_normed, z_raw, xy_raw = conv_backward_split(
            pre_cot, normed, dilations[which_layer], w_z[which_layer], w_xy[which_layer]
        )
        d_back, gain_raw = norm_back(
            d_normed, whitened, inverse_std, norm_gains[which_layer], cell_count
        )
        d_stream = d_stream + d_back
        z_list.insert(0, z_raw)
        xy_list.insert(0, xy_raw)
        point_list.insert(0, point_raw)
        bias_list.insert(0, bias_raw)
        gain_list.insert(0, gain_raw)
    field_grad = jnp.einsum("xyzc,kc->kxyz", d_stream, w_in, precision=highest)
    in_raw = jnp.einsum("kxyz,xyzc->kc", noisy, d_stream, precision=highest)
    z_all, xy_all, point_all, bias_all, gain_all, in_raw, out_raw = lax.psum(
        (
            jnp.stack(z_list),
            jnp.stack(xy_list),
            jnp.stack(point_list),
            jnp.stack(bias_list),
            jnp.stack(gain_list + [out_gain_raw]),
            in_raw,
            out_raw,
        ),
        ("gz", "gx"),
    )
    time_back = jax.vjp(jax.nn.silu, time_raw)[1](jnp.sum(bias_all, axis=0))[0]
    grad_w_time = inv_area * jnp.outer(features, time_back)
    return (
        prediction,
        field_grad,
        inv_area * in_raw,
        grad_w_time,
        inv_area * z_all,
        inv_area * xy_all,
        inv_area * point_all,
        inv_area * bias_all,
        inv_area * gain_all,
        inv_area * out_raw,
    )


def per_device(*args):
    members, groups = lax.axis_size("gz"), lax.axis_size("gx")
    _, rows_x, rows_y, depth = args[0].shape
    small = rows_x == 1 and rows_y == 4 and members == 4 and groups == 8 and depth * members == 2 * REACH
    return per_device_grouped(*args) if small else per_device_split(*args)


def solution(mesh):
    return jax.shard_map(
        per_device,
        mesh=mesh,
        in_specs=(
            P(None, "gx", None, "gz"),
            P(None, "gx", None, "gz"),
            P(),
            P(),
            P(),
            P(),
            P(),
            P(),
            P(),
            P(),
            P(),
            P(),
        ),
        out_specs=(
            P(None, "gx", None, "gz"),
            P(None, "gx", None, "gz"),
            P(),
            P(),
            P(),
            P(),
            P(),
            P(),
            P(),
            P(),
        ),
        check_vma=False,
    )
```

```python
import functools
import math

import jax
import jax.numpy as jnp
from jax import lax
from jax.experimental import pallas as pl
from jax.experimental.pallas import tpu as pltpu
from jax.sharding import PartitionSpec as P

STEPS = 1000
REACH = 256
RIM = 4
TILE = 16
LIMITS = (4, 13, 10, 7, 12, 9, 12, 2)

eps_norm = 1e-05
highest = lax.Precision.HIGHEST
bf16 = jnp.bfloat16
f32 = jnp.float32
plane_offsets = ((-1, -1), (-1, 0), (-1, 1), (0, -1), (0, 1), (1, -1), (1, 0), (1, 1))


def time_terms(timestep, w_time):
    moment = timestep[0].astype(jnp.float32)
    half_width = w_time.shape[0] // 2
    alpha_bar = jnp.cos(0.5 * math.pi * (moment + 0.5) / STEPS) ** 2
    ladder = jnp.exp(-math.log(10000.0) * jnp.arange(half_width, dtype=jnp.float32) / half_width)
    angles = moment * ladder
    features = jnp.concatenate([jnp.sin(angles), jnp.cos(angles)])
    time_raw = jnp.dot(features, w_time, precision=highest)
    return (alpha_bar, features, time_raw, jax.nn.silu(time_raw))


def mm(left, right):
    return lax.dot_general(left, right, (((1,), (0,)), ((), ())), preferred_element_type=f32)


def mm_nt(left, right):
    return lax.dot_general(left, right, (((1,), (1,)), ((), ())), preferred_element_type=f32)


def mm_tn(left, right):
    return lax.dot_general(left, right, (((0,), (0,)), ((), ())), preferred_element_type=f32)


def halves(value):
    high = value.astype(bf16)
    return high, (value - high.astype(f32)).astype(bf16)


def wide(vector):
    return jnp.concatenate([vector] * 4, axis=1)


def folded(vector):
    channels = vector.shape[1] // 4
    return sum(vector[:, y * channels : (y + 1) * channels] for y in range(4))


class Place:
    def __init__(self, sc, rows):
        self.rows = rows
        self.members = lax.axis_size("gz")
        self.member = lax.axis_index("gz")
        self.small = jnp.minimum(sc[0], sc[1])
        self.coarse = self.small >= self.members
        tiles = rows // TILE
        self.tiles = tiles
        self.stride = jnp.where(self.coarse, tiles - 1, tiles)
        self.span = REACH // self.members + 2 * RIM
        far = jnp.where(self.coarse, REACH // self.members, self.span)
        near = jnp.where(self.coarse, self.small // self.members, 1)
        self.steps = [jnp.where(sc[l] == REACH, far, near) for l in range(2)]

    def index(self, shape):
        row = lax.broadcasted_iota(jnp.int32, shape, 0)
        return lax.rem(row, TILE) * self.stride + row // TILE, row // TILE

    def own(self, shape):
        place, tile = self.index(shape)
        inside = lax.rem(place, self.span)
        near = ((inside >= RIM) & (inside < self.span - RIM)).astype(jnp.int32)
        far = (tile < self.tiles - 1).astype(jnp.int32)
        return jnp.where(self.coarse, far, near) == 1

    def pick(self, cells_z):
        shape = (self.rows, cells_z)
        return self.z_of(shape, cells_z) == lax.broadcasted_iota(jnp.int32, shape, 1)

    def z_of(self, shape, cells_z):
        place, _ = self.index(shape)
        residues = jnp.minimum(self.small, self.members)
        part, start = self.member // residues, lax.rem(self.member, residues)
        period = place // self.span
        inside = place - period * self.span - RIM + part * (REACH // self.members)
        near = start + residues * inside + period * REACH
        z = jnp.where(self.coarse, place * self.members + self.member, near)
        return lax.rem(z + 2 * cells_z, cells_z)


def build_taps(block_of, taps, taps_z):
    channels = taps_z.shape[-1] // 2
    zero = jnp.zeros((channels, channels), bf16)
    for i in range(3):
        for j in range(3):
            block = block_of(i, j)
            for q in range(2):
                for side in range(2):
                    y_in = 2 * q + side + j - 1
                    if 0 <= y_in < 4:
                        taps[
                            q,
                            i,
                            y_in * channels : (y_in + 1) * channels,
                            side * channels : (side + 1) * channels,
                        ] = block
        for q in range(2):
            for side in range(2):
                for y_in in range(4):
                    if abs(y_in - 2 * q - side) > 1:
                        taps[
                            q,
                            i,
                            y_in * channels : (y_in + 1) * channels,
                            side * channels : (side + 1) * channels,
                        ] = zero
    for m in range(2):
        build_pair(block_of(3, m), taps_z, m)


def build_pair(block, target, m):
    channels = block.shape[-1]
    zero = jnp.zeros((channels, channels), bf16)
    target[m, :channels, :channels] = block
    target[m, channels:, channels:] = block
    target[m, :channels, channels:] = zero
    target[m, channels:, :channels] = zero


def forward_blocks(w_z, w_xy, layer):
    def block_of(i, j):
        if i == 3:
            return w_z[layer, 2 * j]
        at = i * 3 + j
        return w_z[layer, 1] if at == 4 else w_xy[layer, at - (at > 4)]

    return block_of


def backward_blocks(w_back, layer):
    return lambda i, j: w_back[layer, i * 3 + j]


def kernel_mix(amounts, clean, noise, mixed):
    parts = mixed.shape[0]
    for k in range(3):
        noisy = amounts[0] * clean[k, 0] + amounts[1] * noise[k, 0]
        for part in range(parts):
            mixed[part, 4 * k : 4 * k + 4] = noisy
            mixed[part, 12 + 4 * k : 16 + 4 * k] = noise[k, 0]


def kernel_prepare(w_z, w_xy, w_point, w_in, w_out, w_back, point_back, lift_in, lift_out):
    for layer in range(2):
        forward = forward_blocks(w_z, w_xy, layer)
        for i in range(3):
            for j in range(3):
                w_back[layer, i * 3 + j] = forward(2 - i, 2 - j).T
        for m in range(2):
            w_back[layer, 9 + m] = forward(3, 1 - m).T
        point_back[layer] = w_point[layer].T
    whole = spread_rows(w_in[...], 0)
    high, low = halves(whole)
    lift_in[0:32] = high
    lift_in[32:64] = high
    lift_in[64:96] = low
    lift_in[96:128] = jnp.zeros_like(low)
    high = spread_rows(w_out[...].astype(f32), 3).astype(bf16)
    lift_out[0:32] = high
    lift_out[32:64] = high
    lift_out[64:96] = jnp.zeros_like(high)
    lift_out[96:128] = jnp.zeros_like(high)


def spread_rows(weights, first):
    channels = weights.shape[1]
    zero = jnp.zeros((1, channels), f32)
    rows = [jnp.zeros((1, 4 * channels), f32)] * 32
    for k in range(3):
        for y in range(4):
            parts = [weights[k : k + 1] if at == y else zero for at in range(4)]
            rows[(first + k) * 4 + y] = jnp.concatenate(parts, axis=1)
    return jnp.concatenate(rows, axis=0)


def fill_rims(padded, planes):
    padded[0] = padded[planes]
    padded[planes + 1] = padded[1]


def fill_shifted(place, layer, padded, shifted, planes):
    step, stride = place.steps[layer], place.stride
    for tile in range(place.tiles):
        for way in range(2):
            at = tile - step if way == 0 else tile + step
            moved = at + TILE * stride
            source = lax.rem(moved, stride)
            turn = lax.rem(2 * TILE - moved // stride, TILE)
            rows = padded[1 : planes + 1, pl.ds(pl.multiple_of(source * TILE, TILE), TILE), :]
            rows = pltpu.roll(rows.astype(f32), turn, 1)
            shifted[way, :, tile * TILE : (tile + 1) * TILE, :] = rows.astype(bf16)


def conv_half(padded, shifted, taps, taps_z, x0, count, q):
    rows, lanes = padded.shape[1:]
    half = lanes // 2
    total = None
    for i in range(3):
        part = mm(padded[pl.ds(x0 + i, count)].reshape(count * rows, lanes), taps[q, i])
        total = part if total is None else total + part
    for m in range(2):
        source = shifted[m, pl.ds(x0, count), :, q * half : (q + 1) * half]
        total = total + mm(source.reshape(count * rows, half), taps_z[m])
    return total


def gelu_pair(value):
    scale = math.sqrt(2.0 / math.pi)
    square = value * value
    bent = jnp.tanh(value * (scale + (scale * 0.044715) * square))
    half = 0.5 + 0.5 * bent
    slope = half + value * (0.5 - 0.5 * (bent * bent)) * (scale + (3.0 * 0.044715 * scale) * square)
    return value * half, slope


def members_of(parts):
    found = []
    for part in parts:
        for at in range(0, part.shape[0], 8):
            found.append(part[at : at + 8])
    return found


def merged_stats(parts, per_member):
    found = members_of(parts)
    mean = sum(one[0:1] for one in found) / (per_member * len(found))
    spread = sum(one[1:2] for one in found)
    for one in found:
        gap = one[0:1] / per_member - mean
        spread = spread + per_member * gap * gap
    return mean, lax.rsqrt(spread / (per_member * len(found)) + eps_norm)


def put_rows(ref, *vectors):
    rows = list(vectors)
    rows += [jnp.zeros((1, ref.shape[1]), f32)] * (ref.shape[0] - len(rows))
    ref[...] = jnp.concatenate(rows, axis=0)


def masked_total(mask, value):
    return folded(jnp.sum(jnp.where(mask, value, 0.0), axis=0, keepdims=True))


def layer_forward(place, layer, padded, shifted, taps, taps_z, pair, w_z, w_xy, wp, shift_bias, old,
                  stream, act, slope, stats, acc, per_member):
    planes, rows, lanes = stream.shape
    half = lanes // 2
    count = planes // 2
    build_taps(forward_blocks(w_z, w_xy, layer), taps, taps_z)
    build_pair(wp[layer], pair, 0)
    fill_rims(padded, planes)
    fill_shifted(place, layer, padded, shifted, planes)
    acc[...] = jnp.zeros_like(acc)
    bias = wide(shift_bias[layer : layer + 1, :])[:, :half]

    def body(step, carry):
        x0 = step * count
        for q in range(2):
            side = slice(q * half, (q + 1) * half)
            pre = conv_half(padded, shifted, taps, taps_z, x0, count, q) + bias
            value, grad = gelu_pair(pre)
            value = value.astype(bf16)
            act[pl.ds(x0, count), :, side] = value.reshape(count, rows, half)
            slope[pl.ds(x0, count), :, side] = grad.astype(bf16).reshape(count, rows, half)
            branch = mm(value, pair[0]).reshape(count, rows, half)
            new = old[pl.ds(x0, count), :, side] + branch
            stream[pl.ds(x0, count), :, side] = new
            acc[:, side] += jnp.sum(new, axis=0)
        return carry

    lax.fori_loop(0, planes // count, body, 0)
    mask = place.own((rows, lanes))
    total = masked_total(mask, acc[...])
    mean = wide(total / per_member)
    spread = jnp.zeros((rows, lanes), f32)
    for x in range(planes):
        gap = stream[x] - mean
        spread = spread + gap * gap
    put_rows(stats, total, masked_total(mask, spread))


def kernel_first(cells_z, per_member, sc, near, far, lift_in, w_in, gains, shift_bias, w_z, w_xy, wp,
                 stream, normed, act, slope, gathered, stats, consts,
                 padded, shifted, taps, taps_z, pair, acc, old, source):
    planes, rows, lanes = stream.shape
    channels = lanes // 4
    depth = near.shape[2]
    place = Place(sc, rows)
    cell_count = float(planes * 4 * cells_z)
    comps = [
        jnp.concatenate([ref[:, 4 * k : 4 * k + 4, :] for ref in (near, far)], axis=0) for k in range(3)
    ]

    def all_sum(value):
        value = jnp.sum(jnp.sum(value, axis=0), axis=0, keepdims=True)
        return jnp.sum(value, axis=1, keepdims=True)

    means = [all_sum(comp) / cell_count for comp in comps]
    gaps = [comp - mean[None] for comp, mean in zip(comps, means)]
    covs = {}
    for j in range(3):
        for k in range(j, 3):
            covs[j, k] = all_sum(gaps[j] * gaps[k]) / cell_count
    rows_in = [w_in[k : k + 1, :] for k in range(3)]
    mean_c = sum(means[k] * rows_in[k] for k in range(3))
    var_c = jnp.zeros((1, channels), f32)
    for (j, k), cov in covs.items():
        var_c = var_c + (1.0 if j == k else 2.0) * cov * (rows_in[j] * rows_in[k])
    inv_c = lax.rsqrt(jnp.maximum(var_c, 0.0) + eps_norm)
    flat = [jnp.broadcast_to(value, (1, channels)) for value in means + list(covs.values())]
    put_rows(consts, mean_c, inv_c, *flat)
    blank = jnp.zeros((8, depth), f32)
    core = lax.rem(place.member, 2)
    for slab in range(cells_z // depth):
        ref, side = (near, core) if slab % 2 == 0 else (far, 1 - core)
        at = pl.ds(pl.multiple_of((slab // 2 * 2 + side) * depth, depth), depth)
        for x in range(planes):
            high, low = halves(jnp.concatenate([ref[slab // 2 * planes + x], blank], axis=0))
            source[x, 0:32, at] = high
            source[x, 32:64, at] = low
            source[x, 64:96, at] = high
            source[x, 96:128, at] = jnp.zeros_like(high)
    pick = place.pick(cells_z).astype(f32).astype(bf16)
    scale = wide(inv_c * gains[0:1, :])
    mean_w = wide(mean_c)
    for x in range(planes):
        gathered[x] = mm_nt(pick, source[x]).astype(bf16)
    for x0 in range(0, planes, planes // 2):
        part = slice(x0, x0 + planes // 2)
        value = mm(gathered[part].reshape(planes // 2 * rows, 128), lift_in[...])
        unit = ((value - mean_w) * scale).astype(bf16).reshape(planes // 2, rows, lanes)
        old[part] = value.reshape(planes // 2, rows, lanes)
        padded[x0 + 1 : x0 + 1 + planes // 2] = unit
        normed[part] = unit
    layer_forward(place, 0, padded, shifted, taps, taps_z, pair, w_z, w_xy, wp, shift_bias, old, stream,
                  act, slope, stats, acc, per_member)


def kernel_second(per_member, sc, *refs):
    parts, refs = refs[:4], refs[4:]
    (old, gains, shift_bias, w_z, w_xy, wp, stream, normed, act, slope, stats, consts,
     padded, shifted, taps, taps_z, pair, acc) = refs
    planes, rows, _ = stream.shape
    place = Place(sc, rows)
    mean, inverse = merged_stats(parts, per_member)
    put_rows(consts, mean, inverse)
    mean_w, scale = wide(mean), wide(inverse * gains[1:2, :])
    for x in range(planes):
        unit = ((old[x] - mean_w) * scale).astype(bf16)
        padded[x + 1] = unit
        normed[x] = unit
    layer_forward(place, 1, padded, shifted, taps, taps_z, pair, w_z, w_xy, wp, shift_bias, old, stream,
                  act, slope, stats, acc, per_member)


def kernel_out(per_member, sc, *refs):
    parts, refs = refs[:4], refs[4:]
    stream, gains, gathered, lift_out, prediction, misfit, sums, w_out_raw, consts, unit = refs
    planes, rows, lanes = stream.shape
    place = Place(sc, rows)
    mean, inverse = merged_stats(parts, per_member)
    put_rows(consts, mean, inverse)
    mean_w, inv_w, gain_w = wide(mean), wide(inverse), wide(gains[2:3, :])
    scale = inv_w * gain_w
    for x in range(planes):
        unit[x] = ((stream[x] - mean_w) * scale).astype(bf16)
    row = lax.broadcasted_iota(jnp.int32, (128, 128), 0)
    col = lax.broadcasted_iota(jnp.int32, (128, 128), 1)
    slot = lax.rem(col, 32)
    used = (col < 64) & (slot >= 12) & (slot < 24)
    take = (used & ((row == slot) | (row == slot + 32))).astype(f32).astype(bf16)
    total = mm_nt(unit[...].reshape(planes * rows, lanes), lift_out[...])
    noise = mm(gathered[...].reshape(planes * rows, 128), take)
    gap = total - noise
    high, low = halves(gap)
    lane = lax.broadcasted_iota(jnp.int32, gap.shape, 1)
    both = jnp.where(lane < 32, high.astype(f32), low.astype(f32)).astype(bf16)
    misfit[...] = both.reshape(planes, rows, 128)
    for x in range(planes):
        @pl.when(lax.axis_index("gx") == x)
        def _(x=x):
            prediction[...] = total[x * rows : (x + 1) * rows]
    plain = jnp.zeros((rows, lanes), f32)
    cross = jnp.zeros((rows, lanes), f32)
    for x0 in range(0, planes, planes // 2):
        part = slice(x0 * rows, (x0 + planes // 2) * rows)
        d_out = mm(both[part], lift_out[...]).reshape(planes // 2, rows, lanes)
        for x in range(planes // 2):
            plain = plain + d_out[x]
            cross = cross + d_out[x] * ((stream[x0 + x] - mean_w) * inv_w)
    own = place.own((rows, 128))
    kept = jnp.concatenate([jnp.where(own, misfit[x].astype(f32), 0.0) for x in range(planes)], axis=0)
    raw = mm_tn(kept.astype(bf16), unit[...].reshape(planes * rows, lanes))
    mask = place.own((rows, lanes))
    put_rows(sums, masked_total(mask, plain), masked_total(mask, cross))
    put_rows(w_out_raw, *by_component(raw[0:32] + raw[32:64], 3))


def by_component(raw, first):
    channels = raw.shape[1] // 4
    found = []
    for k in range(first, first + 3):
        found.append(
            sum(raw[k * 4 + y : k * 4 + y + 1, y * channels : (y + 1) * channels] for y in range(4))
        )
    return found


def branch_backward(planes, d_stream_of, pair, slope, padded, scot, bias_acc):
    rows, lanes = padded.shape[1:]
    half = lanes // 2
    count = planes // 2

    def body(step, carry):
        x0 = step * count
        for t in range(count):
            scot[x0 + t] = d_stream_of(x0 + t).astype(bf16)
        for q in range(2):
            side = slice(q * half, (q + 1) * half)
            cot = scot[pl.ds(x0, count), :, side].reshape(count * rows, half)
            d_act = mm(cot, pair[0]).reshape(count, rows, half)
            pre = (d_act * slope[pl.ds(x0, count), :, side].astype(f32)).astype(bf16)
            padded[pl.ds(x0 + 1, count), :, side] = pre
            bias_acc[:, side] += jnp.sum(pre.astype(f32), axis=0)
        return carry

    lax.fori_loop(0, planes // count, body, 0)


def weight_grads(place, planes, padded, shifted, scot, normed, act, keep, give, share):
    rows, lanes = padded.shape[1:]
    channels = lanes // 4
    wide_share = 4 * share
    row = lax.broadcasted_iota(jnp.int32, (lanes, wide_share), 0)
    col = lax.broadcasted_iota(jnp.int32, (lanes, wide_share), 1)
    hit = (row // channels == col // share) & (
        lax.rem(row, channels) == lax.rem(col, share) + lax.axis_index("gx") * share
    )
    choose = hit.astype(f32).astype(bf16)
    mask = jnp.concatenate([place.own((rows, wide_share))] * planes, axis=0)

    def turned(source):
        got = mm(source[...].reshape(planes * rows, lanes), choose)
        return jnp.where(mask, got, 0.0).astype(bf16)

    def add_blocks(raw, j):
        return sum(
            raw[(y + j) * share : (y + j + 1) * share, y * channels : (y + 1) * channels]
            for y in range(4)
            if 0 <= y + j < 4
        )

    odd = lax.rem(place.member, 2) == 1

    def hand(tap, value):
        late = tap >= 6
        at = tap - 6 if late else tap
        stays = odd if late else jnp.logical_not(odd)

        @pl.when(stays)
        def _():
            keep[at] = value

        @pl.when(jnp.logical_not(stays))
        def _():
            give[at] = value

    left = turned(normed)
    for i in range(3):
        raw = mm_tn(left, padded[2 - i : 2 - i + planes].reshape(planes * rows, lanes))
        for j in range(3):
            hand(i * 3 + j, add_blocks(raw, j - 1))
    for m in range(2):
        raw = mm_tn(left, shifted[1 - m].reshape(planes * rows, lanes))
        hand(9 + m, add_blocks(raw, 0))
    raw = mm_tn(turned(act), scot[...].reshape(planes * rows, lanes))
    hand(11, add_blocks(raw, 0))


def conv_backward(planes, padded, shifted, taps, taps_z, emit):
    rows, lanes = padded.shape[1:]
    count = planes // 2

    def body(step, carry):
        x0 = step * count
        for q in range(2):
            emit(x0, count, q, conv_half(padded, shifted, taps, taps_z, x0, count, q))
        return carry

    lax.fori_loop(0, planes // count, body, 0)


def kernel_back_second(share, cell_count, sc, *refs):
    parts, refs = refs[:4], refs[4:]
    (stream, out_consts, gains, misfit, lift_out, act, slope, normed, w_back, point_back,
     d_stream, d_normed, sums, keep, give,
     padded, shifted, taps, taps_z, pair, acc, acc2, scot) = refs
    planes, rows, lanes = stream.shape
    half = lanes // 2
    place = Place(sc, rows)
    sums_out = sum(members_of(parts))
    gain_w = wide(gains[2:3, :])
    mean_w, inv_w = wide(out_consts[0:1]), wide(out_consts[1:2])
    m_plain = gain_w * wide(sums_out[0:1]) / cell_count
    m_cross = gain_w * wide(sums_out[1:2]) / cell_count
    build_pair(point_back[1], pair, 0)
    build_taps(backward_blocks(w_back, 1), taps, taps_z)
    acc[...] = jnp.zeros_like(acc)

    def d_stream_of(x):
        d_out = mm(misfit[x], lift_out[...])
        white = (stream[x] - mean_w) * inv_w
        value = inv_w * (gain_w * d_out - m_plain - white * m_cross)
        d_stream[x] = value
        return value

    branch_backward(planes, d_stream_of, pair, slope, padded, scot, acc)
    mask = place.own((rows, lanes))
    s_bias = masked_total(mask, acc[...])
    acc[...] = jnp.zeros_like(acc)
    acc2[...] = jnp.zeros_like(acc2)
    fill_rims(padded, planes)
    fill_shifted(place, 1, padded, shifted, planes)

    def emit(x0, count, q, value):
        side = slice(q * half, (q + 1) * half)
        value = value.reshape(count, rows, half)
        d_normed[pl.ds(x0, count), :, side] = value
        acc[:, side] += jnp.sum(value, axis=0)
        acc2[:, side] += jnp.sum(value * normed[pl.ds(x0, count), :, side].astype(f32), axis=0)

    conv_backward(planes, padded, shifted, taps, taps_z, emit)
    s_plain = masked_total(mask, acc[...])
    s_cross = masked_total(mask, acc2[...]) / gains[1:2, :]
    put_rows(sums, s_plain, s_cross, s_bias)
    weight_grads(place, planes, padded, shifted, scot, normed, act, keep, give, share)


def kernel_back_first(share, cell_count, sc, *refs):
    parts, refs = refs[:4], refs[4:]
    (consts, d_next, d_normed, normed_next, gains, act, slope, normed, point_back,
     d_stream, pre_cot, sums, keep, give,
     padded, shifted, pair, acc, scot) = refs
    planes, rows, lanes = d_next.shape
    place = Place(sc, rows)
    sums_in = sum(members_of(parts))
    gain_w = wide(gains[1:2, :])
    inv_w = wide(consts[1:2])
    m_plain = gain_w * wide(sums_in[0:1]) / cell_count
    m_cross = wide(sums_in[1:2]) / cell_count
    build_pair(point_back[0], pair, 0)
    acc[...] = jnp.zeros_like(acc)

    def d_stream_of(x):
        back = gain_w * d_normed[x] - m_plain - normed_next[x].astype(f32) * m_cross
        value = d_next[x] + inv_w * back
        d_stream[x] = value
        return value

    branch_backward(planes, d_stream_of, pair, slope, padded, scot, acc)
    put_rows(sums, masked_total(place.own((rows, lanes)), acc[...]))
    fill_rims(padded, planes)
    fill_shifted(place, 0, padded, shifted, planes)
    for x in range(planes):
        pre_cot[x] = padded[x + 1]
    weight_grads(place, planes, padded, shifted, scot, normed, act, keep, give, share)


def kernel_last(depth, sc, pre_cot, d_stream, normed, gains, consts, gathered, lift_in, w_back,
                prediction, sums_bias, out_raw, own_out, out_1, out_2, out_3,
                padded, shifted, taps, taps_z, acc, acc2, high, low):
    planes, rows, lanes = d_stream.shape
    half = lanes // 2
    place = Place(sc, rows)
    for x in range(planes):
        padded[x + 1] = pre_cot[x]
    fill_rims(padded, planes)
    fill_shifted(place, 0, padded, shifted, planes)
    build_taps(backward_blocks(w_back, 0), taps, taps_z)
    acc[...] = jnp.zeros_like(acc)
    acc2[...] = jnp.zeros_like(acc2)
    scale = wide(consts[1:2] * gains[0:1, :])

    def emit(x0, count, q, value):
        side = slice(q * half, (q + 1) * half)
        part = pl.ds(x0, count)
        value = value.reshape(count, rows, half)
        acc[:, side] += jnp.sum(value, axis=0)
        acc2[:, side] += jnp.sum(value * normed[part, :, side].astype(f32), axis=0)
        full = d_stream[part, :, side] + value * scale[:, side]
        first, second = halves(full)
        high[part, :, side] = first
        low[part, :, side] = second

    conv_backward(planes, padded, shifted, taps, taps_z, emit)
    mask = place.own((rows, lanes))
    s_plain = masked_total(mask, acc[...])
    s_cross = masked_total(mask, acc2[...]) / gains[0:1, :]
    own = place.own((rows, 128))
    kept = jnp.concatenate([jnp.where(own, gathered[x].astype(f32), 0.0) for x in range(planes)], axis=0)
    kept = kept.astype(bf16)
    raw = mm_tn(kept, high[...].reshape(planes * rows, lanes))
    raw_low = mm_tn(kept, low[...].reshape(planes * rows, lanes))
    in_raw = by_component(raw[0:32] + raw[32:64] + raw_low[0:32], 0)
    blank = jnp.zeros((1, s_plain.shape[1]), f32)
    tail = jnp.concatenate([s_plain, s_cross] + [blank] * 6 + in_raw + [blank] * 5, axis=0)
    tail = jnp.concatenate([tail, sums_bias[...], out_raw[...]], axis=0)
    here = lax.axis_index("gx")
    lane = lax.broadcasted_iota(jnp.int32, (rows, 128), 1)
    field = mm_nt(high[here], lift_in[...]) + jnp.where(lane < 32, mm_nt(low[here], lift_in[...]), 0.0)
    field = jnp.where((lane >= 32) & (lane < 64), 0.0, field)
    field = field + jnp.where((lane >= 12) & (lane < 24), prediction[...], 0.0)
    cells_z = depth * place.members
    whole = place.z_of((rows, depth), cells_z)
    column = lax.broadcasted_iota(jnp.int32, (rows, depth), 1)
    mask = place.own((rows, depth))
    first, second = halves(field)
    for bit, target in enumerate((own_out, out_1, out_2, out_3)):
        there = lax.bitwise_xor(place.member, bit)
        pick = ((whole == column + there * depth) & mask).astype(f32).astype(bf16)
        out = mm_tn(first, pick) + mm_tn(second, pick)
        target[0:32] = out[0:32] + out[64:96]
        target[32:64] = tail


def call(kernel, outs, scratch, flops, limit, *args, scalars=True, loose=()):
    spec = pl.BlockSpec(memory_space=pltpu.VMEM)
    specs = [pl.BlockSpec(memory_space=pltpu.SMEM)] * scalars + [spec] * (len(args) - scalars)
    for at in loose:
        specs[at] = pl.BlockSpec(memory_space=pl.ANY)
    return pl.pallas_call(
        kernel,
        out_shape=[jax.ShapeDtypeStruct(shape, dtype) for shape, dtype in outs],
        in_specs=specs,
        out_specs=[spec] * len(outs),
        scratch_shapes=[pltpu.VMEM(shape, dtype) for shape, dtype in scratch],
        compiler_params=pltpu.CompilerParams(vmem_limit_bytes=limit * 2**20),
        cost_estimate=pl.CostEstimate(flops=flops, bytes_accessed=2**23, transcendentals=0),
    )(*args)


def swapped(value, axis, bit):
    count = lax.axis_size(axis)
    return lax.ppermute(value, axis, [(i, i ^ bit) for i in range(count)])


def group_parts(value):
    return (value,) + tuple(swapped(value, "gz", bit) for bit in (1, 2, 3))


def group_grads(keep, give):
    mine = keep + swapped(give, "gz", 1)
    return mine + swapped(mine, "gz", 2)


def all_grads(first, second):
    groups = lax.axis_size("gx")
    taps, share, channels = first.shape
    mine = jnp.concatenate([first, second], axis=0).astype(bf16)
    mine = mine.reshape(2 * taps * share, channels)
    near = lax.all_to_all(jnp.broadcast_to(mine[None], (groups,) + mine.shape), "gx", 0, 0)
    far = swapped(near, "gz", 1)
    odd = lax.rem(lax.axis_index("gz"), 2) == 1

    def laid_out(every):
        every = every.reshape(groups, 2, taps, share, channels).transpose(1, 2, 0, 3, 4)
        return every.reshape(2, taps, groups * share, channels)

    near, far = laid_out(near), laid_out(far)
    return jnp.concatenate([jnp.where(odd, far, near), jnp.where(odd, near, far)], axis=1)


def per_device_grouped(clean_field, noise_field, timestep, dilations, w_in, w_time, w_z, w_xy, w_point,
                       biases, norm_gains, w_out):
    members, groups = lax.axis_size("gz"), lax.axis_size("gx")
    depth = clean_field.shape[3]
    planes, cells_z = groups, depth * members
    channels = w_in.shape[1]
    lanes = 4 * channels
    rows = (cells_z // REACH) * (REACH // members + 2 * RIM)
    share = channels // groups
    per_member = float(planes * 4 * depth)
    cell_count = per_member * members
    inv_area = 4.0 / cell_count

    alpha_bar, features, time_raw, time_code = time_terms(timestep, w_time)
    parts = members // 2 * groups
    mixed = call(
        kernel_mix, [((parts, 24, depth), f32)], [], 10**5, LIMITS[7],
        jnp.stack([jnp.sqrt(alpha_bar), jnp.sqrt(1.0 - alpha_bar)]), clean_field, noise_field,
    )[0]
    same_core = [[m * groups + g for m in range(core, members, 2) for g in range(groups)] for core in range(2)]
    near = lax.all_to_all(mixed, ("gz", "gx"), 0, 0, axis_index_groups=same_core)
    far = swapped(near, "gz", 1)
    shift_bias = biases + time_code

    big = (planes, rows, lanes)
    vec = ((8, channels), f32)
    thin = ((planes, rows, 128), bf16)
    lift = ((128, lanes), bf16)
    conv_scratch = [
        ((planes + 2, rows, lanes), bf16),
        ((2,) + big, bf16),
        ((2, 3, lanes, lanes // 2), bf16),
        ((2, lanes // 2, lanes // 2), bf16),
    ]
    pair = ((1, lanes // 2, lanes // 2), bf16)
    flat = ((rows, lanes), f32)
    grad_out = ((6, share, channels), f32)

    w_back, point_back, lift_in, lift_out = call(
        kernel_prepare,
        [((2, 11, channels, channels), bf16), ((2, channels, channels), bf16), lift, lift],
        [], 10**8, LIMITS[0], w_z, w_xy, w_point, w_in, w_out, scalars=False,
    )
    stream1, normed0, act0, slope0, gathered, stats1, consts0 = call(
        functools.partial(kernel_first, cells_z, per_member),
        [(big, f32), (big, bf16), (big, bf16), (big, bf16), thin, vec, ((16, channels), f32)],
        conv_scratch + [pair, flat, (big, f32), ((planes, 128, cells_z), bf16)],
        4 * 10**9, LIMITS[1],
        dilations, near, far, lift_in, w_in, norm_gains, shift_bias, w_z, w_xy, w_point,
    )
    stream2, normed1, act1, slope1, stats2, consts1 = call(
        functools.partial(kernel_second, per_member),
        [(big, f32), (big, bf16), (big, bf16), (big, bf16), vec, vec],
        conv_scratch + [pair, flat],
        4 * 10**9, LIMITS[2],
        dilations, *group_parts(stats1), stream1, norm_gains, shift_bias, w_z, w_xy, w_point,
    )
    prediction, misfit, sums2, out_raw, consts2 = call(
        functools.partial(kernel_out, per_member),
        [((rows, 128), f32), thin, vec, vec, vec],
        [(big, bf16)],
        10**9, LIMITS[3],
        dilations, *group_parts(stats2), stream2, norm_gains, gathered, lift_out,
    )
    parts2 = group_parts(sums2)
    d_stream2, d_normed1, sums1, keep1, give1 = call(
        functools.partial(kernel_back_second, share, cell_count),
        [(big, f32), (big, f32), vec, grad_out, grad_out],
        conv_scratch + [pair, flat, flat, (big, bf16)],
        6 * 10**9, LIMITS[4],
        dilations, *parts2, stream2, consts2, norm_gains, misfit, lift_out, act1, slope1, normed1,
        w_back, point_back,
    )
    parts1 = group_parts(sums1)
    d_stream1, pre_cot0, sums_b0, keep0, give0 = call(
        functools.partial(kernel_back_first, share, cell_count),
        [(big, f32), (big, bf16), vec, grad_out, grad_out],
        conv_scratch[:2] + [pair, flat, (big, bf16)],
        4 * 10**9, LIMITS[5],
        dilations, *parts1, consts1, d_stream2, d_normed1, normed1, norm_gains, act0, slope0, normed0,
        point_back,
    )
    mine1 = group_grads(keep1, give1)
    last = call(
        functools.partial(kernel_last, depth),
        [((64, channels), f32)] * members,
        conv_scratch + [flat, flat, (big, bf16), (big, bf16)],
        4 * 10**9, LIMITS[6],
        dilations, pre_cot0, d_stream1, normed0, norm_gains, consts0, gathered, lift_in, w_back, prediction,
        sums_b0, out_raw,
    )
    every = all_grads(group_grads(keep0, give0), mine1)

    tails = last[0] + sum(swapped(last[bit], "gz", bit) for bit in (1, 2, 3))
    s_plain, s_cross, in_sum = tails[32], tails[33], tails[40:43]
    bias0, out_sum = tails[48], tails[56:59]
    s1 = sum(members_of(parts1))
    s2 = sum(members_of(parts2))
    inverse = consts0[1]
    m_plain = norm_gains[0] * s_plain / cell_count
    m_cross = norm_gains[0] * s_cross / cell_count
    mean_k = consts0[2:5, 0]
    c00, c01, c02, c11, c12, c22 = (consts0[5 + at, 0] for at in range(6))
    cov = jnp.stack([jnp.stack([c00, c01, c02]), jnp.stack([c01, c11, c12]), jnp.stack([c02, c12, c22])])
    offset = jnp.sum(w_in * (inverse * m_plain), axis=1)
    mix = jnp.sum(w_in[:, None, :] * (inverse * inverse * m_cross) * w_in[None, :, :], axis=2)
    landed = tails[:24].reshape(6, 1, 4, depth)
    centered = mixed[0, :12].reshape(3, 1, 4, depth) - mean_k[:, None, None, None]
    field_grad = landed[:3] - offset[:, None, None, None] - sum(
        mix[:, j, None, None, None] * centered[j][None] for j in range(3)
    )
    prediction_out = landed[3:]
    cross_in = jnp.sum(cov[:, :, None] * w_in[None, :, :], axis=1)
    in_raw = in_sum - cell_count * (
        mean_k[:, None] * (inverse * m_plain) + (inverse * inverse * m_cross) * cross_in
    )
    bias_all = jnp.stack([bias0, s1[2]])
    gain_all = jnp.stack([s_cross, s1[1], s2[1]])
    weights = every.astype(f32) * inv_area
    z_all = jnp.stack([weights[:, 9], weights[:, 4], weights[:, 10]], axis=1)
    xy_all = jnp.concatenate([weights[:, :4], weights[:, 5:9]], axis=1)
    time_back = jax.vjp(jax.nn.silu, time_raw)[1](jnp.sum(bias_all, axis=0))[0]
    grad_w_time = inv_area * jnp.outer(features, time_back)
    return (
        prediction_out,
        field_grad,
        inv_area * in_raw,
        grad_w_time,
        z_all,
        xy_all,
        weights[:, 11],
        inv_area * bias_all,
        inv_area * gain_all,
        inv_area * out_sum,
    )


def padded_2(cells, sides, width):
    for axis, dim in sides:
        count = lax.axis_size(axis)
        head = lax.slice_in_dim(cells, 0, width, axis=dim)
        tail = lax.slice_in_dim(cells, cells.shape[dim] - width, cells.shape[dim], axis=dim)
        cells = jnp.concatenate(
            [
                lax.ppermute(tail, axis, [(i, (i + 1) % count) for i in range(count)]),
                cells,
                lax.ppermute(head, axis, [((i + 1) % count, i) for i in range(count)]),
            ],
            axis=dim,
        )
    return cells


def passed_along(value, axis, steps):
    count = lax.axis_size(axis)
    pairs = [(source, (source + steps) % count) for source in range(count)]
    return lax.ppermute(value, axis, pairs)


def contract_cells(left, right):
    return lax.dot_general(
        left, right, (((0, 1, 2), (0, 1, 2)), ((), ())), preferred_element_type=jnp.float32
    )


def plane_tap(padded, shift_x, shift_y, rows_x, rows_y):
    return padded[1 + shift_x : 1 + shift_x + rows_x, 1 + shift_y : 1 + shift_y + rows_y]


def plane_pad(source):
    rimmed = padded_2(source, (("gx", 0),), 1)
    return jnp.pad(rimmed, ((0, 0), (1, 1), (0, 0), (0, 0)))


def slab_windows(source, dilation):
    slab_depth = source.shape[2]
    above = passed_along(source, "gz", -1)
    above_far = passed_along(source, "gz", -2)
    below = passed_along(source, "gz", 1)
    below_far = passed_along(source, "gz", 2)
    ahead_rows = jnp.concatenate([source, above, above_far], axis=2)
    behind_rows = jnp.concatenate([below_far, below, source], axis=2)
    upper = lax.dynamic_slice_in_dim(ahead_rows, dilation, slab_depth, 2)
    lower = lax.dynamic_slice_in_dim(behind_rows, 2 * slab_depth - dilation, slab_depth, 2)
    return (lower, upper)


def normalize(hidden, gains, cell_count):
    average = lax.psum(jnp.sum(hidden, axis=(0, 1, 2)), ("gz", "gx")) / cell_count
    centered = hidden - average
    spread = lax.psum(jnp.sum(centered * centered, axis=(0, 1, 2)), ("gz", "gx")) / cell_count
    inverse_std = lax.rsqrt(spread + eps_norm)
    whitened = (hidden - average) * inverse_std
    return ((whitened * gains).astype(jnp.bfloat16), whitened, inverse_std)


def norm_back(d_normed, whitened, inverse_std, gains, cell_count):
    scaled = d_normed * gains
    sum_grad, sum_cross = lax.psum(
        (jnp.sum(scaled, axis=(0, 1, 2)), jnp.sum(scaled * whitened, axis=(0, 1, 2))), ("gz", "gx")
    )
    d_hidden = inverse_std * (scaled - sum_grad / cell_count - whitened * (sum_cross / cell_count))
    return (d_hidden, jnp.sum(d_normed * whitened, axis=(0, 1, 2)))


def conv_forward(normed, dilation, weights_z, weights_xy):
    rows_x, rows_y = (normed.shape[0], normed.shape[1])
    lower, upper = slab_windows(normed, dilation)
    padded = plane_pad(normed)
    summed = jnp.dot(lower, weights_z[0], preferred_element_type=jnp.float32)
    summed = summed + jnp.dot(normed, weights_z[1], preferred_element_type=jnp.float32)
    summed = summed + jnp.dot(upper, weights_z[2], preferred_element_type=jnp.float32)
    for tap_number, (shift_x, shift_y) in enumerate(plane_offsets):
        summed = summed + jnp.dot(
            plane_tap(padded, shift_x, shift_y, rows_x, rows_y),
            weights_xy[tap_number],
            preferred_element_type=jnp.float32,
        )
    return summed


def conv_backward_split(pre_cot, normed, dilation, weights_z, weights_xy):
    rows_x, rows_y = (normed.shape[0], normed.shape[1])
    lower_cot, upper_cot = slab_windows(pre_cot, dilation)
    padded_cot = plane_pad(pre_cot)
    d_normed = jnp.dot(upper_cot, weights_z[0].T, preferred_element_type=jnp.float32)
    d_normed = d_normed + jnp.dot(pre_cot, weights_z[1].T, preferred_element_type=jnp.float32)
    d_normed = d_normed + jnp.dot(lower_cot, weights_z[2].T, preferred_element_type=jnp.float32)
    xy_terms = []
    for tap_number, (shift_x, shift_y) in enumerate(plane_offsets):
        shifted = plane_tap(padded_cot, -shift_x, -shift_y, rows_x, rows_y)
        d_normed = d_normed + jnp.dot(
            shifted, weights_xy[tap_number].T, preferred_element_type=jnp.float32
        )
        xy_terms.append(contract_cells(normed, shifted))
    z_terms = jnp.stack(
        [
            contract_cells(normed, upper_cot),
            contract_cells(normed, pre_cot),
            contract_cells(normed, lower_cot),
        ]
    )
    return (d_normed, z_terms, jnp.stack(xy_terms))


def per_device_split(
    clean_field,
    noise_field,
    timestep,
    dilations,
    w_in,
    w_time,
    w_z,
    w_xy,
    w_point,
    biases,
    norm_gains,
    w_out,
):
    layer_total = w_z.shape[0]
    rows_x, rows_y, slab_depth = (clean_field.shape[1], clean_field.shape[2], clean_field.shape[3])
    plane_cells = rows_x * lax.axis_size("gx") * slab_depth * lax.axis_size("gz")
    cell_count = float(plane_cells * rows_y)
    inv_area = 1.0 / plane_cells
    alpha_bar, features, time_raw, time_code = time_terms(timestep, w_time)
    noisy = jnp.sqrt(alpha_bar) * clean_field + jnp.sqrt(1.0 - alpha_bar) * noise_field
    stream = jnp.einsum("kxyz,kc->xyzc", noisy, w_in, precision=highest)
    saved = []
    for which_layer in range(layer_total):
        normed, whitened, inverse_std = normalize(stream, norm_gains[which_layer], cell_count)
        pre_act = conv_forward(normed, dilations[which_layer], w_z[which_layer], w_xy[which_layer])
        pre_act = pre_act + biases[which_layer] + time_code
        activated = jax.nn.gelu(pre_act).astype(jnp.bfloat16)
        saved.append((normed, whitened, inverse_std, pre_act, activated))
        stream = stream + jnp.dot(
            activated, w_point[which_layer], preferred_element_type=jnp.float32
        )
    out_normed, out_white, out_inverse = normalize(stream, norm_gains[layer_total], cell_count)
    prediction = jnp.einsum("xyzc,kc->kxyz", out_normed, w_out, preferred_element_type=jnp.float32)
    misfit = prediction - noise_field
    d_out = jnp.einsum("kxyz,kc->xyzc", misfit, w_out.astype(jnp.float32), precision=highest)
    out_raw = jnp.einsum(
        "kxyz,xyzc->kc", misfit, out_normed, precision=highest, preferred_element_type=jnp.float32
    )
    d_stream, out_gain_raw = norm_back(
        d_out, out_white, out_inverse, norm_gains[layer_total], cell_count
    )
    z_list, xy_list, point_list, bias_list, gain_list = ([], [], [], [], [])
    for which_layer in reversed(range(layer_total)):
        normed, whitened, inverse_std, pre_act, activated = saved[which_layer]
        stream_cot = d_stream.astype(jnp.bfloat16)
        point_raw = contract_cells(activated, stream_cot)
        d_act = jnp.dot(stream_cot, w_point[which_layer].T, preferred_element_type=jnp.float32)
        gelu_back = jax.vjp(jax.nn.gelu, pre_act)[1]
        pre_cot = gelu_back(d_act)[0].astype(jnp.bfloat16)
        bias_raw = jnp.sum(pre_cot, axis=(0, 1, 2), dtype=jnp.float32)
        d_normed, z_raw, xy_raw = conv_backward_split(
            pre_cot, normed, dilations[which_layer], w_z[which_layer], w_xy[which_layer]
        )
        d_back, gain_raw = norm_back(
            d_normed, whitened, inverse_std, norm_gains[which_layer], cell_count
        )
        d_stream = d_stream + d_back
        z_list.insert(0, z_raw)
        xy_list.insert(0, xy_raw)
        point_list.insert(0, point_raw)
        bias_list.insert(0, bias_raw)
        gain_list.insert(0, gain_raw)
    field_grad = jnp.einsum("xyzc,kc->kxyz", d_stream, w_in, precision=highest)
    in_raw = jnp.einsum("kxyz,xyzc->kc", noisy, d_stream, precision=highest)
    z_all, xy_all, point_all, bias_all, gain_all, in_raw, out_raw = lax.psum(
        (
            jnp.stack(z_list),
            jnp.stack(xy_list),
            jnp.stack(point_list),
            jnp.stack(bias_list),
            jnp.stack(gain_list + [out_gain_raw]),
            in_raw,
            out_raw,
        ),
        ("gz", "gx"),
    )
    time_back = jax.vjp(jax.nn.silu, time_raw)[1](jnp.sum(bias_all, axis=0))[0]
    grad_w_time = inv_area * jnp.outer(features, time_back)
    return (
        prediction,
        field_grad,
        inv_area * in_raw,
        grad_w_time,
        inv_area * z_all,
        inv_area * xy_all,
        inv_area * point_all,
        inv_area * bias_all,
        inv_area * gain_all,
        inv_area * out_raw,
    )


def per_device(*args):
    members, groups = lax.axis_size("gz"), lax.axis_size("gx")
    _, rows_x, rows_y, depth = args[0].shape
    small = rows_x == 1 and rows_y == 4 and members == 4 and groups == 8 and depth * members == 2 * REACH
    return per_device_grouped(*args) if small else per_device_split(*args)


def solution(mesh):
    return jax.shard_map(
        per_device,
        mesh=mesh,
        in_specs=(
            P(None, "gx", None, "gz"),
            P(None, "gx", None, "gz"),
            P(),
            P(),
            P(),
            P(),
            P(),
            P(),
            P(),
            P(),
            P(),
            P(),
        ),
        out_specs=(
            P(None, "gx", None, "gz"),
            P(None, "gx", None, "gz"),
            P(),
            P(),
            P(),
            P(),
            P(),
            P(),
            P(),
            P(),
        ),
        check_vma=False,
    )
```

```python
import functools
import math

import jax
import jax.numpy as jnp
from jax import lax
from jax.experimental import pallas as pl
from jax.experimental.pallas import tpu as pltpu
from jax.sharding import PartitionSpec as P

STEPS = 1000
REACH = 256
RIM = 4
TILE = 16
LIMITS = (4, 14, 10, 7, 10, 8, 10, 2, 6)

eps_norm = 1e-05
highest = lax.Precision.HIGHEST
bf16 = jnp.bfloat16
f32 = jnp.float32
plane_offsets = ((-1, -1), (-1, 0), (-1, 1), (0, -1), (0, 1), (1, -1), (1, 0), (1, 1))


def time_terms(timestep, w_time):
    moment = timestep[0].astype(jnp.float32)
    half_width = w_time.shape[0] // 2
    alpha_bar = jnp.cos(0.5 * math.pi * (moment + 0.5) / STEPS) ** 2
    ladder = jnp.exp(-math.log(10000.0) * jnp.arange(half_width, dtype=jnp.float32) / half_width)
    angles = moment * ladder
    features = jnp.concatenate([jnp.sin(angles), jnp.cos(angles)])
    time_raw = jnp.dot(features, w_time, precision=highest)
    return (alpha_bar, features, time_raw, jax.nn.silu(time_raw))


def mm(left, right):
    return lax.dot_general(left, right, (((1,), (0,)), ((), ())), preferred_element_type=f32)


def mm_nt(left, right):
    return lax.dot_general(left, right, (((1,), (1,)), ((), ())), preferred_element_type=f32)


def mm_tn(left, right):
    return lax.dot_general(left, right, (((0,), (0,)), ((), ())), preferred_element_type=f32)


def halves(value):
    high = value.astype(bf16)
    return high, (value - high.astype(f32)).astype(bf16)


def wide(vector):
    return jnp.concatenate([vector] * 4, axis=1)


def folded(vector):
    channels = vector.shape[1] // 4
    return sum(vector[:, y * channels : (y + 1) * channels] for y in range(4))


class Place:
    def __init__(self, sc, rows):
        self.rows = rows
        self.members = lax.axis_size("gz")
        self.member = lax.axis_index("gz")
        self.small = jnp.minimum(sc[0], sc[1])
        self.coarse = self.small >= self.members
        tiles = rows // TILE
        self.tiles = tiles
        self.stride = jnp.where(self.coarse, tiles - 1, tiles)
        self.span = REACH // self.members + 2 * RIM
        far = jnp.where(self.coarse, REACH // self.members, self.span)
        near = jnp.where(self.coarse, self.small // self.members, 1)
        self.steps = [jnp.where(sc[l] == REACH, far, near) for l in range(2)]

    def index(self, shape):
        row = lax.broadcasted_iota(jnp.int32, shape, 0)
        return lax.rem(row, TILE) * self.stride + row // TILE, row // TILE

    def own(self, shape):
        place, tile = self.index(shape)
        inside = lax.rem(place, self.span)
        near = ((inside >= RIM) & (inside < self.span - RIM)).astype(jnp.int32)
        far = (tile < self.tiles - 1).astype(jnp.int32)
        return jnp.where(self.coarse, far, near) == 1

    def pick(self, cells_z):
        shape = (self.rows, cells_z)
        return self.z_of(shape, cells_z) == lax.broadcasted_iota(jnp.int32, shape, 1)

    def z_of(self, shape, cells_z):
        place, _ = self.index(shape)
        residues = jnp.minimum(self.small, self.members)
        part, start = self.member // residues, lax.rem(self.member, residues)
        period = place // self.span
        inside = place - period * self.span - RIM + part * (REACH // self.members)
        near = start + residues * inside + period * REACH
        z = jnp.where(self.coarse, place * self.members + self.member, near)
        return lax.rem(z + 2 * cells_z, cells_z)


def build_taps(block_of, taps, taps_z):
    channels = taps_z.shape[-1] // 2
    zero = jnp.zeros((channels, channels), bf16)
    for i in range(3):
        for j in range(3):
            block = block_of(i, j)
            for q in range(2):
                for side in range(2):
                    y_in = 2 * q + side + j - 1
                    if 0 <= y_in < 4:
                        taps[
                            q,
                            i,
                            y_in * channels : (y_in + 1) * channels,
                            side * channels : (side + 1) * channels,
                        ] = block
        for q in range(2):
            for side in range(2):
                for y_in in range(4):
                    if abs(y_in - 2 * q - side) > 1:
                        taps[
                            q,
                            i,
                            y_in * channels : (y_in + 1) * channels,
                            side * channels : (side + 1) * channels,
                        ] = zero
    for m in range(2):
        build_pair(block_of(3, m), taps_z, m)


def build_pair(block, target, m):
    channels = block.shape[-1]
    zero = jnp.zeros((channels, channels), bf16)
    target[m, :channels, :channels] = block
    target[m, channels:, channels:] = block
    target[m, :channels, channels:] = zero
    target[m, channels:, :channels] = zero


def forward_blocks(w_z, w_xy, layer):
    def block_of(i, j):
        if i == 3:
            return w_z[layer, 2 * j]
        at = i * 3 + j
        return w_z[layer, 1] if at == 4 else w_xy[layer, at - (at > 4)]

    return block_of


def taken(weights, layer):
    return lambda i, j: weights[layer, i * 3 + j]


def kernel_mix(amounts, clean_far, noise_far, mixed, clean, noise, sems):
    parts = mixed.shape[0]
    copies = [
        pltpu.make_async_copy(clean_far, clean, sems.at[0]),
        pltpu.make_async_copy(noise_far, noise, sems.at[1]),
    ]
    for copy in copies:
        copy.start()
    for copy in copies:
        copy.wait()
    for k in range(3):
        noisy = amounts[0] * clean[k, 0] + amounts[1] * noise[k, 0]
        for part in range(parts):
            mixed[part, 4 * k : 4 * k + 4] = noisy
            mixed[part, 12 + 4 * k : 16 + 4 * k] = noise[k, 0]


def kernel_prepare(w_z, w_xy, w_point, w_in, w_out, gains, w_front, point, w_back, point_back, lift_in,
                   lift_out, w_in_on, gains_on):
    w_in_on[...] = w_in[...]
    gains_on[...] = gains[...]
    point[...] = w_point[...]
    for layer in range(2):
        forward = forward_blocks(w_z, w_xy, layer)
        for i in range(3):
            for j in range(3):
                w_front[layer, i * 3 + j] = forward(i, j)
        for m in range(2):
            w_front[layer, 9 + m] = forward(3, m)
        for i in range(3):
            for j in range(3):
                w_back[layer, i * 3 + j] = forward(2 - i, 2 - j).T
        for m in range(2):
            w_back[layer, 9 + m] = forward(3, 1 - m).T
        point_back[layer] = w_point[layer].T
    whole = spread_rows(w_in[...], 0)
    high, low = halves(whole)
    lift_in[0:32] = high
    lift_in[32:64] = high
    lift_in[64:96] = low
    lift_in[96:128] = jnp.zeros_like(low)
    high = spread_rows(w_out[...].astype(f32), 3).astype(bf16)
    lift_out[0:32] = high
    lift_out[32:64] = high
    lift_out[64:96] = jnp.zeros_like(high)
    lift_out[96:128] = jnp.zeros_like(high)


def spread_rows(weights, first):
    channels = weights.shape[1]
    zero = jnp.zeros((1, channels), f32)
    rows = [jnp.zeros((1, 4 * channels), f32)] * 32
    for k in range(3):
        for y in range(4):
            parts = [weights[k : k + 1] if at == y else zero for at in range(4)]
            rows[(first + k) * 4 + y] = jnp.concatenate(parts, axis=1)
    return jnp.concatenate(rows, axis=0)


def fill_rims(padded, planes):
    padded[0] = padded[planes]
    padded[planes + 1] = padded[1]


def fill_shifted(place, layer, padded, shifted, planes):
    step, stride = place.steps[layer], place.stride
    for tile in range(place.tiles):
        for way in range(2):
            at = tile - step if way == 0 else tile + step
            moved = at + TILE * stride
            source = lax.rem(moved, stride)
            turn = lax.rem(2 * TILE - moved // stride, TILE)
            rows = padded[1 : planes + 1, pl.ds(pl.multiple_of(source * TILE, TILE), TILE), :]
            rows = pltpu.roll(rows.astype(f32), turn, 1)
            shifted[way, :, tile * TILE : (tile + 1) * TILE, :] = rows.astype(bf16)


def conv_half(padded, shifted, taps, taps_z, x0, count, q):
    rows, lanes = padded.shape[1:]
    half = lanes // 2
    total = None
    for i in range(3):
        part = mm(padded[x0 + i : x0 + i + count].reshape(count * rows, lanes), taps[q, i])
        total = part if total is None else total + part
    for m in range(2):
        source = shifted[m, x0 : x0 + count, :, q * half : (q + 1) * half]
        total = total + mm(source.reshape(count * rows, half), taps_z[m])
    return total


def gelu_pair(value):
    scale = math.sqrt(2.0 / math.pi)
    square = value * value
    bent = jnp.tanh(value * (scale + (scale * 0.044715) * square))
    half = 0.5 + 0.5 * bent
    slope = half + value * (0.5 - 0.5 * (bent * bent)) * (scale + (3.0 * 0.044715 * scale) * square)
    return value * half, slope


def members_of(parts):
    found = []
    for part in parts:
        for at in range(0, part.shape[0], 8):
            found.append(part[at : at + 8])
    return found


def merged_stats(parts, per_member):
    found = members_of(parts)
    mean = sum(one[0:1] for one in found) / (per_member * len(found))
    spread = sum(one[1:2] for one in found)
    for one in found:
        gap = one[0:1] / per_member - mean
        spread = spread + per_member * gap * gap
    return mean, lax.rsqrt(spread / (per_member * len(found)) + eps_norm)


def put_rows(ref, *vectors):
    rows = list(vectors)
    rows += [jnp.zeros((1, ref.shape[1]), f32)] * (ref.shape[0] - len(rows))
    ref[...] = jnp.concatenate(rows, axis=0)


def masked_total(mask, value):
    return folded(jnp.sum(jnp.where(mask, value, 0.0), axis=0, keepdims=True))


def layer_forward(place, layer, padded, shifted, taps, taps_z, pair, w_front, wp, shift_bias, old,
                  stream, act, slope, stats, acc, per_member):
    planes, rows, lanes = stream.shape
    half = lanes // 2
    count = planes // 4
    build_taps(taken(w_front, layer), taps, taps_z)
    build_pair(wp[layer], pair, 0)
    fill_rims(padded, planes)
    fill_shifted(place, layer, padded, shifted, planes)
    acc[...] = jnp.zeros_like(acc)
    bias = wide(shift_bias[layer : layer + 1, :])[:, :half]

    for x0 in range(0, planes, count):
        part = slice(x0, x0 + count)
        for q in range(2):
            side = slice(q * half, (q + 1) * half)
            pre = conv_half(padded, shifted, taps, taps_z, x0, count, q) + bias
            value, grad = gelu_pair(pre)
            act[part, :, side] = value.astype(bf16).reshape(count, rows, half)
            slope[part, :, side] = grad.astype(bf16).reshape(count, rows, half)
    for x0 in range(0, planes, count):
        part = slice(x0, x0 + count)
        for q in range(2):
            side = slice(q * half, (q + 1) * half)
            branch = mm(act[part, :, side].reshape(count * rows, half), pair[0])
            new = old[part, :, side] + branch.reshape(count, rows, half)
            stream[part, :, side] = new
            acc[:, side] += jnp.sum(new, axis=0)
    mask = place.own((rows, lanes))
    total = masked_total(mask, acc[...])
    mean = wide(total / per_member)
    spread = jnp.zeros((rows, lanes), f32)
    for x in range(planes):
        gap = stream[x] - mean
        spread = spread + gap * gap
    put_rows(stats, total, masked_total(mask, spread))


def kernel_first(cells_z, per_member, sc, near, far, lift_in, w_in, gains, shift_bias, w_front, wp,
                 stream, normed, act, slope, gathered, stats, consts,
                 padded, shifted, taps, taps_z, pair, acc, old, source):
    planes, rows, lanes = stream.shape
    channels = lanes // 4
    depth = near.shape[2]
    place = Place(sc, rows)
    cell_count = float(planes * 4 * cells_z)
    comps = [
        jnp.concatenate([ref[:, 4 * k : 4 * k + 4, :] for ref in (near, far)], axis=0) for k in range(3)
    ]

    def all_sum(value):
        value = jnp.sum(jnp.sum(value, axis=0), axis=0, keepdims=True)
        return jnp.sum(value, axis=1, keepdims=True)

    means = [all_sum(comp) / cell_count for comp in comps]
    gaps = [comp - mean[None] for comp, mean in zip(comps, means)]
    covs = {}
    for j in range(3):
        for k in range(j, 3):
            covs[j, k] = all_sum(gaps[j] * gaps[k]) / cell_count
    rows_in = [w_in[k : k + 1, :] for k in range(3)]
    mean_c = sum(means[k] * rows_in[k] for k in range(3))
    var_c = jnp.zeros((1, channels), f32)
    for (j, k), cov in covs.items():
        var_c = var_c + (1.0 if j == k else 2.0) * cov * (rows_in[j] * rows_in[k])
    inv_c = lax.rsqrt(jnp.maximum(var_c, 0.0) + eps_norm)
    flat = [jnp.broadcast_to(value, (1, channels)) for value in means + list(covs.values())]
    put_rows(consts, mean_c, inv_c, *flat)
    blank = jnp.zeros((8, depth), f32)
    core = lax.rem(place.member, 2)
    for slab in range(cells_z // depth):
        ref, side = (near, core) if slab % 2 == 0 else (far, 1 - core)
        at = pl.ds(pl.multiple_of((slab // 2 * 2 + side) * depth, depth), depth)
        for x in range(planes):
            high, low = halves(jnp.concatenate([ref[slab // 2 * planes + x], blank], axis=0))
            source[x, 0:32, at] = high
            source[x, 32:64, at] = low
            source[x, 64:96, at] = high
            source[x, 96:128, at] = jnp.zeros_like(high)
    pick = place.pick(cells_z).astype(f32).astype(bf16)
    scale = wide(inv_c * gains[0:1, :])
    mean_w = wide(mean_c)
    for x in range(planes):
        gathered[x] = mm_nt(pick, source[x]).astype(bf16)
    for x0 in range(0, planes, planes // 2):
        part = slice(x0, x0 + planes // 2)
        value = mm(gathered[part].reshape(planes // 2 * rows, 128), lift_in[...])
        unit = ((value - mean_w) * scale).astype(bf16).reshape(planes // 2, rows, lanes)
        old[part] = value.reshape(planes // 2, rows, lanes)
        padded[x0 + 1 : x0 + 1 + planes // 2] = unit
        normed[part] = unit
    layer_forward(place, 0, padded, shifted, taps, taps_z, pair, w_front, wp, shift_bias, old, stream,
                  act, slope, stats, acc, per_member)


def kernel_second(per_member, sc, *refs):
    parts, refs = refs[:4], refs[4:]
    (old, gains, shift_bias, w_front, wp, stream, normed, act, slope, stats, consts,
     padded, shifted, taps, taps_z, pair, acc) = refs
    planes, rows, _ = stream.shape
    place = Place(sc, rows)
    mean, inverse = merged_stats(parts, per_member)
    put_rows(consts, mean, inverse)
    mean_w, scale = wide(mean), wide(inverse * gains[1:2, :])
    for x in range(planes):
        unit = ((old[x] - mean_w) * scale).astype(bf16)
        padded[x + 1] = unit
        normed[x] = unit
    layer_forward(place, 1, padded, shifted, taps, taps_z, pair, w_front, wp, shift_bias, old, stream,
                  act, slope, stats, acc, per_member)


def kernel_out(per_member, sc, *refs):
    parts, refs = refs[:4], refs[4:]
    stream, gains, gathered, lift_out, prediction, misfit, sums, w_out_raw, consts, unit = refs
    planes, rows, lanes = stream.shape
    place = Place(sc, rows)
    mean, inverse = merged_stats(parts, per_member)
    put_rows(consts, mean, inverse)
    mean_w, inv_w, gain_w = wide(mean), wide(inverse), wide(gains[2:3, :])
    scale = inv_w * gain_w
    for x in range(planes):
        unit[x] = ((stream[x] - mean_w) * scale).astype(bf16)
    row = lax.broadcasted_iota(jnp.int32, (128, 128), 0)
    col = lax.broadcasted_iota(jnp.int32, (128, 128), 1)
    slot = lax.rem(col, 32)
    used = (col < 64) & (slot >= 12) & (slot < 24)
    take = (used & ((row == slot) | (row == slot + 32))).astype(f32).astype(bf16)
    total = mm_nt(unit[...].reshape(planes * rows, lanes), lift_out[...])
    noise = mm(gathered[...].reshape(planes * rows, 128), take)
    gap = total - noise
    high, low = halves(gap)
    lane = lax.broadcasted_iota(jnp.int32, gap.shape, 1)
    both = jnp.where(lane < 32, high.astype(f32), low.astype(f32)).astype(bf16)
    misfit[...] = both.reshape(planes, rows, 128)
    for x in range(planes):
        @pl.when(lax.axis_index("gx") == x)
        def _(x=x):
            prediction[...] = total[x * rows : (x + 1) * rows]
    plain = jnp.zeros((rows, lanes), f32)
    cross = jnp.zeros((rows, lanes), f32)
    for x0 in range(0, planes, planes // 2):
        part = slice(x0 * rows, (x0 + planes // 2) * rows)
        d_out = mm(both[part], lift_out[...]).reshape(planes // 2, rows, lanes)
        for x in range(planes // 2):
            plain = plain + d_out[x]
            cross = cross + d_out[x] * ((stream[x0 + x] - mean_w) * inv_w)
    own = place.own((rows, 128))
    kept = jnp.concatenate([jnp.where(own, misfit[x].astype(f32), 0.0) for x in range(planes)], axis=0)
    raw = mm_tn(kept.astype(bf16), unit[...].reshape(planes * rows, lanes))
    mask = place.own((rows, lanes))
    put_rows(sums, masked_total(mask, plain), masked_total(mask, cross))
    put_rows(w_out_raw, *by_component(raw[0:32] + raw[32:64], 3))


def by_component(raw, first):
    channels = raw.shape[1] // 4
    found = []
    for k in range(first, first + 3):
        found.append(
            sum(raw[k * 4 + y : k * 4 + y + 1, y * channels : (y + 1) * channels] for y in range(4))
        )
    return found


def branch_backward(planes, d_stream_of, pair, slope, padded, scot, bias_acc):
    rows, lanes = padded.shape[1:]
    half = lanes // 2
    count = planes // 2

    for x0 in range(0, planes, count):
        part = slice(x0, x0 + count)
        for x in range(x0, x0 + count):
            scot[x] = d_stream_of(x).astype(bf16)
        for q in range(2):
            side = slice(q * half, (q + 1) * half)
            cot = scot[part, :, side].reshape(count * rows, half)
            d_act = mm(cot, pair[0]).reshape(count, rows, half)
            pre = (d_act * slope[part, :, side].astype(f32)).astype(bf16)
            padded[x0 + 1 : x0 + 1 + count, :, side] = pre
            bias_acc[:, side] += jnp.sum(pre.astype(f32), axis=0)


def weight_grads(place, planes, padded, shifted, scot, normed, act, keep, give, taps_all, share):
    rows, lanes = padded.shape[1:]
    channels = lanes // 4
    wide_share = 4 * share
    row = lax.broadcasted_iota(jnp.int32, (lanes, wide_share), 0)
    col = lax.broadcasted_iota(jnp.int32, (lanes, wide_share), 1)
    hit = (row // channels == col // share) & (
        lax.rem(row, channels) == lax.rem(col, share) + lax.axis_index("gx") * share
    )
    choose = hit.astype(f32).astype(bf16)
    mask = jnp.concatenate([place.own((rows, wide_share))] * planes, axis=0)

    def turned(source):
        got = mm(source[...].reshape(planes * rows, lanes), choose)
        return jnp.where(mask, got, 0.0).astype(bf16)

    def add_blocks(raw, j):
        return sum(
            raw[(y + j) * share : (y + j + 1) * share, y * channels : (y + 1) * channels]
            for y in range(4)
            if 0 <= y + j < 4
        )

    left = turned(normed)
    for i in range(3):
        raw = mm_tn(left, padded[2 - i : 2 - i + planes].reshape(planes * rows, lanes))
        for j in range(3):
            taps_all[i * 3 + j] = add_blocks(raw, j - 1)
    for m in range(2):
        raw = mm_tn(left, shifted[1 - m].reshape(planes * rows, lanes))
        taps_all[9 + m] = add_blocks(raw, 0)
    raw = mm_tn(turned(act), scot[...].reshape(planes * rows, lanes))
    taps_all[11] = add_blocks(raw, 0)
    odd, half = lax.rem(place.member, 2), keep.shape[0]
    keep[...] = taps_all[pl.ds(odd * half, half)]
    give[...] = taps_all[pl.ds((1 - odd) * half, half)]


def conv_backward(planes, padded, shifted, taps, taps_z, emit):
    count = planes // 4

    for x0 in range(0, planes, count):
        for q in range(2):
            emit(x0, count, q, conv_half(padded, shifted, taps, taps_z, x0, count, q))


def kernel_back_second(cell_count, sc, *refs):
    parts, refs = refs[:4], refs[4:]
    (stream, out_consts, gains, misfit, lift_out, slope, normed, w_back, point_back,
     d_stream, d_normed, sums, padded, shifted, scot,
     taps, taps_z, pair, acc, acc2) = refs
    planes, rows, lanes = stream.shape
    half = lanes // 2
    place = Place(sc, rows)
    sums_out = sum(members_of(parts))
    gain_w = wide(gains[2:3, :])
    mean_w, inv_w = wide(out_consts[0:1]), wide(out_consts[1:2])
    m_plain = gain_w * wide(sums_out[0:1]) / cell_count
    m_cross = gain_w * wide(sums_out[1:2]) / cell_count
    build_pair(point_back[1], pair, 0)
    build_taps(taken(w_back, 1), taps, taps_z)
    acc[...] = jnp.zeros_like(acc)

    def d_stream_of(x):
        d_out = mm(misfit[x], lift_out[...])
        white = (stream[x] - mean_w) * inv_w
        value = inv_w * (gain_w * d_out - m_plain - white * m_cross)
        d_stream[x] = value
        return value

    branch_backward(planes, d_stream_of, pair, slope, padded, scot, acc)
    mask = place.own((rows, lanes))
    s_bias = masked_total(mask, acc[...])
    acc[...] = jnp.zeros_like(acc)
    acc2[...] = jnp.zeros_like(acc2)
    fill_rims(padded, planes)
    fill_shifted(place, 1, padded, shifted, planes)

    def emit(x0, count, q, value):
        side = slice(q * half, (q + 1) * half)
        value = value.reshape(count, rows, half)
        d_normed[x0 : x0 + count, :, side] = value
        acc[:, side] += jnp.sum(value, axis=0)
        acc2[:, side] += jnp.sum(value * normed[x0 : x0 + count, :, side].astype(f32), axis=0)

    conv_backward(planes, padded, shifted, taps, taps_z, emit)
    s_plain = masked_total(mask, acc[...])
    s_cross = masked_total(mask, acc2[...]) / gains[1:2, :]
    put_rows(sums, s_plain, s_cross, s_bias)


def kernel_weights_second(share, sc, padded, shifted, scot, normed, act, keep, give, taps_all):
    planes, rows, _ = scot.shape
    weight_grads(Place(sc, rows), planes, padded, shifted, scot, normed, act, keep, give, taps_all, share)


def kernel_back_first(share, cell_count, sc, *refs):
    parts, refs = refs[:4], refs[4:]
    (consts, d_next, d_normed, normed_next, gains, act, slope, normed, point_back,
     d_stream, sums, keep, give, padded, shifted,
     pair, acc, scot, taps_all) = refs
    planes, rows, lanes = d_next.shape
    place = Place(sc, rows)
    sums_in = sum(members_of(parts))
    gain_w = wide(gains[1:2, :])
    inv_w = wide(consts[1:2])
    m_plain = gain_w * wide(sums_in[0:1]) / cell_count
    m_cross = wide(sums_in[1:2]) / cell_count
    build_pair(point_back[0], pair, 0)
    acc[...] = jnp.zeros_like(acc)

    def d_stream_of(x):
        back = gain_w * d_normed[x] - m_plain - normed_next[x].astype(f32) * m_cross
        value = d_next[x] + inv_w * back
        d_stream[x] = value
        return value

    branch_backward(planes, d_stream_of, pair, slope, padded, scot, acc)
    put_rows(sums, masked_total(place.own((rows, lanes)), acc[...]))
    fill_rims(padded, planes)
    fill_shifted(place, 0, padded, shifted, planes)
    weight_grads(place, planes, padded, shifted, scot, normed, act, keep, give, taps_all, share)


def kernel_last(depth, sc, padded, shifted, d_stream, normed, gains, consts, gathered, lift_in, w_back,
                prediction, sums_bias, out_raw, own_out, out_1, out_2, out_3,
                taps, taps_z, acc, acc2, high, low):
    planes, rows, lanes = d_stream.shape
    half = lanes // 2
    place = Place(sc, rows)
    build_taps(taken(w_back, 0), taps, taps_z)
    acc[...] = jnp.zeros_like(acc)
    acc2[...] = jnp.zeros_like(acc2)
    scale = wide(consts[1:2] * gains[0:1, :])

    def emit(x0, count, q, value):
        side = slice(q * half, (q + 1) * half)
        part = slice(x0, x0 + count)
        value = value.reshape(count, rows, half)
        acc[:, side] += jnp.sum(value, axis=0)
        acc2[:, side] += jnp.sum(value * normed[part, :, side].astype(f32), axis=0)
        full = d_stream[part, :, side] + value * scale[:, side]
        first, second = halves(full)
        high[part, :, side] = first
        low[part, :, side] = second

    conv_backward(planes, padded, shifted, taps, taps_z, emit)
    mask = place.own((rows, lanes))
    s_plain = masked_total(mask, acc[...])
    s_cross = masked_total(mask, acc2[...]) / gains[0:1, :]
    own = place.own((rows, 128))
    kept = jnp.concatenate([jnp.where(own, gathered[x].astype(f32), 0.0) for x in range(planes)], axis=0)
    kept = kept.astype(bf16)
    raw = mm_tn(kept, high[...].reshape(planes * rows, lanes))
    raw_low = mm_tn(kept, low[...].reshape(planes * rows, lanes))
    in_raw = by_component(raw[0:32] + raw[32:64] + raw_low[0:32], 0)
    blank = jnp.zeros((1, s_plain.shape[1]), f32)
    tail = jnp.concatenate([s_plain, s_cross] + [blank] * 6 + in_raw + [blank] * 5, axis=0)
    tail = jnp.concatenate([tail, sums_bias[...], out_raw[...]], axis=0)
    here = lax.axis_index("gx")
    lane = lax.broadcasted_iota(jnp.int32, (rows, 128), 1)
    field = mm_nt(high[here], lift_in[...]) + jnp.where(lane < 32, mm_nt(low[here], lift_in[...]), 0.0)
    field = jnp.where((lane >= 32) & (lane < 64), 0.0, field)
    field = field + jnp.where((lane >= 12) & (lane < 24), prediction[...], 0.0)
    cells_z = depth * place.members
    whole = place.z_of((rows, depth), cells_z)
    column = lax.broadcasted_iota(jnp.int32, (rows, depth), 1)
    mask = place.own((rows, depth))
    first, second = halves(field)
    for bit, target in enumerate((own_out, out_1, out_2, out_3)):
        there = lax.bitwise_xor(place.member, bit)
        pick = ((whole == column + there * depth) & mask).astype(f32).astype(bf16)
        out = mm_tn(first, pick) + mm_tn(second, pick)
        target[0:32] = out[0:32] + out[64:96]
        target[32:64] = tail


def call(kernel, outs, scratch, flops, limit, *args, scalars=True, loose=()):
    spec = pl.BlockSpec(memory_space=pltpu.VMEM)
    specs = [pl.BlockSpec(memory_space=pltpu.SMEM)] * scalars + [spec] * (len(args) - scalars)
    for at in loose:
        specs[at] = pl.BlockSpec(memory_space=pl.ANY)
    return pl.pallas_call(
        kernel,
        out_shape=[jax.ShapeDtypeStruct(shape, dtype) for shape, dtype in outs],
        in_specs=specs,
        out_specs=[spec] * len(outs),
        scratch_shapes=[pltpu.VMEM(*one) if isinstance(one, tuple) else one for one in scratch],
        compiler_params=pltpu.CompilerParams(vmem_limit_bytes=limit * 2**20),
        cost_estimate=pl.CostEstimate(flops=flops, bytes_accessed=2**23, transcendentals=0),
    )(*args)


def swapped(value, axis, bit):
    count = lax.axis_size(axis)
    return lax.ppermute(value, axis, [(i, i ^ bit) for i in range(count)])


def group_parts(value):
    return (value,) + tuple(swapped(value, "gz", bit) for bit in (1, 2, 3))


def group_grads(keep, give):
    mine = keep + swapped(give, "gz", 1)
    return mine + swapped(mine, "gz", 2)


def all_grads(first, second):
    groups = lax.axis_size("gx")
    taps, share, channels = first.shape
    mine = jnp.concatenate([first, second], axis=0).astype(bf16)
    mine = mine.reshape(2 * taps * share, channels)
    near = lax.all_to_all(jnp.broadcast_to(mine[None], (groups,) + mine.shape), "gx", 0, 0)
    far = swapped(near, "gz", 1)
    odd = lax.rem(lax.axis_index("gz"), 2) == 1

    def laid_out(every):
        every = every.reshape(groups, 2, taps, share, channels).transpose(1, 2, 0, 3, 4)
        return every.reshape(2, taps, groups * share, channels)

    near, far = laid_out(near), laid_out(far)
    return jnp.concatenate([jnp.where(odd, far, near), jnp.where(odd, near, far)], axis=1)


def per_device_grouped(clean_field, noise_field, timestep, dilations, w_in, w_time, w_z, w_xy, w_point,
                       biases, norm_gains, w_out):
    members, groups = lax.axis_size("gz"), lax.axis_size("gx")
    depth = clean_field.shape[3]
    planes, cells_z = groups, depth * members
    channels = w_in.shape[1]
    lanes = 4 * channels
    rows = (cells_z // REACH) * (REACH // members + 2 * RIM)
    share = channels // groups
    per_member = float(planes * 4 * depth)
    cell_count = per_member * members
    inv_area = 4.0 / cell_count

    alpha_bar, features, time_raw, time_code = time_terms(timestep, w_time)
    parts = members // 2 * groups
    mixed = call(
        kernel_mix, [((parts, 24, depth), f32)],
        [(clean_field.shape, f32), (clean_field.shape, f32), pltpu.SemaphoreType.DMA((2,))], 10**5, LIMITS[7],
        jnp.stack([jnp.sqrt(alpha_bar), jnp.sqrt(1.0 - alpha_bar)]), clean_field, noise_field, loose=(1, 2),
    )[0]
    same_core = [[m * groups + g for m in range(core, members, 2) for g in range(groups)] for core in range(2)]
    near = lax.all_to_all(mixed, ("gz", "gx"), 0, 0, axis_index_groups=same_core)
    far = swapped(near, "gz", 1)
    shift_bias = biases + time_code

    big = (planes, rows, lanes)
    vec = ((8, channels), f32)
    thin = ((planes, rows, 128), bf16)
    lift = ((128, lanes), bf16)
    conv_scratch = [
        ((planes + 2, rows, lanes), bf16),
        ((2,) + big, bf16),
        ((2, 3, lanes, lanes // 2), bf16),
        ((2, lanes // 2, lanes // 2), bf16),
    ]
    pair = ((1, lanes // 2, lanes // 2), bf16)
    flat = ((rows, lanes), f32)
    grad_out = ((6, share, channels), f32)

    taps_out, point_out = ((2, 11, channels, channels), bf16), ((2, channels, channels), bf16)
    w_front, point, w_back, point_back, lift_in, lift_out, w_in_on, gains_on = call(
        kernel_prepare,
        [taps_out, point_out, taps_out, point_out, lift, lift, ((3, channels), f32), ((3, channels), f32)],
        [], 10**8, LIMITS[0], w_z, w_xy, w_point, w_in, w_out, norm_gains, scalars=False,
    )
    stream1, normed0, act0, slope0, gathered, stats1, consts0 = call(
        functools.partial(kernel_first, cells_z, per_member),
        [(big, f32), (big, bf16), (big, bf16), (big, bf16), thin, vec, ((16, channels), f32)],
        conv_scratch + [pair, flat, (big, f32), ((planes, 128, cells_z), bf16)],
        4 * 10**9, LIMITS[1],
        dilations, near, far, lift_in, w_in_on, gains_on, shift_bias, w_front, point,
    )
    stream2, normed1, act1, slope1, stats2, consts1 = call(
        functools.partial(kernel_second, per_member),
        [(big, f32), (big, bf16), (big, bf16), (big, bf16), vec, vec],
        conv_scratch + [pair, flat],
        4 * 10**9, LIMITS[2],
        dilations, *group_parts(stats1), stream1, gains_on, shift_bias, w_front, point,
    )
    prediction, misfit, sums2, out_raw, consts2 = call(
        functools.partial(kernel_out, per_member),
        [((rows, 128), f32), thin, vec, vec, vec],
        [(big, bf16)],
        10**9, LIMITS[3],
        dilations, *group_parts(stats2), stream2, gains_on, gathered, lift_out,
    )
    parts2 = group_parts(sums2)
    d_stream2, d_normed1, sums1, rimmed1, shifted1, scot1 = call(
        functools.partial(kernel_back_second, cell_count),
        [(big, f32), (big, f32), vec] + conv_scratch[:2] + [(big, bf16)],
        conv_scratch[2:] + [pair, flat, flat],
        6 * 10**9, LIMITS[4],
        dilations, *parts2, stream2, consts2, gains_on, misfit, lift_out, slope1, normed1,
        w_back, point_back,
    )
    parts1 = group_parts(sums1)
    keep1, give1 = call(
        functools.partial(kernel_weights_second, share),
        [grad_out, grad_out], [((12, share, channels), f32)], 2 * 10**9, LIMITS[8],
        dilations, rimmed1, shifted1, scot1, normed1, act1,
    )
    d_stream1, sums_b0, keep0, give0, rimmed0, shifted0 = call(
        functools.partial(kernel_back_first, share, cell_count),
        [(big, f32), vec, grad_out, grad_out] + conv_scratch[:2],
        [pair, flat, (big, bf16), ((12, share, channels), f32)],
        4 * 10**9, LIMITS[5],
        dilations, *parts1, consts1, d_stream2, d_normed1, normed1, gains_on, act0, slope0, normed0,
        point_back,
    )
    mine1 = group_grads(keep1, give1)
    last = call(
        functools.partial(kernel_last, depth),
        [((64, channels), f32)] * members,
        conv_scratch[2:] + [flat, flat, (big, bf16), (big, bf16)],
        4 * 10**9, LIMITS[6],
        dilations, rimmed0, shifted0, d_stream1, normed0, gains_on, consts0, gathered, lift_in, w_back, prediction,
        sums_b0, out_raw,
    )
    every = all_grads(group_grads(keep0, give0), mine1)

    tails = last[0] + sum(swapped(last[bit], "gz", bit) for bit in (1, 2, 3))
    s_plain, s_cross, in_sum = tails[32], tails[33], tails[40:43]
    bias0, out_sum = tails[48], tails[56:59]
    s1 = sum(members_of(parts1))
    s2 = sum(members_of(parts2))
    inverse = consts0[1]
    m_plain = norm_gains[0] * s_plain / cell_count
    m_cross = norm_gains[0] * s_cross / cell_count
    mean_k = consts0[2:5, 0]
    c00, c01, c02, c11, c12, c22 = (consts0[5 + at, 0] for at in range(6))
    cov = jnp.stack([jnp.stack([c00, c01, c02]), jnp.stack([c01, c11, c12]), jnp.stack([c02, c12, c22])])
    offset = jnp.sum(w_in * (inverse * m_plain), axis=1)
    mix = jnp.sum(w_in[:, None, :] * (inverse * inverse * m_cross) * w_in[None, :, :], axis=2)
    landed = tails[:24].reshape(6, 1, 4, depth)
    centered = mixed[0, :12].reshape(3, 1, 4, depth) - mean_k[:, None, None, None]
    field_grad = landed[:3] - offset[:, None, None, None] - sum(
        mix[:, j, None, None, None] * centered[j][None] for j in range(3)
    )
    prediction_out = landed[3:]
    cross_in = jnp.sum(cov[:, :, None] * w_in[None, :, :], axis=1)
    in_raw = in_sum - cell_count * (
        mean_k[:, None] * (inverse * m_plain) + (inverse * inverse * m_cross) * cross_in
    )
    bias_all = jnp.stack([bias0, s1[2]])
    gain_all = jnp.stack([s_cross, s1[1], s2[1]])
    weights = every.astype(f32) * inv_area
    z_all = jnp.stack([weights[:, 9], weights[:, 4], weights[:, 10]], axis=1)
    xy_all = jnp.concatenate([weights[:, :4], weights[:, 5:9]], axis=1)
    time_back = jax.vjp(jax.nn.silu, time_raw)[1](jnp.sum(bias_all, axis=0))[0]
    grad_w_time = inv_area * jnp.outer(features, time_back)
    return (
        prediction_out,
        field_grad,
        inv_area * in_raw,
        grad_w_time,
        z_all,
        xy_all,
        weights[:, 11],
        inv_area * bias_all,
        inv_area * gain_all,
        inv_area * out_sum,
    )


def padded_2(cells, sides, width):
    for axis, dim in sides:
        count = lax.axis_size(axis)
        head = lax.slice_in_dim(cells, 0, width, axis=dim)
        tail = lax.slice_in_dim(cells, cells.shape[dim] - width, cells.shape[dim], axis=dim)
        cells = jnp.concatenate(
            [
                lax.ppermute(tail, axis, [(i, (i + 1) % count) for i in range(count)]),
                cells,
                lax.ppermute(head, axis, [((i + 1) % count, i) for i in range(count)]),
            ],
            axis=dim,
        )
    return cells


def passed_along(value, axis, steps):
    count = lax.axis_size(axis)
    pairs = [(source, (source + steps) % count) for source in range(count)]
    return lax.ppermute(value, axis, pairs)


def contract_cells(left, right):
    return lax.dot_general(
        left, right, (((0, 1, 2), (0, 1, 2)), ((), ())), preferred_element_type=jnp.float32
    )


def plane_tap(padded, shift_x, shift_y, rows_x, rows_y):
    return padded[1 + shift_x : 1 + shift_x + rows_x, 1 + shift_y : 1 + shift_y + rows_y]


def plane_pad(source):
    rimmed = padded_2(source, (("gx", 0),), 1)
    return jnp.pad(rimmed, ((0, 0), (1, 1), (0, 0), (0, 0)))


def slab_windows(source, dilation):
    slab_depth = source.shape[2]
    above = passed_along(source, "gz", -1)
    above_far = passed_along(source, "gz", -2)
    below = passed_along(source, "gz", 1)
    below_far = passed_along(source, "gz", 2)
    ahead_rows = jnp.concatenate([source, above, above_far], axis=2)
    behind_rows = jnp.concatenate([below_far, below, source], axis=2)
    upper = lax.dynamic_slice_in_dim(ahead_rows, dilation, slab_depth, 2)
    lower = lax.dynamic_slice_in_dim(behind_rows, 2 * slab_depth - dilation, slab_depth, 2)
    return (lower, upper)


def normalize(hidden, gains, cell_count):
    average = lax.psum(jnp.sum(hidden, axis=(0, 1, 2)), ("gz", "gx")) / cell_count
    centered = hidden - average
    spread = lax.psum(jnp.sum(centered * centered, axis=(0, 1, 2)), ("gz", "gx")) / cell_count
    inverse_std = lax.rsqrt(spread + eps_norm)
    whitened = (hidden - average) * inverse_std
    return ((whitened * gains).astype(jnp.bfloat16), whitened, inverse_std)


def norm_back(d_normed, whitened, inverse_std, gains, cell_count):
    scaled = d_normed * gains
    sum_grad, sum_cross = lax.psum(
        (jnp.sum(scaled, axis=(0, 1, 2)), jnp.sum(scaled * whitened, axis=(0, 1, 2))), ("gz", "gx")
    )
    d_hidden = inverse_std * (scaled - sum_grad / cell_count - whitened * (sum_cross / cell_count))
    return (d_hidden, jnp.sum(d_normed * whitened, axis=(0, 1, 2)))


def conv_forward(normed, dilation, weights_z, weights_xy):
    rows_x, rows_y = (normed.shape[0], normed.shape[1])
    lower, upper = slab_windows(normed, dilation)
    padded = plane_pad(normed)
    summed = jnp.dot(lower, weights_z[0], preferred_element_type=jnp.float32)
    summed = summed + jnp.dot(normed, weights_z[1], preferred_element_type=jnp.float32)
    summed = summed + jnp.dot(upper, weights_z[2], preferred_element_type=jnp.float32)
    for tap_number, (shift_x, shift_y) in enumerate(plane_offsets):
        summed = summed + jnp.dot(
            plane_tap(padded, shift_x, shift_y, rows_x, rows_y),
            weights_xy[tap_number],
            preferred_element_type=jnp.float32,
        )
    return summed


def conv_backward_split(pre_cot, normed, dilation, weights_z, weights_xy):
    rows_x, rows_y = (normed.shape[0], normed.shape[1])
    lower_cot, upper_cot = slab_windows(pre_cot, dilation)
    padded_cot = plane_pad(pre_cot)
    d_normed = jnp.dot(upper_cot, weights_z[0].T, preferred_element_type=jnp.float32)
    d_normed = d_normed + jnp.dot(pre_cot, weights_z[1].T, preferred_element_type=jnp.float32)
    d_normed = d_normed + jnp.dot(lower_cot, weights_z[2].T, preferred_element_type=jnp.float32)
    xy_terms = []
    for tap_number, (shift_x, shift_y) in enumerate(plane_offsets):
        shifted = plane_tap(padded_cot, -shift_x, -shift_y, rows_x, rows_y)
        d_normed = d_normed + jnp.dot(
            shifted, weights_xy[tap_number].T, preferred_element_type=jnp.float32
        )
        xy_terms.append(contract_cells(normed, shifted))
    z_terms = jnp.stack(
        [
            contract_cells(normed, upper_cot),
            contract_cells(normed, pre_cot),
            contract_cells(normed, lower_cot),
        ]
    )
    return (d_normed, z_terms, jnp.stack(xy_terms))


def per_device_split(
    clean_field,
    noise_field,
    timestep,
    dilations,
    w_in,
    w_time,
    w_z,
    w_xy,
    w_point,
    biases,
    norm_gains,
    w_out,
):
    layer_total = w_z.shape[0]
    rows_x, rows_y, slab_depth = (clean_field.shape[1], clean_field.shape[2], clean_field.shape[3])
    plane_cells = rows_x * lax.axis_size("gx") * slab_depth * lax.axis_size("gz")
    cell_count = float(plane_cells * rows_y)
    inv_area = 1.0 / plane_cells
    alpha_bar, features, time_raw, time_code = time_terms(timestep, w_time)
    noisy = jnp.sqrt(alpha_bar) * clean_field + jnp.sqrt(1.0 - alpha_bar) * noise_field
    stream = jnp.einsum("kxyz,kc->xyzc", noisy, w_in, precision=highest)
    saved = []
    for which_layer in range(layer_total):
        normed, whitened, inverse_std = normalize(stream, norm_gains[which_layer], cell_count)
        pre_act = conv_forward(normed, dilations[which_layer], w_z[which_layer], w_xy[which_layer])
        pre_act = pre_act + biases[which_layer] + time_code
        activated = jax.nn.gelu(pre_act).astype(jnp.bfloat16)
        saved.append((normed, whitened, inverse_std, pre_act, activated))
        stream = stream + jnp.dot(
            activated, w_point[which_layer], preferred_element_type=jnp.float32
        )
    out_normed, out_white, out_inverse = normalize(stream, norm_gains[layer_total], cell_count)
    prediction = jnp.einsum("xyzc,kc->kxyz", out_normed, w_out, preferred_element_type=jnp.float32)
    misfit = prediction - noise_field
    d_out = jnp.einsum("kxyz,kc->xyzc", misfit, w_out.astype(jnp.float32), precision=highest)
    out_raw = jnp.einsum(
        "kxyz,xyzc->kc", misfit, out_normed, precision=highest, preferred_element_type=jnp.float32
    )
    d_stream, out_gain_raw = norm_back(
        d_out, out_white, out_inverse, norm_gains[layer_total], cell_count
    )
    z_list, xy_list, point_list, bias_list, gain_list = ([], [], [], [], [])
    for which_layer in reversed(range(layer_total)):
        normed, whitened, inverse_std, pre_act, activated = saved[which_layer]
        stream_cot = d_stream.astype(jnp.bfloat16)
        point_raw = contract_cells(activated, stream_cot)
        d_act = jnp.dot(stream_cot, w_point[which_layer].T, preferred_element_type=jnp.float32)
        gelu_back = jax.vjp(jax.nn.gelu, pre_act)[1]
        pre_cot = gelu_back(d_act)[0].astype(jnp.bfloat16)
        bias_raw = jnp.sum(pre_cot, axis=(0, 1, 2), dtype=jnp.float32)
        d_normed, z_raw, xy_raw = conv_backward_split(
            pre_cot, normed, dilations[which_layer], w_z[which_layer], w_xy[which_layer]
        )
        d_back, gain_raw = norm_back(
            d_normed, whitened, inverse_std, norm_gains[which_layer], cell_count
        )
        d_stream = d_stream + d_back
        z_list.insert(0, z_raw)
        xy_list.insert(0, xy_raw)
        point_list.insert(0, point_raw)
        bias_list.insert(0, bias_raw)
        gain_list.insert(0, gain_raw)
    field_grad = jnp.einsum("xyzc,kc->kxyz", d_stream, w_in, precision=highest)
    in_raw = jnp.einsum("kxyz,xyzc->kc", noisy, d_stream, precision=highest)
    z_all, xy_all, point_all, bias_all, gain_all, in_raw, out_raw = lax.psum(
        (
            jnp.stack(z_list),
            jnp.stack(xy_list),
            jnp.stack(point_list),
            jnp.stack(bias_list),
            jnp.stack(gain_list + [out_gain_raw]),
            in_raw,
            out_raw,
        ),
        ("gz", "gx"),
    )
    time_back = jax.vjp(jax.nn.silu, time_raw)[1](jnp.sum(bias_all, axis=0))[0]
    grad_w_time = inv_area * jnp.outer(features, time_back)
    return (
        prediction,
        field_grad,
        inv_area * in_raw,
        grad_w_time,
        inv_area * z_all,
        inv_area * xy_all,
        inv_area * point_all,
        inv_area * bias_all,
        inv_area * gain_all,
        inv_area * out_raw,
    )


def per_device(*args):
    members, groups = lax.axis_size("gz"), lax.axis_size("gx")
    _, rows_x, rows_y, depth = args[0].shape
    small = rows_x == 1 and rows_y == 4 and members == 4 and groups == 8 and depth * members == 2 * REACH
    return per_device_grouped(*args) if small else per_device_split(*args)


def solution(mesh):
    return jax.shard_map(
        per_device,
        mesh=mesh,
        in_specs=(
            P(None, "gx", None, "gz"),
            P(None, "gx", None, "gz"),
            P(),
            P(),
            P(),
            P(),
            P(),
            P(),
            P(),
            P(),
            P(),
            P(),
        ),
        out_specs=(
            P(None, "gx", None, "gz"),
            P(None, "gx", None, "gz"),
            P(),
            P(),
            P(),
            P(),
            P(),
            P(),
            P(),
            P(),
        ),
        check_vma=False,
    )
```

```python
import functools
import math

import jax
import jax.numpy as jnp
from jax import lax
from jax.experimental import pallas as pl
from jax.experimental.pallas import tpu as pltpu
from jax.sharding import PartitionSpec as P

STEPS = 1000
REACH = 256
RIM = 4
TILE = 16
LIMITS = (4, 14, 10, 7, 10, 8, 10, 2, 6, 2, 2, 3)

eps_norm = 1e-05
highest = lax.Precision.HIGHEST
bf16 = jnp.bfloat16
f32 = jnp.float32
plane_offsets = ((-1, -1), (-1, 0), (-1, 1), (0, -1), (0, 1), (1, -1), (1, 0), (1, 1))


def time_terms(timestep, w_time):
    moment = timestep[0].astype(jnp.float32)
    half_width = w_time.shape[0] // 2
    alpha_bar = jnp.cos(0.5 * math.pi * (moment + 0.5) / STEPS) ** 2
    ladder = jnp.exp(-math.log(10000.0) * jnp.arange(half_width, dtype=jnp.float32) / half_width)
    angles = moment * ladder
    features = jnp.concatenate([jnp.sin(angles), jnp.cos(angles)])
    time_raw = jnp.dot(features, w_time, precision=highest)
    return (alpha_bar, features, time_raw, jax.nn.silu(time_raw))


def mm(left, right):
    return lax.dot_general(left, right, (((1,), (0,)), ((), ())), preferred_element_type=f32)


def mm_nt(left, right):
    return lax.dot_general(left, right, (((1,), (1,)), ((), ())), preferred_element_type=f32)


def mm_tn(left, right):
    return lax.dot_general(left, right, (((0,), (0,)), ((), ())), preferred_element_type=f32)


def halves(value):
    high = value.astype(bf16)
    return high, (value - high.astype(f32)).astype(bf16)


def wide(vector):
    return jnp.concatenate([vector] * 4, axis=1)


def folded(vector):
    channels = vector.shape[1] // 4
    return sum(vector[:, y * channels : (y + 1) * channels] for y in range(4))


class Place:
    def __init__(self, sc, rows):
        self.rows = rows
        self.members = lax.axis_size("gz")
        self.member = lax.axis_index("gz")
        self.small = jnp.minimum(sc[0], sc[1])
        self.coarse = self.small >= self.members
        tiles = rows // TILE
        self.tiles = tiles
        self.stride = jnp.where(self.coarse, tiles - 1, tiles)
        self.span = REACH // self.members + 2 * RIM
        far = jnp.where(self.coarse, REACH // self.members, self.span)
        near = jnp.where(self.coarse, self.small // self.members, 1)
        self.steps = [jnp.where(sc[l] == REACH, far, near) for l in range(2)]

    def index(self, shape):
        row = lax.broadcasted_iota(jnp.int32, shape, 0)
        return lax.rem(row, TILE) * self.stride + row // TILE, row // TILE

    def own(self, shape):
        place, tile = self.index(shape)
        inside = lax.rem(place, self.span)
        near = ((inside >= RIM) & (inside < self.span - RIM)).astype(jnp.int32)
        far = (tile < self.tiles - 1).astype(jnp.int32)
        return jnp.where(self.coarse, far, near) == 1

    def pick(self, cells_z):
        shape = (self.rows, cells_z)
        return self.z_of(shape, cells_z) == lax.broadcasted_iota(jnp.int32, shape, 1)

    def z_of(self, shape, cells_z):
        place, _ = self.index(shape)
        residues = jnp.minimum(self.small, self.members)
        part, start = self.member // residues, lax.rem(self.member, residues)
        period = place // self.span
        inside = place - period * self.span - RIM + part * (REACH // self.members)
        near = start + residues * inside + period * REACH
        z = jnp.where(self.coarse, place * self.members + self.member, near)
        return lax.rem(z + 2 * cells_z, cells_z)


def build_taps(block_of, taps, taps_z):
    channels = taps_z.shape[-1] // 2
    zero = jnp.zeros((channels, channels), bf16)
    for i in range(3):
        for j in range(3):
            block = block_of(i, j)
            for q in range(2):
                for side in range(2):
                    y_in = 2 * q + side + j - 1
                    if 0 <= y_in < 4:
                        taps[
                            q,
                            i,
                            y_in * channels : (y_in + 1) * channels,
                            side * channels : (side + 1) * channels,
                        ] = block
        for q in range(2):
            for side in range(2):
                for y_in in range(4):
                    if abs(y_in - 2 * q - side) > 1:
                        taps[
                            q,
                            i,
                            y_in * channels : (y_in + 1) * channels,
                            side * channels : (side + 1) * channels,
                        ] = zero
    for m in range(2):
        build_pair(block_of(3, m), taps_z, m)


def build_pair(block, target, m):
    channels = block.shape[-1]
    zero = jnp.zeros((channels, channels), bf16)
    target[m, :channels, :channels] = block
    target[m, channels:, channels:] = block
    target[m, :channels, channels:] = zero
    target[m, channels:, :channels] = zero


def forward_blocks(w_z, w_xy, layer):
    def block_of(i, j):
        if i == 3:
            return w_z[layer, 2 * j]
        at = i * 3 + j
        return w_z[layer, 1] if at == 4 else w_xy[layer, at - (at > 4)]

    return block_of


def taken(weights, layer):
    return lambda i, j: weights[layer, i * 3 + j]


def kernel_mix(timestep, clean_far, noise_far, mixed, mixed_own, clean, noise, sems):
    parts = mixed.shape[0]
    copies = [
        pltpu.make_async_copy(clean_far, clean, sems.at[0]),
        pltpu.make_async_copy(noise_far, noise, sems.at[1]),
    ]
    for copy in copies:
        copy.start()
    moment = jnp.full((1, clean.shape[3]), timestep[0], jnp.int32).astype(f32)
    alpha_bar = jnp.cos(0.5 * math.pi * (moment + 0.5) / STEPS) ** 2
    keep, add = jnp.sqrt(alpha_bar), jnp.sqrt(1.0 - alpha_bar)
    for copy in copies:
        copy.wait()
    for k in range(3):
        noisy = keep * clean[k, 0] + add * noise[k, 0]
        mixed_own[4 * k : 4 * k + 4] = noisy
        for part in range(parts):
            mixed[part, 4 * k : 4 * k + 4] = noisy
            mixed[part, 12 + 4 * k : 16 + 4 * k] = noise[k, 0]


def kernel_prepare(w_z, w_xy, w_point, w_in, w_out, gains, w_front, point, w_back, point_back, lift_in,
                   lift_out, w_in_on, gains_on):
    w_in_on[...] = w_in[...]
    gains_on[...] = gains[...]
    point[...] = w_point[...]
    for layer in range(2):
        forward = forward_blocks(w_z, w_xy, layer)
        for i in range(3):
            for j in range(3):
                w_front[layer, i * 3 + j] = forward(i, j)
        for m in range(2):
            w_front[layer, 9 + m] = forward(3, m)
        for i in range(3):
            for j in range(3):
                w_back[layer, i * 3 + j] = forward(2 - i, 2 - j).T
        for m in range(2):
            w_back[layer, 9 + m] = forward(3, 1 - m).T
        point_back[layer] = w_point[layer].T
    whole = spread_rows(w_in[...], 0)
    high, low = halves(whole)
    lift_in[0:32] = high
    lift_in[32:64] = high
    lift_in[64:96] = low
    lift_in[96:128] = jnp.zeros_like(low)
    high = spread_rows(w_out[...].astype(f32), 3).astype(bf16)
    lift_out[0:32] = high
    lift_out[32:64] = high
    lift_out[64:96] = jnp.zeros_like(high)
    lift_out[96:128] = jnp.zeros_like(high)


def spread_rows(weights, first):
    channels = weights.shape[1]
    zero = jnp.zeros((1, channels), f32)
    rows = [jnp.zeros((1, 4 * channels), f32)] * 32
    for k in range(3):
        for y in range(4):
            parts = [weights[k : k + 1] if at == y else zero for at in range(4)]
            rows[(first + k) * 4 + y] = jnp.concatenate(parts, axis=1)
    return jnp.concatenate(rows, axis=0)


def fill_rims(padded, planes):
    padded[0] = padded[planes]
    padded[planes + 1] = padded[1]


def fill_shifted(place, layer, padded, shifted, planes):
    step, stride = place.steps[layer], place.stride
    for tile in range(place.tiles):
        for way in range(2):
            at = tile - step if way == 0 else tile + step
            moved = at + TILE * stride
            source = lax.rem(moved, stride)
            turn = lax.rem(2 * TILE - moved // stride, TILE)
            rows = padded[1 : planes + 1, pl.ds(pl.multiple_of(source * TILE, TILE), TILE), :]
            rows = pltpu.roll(rows.astype(f32), turn, 1)
            shifted[way, :, tile * TILE : (tile + 1) * TILE, :] = rows.astype(bf16)


def conv_half(padded, shifted, taps, taps_z, x0, count, q):
    rows, lanes = padded.shape[1:]
    half = lanes // 2
    total = None
    for i in range(3):
        part = mm(padded[x0 + i : x0 + i + count].reshape(count * rows, lanes), taps[q, i])
        total = part if total is None else total + part
    for m in range(2):
        source = shifted[m, x0 : x0 + count, :, q * half : (q + 1) * half]
        total = total + mm(source.reshape(count * rows, half), taps_z[m])
    return total


def gelu_pair(value):
    scale = math.sqrt(2.0 / math.pi)
    square = value * value
    bent = jnp.tanh(value * (scale + (scale * 0.044715) * square))
    half = 0.5 + 0.5 * bent
    slope = half + value * (0.5 - 0.5 * (bent * bent)) * (scale + (3.0 * 0.044715 * scale) * square)
    return value * half, slope


def members_of(parts):
    found = []
    for part in parts:
        for at in range(0, part.shape[0], 8):
            found.append(part[at : at + 8])
    return found


def merged_stats(parts, per_member):
    found = members_of(parts)
    mean = sum(one[0:1] for one in found) / (per_member * len(found))
    spread = sum(one[1:2] for one in found)
    for one in found:
        gap = one[0:1] / per_member - mean
        spread = spread + per_member * gap * gap
    return mean, lax.rsqrt(spread / (per_member * len(found)) + eps_norm)


def put_rows(ref, *vectors):
    rows = list(vectors)
    rows += [jnp.zeros((1, ref.shape[1]), f32)] * (ref.shape[0] - len(rows))
    ref[...] = jnp.concatenate(rows, axis=0)


def masked_total(mask, value):
    return folded(jnp.sum(jnp.where(mask, value, 0.0), axis=0, keepdims=True))


def layer_forward(place, layer, padded, shifted, taps, taps_z, pair, w_front, wp, shift_bias, old,
                  stream, act, slope, stats, acc, per_member):
    planes, rows, lanes = stream.shape
    half = lanes // 2
    count = planes // 4
    build_taps(taken(w_front, layer), taps, taps_z)
    build_pair(wp[layer], pair, 0)
    fill_rims(padded, planes)
    fill_shifted(place, layer, padded, shifted, planes)
    acc[...] = jnp.zeros_like(acc)
    bias = wide(shift_bias[layer : layer + 1, :])[:, :half]

    for x0 in range(0, planes, count):
        part = slice(x0, x0 + count)
        for q in range(2):
            side = slice(q * half, (q + 1) * half)
            pre = conv_half(padded, shifted, taps, taps_z, x0, count, q) + bias
            value, grad = gelu_pair(pre)
            act[part, :, side] = value.astype(bf16).reshape(count, rows, half)
            slope[part, :, side] = grad.astype(bf16).reshape(count, rows, half)
    for x0 in range(0, planes, count):
        part = slice(x0, x0 + count)
        for q in range(2):
            side = slice(q * half, (q + 1) * half)
            branch = mm(act[part, :, side].reshape(count * rows, half), pair[0])
            new = old[part, :, side] + branch.reshape(count, rows, half)
            stream[part, :, side] = new
            acc[:, side] += jnp.sum(new, axis=0)
    mask = place.own((rows, lanes))
    total = masked_total(mask, acc[...])
    mean = wide(total / per_member)
    spread = jnp.zeros((rows, lanes), f32)
    for x in range(planes):
        gap = stream[x] - mean
        spread = spread + gap * gap
    put_rows(stats, total, masked_total(mask, spread))


def kernel_first(cells_z, per_member, sc, near, far, lift_in, w_in, gains, shift_bias, w_front, wp,
                 stream, normed, act, slope, gathered, stats, consts,
                 padded, shifted, taps, taps_z, pair, acc, old, source):
    planes, rows, lanes = stream.shape
    channels = lanes // 4
    depth = near.shape[2]
    place = Place(sc, rows)
    cell_count = float(planes * 4 * cells_z)
    comps = [
        jnp.concatenate([ref[:, 4 * k : 4 * k + 4, :] for ref in (near, far)], axis=0) for k in range(3)
    ]

    def all_sum(value):
        value = jnp.sum(jnp.sum(value, axis=0), axis=0, keepdims=True)
        return jnp.sum(value, axis=1, keepdims=True)

    means = [all_sum(comp) / cell_count for comp in comps]
    gaps = [comp - mean[None] for comp, mean in zip(comps, means)]
    covs = {}
    for j in range(3):
        for k in range(j, 3):
            covs[j, k] = all_sum(gaps[j] * gaps[k]) / cell_count
    rows_in = [w_in[k : k + 1, :] for k in range(3)]
    mean_c = sum(means[k] * rows_in[k] for k in range(3))
    var_c = jnp.zeros((1, channels), f32)
    for (j, k), cov in covs.items():
        var_c = var_c + (1.0 if j == k else 2.0) * cov * (rows_in[j] * rows_in[k])
    inv_c = lax.rsqrt(jnp.maximum(var_c, 0.0) + eps_norm)
    flat = [jnp.broadcast_to(value, (1, channels)) for value in means + list(covs.values())]
    put_rows(consts, mean_c, inv_c, *flat)
    blank = jnp.zeros((8, depth), f32)
    core = lax.rem(place.member, 2)
    for slab in range(cells_z // depth):
        ref, side = (near, core) if slab % 2 == 0 else (far, 1 - core)
        at = pl.ds(pl.multiple_of((slab // 2 * 2 + side) * depth, depth), depth)
        for x in range(planes):
            high, low = halves(jnp.concatenate([ref[slab // 2 * planes + x], blank], axis=0))
            source[x, 0:32, at] = high
            source[x, 32:64, at] = low
            source[x, 64:96, at] = high
            source[x, 96:128, at] = jnp.zeros_like(high)
    pick = place.pick(cells_z).astype(f32).astype(bf16)
    scale = wide(inv_c * gains[0:1, :])
    mean_w = wide(mean_c)
    for x in range(planes):
        gathered[x] = mm_nt(pick, source[x]).astype(bf16)
    for x0 in range(0, planes, planes // 2):
        part = slice(x0, x0 + planes // 2)
        value = mm(gathered[part].reshape(planes // 2 * rows, 128), lift_in[...])
        unit = ((value - mean_w) * scale).astype(bf16).reshape(planes // 2, rows, lanes)
        old[part] = value.reshape(planes // 2, rows, lanes)
        padded[x0 + 1 : x0 + 1 + planes // 2] = unit
        normed[part] = unit
    layer_forward(place, 0, padded, shifted, taps, taps_z, pair, w_front, wp, shift_bias, old, stream,
                  act, slope, stats, acc, per_member)


def kernel_second(per_member, sc, *refs):
    parts, refs = refs[:4], refs[4:]
    (old, gains, shift_bias, w_front, wp, stream, normed, act, slope, stats, consts,
     padded, shifted, taps, taps_z, pair, acc) = refs
    planes, rows, _ = stream.shape
    place = Place(sc, rows)
    mean, inverse = merged_stats(parts, per_member)
    put_rows(consts, mean, inverse)
    mean_w, scale = wide(mean), wide(inverse * gains[1:2, :])
    for x in range(planes):
        unit = ((old[x] - mean_w) * scale).astype(bf16)
        padded[x + 1] = unit
        normed[x] = unit
    layer_forward(place, 1, padded, shifted, taps, taps_z, pair, w_front, wp, shift_bias, old, stream,
                  act, slope, stats, acc, per_member)


def kernel_out(per_member, sc, *refs):
    parts, refs = refs[:4], refs[4:]
    stream, gains, gathered, lift_out, prediction, misfit, sums, w_out_raw, consts, unit = refs
    planes, rows, lanes = stream.shape
    place = Place(sc, rows)
    mean, inverse = merged_stats(parts, per_member)
    put_rows(consts, mean, inverse)
    mean_w, inv_w, gain_w = wide(mean), wide(inverse), wide(gains[2:3, :])
    scale = inv_w * gain_w
    for x in range(planes):
        unit[x] = ((stream[x] - mean_w) * scale).astype(bf16)
    row = lax.broadcasted_iota(jnp.int32, (128, 128), 0)
    col = lax.broadcasted_iota(jnp.int32, (128, 128), 1)
    slot = lax.rem(col, 32)
    used = (col < 64) & (slot >= 12) & (slot < 24)
    take = (used & ((row == slot) | (row == slot + 32))).astype(f32).astype(bf16)
    total = mm_nt(unit[...].reshape(planes * rows, lanes), lift_out[...])
    noise = mm(gathered[...].reshape(planes * rows, 128), take)
    gap = total - noise
    high, low = halves(gap)
    lane = lax.broadcasted_iota(jnp.int32, gap.shape, 1)
    both = jnp.where(lane < 32, high.astype(f32), low.astype(f32)).astype(bf16)
    misfit[...] = both.reshape(planes, rows, 128)
    for x in range(planes):
        @pl.when(lax.axis_index("gx") == x)
        def _(x=x):
            prediction[...] = total[x * rows : (x + 1) * rows]
    plain = jnp.zeros((rows, lanes), f32)
    cross = jnp.zeros((rows, lanes), f32)
    for x0 in range(0, planes, planes // 2):
        part = slice(x0 * rows, (x0 + planes // 2) * rows)
        d_out = mm(both[part], lift_out[...]).reshape(planes // 2, rows, lanes)
        for x in range(planes // 2):
            plain = plain + d_out[x]
            cross = cross + d_out[x] * ((stream[x0 + x] - mean_w) * inv_w)
    own = place.own((rows, 128))
    kept = jnp.concatenate([jnp.where(own, misfit[x].astype(f32), 0.0) for x in range(planes)], axis=0)
    raw = mm_tn(kept.astype(bf16), unit[...].reshape(planes * rows, lanes))
    mask = place.own((rows, lanes))
    put_rows(sums, masked_total(mask, plain), masked_total(mask, cross))
    put_rows(w_out_raw, *by_component(raw[0:32] + raw[32:64], 3))


def by_component(raw, first):
    channels = raw.shape[1] // 4
    found = []
    for k in range(first, first + 3):
        found.append(
            sum(raw[k * 4 + y : k * 4 + y + 1, y * channels : (y + 1) * channels] for y in range(4))
        )
    return found


def branch_backward(planes, d_stream_of, pair, slope, padded, scot, bias_acc):
    rows, lanes = padded.shape[1:]
    half = lanes // 2
    count = planes // 2

    for x0 in range(0, planes, count):
        part = slice(x0, x0 + count)
        for x in range(x0, x0 + count):
            scot[x] = d_stream_of(x).astype(bf16)
        for q in range(2):
            side = slice(q * half, (q + 1) * half)
            cot = scot[part, :, side].reshape(count * rows, half)
            d_act = mm(cot, pair[0]).reshape(count, rows, half)
            pre = (d_act * slope[part, :, side].astype(f32)).astype(bf16)
            padded[x0 + 1 : x0 + 1 + count, :, side] = pre
            bias_acc[:, side] += jnp.sum(pre.astype(f32), axis=0)


def weight_grads(place, planes, padded, shifted, scot, normed, act, keep, give, taps_all, share):
    rows, lanes = padded.shape[1:]
    channels = lanes // 4
    wide_share = 4 * share
    row = lax.broadcasted_iota(jnp.int32, (lanes, wide_share), 0)
    col = lax.broadcasted_iota(jnp.int32, (lanes, wide_share), 1)
    hit = (row // channels == col // share) & (
        lax.rem(row, channels) == lax.rem(col, share) + lax.axis_index("gx") * share
    )
    choose = hit.astype(f32).astype(bf16)
    mask = jnp.concatenate([place.own((rows, wide_share))] * planes, axis=0)

    def turned(source):
        got = mm(source[...].reshape(planes * rows, lanes), choose)
        return jnp.where(mask, got, 0.0).astype(bf16)

    def add_blocks(raw, j):
        return sum(
            raw[(y + j) * share : (y + j + 1) * share, y * channels : (y + 1) * channels]
            for y in range(4)
            if 0 <= y + j < 4
        )

    left = turned(normed)
    for i in range(3):
        raw = mm_tn(left, padded[2 - i : 2 - i + planes].reshape(planes * rows, lanes))
        for j in range(3):
            taps_all[i * 3 + j] = add_blocks(raw, j - 1)
    for m in range(2):
        raw = mm_tn(left, shifted[1 - m].reshape(planes * rows, lanes))
        taps_all[9 + m] = add_blocks(raw, 0)
    raw = mm_tn(turned(act), scot[...].reshape(planes * rows, lanes))
    taps_all[11] = add_blocks(raw, 0)
    odd, half = lax.rem(place.member, 2), keep.shape[0]
    keep[...] = taps_all[pl.ds(odd * half, half)]
    give[...] = taps_all[pl.ds((1 - odd) * half, half)]


def conv_backward(planes, padded, shifted, taps, taps_z, emit):
    count = planes // 4

    for x0 in range(0, planes, count):
        for q in range(2):
            emit(x0, count, q, conv_half(padded, shifted, taps, taps_z, x0, count, q))


def kernel_back_second(cell_count, sc, *refs):
    parts, refs = refs[:4], refs[4:]
    (stream, out_consts, gains, misfit, lift_out, slope, normed, w_back, point_back,
     d_stream, d_normed, sums, padded, shifted, scot,
     taps, taps_z, pair, acc, acc2) = refs
    planes, rows, lanes = stream.shape
    half = lanes // 2
    place = Place(sc, rows)
    sums_out = sum(members_of(parts))
    gain_w = wide(gains[2:3, :])
    mean_w, inv_w = wide(out_consts[0:1]), wide(out_consts[1:2])
    m_plain = gain_w * wide(sums_out[0:1]) / cell_count
    m_cross = gain_w * wide(sums_out[1:2]) / cell_count
    build_pair(point_back[1], pair, 0)
    build_taps(taken(w_back, 1), taps, taps_z)
    acc[...] = jnp.zeros_like(acc)

    def d_stream_of(x):
        d_out = mm(misfit[x], lift_out[...])
        white = (stream[x] - mean_w) * inv_w
        value = inv_w * (gain_w * d_out - m_plain - white * m_cross)
        d_stream[x] = value
        return value

    branch_backward(planes, d_stream_of, pair, slope, padded, scot, acc)
    mask = place.own((rows, lanes))
    s_bias = masked_total(mask, acc[...])
    acc[...] = jnp.zeros_like(acc)
    acc2[...] = jnp.zeros_like(acc2)
    fill_rims(padded, planes)
    fill_shifted(place, 1, padded, shifted, planes)

    def emit(x0, count, q, value):
        side = slice(q * half, (q + 1) * half)
        value = value.reshape(count, rows, half)
        d_normed[x0 : x0 + count, :, side] = value
        acc[:, side] += jnp.sum(value, axis=0)
        acc2[:, side] += jnp.sum(value * normed[x0 : x0 + count, :, side].astype(f32), axis=0)

    conv_backward(planes, padded, shifted, taps, taps_z, emit)
    s_plain = masked_total(mask, acc[...])
    s_cross = masked_total(mask, acc2[...]) / gains[1:2, :]
    put_rows(sums, s_plain, s_cross, s_bias)


def kernel_weights_second(share, sc, padded, shifted, scot, normed, act, keep, give, taps_all):
    planes, rows, _ = scot.shape
    weight_grads(Place(sc, rows), planes, padded, shifted, scot, normed, act, keep, give, taps_all, share)


def kernel_back_first(share, cell_count, sc, *refs):
    parts, refs = refs[:4], refs[4:]
    (consts, d_next, d_normed, normed_next, gains, act, slope, normed, point_back,
     d_stream, sums, keep, give, padded, shifted,
     pair, acc, scot, taps_all) = refs
    planes, rows, lanes = d_next.shape
    place = Place(sc, rows)
    sums_in = sum(members_of(parts))
    gain_w = wide(gains[1:2, :])
    inv_w = wide(consts[1:2])
    m_plain = gain_w * wide(sums_in[0:1]) / cell_count
    m_cross = wide(sums_in[1:2]) / cell_count
    build_pair(point_back[0], pair, 0)
    acc[...] = jnp.zeros_like(acc)

    def d_stream_of(x):
        back = gain_w * d_normed[x] - m_plain - normed_next[x].astype(f32) * m_cross
        value = d_next[x] + inv_w * back
        d_stream[x] = value
        return value

    branch_backward(planes, d_stream_of, pair, slope, padded, scot, acc)
    put_rows(sums, masked_total(place.own((rows, lanes)), acc[...]))
    fill_rims(padded, planes)
    fill_shifted(place, 0, padded, shifted, planes)
    weight_grads(place, planes, padded, shifted, scot, normed, act, keep, give, taps_all, share)


def kernel_last(depth, sc, padded, shifted, d_stream, normed, gains, consts, gathered, lift_in, w_back,
                prediction, sums_bias, out_raw, ready0, ready1, own_out, out_1, out_2, out_3,
                taps, taps_z, acc, acc2, high, low):
    planes, rows, lanes = d_stream.shape
    half = lanes // 2
    place = Place(sc, rows)
    build_taps(taken(w_back, 0), taps, taps_z)
    acc[...] = jnp.zeros_like(acc)
    acc2[...] = jnp.zeros_like(acc2)
    scale = wide(consts[1:2] * gains[0:1, :])

    def emit(x0, count, q, value):
        side = slice(q * half, (q + 1) * half)
        part = slice(x0, x0 + count)
        value = value.reshape(count, rows, half)
        acc[:, side] += jnp.sum(value, axis=0)
        acc2[:, side] += jnp.sum(value * normed[part, :, side].astype(f32), axis=0)
        full = d_stream[part, :, side] + value * scale[:, side]
        first, second = halves(full)
        high[part, :, side] = first
        low[part, :, side] = second

    conv_backward(planes, padded, shifted, taps, taps_z, emit)
    mask = place.own((rows, lanes))
    s_plain = masked_total(mask, acc[...])
    s_cross = masked_total(mask, acc2[...]) / gains[0:1, :]
    own = place.own((rows, 128))
    kept = jnp.concatenate([jnp.where(own, gathered[x].astype(f32), 0.0) for x in range(planes)], axis=0)
    kept = kept.astype(bf16)
    raw = mm_tn(kept, high[...].reshape(planes * rows, lanes))
    raw_low = mm_tn(kept, low[...].reshape(planes * rows, lanes))
    in_raw = by_component(raw[0:32] + raw[32:64] + raw_low[0:32], 0)
    blank = jnp.zeros((1, s_plain.shape[1]), f32)
    tail = jnp.concatenate([s_plain, s_cross] + [blank] * 6 + in_raw + [blank] * 5, axis=0)
    tail = jnp.concatenate([tail, sums_bias[...], out_raw[...]], axis=0)
    here = lax.axis_index("gx")
    lane = lax.broadcasted_iota(jnp.int32, (rows, 128), 1)
    field = mm_nt(high[here], lift_in[...]) + jnp.where(lane < 32, mm_nt(low[here], lift_in[...]), 0.0)
    field = jnp.where((lane >= 32) & (lane < 64), 0.0, field)
    field = field + jnp.where((lane >= 12) & (lane < 24), prediction[...], 0.0)
    cells_z = depth * place.members
    whole = place.z_of((rows, depth), cells_z)
    column = lax.broadcasted_iota(jnp.int32, (rows, depth), 1)
    mask = place.own((rows, depth))
    first, second = halves(field)
    for bit, target in enumerate((own_out, out_1, out_2, out_3)):
        there = lax.bitwise_xor(place.member, bit)
        pick = ((whole == column + there * depth) & mask).astype(f32).astype(bf16)
        out = mm_tn(first, pick) + mm_tn(second, pick)
        target[0:32] = out[0:32] + out[64:96]
        target[32:64] = tail


def call(kernel, outs, scratch, flops, limit, *args, scalars=True, loose=(), ready=()):
    spec = pl.BlockSpec(memory_space=pltpu.VMEM)
    specs = [pl.BlockSpec(memory_space=pltpu.SMEM)] * scalars + [spec] * (len(args) - scalars)
    for at in ready:
        specs[at] = pl.BlockSpec(memory_space=pl.ANY)
    for at in loose:
        specs[at] = pl.BlockSpec(memory_space=pltpu.HBM)
    return pl.pallas_call(
        kernel,
        out_shape=[jax.ShapeDtypeStruct(shape, dtype) for shape, dtype in outs],
        in_specs=specs,
        out_specs=[spec] * len(outs),
        scratch_shapes=[pltpu.VMEM(*one) if isinstance(one, tuple) else one for one in scratch],
        compiler_params=pltpu.CompilerParams(vmem_limit_bytes=limit * 2**20),
        cost_estimate=pl.CostEstimate(flops=flops, bytes_accessed=2**23, transcendentals=0),
    )(*args)


def swapped(value, axis, bit):
    count = lax.axis_size(axis)
    return lax.ppermute(value, axis, [(i, i ^ bit) for i in range(count)])


def group_parts(value):
    return (value,) + tuple(swapped(value, "gz", bit) for bit in (1, 2, 3))


def kernel_spread(first, first_far, second, second_far, ready, spread):
    taps, share, channels = first.shape
    for layer, (own, other) in enumerate(((first, first_far), (second, second_far))):
        value = (own[...] + other[...]).reshape(taps * share, channels).astype(bf16)
        for part in range(spread.shape[0]):
            spread[part, layer * taps * share : (layer + 1) * taps * share] = value


def kernel_layout(scale, share, near, far, grad_w_z, grad_w_xy, grad_w_point):
    groups = near.shape[0]
    taps = near.shape[1] // share // 2
    odd = lax.rem(lax.axis_index("gz"), 2) == 1
    for layer in range(2):
        for tap in range(taps):
            at = (layer * taps + tap) * share
            one = near[:, at : at + share].astype(f32) * scale
            two = far[:, at : at + share].astype(f32) * scale
            for side in range(2):
                value = jnp.where(odd, one if side else two, two if side else one)
                value = value.reshape(groups * share, value.shape[2])
                whole = side * taps + tap
                if whole == 4:
                    grad_w_z[layer, 1] = value
                elif whole < 9:
                    grad_w_xy[layer, whole - (whole > 4)] = value
                elif whole < 11:
                    grad_w_z[layer, 2 * (whole - 9)] = value
                else:
                    grad_w_point[layer] = value


def kernel_tail(cell_count, inv_area, *refs):
    tails, parts1, parts2, refs = refs[:4], refs[4:8], refs[8:12], refs[12:]
    (consts, w_in, gains, mixed, features, time_raw,
     prediction, field_grad, grad_w_in, grad_w_time, grad_biases, grad_gains, grad_w_out) = refs
    tail = sum(ref[...] for ref in tails)
    s1, s2 = sum(ref[...] for ref in parts1), sum(ref[...] for ref in parts2)
    inverse = consts[1:2]
    m_plain = inverse * (gains[0:1] * tail[32:33] / cell_count)
    m_cross = inverse * inverse * (gains[0:1] * tail[33:34] / cell_count)
    at = {(0, 0): 5, (0, 1): 6, (0, 2): 7, (1, 1): 8, (1, 2): 9, (2, 2): 10}
    rows_in = [w_in[k : k + 1] for k in range(3)]
    depth = mixed.shape[1]
    gaps = [mixed[4 * k : 4 * k + 4] - consts[2 + k : 3 + k, 0:1] for k in range(3)]
    for k in range(3):
        offset = jnp.sum(rows_in[k] * m_plain, axis=1, keepdims=True)
        value = tail[4 * k : 4 * k + 4] - offset
        cross = jnp.zeros_like(m_plain)
        for j in range(3):
            mix = jnp.sum(rows_in[k] * m_cross * rows_in[j], axis=1, keepdims=True)
            value = value - mix * gaps[j]
            row = at[min(j, k), max(j, k)]
            cross = cross + consts[row : row + 1] * rows_in[j]
        field_grad[k, 0] = value
        prediction[k, 0] = tail[12 + 4 * k : 16 + 4 * k]
        in_sum = tail[40 + k : 41 + k] - cell_count * (consts[2 + k : 3 + k] * m_plain + m_cross * cross)
        grad_w_in[k : k + 1] = inv_area * in_sum
    bias0, bias1 = tail[48:49], s1[2:3]
    grad_biases[...] = inv_area * jnp.concatenate([bias0, bias1], axis=0)
    grad_gains[...] = inv_area * jnp.concatenate([tail[33:34], s1[1:2], s2[1:2]], axis=0)
    grad_w_out[...] = inv_area * tail[56:59]
    raw = time_raw[...]
    gate = 1.0 / (1.0 + jnp.exp(-raw))
    back = (bias0 + bias1) * (gate * (1.0 + raw * (1.0 - gate)))
    spread = jnp.broadcast_to(features[...], grad_w_time.shape).T
    grad_w_time[...] = inv_area * (spread * back)


def per_device_grouped(clean_field, noise_field, timestep, dilations, w_in, w_time, w_z, w_xy, w_point,
                       biases, norm_gains, w_out):
    members, groups = lax.axis_size("gz"), lax.axis_size("gx")
    depth = clean_field.shape[3]
    planes, cells_z = groups, depth * members
    channels = w_in.shape[1]
    lanes = 4 * channels
    rows = (cells_z // REACH) * (REACH // members + 2 * RIM)
    share = channels // groups
    per_member = float(planes * 4 * depth)
    cell_count = per_member * members
    inv_area = 4.0 / cell_count

    _, features, time_raw, time_code = time_terms(timestep, w_time)
    parts = members // 2 * groups
    mixed, mixed_own = call(
        kernel_mix, [((parts, 24, depth), f32), ((12, depth), f32)],
        [(clean_field.shape, f32), (clean_field.shape, f32), pltpu.SemaphoreType.DMA((2,))], 10**5, LIMITS[7],
        timestep, clean_field, noise_field, loose=(1, 2),
    )
    same_core = [[m * groups + g for m in range(core, members, 2) for g in range(groups)] for core in range(2)]
    near = lax.all_to_all(mixed, ("gz", "gx"), 0, 0, axis_index_groups=same_core)
    far = swapped(near, "gz", 1)
    shift_bias = biases + time_code

    big = (planes, rows, lanes)
    vec = ((8, channels), f32)
    thin = ((planes, rows, 128), bf16)
    lift = ((128, lanes), bf16)
    conv_scratch = [
        ((planes + 2, rows, lanes), bf16),
        ((2,) + big, bf16),
        ((2, 3, lanes, lanes // 2), bf16),
        ((2, lanes // 2, lanes // 2), bf16),
    ]
    pair = ((1, lanes // 2, lanes // 2), bf16)
    flat = ((rows, lanes), f32)
    grad_out = ((6, share, channels), f32)

    taps_out, point_out = ((2, 11, channels, channels), bf16), ((2, channels, channels), bf16)
    w_front, point, w_back, point_back, lift_in, lift_out, w_in_on, gains_on = call(
        kernel_prepare,
        [taps_out, point_out, taps_out, point_out, lift, lift, ((3, channels), f32), ((3, channels), f32)],
        [], 10**8, LIMITS[0], w_z, w_xy, w_point, w_in, w_out, norm_gains, scalars=False,
    )
    stream1, normed0, act0, slope0, gathered, stats1, consts0 = call(
        functools.partial(kernel_first, cells_z, per_member),
        [(big, f32), (big, bf16), (big, bf16), (big, bf16), thin, vec, ((16, channels), f32)],
        conv_scratch + [pair, flat, (big, f32), ((planes, 128, cells_z), bf16)],
        4 * 10**9, LIMITS[1],
        dilations, near, far, lift_in, w_in_on, gains_on, shift_bias, w_front, point,
    )
    stream2, normed1, act1, slope1, stats2, consts1 = call(
        functools.partial(kernel_second, per_member),
        [(big, f32), (big, bf16), (big, bf16), (big, bf16), vec, vec],
        conv_scratch + [pair, flat],
        4 * 10**9, LIMITS[2],
        dilations, *group_parts(stats1), stream1, gains_on, shift_bias, w_front, point,
    )
    prediction, misfit, sums2, out_raw, consts2 = call(
        functools.partial(kernel_out, per_member),
        [((rows, 128), f32), thin, vec, vec, vec],
        [(big, bf16)],
        10**9, LIMITS[3],
        dilations, *group_parts(stats2), stream2, gains_on, gathered, lift_out,
    )
    parts2 = group_parts(sums2)
    d_stream2, d_normed1, sums1, rimmed1, shifted1, scot1 = call(
        functools.partial(kernel_back_second, cell_count),
        [(big, f32), (big, f32), vec] + conv_scratch[:2] + [(big, bf16)],
        conv_scratch[2:] + [pair, flat, flat],
        6 * 10**9, LIMITS[4],
        dilations, *parts2, stream2, consts2, gains_on, misfit, lift_out, slope1, normed1,
        w_back, point_back,
    )
    parts1 = group_parts(sums1)
    keep1, give1 = call(
        functools.partial(kernel_weights_second, share),
        [grad_out, grad_out], [((12, share, channels), f32)], 2 * 10**9, LIMITS[8],
        dilations, rimmed1, shifted1, scot1, normed1, act1,
    )
    d_stream1, sums_b0, keep0, give0, rimmed0, shifted0 = call(
        functools.partial(kernel_back_first, share, cell_count),
        [(big, f32), vec, grad_out, grad_out] + conv_scratch[:2],
        [pair, flat, (big, bf16), ((12, share, channels), f32)],
        4 * 10**9, LIMITS[5],
        dilations, *parts1, consts1, d_stream2, d_normed1, normed1, gains_on, act0, slope0, normed0,
        point_back,
    )
    chip0 = keep0 + swapped(give0, "gz", 1)
    chip1 = keep1 + swapped(give1, "gz", 1)
    last = call(
        functools.partial(kernel_last, depth),
        [((64, channels), f32)] * members,
        conv_scratch[2:] + [flat, flat, (big, bf16), (big, bf16)],
        4 * 10**9, LIMITS[6],
        dilations, rimmed0, shifted0, d_stream1, normed0, gains_on, consts0, gathered, lift_in, w_back, prediction,
        sums_b0, out_raw, chip0, chip1, ready=(13, 14),
    )
    spread = call(
        kernel_spread, [((groups, 12 * share, channels), bf16)], [], 10**5, LIMITS[9],
        chip0, swapped(chip0, "gz", 2), chip1, swapped(chip1, "gz", 2), last[0], scalars=False, ready=(4,),
    )[0]
    near_grads = lax.all_to_all(spread, "gx", 0, 0)

    prediction, field_grad, grad_w_in, grad_w_time, grad_biases, grad_gains, grad_w_out = call(
        functools.partial(kernel_tail, cell_count, inv_area),
        [(clean_field.shape, f32), (clean_field.shape, f32), ((3, channels), f32), (w_time.shape, f32),
         ((2, channels), f32), ((3, channels), f32), ((3, channels), f32)],
        [], 10**6, LIMITS[10],
        last[0], *(swapped(last[bit], "gz", bit) for bit in (1, 2, 3)), *parts1, *parts2, consts0, w_in_on,
        gains_on, mixed_own, features[None], time_raw[None], scalars=False,
    )
    tied, _ = lax.optimization_barrier((near_grads, field_grad))
    far_grads = swapped(tied, "gz", 1)
    grad_w_z, grad_w_xy, grad_w_point = call(
        functools.partial(kernel_layout, inv_area, share),
        [(w_z.shape, f32), (w_xy.shape, f32), (w_point.shape, f32)],
        [], 10**6, LIMITS[11], near_grads, far_grads, scalars=False,
    )
    return (
        prediction,
        field_grad,
        grad_w_in,
        grad_w_time,
        grad_w_z,
        grad_w_xy,
        grad_w_point,
        grad_biases,
        grad_gains,
        grad_w_out,
    )


def padded_2(cells, sides, width):
    for axis, dim in sides:
        count = lax.axis_size(axis)
        head = lax.slice_in_dim(cells, 0, width, axis=dim)
        tail = lax.slice_in_dim(cells, cells.shape[dim] - width, cells.shape[dim], axis=dim)
        cells = jnp.concatenate(
            [
                lax.ppermute(tail, axis, [(i, (i + 1) % count) for i in range(count)]),
                cells,
                lax.ppermute(head, axis, [((i + 1) % count, i) for i in range(count)]),
            ],
            axis=dim,
        )
    return cells


def passed_along(value, axis, steps):
    count = lax.axis_size(axis)
    pairs = [(source, (source + steps) % count) for source in range(count)]
    return lax.ppermute(value, axis, pairs)


def contract_cells(left, right):
    return lax.dot_general(
        left, right, (((0, 1, 2), (0, 1, 2)), ((), ())), preferred_element_type=jnp.float32
    )


def plane_tap(padded, shift_x, shift_y, rows_x, rows_y):
    return padded[1 + shift_x : 1 + shift_x + rows_x, 1 + shift_y : 1 + shift_y + rows_y]


def plane_pad(source):
    rimmed = padded_2(source, (("gx", 0),), 1)
    return jnp.pad(rimmed, ((0, 0), (1, 1), (0, 0), (0, 0)))


def slab_windows(source, dilation):
    slab_depth = source.shape[2]
    above = passed_along(source, "gz", -1)
    above_far = passed_along(source, "gz", -2)
    below = passed_along(source, "gz", 1)
    below_far = passed_along(source, "gz", 2)
    ahead_rows = jnp.concatenate([source, above, above_far], axis=2)
    behind_rows = jnp.concatenate([below_far, below, source], axis=2)
    upper = lax.dynamic_slice_in_dim(ahead_rows, dilation, slab_depth, 2)
    lower = lax.dynamic_slice_in_dim(behind_rows, 2 * slab_depth - dilation, slab_depth, 2)
    return (lower, upper)


def normalize(hidden, gains, cell_count):
    average = lax.psum(jnp.sum(hidden, axis=(0, 1, 2)), ("gz", "gx")) / cell_count
    centered = hidden - average
    spread = lax.psum(jnp.sum(centered * centered, axis=(0, 1, 2)), ("gz", "gx")) / cell_count
    inverse_std = lax.rsqrt(spread + eps_norm)
    whitened = (hidden - average) * inverse_std
    return ((whitened * gains).astype(jnp.bfloat16), whitened, inverse_std)


def norm_back(d_normed, whitened, inverse_std, gains, cell_count):
    scaled = d_normed * gains
    sum_grad, sum_cross = lax.psum(
        (jnp.sum(scaled, axis=(0, 1, 2)), jnp.sum(scaled * whitened, axis=(0, 1, 2))), ("gz", "gx")
    )
    d_hidden = inverse_std * (scaled - sum_grad / cell_count - whitened * (sum_cross / cell_count))
    return (d_hidden, jnp.sum(d_normed * whitened, axis=(0, 1, 2)))


def conv_forward(normed, dilation, weights_z, weights_xy):
    rows_x, rows_y = (normed.shape[0], normed.shape[1])
    lower, upper = slab_windows(normed, dilation)
    padded = plane_pad(normed)
    summed = jnp.dot(lower, weights_z[0], preferred_element_type=jnp.float32)
    summed = summed + jnp.dot(normed, weights_z[1], preferred_element_type=jnp.float32)
    summed = summed + jnp.dot(upper, weights_z[2], preferred_element_type=jnp.float32)
    for tap_number, (shift_x, shift_y) in enumerate(plane_offsets):
        summed = summed + jnp.dot(
            plane_tap(padded, shift_x, shift_y, rows_x, rows_y),
            weights_xy[tap_number],
            preferred_element_type=jnp.float32,
        )
    return summed


def conv_backward_split(pre_cot, normed, dilation, weights_z, weights_xy):
    rows_x, rows_y = (normed.shape[0], normed.shape[1])
    lower_cot, upper_cot = slab_windows(pre_cot, dilation)
    padded_cot = plane_pad(pre_cot)
    d_normed = jnp.dot(upper_cot, weights_z[0].T, preferred_element_type=jnp.float32)
    d_normed = d_normed + jnp.dot(pre_cot, weights_z[1].T, preferred_element_type=jnp.float32)
    d_normed = d_normed + jnp.dot(lower_cot, weights_z[2].T, preferred_element_type=jnp.float32)
    xy_terms = []
    for tap_number, (shift_x, shift_y) in enumerate(plane_offsets):
        shifted = plane_tap(padded_cot, -shift_x, -shift_y, rows_x, rows_y)
        d_normed = d_normed + jnp.dot(
            shifted, weights_xy[tap_number].T, preferred_element_type=jnp.float32
        )
        xy_terms.append(contract_cells(normed, shifted))
    z_terms = jnp.stack(
        [
            contract_cells(normed, upper_cot),
            contract_cells(normed, pre_cot),
            contract_cells(normed, lower_cot),
        ]
    )
    return (d_normed, z_terms, jnp.stack(xy_terms))


def per_device_split(
    clean_field,
    noise_field,
    timestep,
    dilations,
    w_in,
    w_time,
    w_z,
    w_xy,
    w_point,
    biases,
    norm_gains,
    w_out,
):
    layer_total = w_z.shape[0]
    rows_x, rows_y, slab_depth = (clean_field.shape[1], clean_field.shape[2], clean_field.shape[3])
    plane_cells = rows_x * lax.axis_size("gx") * slab_depth * lax.axis_size("gz")
    cell_count = float(plane_cells * rows_y)
    inv_area = 1.0 / plane_cells
    alpha_bar, features, time_raw, time_code = time_terms(timestep, w_time)
    noisy = jnp.sqrt(alpha_bar) * clean_field + jnp.sqrt(1.0 - alpha_bar) * noise_field
    stream = jnp.einsum("kxyz,kc->xyzc", noisy, w_in, precision=highest)
    saved = []
    for which_layer in range(layer_total):
        normed, whitened, inverse_std = normalize(stream, norm_gains[which_layer], cell_count)
        pre_act = conv_forward(normed, dilations[which_layer], w_z[which_layer], w_xy[which_layer])
        pre_act = pre_act + biases[which_layer] + time_code
        activated = jax.nn.gelu(pre_act).astype(jnp.bfloat16)
        saved.append((normed, whitened, inverse_std, pre_act, activated))
        stream = stream + jnp.dot(
            activated, w_point[which_layer], preferred_element_type=jnp.float32
        )
    out_normed, out_white, out_inverse = normalize(stream, norm_gains[layer_total], cell_count)
    prediction = jnp.einsum("xyzc,kc->kxyz", out_normed, w_out, preferred_element_type=jnp.float32)
    misfit = prediction - noise_field
    d_out = jnp.einsum("kxyz,kc->xyzc", misfit, w_out.astype(jnp.float32), precision=highest)
    out_raw = jnp.einsum(
        "kxyz,xyzc->kc", misfit, out_normed, precision=highest, preferred_element_type=jnp.float32
    )
    d_stream, out_gain_raw = norm_back(
        d_out, out_white, out_inverse, norm_gains[layer_total], cell_count
    )
    z_list, xy_list, point_list, bias_list, gain_list = ([], [], [], [], [])
    for which_layer in reversed(range(layer_total)):
        normed, whitened, inverse_std, pre_act, activated = saved[which_layer]
        stream_cot = d_stream.astype(jnp.bfloat16)
        point_raw = contract_cells(activated, stream_cot)
        d_act = jnp.dot(stream_cot, w_point[which_layer].T, preferred_element_type=jnp.float32)
        gelu_back = jax.vjp(jax.nn.gelu, pre_act)[1]
        pre_cot = gelu_back(d_act)[0].astype(jnp.bfloat16)
        bias_raw = jnp.sum(pre_cot, axis=(0, 1, 2), dtype=jnp.float32)
        d_normed, z_raw, xy_raw = conv_backward_split(
            pre_cot, normed, dilations[which_layer], w_z[which_layer], w_xy[which_layer]
        )
        d_back, gain_raw = norm_back(
            d_normed, whitened, inverse_std, norm_gains[which_layer], cell_count
        )
        d_stream = d_stream + d_back
        z_list.insert(0, z_raw)
        xy_list.insert(0, xy_raw)
        point_list.insert(0, point_raw)
        bias_list.insert(0, bias_raw)
        gain_list.insert(0, gain_raw)
    field_grad = jnp.einsum("xyzc,kc->kxyz", d_stream, w_in, precision=highest)
    in_raw = jnp.einsum("kxyz,xyzc->kc", noisy, d_stream, precision=highest)
    z_all, xy_all, point_all, bias_all, gain_all, in_raw, out_raw = lax.psum(
        (
            jnp.stack(z_list),
            jnp.stack(xy_list),
            jnp.stack(point_list),
            jnp.stack(bias_list),
            jnp.stack(gain_list + [out_gain_raw]),
            in_raw,
            out_raw,
        ),
        ("gz", "gx"),
    )
    time_back = jax.vjp(jax.nn.silu, time_raw)[1](jnp.sum(bias_all, axis=0))[0]
    grad_w_time = inv_area * jnp.outer(features, time_back)
    return (
        prediction,
        field_grad,
        inv_area * in_raw,
        grad_w_time,
        inv_area * z_all,
        inv_area * xy_all,
        inv_area * point_all,
        inv_area * bias_all,
        inv_area * gain_all,
        inv_area * out_raw,
    )


def per_device(*args):
    members, groups = lax.axis_size("gz"), lax.axis_size("gx")
    _, rows_x, rows_y, depth = args[0].shape
    small = rows_x == 1 and rows_y == 4 and members == 4 and groups == 8 and depth * members == 2 * REACH
    return per_device_grouped(*args) if small else per_device_split(*args)


def solution(mesh):
    return jax.shard_map(
        per_device,
        mesh=mesh,
        in_specs=(
            P(None, "gx", None, "gz"),
            P(None, "gx", None, "gz"),
            P(),
            P(),
            P(),
            P(),
            P(),
            P(),
            P(),
            P(),
            P(),
            P(),
        ),
        out_specs=(
            P(None, "gx", None, "gz"),
            P(None, "gx", None, "gz"),
            P(),
            P(),
            P(),
            P(),
            P(),
            P(),
            P(),
            P(),
        ),
        check_vma=False,
    )
```

```python
import functools
import math

import jax
import jax.numpy as jnp
from jax import lax
from jax.experimental import pallas as pl
from jax.experimental.pallas import tpu as pltpu
from jax.sharding import PartitionSpec as P

STEPS = 1000
REACH = 256
RIM = 4
TILE = 16
LIMITS = (4, 13, 9, 7, 9, 8, 10, 2, 6, 2, 2, 3)

eps_norm = 1e-05
highest = lax.Precision.HIGHEST
bf16 = jnp.bfloat16
f32 = jnp.float32
plane_offsets = ((-1, -1), (-1, 0), (-1, 1), (0, -1), (0, 1), (1, -1), (1, 0), (1, 1))


def time_terms(timestep, w_time):
    moment = timestep[0].astype(jnp.float32)
    half_width = w_time.shape[0] // 2
    alpha_bar = jnp.cos(0.5 * math.pi * (moment + 0.5) / STEPS) ** 2
    ladder = jnp.exp(-math.log(10000.0) * jnp.arange(half_width, dtype=jnp.float32) / half_width)
    angles = moment * ladder
    features = jnp.concatenate([jnp.sin(angles), jnp.cos(angles)])
    time_raw = jnp.dot(features, w_time, precision=highest)
    return (alpha_bar, features, time_raw, jax.nn.silu(time_raw))


def mm(left, right):
    return lax.dot_general(left, right, (((1,), (0,)), ((), ())), preferred_element_type=f32)


def mm_nt(left, right):
    return lax.dot_general(left, right, (((1,), (1,)), ((), ())), preferred_element_type=f32)


def mm_tn(left, right):
    return lax.dot_general(left, right, (((0,), (0,)), ((), ())), preferred_element_type=f32)


def halves(value):
    high = value.astype(bf16)
    return high, (value - high.astype(f32)).astype(bf16)


def wide(vector):
    return jnp.concatenate([vector] * 4, axis=1)


def folded(vector):
    channels = vector.shape[1] // 4
    return sum(vector[:, y * channels : (y + 1) * channels] for y in range(4))


class Place:
    def __init__(self, sc, rows):
        self.rows = rows
        self.members = lax.axis_size("gz")
        self.member = lax.axis_index("gz")
        self.small = jnp.minimum(sc[0], sc[1])
        self.coarse = self.small >= self.members
        tiles = rows // TILE
        self.tiles = tiles
        self.stride = jnp.where(self.coarse, tiles - 1, tiles)
        self.span = REACH // self.members + 2 * RIM
        far = jnp.where(self.coarse, REACH // self.members, self.span)
        near = jnp.where(self.coarse, self.small // self.members, 1)
        self.steps = [jnp.where(sc[l] == REACH, far, near) for l in range(2)]

    def index(self, shape):
        row = lax.broadcasted_iota(jnp.int32, shape, 0)
        return lax.rem(row, TILE) * self.stride + row // TILE, row // TILE

    def own(self, shape):
        place, tile = self.index(shape)
        inside = lax.rem(place, self.span)
        near = ((inside >= RIM) & (inside < self.span - RIM)).astype(jnp.int32)
        far = (tile < self.tiles - 1).astype(jnp.int32)
        return jnp.where(self.coarse, far, near) == 1

    def pick(self, cells_z):
        shape = (self.rows, cells_z)
        return self.z_of(shape, cells_z) == lax.broadcasted_iota(jnp.int32, shape, 1)

    def z_of(self, shape, cells_z):
        place, _ = self.index(shape)
        residues = jnp.minimum(self.small, self.members)
        part, start = self.member // residues, lax.rem(self.member, residues)
        period = place // self.span
        inside = place - period * self.span - RIM + part * (REACH // self.members)
        near = start + residues * inside + period * REACH
        z = jnp.where(self.coarse, place * self.members + self.member, near)
        return lax.rem(z + 2 * cells_z, cells_z)


def build_taps(block_of, taps):
    channels = taps.shape[-1] // 2
    zero = jnp.zeros((channels, channels), bf16)
    near, far = slice(0, channels), slice(channels, 2 * channels)
    for i in range(3):
        down, here, up = (block_of(i, j) for j in range(3))
        taps[i, near, near] = here
        taps[i, far, far] = here
        taps[i, near, far] = down
        taps[i, far, near] = up
        taps[3 + i, near, near] = zero
        taps[3 + i, far, far] = zero
        taps[3 + i, near, far] = down
        taps[3 + i, far, near] = up
    for m in range(2):
        build_pair(block_of(3, m), taps, 6 + m)


def build_pair(block, target, m):
    channels = block.shape[-1]
    zero = jnp.zeros((channels, channels), bf16)
    target[m, :channels, :channels] = block
    target[m, channels:, channels:] = block
    target[m, :channels, channels:] = zero
    target[m, channels:, :channels] = zero


def forward_blocks(w_z, w_xy, layer):
    def block_of(i, j):
        if i == 3:
            return w_z[layer, 2 * j]
        at = i * 3 + j
        return w_z[layer, 1] if at == 4 else w_xy[layer, at - (at > 4)]

    return block_of


def taken(weights, layer):
    return lambda i, j: weights[layer, i * 3 + j]


def kernel_mix(block, mixed, mixed_own):
    parts = mixed.shape[0]
    alpha_bar = jnp.cos(0.5 * math.pi * (block[6, 0, 0:1] + 0.5) / STEPS) ** 2
    keep, add = jnp.sqrt(alpha_bar), jnp.sqrt(1.0 - alpha_bar)
    for k in range(3):
        noise = block[3 + k, 0]
        noisy = keep * block[k, 0] + add * noise
        mixed_own[4 * k : 4 * k + 4] = noisy
        for part in range(parts):
            mixed[part, 4 * k : 4 * k + 4] = noisy
            mixed[part, 12 + 4 * k : 16 + 4 * k] = noise


def kernel_prepare(steps, w_z, w_xy, w_point, small, w_front, point, w_back, point_back, lift_in, lift_out,
                   steps_on):
    steps_on[0], steps_on[1] = steps[0], steps[1]
    point[...] = w_point[...]
    for layer in range(2):
        forward = forward_blocks(w_z, w_xy, layer)
        for i in range(3):
            for j in range(3):
                w_front[layer, i * 3 + j] = forward(i, j)
        for m in range(2):
            w_front[layer, 9 + m] = forward(3, m)
        for i in range(3):
            for j in range(3):
                w_back[layer, i * 3 + j] = forward(2 - i, 2 - j).T
        for m in range(2):
            w_back[layer, 9 + m] = forward(3, 1 - m).T
        point_back[layer] = w_point[layer].T
    whole = spread_rows(small[0:3], 0)
    high, low = halves(whole)
    lift_in[0:32] = high
    lift_in[32:64] = high
    lift_in[64:96] = low
    lift_in[96:128] = jnp.zeros_like(low)
    high = spread_rows(small[6:9], 3).astype(bf16)
    lift_out[0:32] = high
    lift_out[32:64] = high
    lift_out[64:96] = jnp.zeros_like(high)
    lift_out[96:128] = jnp.zeros_like(high)


def spread_rows(weights, first):
    channels = weights.shape[1]
    zero = jnp.zeros((1, channels), f32)
    rows = [jnp.zeros((1, 4 * channels), f32)] * 32
    for k in range(3):
        for y in range(4):
            parts = [weights[k : k + 1] if at == y else zero for at in range(4)]
            rows[(first + k) * 4 + y] = jnp.concatenate(parts, axis=1)
    return jnp.concatenate(rows, axis=0)


def fill_rims(padded, planes):
    padded[0] = padded[planes]
    padded[planes + 1] = padded[1]


def fill_shifted(place, layer, padded, shifted, planes):
    step, stride = place.steps[layer], place.stride
    for tile in range(place.tiles):
        for way in range(2):
            at = tile - step if way == 0 else tile + step
            moved = at + TILE * stride
            source = lax.rem(moved, stride)
            turn = lax.rem(2 * TILE - moved // stride, TILE)
            rows = padded[1 : planes + 1, pl.ds(pl.multiple_of(source * TILE, TILE), TILE), :]
            rows = pltpu.roll(rows.astype(f32), turn, 1)
            shifted[way, :, tile * TILE : (tile + 1) * TILE, :] = rows.astype(bf16)


def conv_pair(padded, shifted, taps, x0, count):
    rows, lanes = padded.shape[1:]
    half, quarter = lanes // 2, lanes // 4
    totals = [None, None, None]

    def add(at, left, right):
        part = mm(left.reshape(count * rows, half), right)
        totals[at] = part if totals[at] is None else totals[at] + part

    for q in range(2):
        side = slice(q * half, (q + 1) * half)
        for i in range(3):
            add(q, padded[x0 + i : x0 + i + count, :, side], taps[i])
        for m in range(2):
            add(q, shifted[m, x0 : x0 + count, :, side], taps[6 + m])
    for i in range(3):
        add(2, padded[x0 + i : x0 + i + count, :, quarter : 3 * quarter], taps[3 + i])
    first, second, middle = totals
    first = jnp.concatenate([first[:, :quarter], first[:, quarter:] + middle[:, :quarter]], axis=1)
    second = jnp.concatenate([second[:, :quarter] + middle[:, quarter:], second[:, quarter:]], axis=1)
    return first, second


def gelu_pair(value):
    scale = math.sqrt(2.0 / math.pi)
    square = value * value
    bent = jnp.tanh(value * (scale + (scale * 0.044715) * square))
    half = 0.5 + 0.5 * bent
    slope = half + value * (0.5 - 0.5 * (bent * bent)) * (scale + (3.0 * 0.044715 * scale) * square)
    return value * half, slope


def members_of(parts):
    found = []
    for part in parts:
        for at in range(0, part.shape[0], 8):
            found.append(part[at : at + 8])
    return found


def merged_stats(parts, per_member):
    found = members_of(parts)
    mean = sum(one[0:1] for one in found) / (per_member * len(found))
    spread = sum(one[1:2] for one in found)
    for one in found:
        gap = one[0:1] / per_member - mean
        spread = spread + per_member * gap * gap
    return mean, lax.rsqrt(spread / (per_member * len(found)) + eps_norm)


def put_rows(ref, *vectors):
    rows = list(vectors)
    rows += [jnp.zeros((1, ref.shape[1]), f32)] * (ref.shape[0] - len(rows))
    ref[...] = jnp.concatenate(rows, axis=0)


def masked_total(mask, value):
    return folded(jnp.sum(jnp.where(mask, value, 0.0), axis=0, keepdims=True))


def layer_forward(place, layer, padded, shifted, taps, pair, w_front, wp, shift_bias, old,
                  stream, act, slope, stats, acc, per_member):
    planes, rows, lanes = stream.shape
    half = lanes // 2
    count = planes // 4
    build_taps(taken(w_front, layer), taps)
    build_pair(wp[layer], pair, 0)
    fill_rims(padded, planes)
    fill_shifted(place, layer, padded, shifted, planes)
    acc[...] = jnp.zeros_like(acc)
    bias = wide(shift_bias[layer : layer + 1, :])[:, :half]

    for x0 in range(0, planes, count):
        part = slice(x0, x0 + count)
        for q, total in enumerate(conv_pair(padded, shifted, taps, x0, count)):
            side = slice(q * half, (q + 1) * half)
            value, grad = gelu_pair(total + bias)
            act[part, :, side] = value.astype(bf16).reshape(count, rows, half)
            slope[part, :, side] = grad.astype(bf16).reshape(count, rows, half)
    for x0 in range(0, planes, count):
        part = slice(x0, x0 + count)
        for q in range(2):
            side = slice(q * half, (q + 1) * half)
            branch = mm(act[part, :, side].reshape(count * rows, half), pair[0])
            new = old[part, :, side] + branch.reshape(count, rows, half)
            stream[part, :, side] = new
            acc[:, side] += jnp.sum(new, axis=0)
    mask = place.own((rows, lanes))
    total = masked_total(mask, acc[...])
    mean = wide(total / per_member)
    spread = jnp.zeros((rows, lanes), f32)
    for x in range(planes):
        gap = stream[x] - mean
        spread = spread + gap * gap
    put_rows(stats, total, masked_total(mask, spread))


def kernel_first(cells_z, per_member, sc, near, far, lift_in, small, shift_bias, w_front, wp,
                 stream, padded, act, slope, gathered, stats, consts,
                 shifted, taps, pair, acc, old, source):
    planes, rows, lanes = stream.shape
    channels = lanes // 4
    depth = near.shape[2]
    place = Place(sc, rows)
    cell_count = float(planes * 4 * cells_z)
    comps = [
        jnp.concatenate([ref[:, 4 * k : 4 * k + 4, :] for ref in (near, far)], axis=0) for k in range(3)
    ]

    def all_sum(value):
        value = jnp.sum(jnp.sum(value, axis=0), axis=0, keepdims=True)
        return jnp.sum(value, axis=1, keepdims=True)

    means = [all_sum(comp) / cell_count for comp in comps]
    gaps = [comp - mean[None] for comp, mean in zip(comps, means)]
    covs = {}
    for j in range(3):
        for k in range(j, 3):
            covs[j, k] = all_sum(gaps[j] * gaps[k]) / cell_count
    rows_in = [small[k : k + 1, :] for k in range(3)]
    mean_c = sum(means[k] * rows_in[k] for k in range(3))
    var_c = jnp.zeros((1, channels), f32)
    for (j, k), cov in covs.items():
        var_c = var_c + (1.0 if j == k else 2.0) * cov * (rows_in[j] * rows_in[k])
    inv_c = lax.rsqrt(jnp.maximum(var_c, 0.0) + eps_norm)
    flat = [jnp.broadcast_to(value, (1, channels)) for value in means + list(covs.values())]
    put_rows(consts, mean_c, inv_c, *flat)
    blank = jnp.zeros((8, depth), f32)
    core = lax.rem(place.member, 2)
    for slab in range(cells_z // depth):
        ref, side = (near, core) if slab % 2 == 0 else (far, 1 - core)
        at = pl.ds(pl.multiple_of((slab // 2 * 2 + side) * depth, depth), depth)
        for x in range(planes):
            high, low = halves(jnp.concatenate([ref[slab // 2 * planes + x], blank], axis=0))
            source[x, 0:32, at] = high
            source[x, 32:64, at] = low
            source[x, 64:96, at] = high
            source[x, 96:128, at] = jnp.zeros_like(high)
    pick = place.pick(cells_z).astype(f32).astype(bf16)
    scale = wide(inv_c * small[3:4, :])
    mean_w = wide(mean_c)
    for x in range(planes):
        gathered[x] = mm_nt(pick, source[x]).astype(bf16)
    for x0 in range(0, planes, planes // 2):
        part = slice(x0, x0 + planes // 2)
        value = mm(gathered[part].reshape(planes // 2 * rows, 128), lift_in[...])
        unit = ((value - mean_w) * scale).astype(bf16).reshape(planes // 2, rows, lanes)
        old[part] = value.reshape(planes // 2, rows, lanes)
        padded[x0 + 1 : x0 + 1 + planes // 2] = unit
    layer_forward(place, 0, padded, shifted, taps, pair, w_front, wp, shift_bias, old, stream,
                  act, slope, stats, acc, per_member)


def kernel_second(per_member, sc, *refs):
    parts, refs = refs[:4], refs[4:]
    (old, small, shift_bias, w_front, wp, stream, padded, act, slope, stats, consts,
     shifted, taps, pair, acc) = refs
    planes, rows, _ = stream.shape
    place = Place(sc, rows)
    mean, inverse = merged_stats(parts, per_member)
    put_rows(consts, mean, inverse)
    mean_w, scale = wide(mean), wide(inverse * small[4:5, :])
    for x in range(planes):
        padded[x + 1] = ((old[x] - mean_w) * scale).astype(bf16)
    layer_forward(place, 1, padded, shifted, taps, pair, w_front, wp, shift_bias, old, stream,
                  act, slope, stats, acc, per_member)


def kernel_out(per_member, sc, *refs):
    parts, refs = refs[:4], refs[4:]
    stream, small, gathered, lift_out, prediction, misfit, sums, w_out_raw, consts, unit = refs
    planes, rows, lanes = stream.shape
    place = Place(sc, rows)
    mean, inverse = merged_stats(parts, per_member)
    put_rows(consts, mean, inverse)
    mean_w, inv_w, gain_w = wide(mean), wide(inverse), wide(small[5:6, :])
    scale = inv_w * gain_w
    for x in range(planes):
        unit[x] = ((stream[x] - mean_w) * scale).astype(bf16)
    row = lax.broadcasted_iota(jnp.int32, (128, 128), 0)
    col = lax.broadcasted_iota(jnp.int32, (128, 128), 1)
    slot = lax.rem(col, 32)
    used = (col < 64) & (slot >= 12) & (slot < 24)
    take = (used & ((row == slot) | (row == slot + 32))).astype(f32).astype(bf16)
    total = mm_nt(unit[...].reshape(planes * rows, lanes), lift_out[...])
    noise = mm(gathered[...].reshape(planes * rows, 128), take)
    gap = total - noise
    high, low = halves(gap)
    lane = lax.broadcasted_iota(jnp.int32, gap.shape, 1)
    both = jnp.where(lane < 32, high.astype(f32), low.astype(f32)).astype(bf16)
    misfit[...] = both.reshape(planes, rows, 128)
    for x in range(planes):
        @pl.when(lax.axis_index("gx") == x)
        def _(x=x):
            prediction[...] = total[x * rows : (x + 1) * rows]
    plain = jnp.zeros((rows, lanes), f32)
    cross = jnp.zeros((rows, lanes), f32)
    for x0 in range(0, planes, planes // 2):
        part = slice(x0 * rows, (x0 + planes // 2) * rows)
        d_out = mm(both[part], lift_out[...]).reshape(planes // 2, rows, lanes)
        for x in range(planes // 2):
            plain = plain + d_out[x]
            cross = cross + d_out[x] * ((stream[x0 + x] - mean_w) * inv_w)
    own = place.own((rows, 128))
    kept = jnp.concatenate([jnp.where(own, misfit[x].astype(f32), 0.0) for x in range(planes)], axis=0)
    raw = mm_tn(kept.astype(bf16), unit[...].reshape(planes * rows, lanes))
    mask = place.own((rows, lanes))
    put_rows(sums, masked_total(mask, plain), masked_total(mask, cross))
    put_rows(w_out_raw, *by_component(raw[0:32] + raw[32:64], 3))


def by_component(raw, first):
    channels = raw.shape[1] // 4
    found = []
    for k in range(first, first + 3):
        found.append(
            sum(raw[k * 4 + y : k * 4 + y + 1, y * channels : (y + 1) * channels] for y in range(4))
        )
    return found


def branch_backward(planes, d_stream_of, pair, slope, padded, scot, bias_acc):
    rows, lanes = padded.shape[1:]
    half = lanes // 2
    count = planes // 2

    for x0 in range(0, planes, count):
        part = slice(x0, x0 + count)
        for x in range(x0, x0 + count):
            scot[x] = d_stream_of(x).astype(bf16)
        for q in range(2):
            side = slice(q * half, (q + 1) * half)
            cot = scot[part, :, side].reshape(count * rows, half)
            d_act = mm(cot, pair[0]).reshape(count, rows, half)
            pre = (d_act * slope[part, :, side].astype(f32)).astype(bf16)
            padded[x0 + 1 : x0 + 1 + count, :, side] = pre
            bias_acc[:, side] += jnp.sum(pre.astype(f32), axis=0)


def weight_grads(place, planes, padded, shifted, scot, normed, act, keep, give, taps_all, share):
    rows, lanes = padded.shape[1:]
    channels = lanes // 4
    wide_share = 4 * share
    row = lax.broadcasted_iota(jnp.int32, (lanes, wide_share), 0)
    col = lax.broadcasted_iota(jnp.int32, (lanes, wide_share), 1)
    hit = (row // channels == col // share) & (
        lax.rem(row, channels) == lax.rem(col, share) + lax.axis_index("gx") * share
    )
    choose = hit.astype(f32).astype(bf16)
    mask = jnp.concatenate([place.own((rows, wide_share))] * planes, axis=0)

    def turned(source):
        got = mm(source.reshape(planes * rows, lanes), choose)
        return jnp.where(mask, got, 0.0).astype(bf16)

    def add_blocks(raw, j):
        return sum(
            raw[(y + j) * share : (y + j + 1) * share, y * channels : (y + 1) * channels]
            for y in range(4)
            if 0 <= y + j < 4
        )

    left = turned(normed[1 : planes + 1])
    for i in range(3):
        raw = mm_tn(left, padded[2 - i : 2 - i + planes].reshape(planes * rows, lanes))
        for j in range(3):
            taps_all[i * 3 + j] = add_blocks(raw, j - 1)
    for m in range(2):
        raw = mm_tn(left, shifted[1 - m].reshape(planes * rows, lanes))
        taps_all[9 + m] = add_blocks(raw, 0)
    raw = mm_tn(turned(act[...]), scot[...].reshape(planes * rows, lanes))
    taps_all[11] = add_blocks(raw, 0)
    odd, half = lax.rem(place.member, 2), keep.shape[0]
    keep[...] = taps_all[pl.ds(odd * half, half)]
    give[...] = taps_all[pl.ds((1 - odd) * half, half)]


def conv_backward(planes, padded, shifted, taps, emit):
    count = planes // 4

    for x0 in range(0, planes, count):
        for q, total in enumerate(conv_pair(padded, shifted, taps, x0, count)):
            emit(x0, count, q, total)


def kernel_back_second(cell_count, sc, *refs):
    parts, refs = refs[:4], refs[4:]
    (stream, out_consts, small, misfit, lift_out, slope, normed, w_back, point_back,
     d_stream, d_normed, sums, padded, shifted, scot,
     taps, pair, acc, acc2) = refs
    planes, rows, lanes = stream.shape
    half = lanes // 2
    place = Place(sc, rows)
    sums_out = sum(members_of(parts))
    gain_w = wide(small[5:6, :])
    mean_w, inv_w = wide(out_consts[0:1]), wide(out_consts[1:2])
    m_plain = gain_w * wide(sums_out[0:1]) / cell_count
    m_cross = gain_w * wide(sums_out[1:2]) / cell_count
    build_pair(point_back[1], pair, 0)
    build_taps(taken(w_back, 1), taps)
    acc[...] = jnp.zeros_like(acc)

    def d_stream_of(x):
        d_out = mm(misfit[x], lift_out[...])
        white = (stream[x] - mean_w) * inv_w
        value = inv_w * (gain_w * d_out - m_plain - white * m_cross)
        d_stream[x] = value
        return value

    branch_backward(planes, d_stream_of, pair, slope, padded, scot, acc)
    mask = place.own((rows, lanes))
    s_bias = masked_total(mask, acc[...])
    acc[...] = jnp.zeros_like(acc)
    acc2[...] = jnp.zeros_like(acc2)
    fill_rims(padded, planes)
    fill_shifted(place, 1, padded, shifted, planes)

    def emit(x0, count, q, value):
        side = slice(q * half, (q + 1) * half)
        value = value.reshape(count, rows, half)
        d_normed[x0 : x0 + count, :, side] = value
        acc[:, side] += jnp.sum(value, axis=0)
        acc2[:, side] += jnp.sum(value * normed[x0 + 1 : x0 + 1 + count, :, side].astype(f32), axis=0)

    conv_backward(planes, padded, shifted, taps, emit)
    s_plain = masked_total(mask, acc[...])
    s_cross = masked_total(mask, acc2[...]) / small[4:5, :]
    put_rows(sums, s_plain, s_cross, s_bias)


def kernel_weights_second(share, sc, padded, shifted, scot, normed, act, keep, give, taps_all):
    planes, rows, _ = scot.shape
    weight_grads(Place(sc, rows), planes, padded, shifted, scot, normed, act, keep, give, taps_all, share)


def kernel_back_first(share, cell_count, sc, *refs):
    parts, refs = refs[:4], refs[4:]
    (consts, d_next, d_normed, normed_next, small, act, slope, normed, point_back,
     d_stream, sums, keep, give, padded, shifted,
     pair, acc, scot, taps_all) = refs
    planes, rows, lanes = d_next.shape
    place = Place(sc, rows)
    sums_in = sum(members_of(parts))
    gain_w = wide(small[4:5, :])
    inv_w = wide(consts[1:2])
    m_plain = gain_w * wide(sums_in[0:1]) / cell_count
    m_cross = wide(sums_in[1:2]) / cell_count
    build_pair(point_back[0], pair, 0)
    acc[...] = jnp.zeros_like(acc)

    def d_stream_of(x):
        back = gain_w * d_normed[x] - m_plain - normed_next[x + 1].astype(f32) * m_cross
        value = d_next[x] + inv_w * back
        d_stream[x] = value
        return value

    branch_backward(planes, d_stream_of, pair, slope, padded, scot, acc)
    put_rows(sums, masked_total(place.own((rows, lanes)), acc[...]))
    fill_rims(padded, planes)
    fill_shifted(place, 0, padded, shifted, planes)
    weight_grads(place, planes, padded, shifted, scot, normed, act, keep, give, taps_all, share)


def kernel_last(depth, sc, padded, shifted, d_stream, normed, small, consts, gathered, lift_in, w_back,
                prediction, sums_bias, out_raw, ready0, ready1, own_out, out_1, out_2, out_3,
                taps, acc, acc2, high, low):
    planes, rows, lanes = d_stream.shape
    half = lanes // 2
    place = Place(sc, rows)
    build_taps(taken(w_back, 0), taps)
    acc[...] = jnp.zeros_like(acc)
    acc2[...] = jnp.zeros_like(acc2)
    scale = wide(consts[1:2] * small[3:4, :])

    def emit(x0, count, q, value):
        side = slice(q * half, (q + 1) * half)
        part = slice(x0, x0 + count)
        value = value.reshape(count, rows, half)
        acc[:, side] += jnp.sum(value, axis=0)
        acc2[:, side] += jnp.sum(value * normed[x0 + 1 : x0 + 1 + count, :, side].astype(f32), axis=0)
        full = d_stream[part, :, side] + value * scale[:, side]
        first, second = halves(full)
        high[part, :, side] = first
        low[part, :, side] = second

    conv_backward(planes, padded, shifted, taps, emit)
    mask = place.own((rows, lanes))
    s_plain = masked_total(mask, acc[...])
    s_cross = masked_total(mask, acc2[...]) / small[3:4, :]
    own = place.own((rows, 128))
    kept = jnp.concatenate([jnp.where(own, gathered[x].astype(f32), 0.0) for x in range(planes)], axis=0)
    kept = kept.astype(bf16)
    raw = mm_tn(kept, high[...].reshape(planes * rows, lanes))
    raw_low = mm_tn(kept, low[...].reshape(planes * rows, lanes))
    in_raw = by_component(raw[0:32] + raw[32:64] + raw_low[0:32], 0)
    blank = jnp.zeros((1, s_plain.shape[1]), f32)
    tail = jnp.concatenate([s_plain, s_cross] + [blank] * 6 + in_raw + [blank] * 5, axis=0)
    tail = jnp.concatenate([tail, sums_bias[...], out_raw[...]], axis=0)
    here = lax.axis_index("gx")
    lane = lax.broadcasted_iota(jnp.int32, (rows, 128), 1)
    field = mm_nt(high[here], lift_in[...]) + jnp.where(lane < 32, mm_nt(low[here], lift_in[...]), 0.0)
    field = jnp.where((lane >= 32) & (lane < 64), 0.0, field)
    field = field + jnp.where((lane >= 12) & (lane < 24), prediction[...], 0.0)
    cells_z = depth * place.members
    whole = place.z_of((rows, depth), cells_z)
    column = lax.broadcasted_iota(jnp.int32, (rows, depth), 1)
    mask = place.own((rows, depth))
    first, second = halves(field)
    for bit, target in enumerate((own_out, out_1, out_2, out_3)):
        there = lax.bitwise_xor(place.member, bit)
        pick = ((whole == column + there * depth) & mask).astype(f32).astype(bf16)
        out = mm_tn(first, pick) + mm_tn(second, pick)
        target[0:32] = out[0:32] + out[64:96]
        target[32:64] = tail


def call(kernel, outs, scratch, flops, limit, *args, scalars=True, scalar_out=0, ready=()):
    spec = pl.BlockSpec(memory_space=pltpu.VMEM)
    specs = [pl.BlockSpec(memory_space=pltpu.SMEM)] * scalars + [spec] * (len(args) - scalars)
    for at in ready:
        specs[at] = pl.BlockSpec(memory_space=pl.ANY)
    smem = pl.BlockSpec(memory_space=pltpu.SMEM)
    return pl.pallas_call(
        kernel,
        out_shape=[jax.ShapeDtypeStruct(shape, dtype) for shape, dtype in outs],
        in_specs=specs,
        out_specs=[spec] * (len(outs) - scalar_out) + [smem] * scalar_out,
        scratch_shapes=[pltpu.VMEM(*one) if isinstance(one, tuple) else one for one in scratch],
        compiler_params=pltpu.CompilerParams(vmem_limit_bytes=limit * 2**20),
        cost_estimate=pl.CostEstimate(flops=flops, bytes_accessed=2**23, transcendentals=0),
    )(*args)


def swapped(value, axis, bit):
    count = lax.axis_size(axis)
    return lax.ppermute(value, axis, [(i, i ^ bit) for i in range(count)])


def group_parts(value):
    return (value,) + tuple(swapped(value, "gz", bit) for bit in (1, 2, 3))


def kernel_spread(first, first_far, second, second_far, ready, spread):
    taps, share, channels = first.shape
    for layer, (own, other) in enumerate(((first, first_far), (second, second_far))):
        value = (own[...] + other[...]).reshape(taps * share, channels).astype(bf16)
        for part in range(spread.shape[0]):
            spread[part, layer * taps * share : (layer + 1) * taps * share] = value


def kernel_layout(scale, share, near, far, grad_w_z, grad_w_xy, grad_w_point):
    groups = near.shape[0]
    taps = near.shape[1] // share // 2
    odd = lax.rem(lax.axis_index("gz"), 2) == 1
    for layer in range(2):
        for tap in range(taps):
            at = (layer * taps + tap) * share
            one = near[:, at : at + share].astype(f32) * scale
            two = far[:, at : at + share].astype(f32) * scale
            for side in range(2):
                value = jnp.where(odd, one if side else two, two if side else one)
                value = value.reshape(groups * share, value.shape[2])
                whole = side * taps + tap
                if whole == 4:
                    grad_w_z[layer, 1] = value
                elif whole < 9:
                    grad_w_xy[layer, whole - (whole > 4)] = value
                elif whole < 11:
                    grad_w_z[layer, 2 * (whole - 9)] = value
                else:
                    grad_w_point[layer] = value


def kernel_tail(cell_count, inv_area, *refs):
    tails, parts1, parts2, refs = refs[:4], refs[4:8], refs[8:12], refs[12:]
    (consts, small, mixed, features, time_raw,
     prediction, field_grad, grad_w_in, grad_w_time, grad_biases, grad_gains, grad_w_out) = refs
    tail = sum(ref[...] for ref in tails)
    s1, s2 = sum(ref[...] for ref in parts1), sum(ref[...] for ref in parts2)
    inverse = consts[1:2]
    m_plain = inverse * (small[3:4] * tail[32:33] / cell_count)
    m_cross = inverse * inverse * (small[3:4] * tail[33:34] / cell_count)
    at = {(0, 0): 5, (0, 1): 6, (0, 2): 7, (1, 1): 8, (1, 2): 9, (2, 2): 10}
    rows_in = [small[k : k + 1] for k in range(3)]
    depth = mixed.shape[1]
    gaps = [mixed[4 * k : 4 * k + 4] - consts[2 + k : 3 + k, 0:1] for k in range(3)]
    for k in range(3):
        offset = jnp.sum(rows_in[k] * m_plain, axis=1, keepdims=True)
        value = tail[4 * k : 4 * k + 4] - offset
        cross = jnp.zeros_like(m_plain)
        for j in range(3):
            mix = jnp.sum(rows_in[k] * m_cross * rows_in[j], axis=1, keepdims=True)
            value = value - mix * gaps[j]
            row = at[min(j, k), max(j, k)]
            cross = cross + consts[row : row + 1] * rows_in[j]
        field_grad[k, 0] = value
        prediction[k, 0] = tail[12 + 4 * k : 16 + 4 * k]
        in_sum = tail[40 + k : 41 + k] - cell_count * (consts[2 + k : 3 + k] * m_plain + m_cross * cross)
        grad_w_in[k : k + 1] = inv_area * in_sum
    bias0, bias1 = tail[48:49], s1[2:3]
    grad_biases[...] = inv_area * jnp.concatenate([bias0, bias1], axis=0)
    grad_gains[...] = inv_area * jnp.concatenate([tail[33:34], s1[1:2], s2[1:2]], axis=0)
    grad_w_out[...] = inv_area * tail[56:59]
    raw = time_raw[...]
    gate = 1.0 / (1.0 + jnp.exp(-raw))
    back = (bias0 + bias1) * (gate * (1.0 + raw * (1.0 - gate)))
    spread = jnp.broadcast_to(features[...], grad_w_time.shape).T
    grad_w_time[...] = inv_area * (spread * back)


def per_device_grouped(clean_field, noise_field, timestep, dilations, w_in, w_time, w_z, w_xy, w_point,
                       biases, norm_gains, w_out):
    members, groups = lax.axis_size("gz"), lax.axis_size("gx")
    depth = clean_field.shape[3]
    planes, cells_z = groups, depth * members
    channels = w_in.shape[1]
    lanes = 4 * channels
    rows = (cells_z // REACH) * (REACH // members + 2 * RIM)
    share = channels // groups
    per_member = float(planes * 4 * depth)
    cell_count = per_member * members
    inv_area = 4.0 / cell_count

    _, features, time_raw, time_code = time_terms(timestep, w_time)
    parts = members // 2 * groups
    moment = jnp.broadcast_to(timestep.astype(f32).reshape(1, 1, 1, 1), (1,) + clean_field.shape[1:])
    block = jnp.concatenate([clean_field, noise_field, moment], axis=0)
    mixed, mixed_own = call(
        kernel_mix, [((parts, 24, depth), f32), ((12, depth), f32)], [], 10**5, LIMITS[7], block, scalars=False,
    )
    same_core = [[m * groups + g for m in range(core, members, 2) for g in range(groups)] for core in range(2)]
    near = lax.all_to_all(mixed, ("gz", "gx"), 0, 0, axis_index_groups=same_core)
    far = swapped(near, "gz", 1)
    shift_bias = biases + time_code

    big = (planes, rows, lanes)
    vec = ((8, channels), f32)
    thin = ((planes, rows, 128), bf16)
    lift = ((128, lanes), bf16)
    conv_scratch = [
        ((planes + 2, rows, lanes), bf16),
        ((2,) + big, bf16),
        ((8, lanes // 2, lanes // 2), bf16),
    ]
    pair = ((1, lanes // 2, lanes // 2), bf16)
    flat = ((rows, lanes), f32)
    grad_out = ((6, share, channels), f32)

    taps_out, point_out = ((2, 11, channels, channels), bf16), ((2, channels, channels), bf16)
    small = jnp.concatenate([w_in, norm_gains, w_out.astype(f32)], axis=0)
    w_front, point, w_back, point_back, lift_in, lift_out, steps_on = call(
        kernel_prepare,
        [taps_out, point_out, taps_out, point_out, lift, lift, ((2,), jnp.int32)],
        [], 10**8, LIMITS[0], dilations, w_z, w_xy, w_point, small, scalar_out=1,
    )
    stream1, normed0, act0, slope0, gathered, stats1, consts0 = call(
        functools.partial(kernel_first, cells_z, per_member),
        [(big, f32), conv_scratch[0], (big, bf16), (big, bf16), thin, vec, ((16, channels), f32)],
        conv_scratch[1:] + [pair, flat, (big, f32), ((planes, 128, cells_z), bf16)],
        4 * 10**9, LIMITS[1],
        steps_on, near, far, lift_in, small, shift_bias, w_front, point,
    )
    stream2, normed1, act1, slope1, stats2, consts1 = call(
        functools.partial(kernel_second, per_member),
        [(big, f32), conv_scratch[0], (big, bf16), (big, bf16), vec, vec],
        conv_scratch[1:] + [pair, flat],
        4 * 10**9, LIMITS[2],
        steps_on, *group_parts(stats1), stream1, small, shift_bias, w_front, point,
    )
    prediction, misfit, sums2, out_raw, consts2 = call(
        functools.partial(kernel_out, per_member),
        [((rows, 128), f32), thin, vec, vec, vec],
        [(big, bf16)],
        10**9, LIMITS[3],
        steps_on, *group_parts(stats2), stream2, small, gathered, lift_out,
    )
    parts2 = group_parts(sums2)
    d_stream2, d_normed1, sums1, rimmed1, shifted1, scot1 = call(
        functools.partial(kernel_back_second, cell_count),
        [(big, f32), (big, f32), vec] + conv_scratch[:2] + [(big, bf16)],
        conv_scratch[2:] + [pair, flat, flat],
        6 * 10**9, LIMITS[4],
        steps_on, *parts2, stream2, consts2, small, misfit, lift_out, slope1, normed1,
        w_back, point_back,
    )
    parts1 = group_parts(sums1)
    keep1, give1 = call(
        functools.partial(kernel_weights_second, share),
        [grad_out, grad_out], [((12, share, channels), f32)], 2 * 10**9, LIMITS[8],
        steps_on, rimmed1, shifted1, scot1, normed1, act1,
    )
    d_stream1, sums_b0, keep0, give0, rimmed0, shifted0 = call(
        functools.partial(kernel_back_first, share, cell_count),
        [(big, f32), vec, grad_out, grad_out] + conv_scratch[:2],
        [pair, flat, (big, bf16), ((12, share, channels), f32)],
        4 * 10**9, LIMITS[5],
        steps_on, *parts1, consts1, d_stream2, d_normed1, normed1, small, act0, slope0, normed0,
        point_back,
    )
    chip0 = keep0 + swapped(give0, "gz", 1)
    chip1 = keep1 + swapped(give1, "gz", 1)
    last = call(
        functools.partial(kernel_last, depth),
        [((64, channels), f32)] * members,
        conv_scratch[2:] + [flat, flat, (big, bf16), (big, bf16)],
        4 * 10**9, LIMITS[6],
        steps_on, rimmed0, shifted0, d_stream1, normed0, small, consts0, gathered, lift_in, w_back, prediction,
        sums_b0, out_raw, chip0, chip1, ready=(13, 14),
    )
    spread = call(
        kernel_spread, [((groups, 12 * share, channels), bf16)], [], 10**5, LIMITS[9],
        chip0, swapped(chip0, "gz", 2), chip1, swapped(chip1, "gz", 2), last[0], scalars=False, ready=(4,),
    )[0]
    near_grads = lax.all_to_all(spread, "gx", 0, 0)

    prediction, field_grad, grad_w_in, grad_w_time, grad_biases, grad_gains, grad_w_out = call(
        functools.partial(kernel_tail, cell_count, inv_area),
        [(clean_field.shape, f32), (clean_field.shape, f32), ((3, channels), f32), (w_time.shape, f32),
         ((2, channels), f32), ((3, channels), f32), ((3, channels), f32)],
        [], 10**6, LIMITS[10],
        last[0], *(swapped(last[bit], "gz", bit) for bit in (1, 2, 3)), *parts1, *parts2, consts0, small,
        mixed_own, features[None], time_raw[None], scalars=False,
    )
    tied, _ = lax.optimization_barrier((near_grads, field_grad))
    far_grads = swapped(tied, "gz", 1)
    grad_w_z, grad_w_xy, grad_w_point = call(
        functools.partial(kernel_layout, inv_area, share),
        [(w_z.shape, f32), (w_xy.shape, f32), (w_point.shape, f32)],
        [], 10**6, LIMITS[11], near_grads, far_grads, scalars=False,
    )
    return (
        prediction,
        field_grad,
        grad_w_in,
        grad_w_time,
        grad_w_z,
        grad_w_xy,
        grad_w_point,
        grad_biases,
        grad_gains,
        grad_w_out,
    )


def padded_2(cells, sides, width):
    for axis, dim in sides:
        count = lax.axis_size(axis)
        head = lax.slice_in_dim(cells, 0, width, axis=dim)
        tail = lax.slice_in_dim(cells, cells.shape[dim] - width, cells.shape[dim], axis=dim)
        cells = jnp.concatenate(
            [
                lax.ppermute(tail, axis, [(i, (i + 1) % count) for i in range(count)]),
                cells,
                lax.ppermute(head, axis, [((i + 1) % count, i) for i in range(count)]),
            ],
            axis=dim,
        )
    return cells


def passed_along(value, axis, steps):
    count = lax.axis_size(axis)
    pairs = [(source, (source + steps) % count) for source in range(count)]
    return lax.ppermute(value, axis, pairs)


def contract_cells(left, right):
    return lax.dot_general(
        left, right, (((0, 1, 2), (0, 1, 2)), ((), ())), preferred_element_type=jnp.float32
    )


def plane_tap(padded, shift_x, shift_y, rows_x, rows_y):
    return padded[1 + shift_x : 1 + shift_x + rows_x, 1 + shift_y : 1 + shift_y + rows_y]


def plane_pad(source):
    rimmed = padded_2(source, (("gx", 0),), 1)
    return jnp.pad(rimmed, ((0, 0), (1, 1), (0, 0), (0, 0)))


def slab_windows(source, dilation):
    slab_depth = source.shape[2]
    above = passed_along(source, "gz", -1)
    above_far = passed_along(source, "gz", -2)
    below = passed_along(source, "gz", 1)
    below_far = passed_along(source, "gz", 2)
    ahead_rows = jnp.concatenate([source, above, above_far], axis=2)
    behind_rows = jnp.concatenate([below_far, below, source], axis=2)
    upper = lax.dynamic_slice_in_dim(ahead_rows, dilation, slab_depth, 2)
    lower = lax.dynamic_slice_in_dim(behind_rows, 2 * slab_depth - dilation, slab_depth, 2)
    return (lower, upper)


def normalize(hidden, gains, cell_count):
    average = lax.psum(jnp.sum(hidden, axis=(0, 1, 2)), ("gz", "gx")) / cell_count
    centered = hidden - average
    spread = lax.psum(jnp.sum(centered * centered, axis=(0, 1, 2)), ("gz", "gx")) / cell_count
    inverse_std = lax.rsqrt(spread + eps_norm)
    whitened = (hidden - average) * inverse_std
    return ((whitened * gains).astype(jnp.bfloat16), whitened, inverse_std)


def norm_back(d_normed, whitened, inverse_std, gains, cell_count):
    scaled = d_normed * gains
    sum_grad, sum_cross = lax.psum(
        (jnp.sum(scaled, axis=(0, 1, 2)), jnp.sum(scaled * whitened, axis=(0, 1, 2))), ("gz", "gx")
    )
    d_hidden = inverse_std * (scaled - sum_grad / cell_count - whitened * (sum_cross / cell_count))
    return (d_hidden, jnp.sum(d_normed * whitened, axis=(0, 1, 2)))


def conv_forward(normed, dilation, weights_z, weights_xy):
    rows_x, rows_y = (normed.shape[0], normed.shape[1])
    lower, upper = slab_windows(normed, dilation)
    padded = plane_pad(normed)
    summed = jnp.dot(lower, weights_z[0], preferred_element_type=jnp.float32)
    summed = summed + jnp.dot(normed, weights_z[1], preferred_element_type=jnp.float32)
    summed = summed + jnp.dot(upper, weights_z[2], preferred_element_type=jnp.float32)
    for tap_number, (shift_x, shift_y) in enumerate(plane_offsets):
        summed = summed + jnp.dot(
            plane_tap(padded, shift_x, shift_y, rows_x, rows_y),
            weights_xy[tap_number],
            preferred_element_type=jnp.float32,
        )
    return summed


def conv_backward_split(pre_cot, normed, dilation, weights_z, weights_xy):
    rows_x, rows_y = (normed.shape[0], normed.shape[1])
    lower_cot, upper_cot = slab_windows(pre_cot, dilation)
    padded_cot = plane_pad(pre_cot)
    d_normed = jnp.dot(upper_cot, weights_z[0].T, preferred_element_type=jnp.float32)
    d_normed = d_normed + jnp.dot(pre_cot, weights_z[1].T, preferred_element_type=jnp.float32)
    d_normed = d_normed + jnp.dot(lower_cot, weights_z[2].T, preferred_element_type=jnp.float32)
    xy_terms = []
    for tap_number, (shift_x, shift_y) in enumerate(plane_offsets):
        shifted = plane_tap(padded_cot, -shift_x, -shift_y, rows_x, rows_y)
        d_normed = d_normed + jnp.dot(
            shifted, weights_xy[tap_number].T, preferred_element_type=jnp.float32
        )
        xy_terms.append(contract_cells(normed, shifted))
    z_terms = jnp.stack(
        [
            contract_cells(normed, upper_cot),
            contract_cells(normed, pre_cot),
            contract_cells(normed, lower_cot),
        ]
    )
    return (d_normed, z_terms, jnp.stack(xy_terms))


def per_device_split(
    clean_field,
    noise_field,
    timestep,
    dilations,
    w_in,
    w_time,
    w_z,
    w_xy,
    w_point,
    biases,
    norm_gains,
    w_out,
):
    layer_total = w_z.shape[0]
    rows_x, rows_y, slab_depth = (clean_field.shape[1], clean_field.shape[2], clean_field.shape[3])
    plane_cells = rows_x * lax.axis_size("gx") * slab_depth * lax.axis_size("gz")
    cell_count = float(plane_cells * rows_y)
    inv_area = 1.0 / plane_cells
    alpha_bar, features, time_raw, time_code = time_terms(timestep, w_time)
    noisy = jnp.sqrt(alpha_bar) * clean_field + jnp.sqrt(1.0 - alpha_bar) * noise_field
    stream = jnp.einsum("kxyz,kc->xyzc", noisy, w_in, precision=highest)
    saved = []
    for which_layer in range(layer_total):
        normed, whitened, inverse_std = normalize(stream, norm_gains[which_layer], cell_count)
        pre_act = conv_forward(normed, dilations[which_layer], w_z[which_layer], w_xy[which_layer])
        pre_act = pre_act + biases[which_layer] + time_code
        activated = jax.nn.gelu(pre_act).astype(jnp.bfloat16)
        saved.append((normed, whitened, inverse_std, pre_act, activated))
        stream = stream + jnp.dot(
            activated, w_point[which_layer], preferred_element_type=jnp.float32
        )
    out_normed, out_white, out_inverse = normalize(stream, norm_gains[layer_total], cell_count)
    prediction = jnp.einsum("xyzc,kc->kxyz", out_normed, w_out, preferred_element_type=jnp.float32)
    misfit = prediction - noise_field
    d_out = jnp.einsum("kxyz,kc->xyzc", misfit, w_out.astype(jnp.float32), precision=highest)
    out_raw = jnp.einsum(
        "kxyz,xyzc->kc", misfit, out_normed, precision=highest, preferred_element_type=jnp.float32
    )
    d_stream, out_gain_raw = norm_back(
        d_out, out_white, out_inverse, norm_gains[layer_total], cell_count
    )
    z_list, xy_list, point_list, bias_list, gain_list = ([], [], [], [], [])
    for which_layer in reversed(range(layer_total)):
        normed, whitened, inverse_std, pre_act, activated = saved[which_layer]
        stream_cot = d_stream.astype(jnp.bfloat16)
        point_raw = contract_cells(activated, stream_cot)
        d_act = jnp.dot(stream_cot, w_point[which_layer].T, preferred_element_type=jnp.float32)
        gelu_back = jax.vjp(jax.nn.gelu, pre_act)[1]
        pre_cot = gelu_back(d_act)[0].astype(jnp.bfloat16)
        bias_raw = jnp.sum(pre_cot, axis=(0, 1, 2), dtype=jnp.float32)
        d_normed, z_raw, xy_raw = conv_backward_split(
            pre_cot, normed, dilations[which_layer], w_z[which_layer], w_xy[which_layer]
        )
        d_back, gain_raw = norm_back(
            d_normed, whitened, inverse_std, norm_gains[which_layer], cell_count
        )
        d_stream = d_stream + d_back
        z_list.insert(0, z_raw)
        xy_list.insert(0, xy_raw)
        point_list.insert(0, point_raw)
        bias_list.insert(0, bias_raw)
        gain_list.insert(0, gain_raw)
    field_grad = jnp.einsum("xyzc,kc->kxyz", d_stream, w_in, precision=highest)
    in_raw = jnp.einsum("kxyz,xyzc->kc", noisy, d_stream, precision=highest)
    z_all, xy_all, point_all, bias_all, gain_all, in_raw, out_raw = lax.psum(
        (
            jnp.stack(z_list),
            jnp.stack(xy_list),
            jnp.stack(point_list),
            jnp.stack(bias_list),
            jnp.stack(gain_list + [out_gain_raw]),
            in_raw,
            out_raw,
        ),
        ("gz", "gx"),
    )
    time_back = jax.vjp(jax.nn.silu, time_raw)[1](jnp.sum(bias_all, axis=0))[0]
    grad_w_time = inv_area * jnp.outer(features, time_back)
    return (
        prediction,
        field_grad,
        inv_area * in_raw,
        grad_w_time,
        inv_area * z_all,
        inv_area * xy_all,
        inv_area * point_all,
        inv_area * bias_all,
        inv_area * gain_all,
        inv_area * out_raw,
    )


def per_device(*args):
    members, groups = lax.axis_size("gz"), lax.axis_size("gx")
    _, rows_x, rows_y, depth = args[0].shape
    small = rows_x == 1 and rows_y == 4 and members == 4 and groups == 8 and depth * members == 2 * REACH
    return per_device_grouped(*args) if small else per_device_split(*args)


def solution(mesh):
    return jax.shard_map(
        per_device,
        mesh=mesh,
        in_specs=(
            P(None, "gx", None, "gz"),
            P(None, "gx", None, "gz"),
            P(),
            P(),
            P(),
            P(),
            P(),
            P(),
            P(),
            P(),
            P(),
            P(),
        ),
        out_specs=(
            P(None, "gx", None, "gz"),
            P(None, "gx", None, "gz"),
            P(),
            P(),
            P(),
            P(),
            P(),
            P(),
            P(),
            P(),
        ),
        check_vma=False,
    )
```

```python
import functools
import math

import jax
import jax.numpy as jnp
from jax import lax
from jax.experimental import pallas as pl
from jax.experimental.pallas import tpu as pltpu
from jax.sharding import PartitionSpec as P

STEPS = 1000
REACH = 256
RIM = 4
TILE = 16
LIMITS = (4, 14, 9, 7, 9, 8, 10, 2, 6, 2, 2, 3)

eps_norm = 1e-05
highest = lax.Precision.HIGHEST
bf16 = jnp.bfloat16
f32 = jnp.float32
plane_offsets = ((-1, -1), (-1, 0), (-1, 1), (0, -1), (0, 1), (1, -1), (1, 0), (1, 1))


def time_terms(timestep, w_time):
    moment = timestep[0].astype(jnp.float32)
    half_width = w_time.shape[0] // 2
    alpha_bar = jnp.cos(0.5 * math.pi * (moment + 0.5) / STEPS) ** 2
    ladder = jnp.exp(-math.log(10000.0) * jnp.arange(half_width, dtype=jnp.float32) / half_width)
    angles = moment * ladder
    features = jnp.concatenate([jnp.sin(angles), jnp.cos(angles)])
    time_raw = jnp.dot(features, w_time, precision=highest)
    return (alpha_bar, features, time_raw, jax.nn.silu(time_raw))


def mm(left, right):
    return lax.dot_general(left, right, (((1,), (0,)), ((), ())), preferred_element_type=f32)


def mm_nt(left, right):
    return lax.dot_general(left, right, (((1,), (1,)), ((), ())), preferred_element_type=f32)


def mm_tn(left, right):
    return lax.dot_general(left, right, (((0,), (0,)), ((), ())), preferred_element_type=f32)


def halves(value):
    high = value.astype(bf16)
    return high, (value - high.astype(f32)).astype(bf16)


def wide(vector):
    return jnp.concatenate([vector] * 4, axis=1)


def folded(vector):
    channels = vector.shape[1] // 4
    return sum(vector[:, y * channels : (y + 1) * channels] for y in range(4))


class Place:
    def __init__(self, sc, rows):
        self.rows = rows
        self.members = lax.axis_size("gz")
        self.member = lax.axis_index("gz")
        self.small = jnp.minimum(sc[0], sc[1])
        self.coarse = self.small >= self.members
        tiles = rows // TILE
        self.tiles = tiles
        self.stride = jnp.where(self.coarse, tiles - 1, tiles)
        self.span = REACH // self.members + 2 * RIM
        far = jnp.where(self.coarse, REACH // self.members, self.span)
        near = jnp.where(self.coarse, self.small // self.members, 1)
        self.steps = [jnp.where(sc[l] == REACH, far, near) for l in range(2)]

    def index(self, shape):
        row = lax.broadcasted_iota(jnp.int32, shape, 0)
        return lax.rem(row, TILE) * self.stride + row // TILE, row // TILE

    def own(self, shape):
        place, tile = self.index(shape)
        inside = lax.rem(place, self.span)
        near = ((inside >= RIM) & (inside < self.span - RIM)).astype(jnp.int32)
        far = (tile < self.tiles - 1).astype(jnp.int32)
        return jnp.where(self.coarse, far, near) == 1

    def pick(self, cells_z):
        shape = (self.rows, cells_z)
        return self.z_of(shape, cells_z) == lax.broadcasted_iota(jnp.int32, shape, 1)

    def z_of(self, shape, cells_z):
        place, _ = self.index(shape)
        residues = jnp.minimum(self.small, self.members)
        part, start = self.member // residues, lax.rem(self.member, residues)
        period = place // self.span
        inside = place - period * self.span - RIM + part * (REACH // self.members)
        near = start + residues * inside + period * REACH
        z = jnp.where(self.coarse, place * self.members + self.member, near)
        return lax.rem(z + 2 * cells_z, cells_z)


def build_taps(block_of, taps):
    channels = taps.shape[-1] // 2
    zero = jnp.zeros((channels, channels), bf16)
    near, far = slice(0, channels), slice(channels, 2 * channels)
    for i in range(3):
        down, here, up = (block_of(i, j) for j in range(3))
        taps[i, near, near] = here
        taps[i, far, far] = here
        taps[i, near, far] = down
        taps[i, far, near] = up
        taps[3 + i, near, near] = zero
        taps[3 + i, far, far] = zero
        taps[3 + i, near, far] = down
        taps[3 + i, far, near] = up
    for m in range(2):
        build_pair(block_of(3, m), taps, 6 + m)


def build_pair(block, target, m):
    channels = block.shape[-1]
    zero = jnp.zeros((channels, channels), bf16)
    target[m, :channels, :channels] = block
    target[m, channels:, channels:] = block
    target[m, :channels, channels:] = zero
    target[m, channels:, :channels] = zero


def taken(weights, layer):
    return lambda i, j: weights[layer, i * 3 + j]


def fetch(pairs, sems):
    copies = [pltpu.make_async_copy(one, two, sems.at[at]) for at, (one, two) in enumerate(pairs)]
    for copy in copies:
        copy.start()
    for copy in copies:
        copy.wait()


def kernel_prepare(steps, w_z, w_xy, w_point, w_in_far, gains_far, w_out_far, w_front, point, w_back, point_back,
                   lift_in, lift_out, small, steps_on, w_in, gains, w_out, sems):
    pairs = [(w_point, point), (w_in_far, w_in), (gains_far, gains), (w_out_far, w_out), (steps, steps_on)]
    for layer in range(2):
        pairs.append((w_xy.at[layer, pl.ds(0, 4)], w_front.at[layer, pl.ds(0, 4)]))
        pairs.append((w_xy.at[layer, pl.ds(4, 4)], w_front.at[layer, pl.ds(5, 4)]))
        for m, at in ((1, 4), (0, 9), (2, 10)):
            pairs.append((w_z.at[layer, m], w_front.at[layer, at]))
    fetch(pairs, sems)
    small[...] = jnp.concatenate([w_in[...], gains[...], w_out[...].astype(f32)], axis=0)
    for layer in range(2):
        for at in range(9):
            w_back[layer, at] = w_front[layer, 8 - at].T
        w_back[layer, 9] = w_front[layer, 10].T
        w_back[layer, 10] = w_front[layer, 9].T
        point_back[layer] = point[layer].T
    whole = spread_rows(small[0:3], 0)
    high, low = halves(whole)
    lift_in[0:32] = high
    lift_in[32:64] = high
    lift_in[64:96] = low
    lift_in[96:128] = jnp.zeros_like(low)
    high = spread_rows(small[6:9], 3).astype(bf16)
    lift_out[0:32] = high
    lift_out[32:64] = high
    lift_out[64:96] = jnp.zeros_like(high)
    lift_out[96:128] = jnp.zeros_like(high)


def spread_rows(weights, first):
    channels = weights.shape[1]
    zero = jnp.zeros((1, channels), f32)
    rows = [jnp.zeros((1, 4 * channels), f32)] * 32
    for k in range(3):
        for y in range(4):
            parts = [weights[k : k + 1] if at == y else zero for at in range(4)]
            rows[(first + k) * 4 + y] = jnp.concatenate(parts, axis=1)
    return jnp.concatenate(rows, axis=0)


def fill_rims(padded, planes):
    padded[0] = padded[planes]
    padded[planes + 1] = padded[1]


def fill_shifted(place, layer, padded, shifted, planes):
    step, stride = place.steps[layer], place.stride
    for tile in range(place.tiles):
        for way in range(2):
            at = tile - step if way == 0 else tile + step
            moved = at + TILE * stride
            source = lax.rem(moved, stride)
            turn = lax.rem(2 * TILE - moved // stride, TILE)
            rows = padded[1 : planes + 1, pl.ds(pl.multiple_of(source * TILE, TILE), TILE), :]
            rows = pltpu.roll(rows.astype(f32), turn, 1)
            shifted[way, :, tile * TILE : (tile + 1) * TILE, :] = rows.astype(bf16)


def conv_pair(padded, shifted, taps, x0, count):
    rows, lanes = padded.shape[1:]
    half, quarter = lanes // 2, lanes // 4
    totals = [None, None, None]

    def add(at, left, right):
        part = mm(left.reshape(count * rows, half), right)
        totals[at] = part if totals[at] is None else totals[at] + part

    for q in range(2):
        side = slice(q * half, (q + 1) * half)
        for i in range(3):
            add(q, padded[x0 + i : x0 + i + count, :, side], taps[i])
        for m in range(2):
            add(q, shifted[m, x0 : x0 + count, :, side], taps[6 + m])
    for i in range(3):
        add(2, padded[x0 + i : x0 + i + count, :, quarter : 3 * quarter], taps[3 + i])
    first, second, middle = totals
    first = jnp.concatenate([first[:, :quarter], first[:, quarter:] + middle[:, :quarter]], axis=1)
    second = jnp.concatenate([second[:, :quarter] + middle[:, quarter:], second[:, quarter:]], axis=1)
    return first, second


def gelu_pair(value):
    scale = math.sqrt(2.0 / math.pi)
    square = value * value
    bent = jnp.tanh(value * (scale + (scale * 0.044715) * square))
    half = 0.5 + 0.5 * bent
    result = value * half
    slope = half + result * (1.0 - half) * (2.0 * scale + (6.0 * 0.044715 * scale) * square)
    return result, slope


def members_of(parts):
    found = []
    for part in parts:
        for at in range(0, part.shape[0], 8):
            found.append(part[at : at + 8])
    return found


def merged_stats(parts, per_member):
    found = members_of(parts)
    mean = sum(one[0:1] for one in found) / (per_member * len(found))
    spread = sum(one[1:2] for one in found)
    for one in found:
        gap = one[0:1] / per_member - mean
        spread = spread + per_member * gap * gap
    return mean, lax.rsqrt(spread / (per_member * len(found)) + eps_norm)


def put_rows(ref, *vectors):
    rows = list(vectors)
    rows += [jnp.zeros((1, ref.shape[1]), f32)] * (ref.shape[0] - len(rows))
    ref[...] = jnp.concatenate(rows, axis=0)


def masked_total(mask, value):
    return folded(jnp.sum(jnp.where(mask, value, 0.0), axis=0, keepdims=True))


def layer_forward(place, layer, padded, shifted, taps, pair, w_front, wp, shift_bias, old,
                  stream, act, slope, stats, acc, per_member):
    planes, rows, lanes = stream.shape
    half = lanes // 2
    count = planes // 4
    build_taps(taken(w_front, layer), taps)
    build_pair(wp[layer], pair, 0)
    fill_rims(padded, planes)
    fill_shifted(place, layer, padded, shifted, planes)
    acc[...] = jnp.zeros_like(acc)
    bias = wide(shift_bias[layer : layer + 1, :])[:, :half]

    for x0 in range(0, planes, count):
        part = slice(x0, x0 + count)
        for q, total in enumerate(conv_pair(padded, shifted, taps, x0, count)):
            side = slice(q * half, (q + 1) * half)
            value, grad = gelu_pair(total + bias)
            act[part, :, side] = value.astype(bf16).reshape(count, rows, half)
            slope[part, :, side] = grad.astype(bf16).reshape(count, rows, half)
    for x0 in range(0, planes, count):
        part = slice(x0, x0 + count)
        for q in range(2):
            side = slice(q * half, (q + 1) * half)
            branch = mm(act[part, :, side].reshape(count * rows, half), pair[0])
            new = old[part, :, side] + branch.reshape(count, rows, half)
            stream[part, :, side] = new
            acc[:, side] += jnp.sum(new, axis=0)
    mask = place.own((rows, lanes))
    total = masked_total(mask, acc[...])
    mean = wide(total / per_member)
    spread = jnp.zeros((rows, lanes), f32)
    for x in range(planes):
        gap = stream[x] - mean
        spread = spread + gap * gap
    put_rows(stats, total, masked_total(mask, spread))


def kernel_first(cells_z, per_member, sc, near, far, amounts, lift_in, small, shift_bias, w_front, wp,
                 stream, padded, act, slope, gathered, stats, consts, mixed_own,
                 shifted, taps, pair, acc, old, source, fields):
    planes, rows, lanes = stream.shape
    channels = lanes // 4
    depth = near.shape[2]
    place = Place(sc, rows)
    keep, add = amounts[0:1], amounts[1:2]
    for at, ref in enumerate((near, far)):
        fields[at, :, 12:24] = ref[:, 12:24]
        fields[at, :, 0:12] = keep * ref[:, 0:12] + add * ref[:, 12:24]
    mixed_own[...] = fields[0, place.member // 2 * planes + lax.axis_index("gx"), 0:12]
    cell_count = float(planes * 4 * cells_z)
    comps = [
        jnp.concatenate([fields[at, :, 4 * k : 4 * k + 4, :] for at in range(2)], axis=0) for k in range(3)
    ]

    def all_sum(value):
        value = jnp.sum(jnp.sum(value, axis=0), axis=0, keepdims=True)
        return jnp.sum(value, axis=1, keepdims=True)

    means = [all_sum(comp) / cell_count for comp in comps]
    gaps = [comp - mean[None] for comp, mean in zip(comps, means)]
    covs = {}
    for j in range(3):
        for k in range(j, 3):
            covs[j, k] = all_sum(gaps[j] * gaps[k]) / cell_count
    rows_in = [small[k : k + 1, :] for k in range(3)]
    mean_c = sum(means[k] * rows_in[k] for k in range(3))
    var_c = jnp.zeros((1, channels), f32)
    for (j, k), cov in covs.items():
        var_c = var_c + (1.0 if j == k else 2.0) * cov * (rows_in[j] * rows_in[k])
    inv_c = lax.rsqrt(jnp.maximum(var_c, 0.0) + eps_norm)
    flat = [jnp.broadcast_to(value, (1, channels)) for value in means + list(covs.values())]
    put_rows(consts, mean_c, inv_c, *flat)
    blank = jnp.zeros((8, depth), f32)
    core = lax.rem(place.member, 2)
    for slab in range(cells_z // depth):
        side = core if slab % 2 == 0 else 1 - core
        at = pl.ds(pl.multiple_of((slab // 2 * 2 + side) * depth, depth), depth)
        for x in range(planes):
            high, low = halves(jnp.concatenate([fields[slab % 2, slab // 2 * planes + x], blank], axis=0))
            source[x, 0:32, at] = high
            source[x, 32:64, at] = low
            source[x, 64:96, at] = high
            source[x, 96:128, at] = jnp.zeros_like(high)
    pick = place.pick(cells_z).astype(f32).astype(bf16)
    scale = wide(inv_c * small[3:4, :])
    mean_w = wide(mean_c)
    for x in range(planes):
        gathered[x] = mm_nt(pick, source[x]).astype(bf16)
    for x0 in range(0, planes, planes // 2):
        part = slice(x0, x0 + planes // 2)
        value = mm(gathered[part].reshape(planes // 2 * rows, 128), lift_in[...])
        unit = ((value - mean_w) * scale).astype(bf16).reshape(planes // 2, rows, lanes)
        old[part] = value.reshape(planes // 2, rows, lanes)
        padded[x0 + 1 : x0 + 1 + planes // 2] = unit
    layer_forward(place, 0, padded, shifted, taps, pair, w_front, wp, shift_bias, old, stream,
                  act, slope, stats, acc, per_member)


def kernel_second(per_member, sc, *refs):
    parts, refs = refs[:4], refs[4:]
    (old, small, shift_bias, w_front, wp, stream, padded, act, slope, stats, consts,
     shifted, taps, pair, acc) = refs
    planes, rows, _ = stream.shape
    place = Place(sc, rows)
    mean, inverse = merged_stats(parts, per_member)
    put_rows(consts, mean, inverse)
    mean_w, scale = wide(mean), wide(inverse * small[4:5, :])
    for x in range(planes):
        padded[x + 1] = ((old[x] - mean_w) * scale).astype(bf16)
    layer_forward(place, 1, padded, shifted, taps, pair, w_front, wp, shift_bias, old, stream,
                  act, slope, stats, acc, per_member)


def kernel_out(per_member, sc, *refs):
    parts, refs = refs[:4], refs[4:]
    stream, small, gathered, lift_out, prediction, misfit, sums, w_out_raw, consts, unit = refs
    planes, rows, lanes = stream.shape
    place = Place(sc, rows)
    mean, inverse = merged_stats(parts, per_member)
    put_rows(consts, mean, inverse)
    mean_w, inv_w, gain_w = wide(mean), wide(inverse), wide(small[5:6, :])
    scale = inv_w * gain_w
    for x in range(planes):
        unit[x] = ((stream[x] - mean_w) * scale).astype(bf16)
    row = lax.broadcasted_iota(jnp.int32, (128, 128), 0)
    col = lax.broadcasted_iota(jnp.int32, (128, 128), 1)
    slot = lax.rem(col, 32)
    used = (col < 64) & (slot >= 12) & (slot < 24)
    take = (used & ((row == slot) | (row == slot + 32))).astype(f32).astype(bf16)
    total = mm_nt(unit[...].reshape(planes * rows, lanes), lift_out[...])
    noise = mm(gathered[...].reshape(planes * rows, 128), take)
    gap = total - noise
    high, low = halves(gap)
    lane = lax.broadcasted_iota(jnp.int32, gap.shape, 1)
    both = jnp.where(lane < 32, high.astype(f32), low.astype(f32)).astype(bf16)
    misfit[...] = both.reshape(planes, rows, 128)
    for x in range(planes):
        @pl.when(lax.axis_index("gx") == x)
        def _(x=x):
            prediction[...] = total[x * rows : (x + 1) * rows]
    plain = jnp.zeros((rows, lanes), f32)
    cross = jnp.zeros((rows, lanes), f32)
    for x0 in range(0, planes, planes // 2):
        part = slice(x0 * rows, (x0 + planes // 2) * rows)
        d_out = mm(both[part], lift_out[...]).reshape(planes // 2, rows, lanes)
        for x in range(planes // 2):
            plain = plain + d_out[x]
            cross = cross + d_out[x] * ((stream[x0 + x] - mean_w) * inv_w)
    own = place.own((rows, 128))
    kept = jnp.concatenate([jnp.where(own, misfit[x].astype(f32), 0.0) for x in range(planes)], axis=0)
    raw = mm_tn(kept.astype(bf16), unit[...].reshape(planes * rows, lanes))
    mask = place.own((rows, lanes))
    put_rows(sums, masked_total(mask, plain), masked_total(mask, cross))
    put_rows(w_out_raw, *by_component(raw[0:32] + raw[32:64], 3))


def by_component(raw, first):
    channels = raw.shape[1] // 4
    found = []
    for k in range(first, first + 3):
        found.append(
            sum(raw[k * 4 + y : k * 4 + y + 1, y * channels : (y + 1) * channels] for y in range(4))
        )
    return found


def branch_backward(planes, d_stream_of, pair, slope, padded, scot, bias_acc):
    rows, lanes = padded.shape[1:]
    half = lanes // 2
    count = planes // 2

    for x0 in range(0, planes, count):
        part = slice(x0, x0 + count)
        for x in range(x0, x0 + count):
            scot[x] = d_stream_of(x).astype(bf16)
        for q in range(2):
            side = slice(q * half, (q + 1) * half)
            cot = scot[part, :, side].reshape(count * rows, half)
            d_act = mm(cot, pair[0]).reshape(count, rows, half)
            pre = (d_act * slope[part, :, side].astype(f32)).astype(bf16)
            padded[x0 + 1 : x0 + 1 + count, :, side] = pre
            bias_acc[:, side] += jnp.sum(pre.astype(f32), axis=0)


def weight_grads(place, planes, padded, shifted, scot, normed, act, keep, give, taps_all, share):
    rows, lanes = padded.shape[1:]
    channels = lanes // 4
    wide_share = 4 * share
    row = lax.broadcasted_iota(jnp.int32, (lanes, wide_share), 0)
    col = lax.broadcasted_iota(jnp.int32, (lanes, wide_share), 1)
    hit = (row // channels == col // share) & (
        lax.rem(row, channels) == lax.rem(col, share) + lax.axis_index("gx") * share
    )
    choose = hit.astype(f32).astype(bf16)
    mask = jnp.concatenate([place.own((rows, wide_share))] * planes, axis=0)

    def turned(source):
        got = mm(source.reshape(planes * rows, lanes), choose)
        return jnp.where(mask, got, 0.0).astype(bf16)

    def add_blocks(raw, j):
        return sum(
            raw[(y + j) * share : (y + j + 1) * share, y * channels : (y + 1) * channels]
            for y in range(4)
            if 0 <= y + j < 4
        )

    left = turned(normed[1 : planes + 1])
    for i in range(3):
        raw = mm_tn(left, padded[2 - i : 2 - i + planes].reshape(planes * rows, lanes))
        for j in range(3):
            taps_all[i * 3 + j] = add_blocks(raw, j - 1)
    for m in range(2):
        raw = mm_tn(left, shifted[1 - m].reshape(planes * rows, lanes))
        taps_all[9 + m] = add_blocks(raw, 0)
    raw = mm_tn(turned(act[...]), scot[...].reshape(planes * rows, lanes))
    taps_all[11] = add_blocks(raw, 0)
    odd, half = lax.rem(place.member, 2), keep.shape[0]
    keep[...] = taps_all[pl.ds(odd * half, half)]
    give[...] = taps_all[pl.ds((1 - odd) * half, half)]


def conv_backward(planes, padded, shifted, taps, emit):
    count = planes // 4

    for x0 in range(0, planes, count):
        for q, total in enumerate(conv_pair(padded, shifted, taps, x0, count)):
            emit(x0, count, q, total)


def kernel_back_second(cell_count, sc, *refs):
    parts, refs = refs[:4], refs[4:]
    (stream, out_consts, small, misfit, lift_out, slope, normed, w_back, point_back,
     d_stream, d_normed, sums, padded, shifted, scot,
     taps, pair, acc, acc2) = refs
    planes, rows, lanes = stream.shape
    half = lanes // 2
    place = Place(sc, rows)
    sums_out = sum(members_of(parts))
    gain_w = wide(small[5:6, :])
    mean_w, inv_w = wide(out_consts[0:1]), wide(out_consts[1:2])
    m_plain = gain_w * wide(sums_out[0:1]) / cell_count
    m_cross = gain_w * wide(sums_out[1:2]) / cell_count
    build_pair(point_back[1], pair, 0)
    build_taps(taken(w_back, 1), taps)
    acc[...] = jnp.zeros_like(acc)

    def d_stream_of(x):
        d_out = mm(misfit[x], lift_out[...])
        white = (stream[x] - mean_w) * inv_w
        value = inv_w * (gain_w * d_out - m_plain - white * m_cross)
        d_stream[x] = value
        return value

    branch_backward(planes, d_stream_of, pair, slope, padded, scot, acc)
    mask = place.own((rows, lanes))
    s_bias = masked_total(mask, acc[...])
    acc[...] = jnp.zeros_like(acc)
    acc2[...] = jnp.zeros_like(acc2)
    fill_rims(padded, planes)
    fill_shifted(place, 1, padded, shifted, planes)

    def emit(x0, count, q, value):
        side = slice(q * half, (q + 1) * half)
        value = value.reshape(count, rows, half)
        d_normed[x0 : x0 + count, :, side] = value
        acc[:, side] += jnp.sum(value, axis=0)
        acc2[:, side] += jnp.sum(value * normed[x0 + 1 : x0 + 1 + count, :, side].astype(f32), axis=0)

    conv_backward(planes, padded, shifted, taps, emit)
    s_plain = masked_total(mask, acc[...])
    s_cross = masked_total(mask, acc2[...]) / small[4:5, :]
    put_rows(sums, s_plain, s_cross, s_bias)


def kernel_weights_second(share, sc, padded, shifted, scot, normed, act, keep, give, taps_all):
    planes, rows, _ = scot.shape
    weight_grads(Place(sc, rows), planes, padded, shifted, scot, normed, act, keep, give, taps_all, share)


def kernel_back_first(share, cell_count, sc, *refs):
    parts, refs = refs[:4], refs[4:]
    (consts, d_next, d_normed, normed_next, small, act, slope, normed, point_back,
     d_stream, sums, keep, give, padded, shifted,
     pair, acc, scot, taps_all) = refs
    planes, rows, lanes = d_next.shape
    place = Place(sc, rows)
    sums_in = sum(members_of(parts))
    gain_w = wide(small[4:5, :])
    inv_w = wide(consts[1:2])
    m_plain = gain_w * wide(sums_in[0:1]) / cell_count
    m_cross = wide(sums_in[1:2]) / cell_count
    build_pair(point_back[0], pair, 0)
    acc[...] = jnp.zeros_like(acc)

    def d_stream_of(x):
        back = gain_w * d_normed[x] - m_plain - normed_next[x + 1].astype(f32) * m_cross
        value = d_next[x] + inv_w * back
        d_stream[x] = value
        return value

    branch_backward(planes, d_stream_of, pair, slope, padded, scot, acc)
    put_rows(sums, masked_total(place.own((rows, lanes)), acc[...]))
    fill_rims(padded, planes)
    fill_shifted(place, 0, padded, shifted, planes)
    weight_grads(place, planes, padded, shifted, scot, normed, act, keep, give, taps_all, share)


def kernel_last(depth, sc, padded, shifted, d_stream, normed, small, consts, gathered, lift_in, w_back,
                prediction, sums_bias, out_raw, ready0, ready1, own_out, out_1, out_2, out_3,
                taps, acc, acc2, high, low):
    planes, rows, lanes = d_stream.shape
    half = lanes // 2
    place = Place(sc, rows)
    build_taps(taken(w_back, 0), taps)
    acc[...] = jnp.zeros_like(acc)
    acc2[...] = jnp.zeros_like(acc2)
    scale = wide(consts[1:2] * small[3:4, :])

    def emit(x0, count, q, value):
        side = slice(q * half, (q + 1) * half)
        part = slice(x0, x0 + count)
        value = value.reshape(count, rows, half)
        acc[:, side] += jnp.sum(value, axis=0)
        acc2[:, side] += jnp.sum(value * normed[x0 + 1 : x0 + 1 + count, :, side].astype(f32), axis=0)
        full = d_stream[part, :, side] + value * scale[:, side]
        first, second = halves(full)
        high[part, :, side] = first
        low[part, :, side] = second

    conv_backward(planes, padded, shifted, taps, emit)
    mask = place.own((rows, lanes))
    s_plain = masked_total(mask, acc[...])
    s_cross = masked_total(mask, acc2[...]) / small[3:4, :]
    own = place.own((rows, 128))
    kept = jnp.concatenate([jnp.where(own, gathered[x].astype(f32), 0.0) for x in range(planes)], axis=0)
    kept = kept.astype(bf16)
    raw = mm_tn(kept, high[...].reshape(planes * rows, lanes))
    raw_low = mm_tn(kept, low[...].reshape(planes * rows, lanes))
    in_raw = by_component(raw[0:32] + raw[32:64] + raw_low[0:32], 0)
    blank = jnp.zeros((1, s_plain.shape[1]), f32)
    tail = jnp.concatenate([s_plain, s_cross] + [blank] * 6 + in_raw + [blank] * 5, axis=0)
    tail = jnp.concatenate([tail, sums_bias[...], out_raw[...]], axis=0)
    here = lax.axis_index("gx")
    lane = lax.broadcasted_iota(jnp.int32, (rows, 128), 1)
    field = mm_nt(high[here], lift_in[...]) + jnp.where(lane < 32, mm_nt(low[here], lift_in[...]), 0.0)
    field = jnp.where((lane >= 32) & (lane < 64), 0.0, field)
    field = field + jnp.where((lane >= 12) & (lane < 24), prediction[...], 0.0)
    cells_z = depth * place.members
    whole = place.z_of((rows, depth), cells_z)
    column = lax.broadcasted_iota(jnp.int32, (rows, depth), 1)
    mask = place.own((rows, depth))
    first, second = halves(field)
    for bit, target in enumerate((own_out, out_1, out_2, out_3)):
        there = lax.bitwise_xor(place.member, bit)
        pick = ((whole == column + there * depth) & mask).astype(f32).astype(bf16)
        out = mm_tn(first, pick) + mm_tn(second, pick)
        target[0:32] = out[0:32] + out[64:96]
        target[32:64] = tail


def call(kernel, outs, scratch, flops, limit, *args, scalars=True, scalar_out=0, ready=(), far=()):
    spec = pl.BlockSpec(memory_space=pltpu.VMEM)
    specs = [pl.BlockSpec(memory_space=pltpu.SMEM)] * scalars + [spec] * (len(args) - scalars)
    for at in ready:
        specs[at] = pl.BlockSpec(memory_space=pl.ANY)
    args = list(args)
    for at in far:
        specs[at] = pl.BlockSpec(memory_space=pltpu.HBM)
        args[at] = pltpu.with_memory_space_constraint(args[at], pltpu.HBM)
    smem = pl.BlockSpec(memory_space=pltpu.SMEM)
    return pl.pallas_call(
        kernel,
        out_shape=[jax.ShapeDtypeStruct(shape, dtype) for shape, dtype in outs],
        in_specs=specs,
        out_specs=[spec] * (len(outs) - scalar_out) + [smem] * scalar_out,
        scratch_shapes=[pltpu.VMEM(*one) if isinstance(one, tuple) else one for one in scratch],
        compiler_params=pltpu.CompilerParams(vmem_limit_bytes=limit * 2**20),
        cost_estimate=pl.CostEstimate(flops=flops, bytes_accessed=2**23, transcendentals=0),
    )(*args)


def swapped(value, axis, bit):
    count = lax.axis_size(axis)
    return lax.ppermute(value, axis, [(i, i ^ bit) for i in range(count)])


def group_parts(value):
    return (value,) + tuple(swapped(value, "gz", bit) for bit in (1, 2, 3))


def kernel_spread(first, first_far, second, second_far, ready, spread):
    taps, share, channels = first.shape
    for layer, (own, other) in enumerate(((first, first_far), (second, second_far))):
        value = (own[...] + other[...]).reshape(taps * share, channels).astype(bf16)
        for part in range(spread.shape[0]):
            spread[part, layer * taps * share : (layer + 1) * taps * share] = value


def kernel_layout(scale, share, near, far, grad_w_z, grad_w_xy, grad_w_point):
    groups = near.shape[0]
    taps = near.shape[1] // share // 2
    odd = lax.rem(lax.axis_index("gz"), 2) == 1
    for layer in range(2):
        for tap in range(taps):
            at = (layer * taps + tap) * share
            one = near[:, at : at + share].astype(f32) * scale
            two = far[:, at : at + share].astype(f32) * scale
            for side in range(2):
                value = jnp.where(odd, one if side else two, two if side else one)
                value = value.reshape(groups * share, value.shape[2])
                whole = side * taps + tap
                if whole == 4:
                    grad_w_z[layer, 1] = value
                elif whole < 9:
                    grad_w_xy[layer, whole - (whole > 4)] = value
                elif whole < 11:
                    grad_w_z[layer, 2 * (whole - 9)] = value
                else:
                    grad_w_point[layer] = value


def kernel_tail(cell_count, inv_area, *refs):
    tails, parts1, parts2, refs = refs[:4], refs[4:8], refs[8:12], refs[12:]
    (consts, small, mixed, features, time_raw,
     prediction, field_grad, grad_w_in, grad_w_time, grad_biases, grad_gains, grad_w_out) = refs
    tail = sum(ref[...] for ref in tails)
    s1, s2 = sum(ref[...] for ref in parts1), sum(ref[...] for ref in parts2)
    inverse = consts[1:2]
    m_plain = inverse * (small[3:4] * tail[32:33] / cell_count)
    m_cross = inverse * inverse * (small[3:4] * tail[33:34] / cell_count)
    at = {(0, 0): 5, (0, 1): 6, (0, 2): 7, (1, 1): 8, (1, 2): 9, (2, 2): 10}
    rows_in = [small[k : k + 1] for k in range(3)]
    depth = mixed.shape[1]
    gaps = [mixed[4 * k : 4 * k + 4] - consts[2 + k : 3 + k, 0:1] for k in range(3)]
    for k in range(3):
        offset = jnp.sum(rows_in[k] * m_plain, axis=1, keepdims=True)
        value = tail[4 * k : 4 * k + 4] - offset
        cross = jnp.zeros_like(m_plain)
        for j in range(3):
            mix = jnp.sum(rows_in[k] * m_cross * rows_in[j], axis=1, keepdims=True)
            value = value - mix * gaps[j]
            row = at[min(j, k), max(j, k)]
            cross = cross + consts[row : row + 1] * rows_in[j]
        field_grad[k, 0] = value
        prediction[k, 0] = tail[12 + 4 * k : 16 + 4 * k]
        in_sum = tail[40 + k : 41 + k] - cell_count * (consts[2 + k : 3 + k] * m_plain + m_cross * cross)
        grad_w_in[k : k + 1] = inv_area * in_sum
    bias0, bias1 = tail[48:49], s1[2:3]
    grad_biases[...] = inv_area * jnp.concatenate([bias0, bias1], axis=0)
    grad_gains[...] = inv_area * jnp.concatenate([tail[33:34], s1[1:2], s2[1:2]], axis=0)
    grad_w_out[...] = inv_area * tail[56:59]
    raw = time_raw[...]
    gate = 1.0 / (1.0 + jnp.exp(-raw))
    back = (bias0 + bias1) * (gate * (1.0 + raw * (1.0 - gate)))
    spread = jnp.broadcast_to(features[...], grad_w_time.shape).T
    grad_w_time[...] = inv_area * (spread * back)


def per_device_grouped(clean_field, noise_field, timestep, dilations, w_in, w_time, w_z, w_xy, w_point,
                       biases, norm_gains, w_out):
    members, groups = lax.axis_size("gz"), lax.axis_size("gx")
    depth = clean_field.shape[3]
    planes, cells_z = groups, depth * members
    channels = w_in.shape[1]
    lanes = 4 * channels
    rows = (cells_z // REACH) * (REACH // members + 2 * RIM)
    share = channels // groups
    per_member = float(planes * 4 * depth)
    cell_count = per_member * members
    inv_area = 4.0 / cell_count

    alpha_bar, features, time_raw, time_code = time_terms(timestep, w_time)
    parts = members // 2 * groups
    block = jnp.concatenate([clean_field, noise_field], axis=0).reshape(24, depth)
    block = jnp.broadcast_to(block[None], (parts, 24, depth))
    amounts = jnp.stack([jnp.sqrt(alpha_bar), jnp.sqrt(1.0 - alpha_bar)])
    amounts = jnp.broadcast_to(amounts[:, None], (2, depth))
    same_core = [[m * groups + g for m in range(core, members, 2) for g in range(groups)] for core in range(2)]
    near = lax.all_to_all(block, ("gz", "gx"), 0, 0, axis_index_groups=same_core)
    far = swapped(near, "gz", 1)
    shift_bias = biases + time_code

    big = (planes, rows, lanes)
    vec = ((8, channels), f32)
    thin = ((planes, rows, 128), bf16)
    lift = ((128, lanes), bf16)
    conv_scratch = [
        ((planes + 2, rows, lanes), bf16),
        ((2,) + big, bf16),
        ((8, lanes // 2, lanes // 2), bf16),
    ]
    pair = ((1, lanes // 2, lanes // 2), bf16)
    flat = ((rows, lanes), f32)
    grad_out = ((6, share, channels), f32)

    taps_out, point_out = ((2, 11, channels, channels), bf16), ((2, channels, channels), bf16)
    w_front, point, w_back, point_back, lift_in, lift_out, small, steps_on = call(
        kernel_prepare,
        [taps_out, point_out, taps_out, point_out, lift, lift, ((9, channels), f32), ((2,), jnp.int32)],
        [((3, channels), f32), ((3, channels), f32), ((3, channels), bf16), pltpu.SemaphoreType.DMA((15,))],
        10**8, LIMITS[0], dilations, w_z, w_xy, w_point, w_in, norm_gains, w_out, scalar_out=1,
        far=tuple(range(7)),
    )
    stream1, normed0, act0, slope0, gathered, stats1, consts0, mixed_own = call(
        functools.partial(kernel_first, cells_z, per_member),
        [(big, f32), conv_scratch[0], (big, bf16), (big, bf16), thin, vec, ((16, channels), f32), ((12, depth), f32)],
        conv_scratch[1:] + [pair, flat, (big, f32), ((planes, 128, cells_z), bf16), ((2, parts, 24, depth), f32)],
        4 * 10**9, LIMITS[1],
        steps_on, near, far, amounts, lift_in, small, shift_bias, w_front, point,
    )
    stream2, normed1, act1, slope1, stats2, consts1 = call(
        functools.partial(kernel_second, per_member),
        [(big, f32), conv_scratch[0], (big, bf16), (big, bf16), vec, vec],
        conv_scratch[1:] + [pair, flat],
        4 * 10**9, LIMITS[2],
        steps_on, *group_parts(stats1), stream1, small, shift_bias, w_front, point,
    )
    prediction, misfit, sums2, out_raw, consts2 = call(
        functools.partial(kernel_out, per_member),
        [((rows, 128), f32), thin, vec, vec, vec],
        [(big, bf16)],
        10**9, LIMITS[3],
        steps_on, *group_parts(stats2), stream2, small, gathered, lift_out,
    )
    parts2 = group_parts(sums2)
    d_stream2, d_normed1, sums1, rimmed1, shifted1, scot1 = call(
        functools.partial(kernel_back_second, cell_count),
        [(big, f32), (big, f32), vec] + conv_scratch[:2] + [(big, bf16)],
        conv_scratch[2:] + [pair, flat, flat],
        6 * 10**9, LIMITS[4],
        steps_on, *parts2, stream2, consts2, small, misfit, lift_out, slope1, normed1,
        w_back, point_back,
    )
    parts1 = group_parts(sums1)
    keep1, give1 = call(
        functools.partial(kernel_weights_second, share),
        [grad_out, grad_out], [((12, share, channels), f32)], 2 * 10**9, LIMITS[8],
        steps_on, rimmed1, shifted1, scot1, normed1, act1,
    )
    d_stream1, sums_b0, keep0, give0, rimmed0, shifted0 = call(
        functools.partial(kernel_back_first, share, cell_count),
        [(big, f32), vec, grad_out, grad_out] + conv_scratch[:2],
        [pair, flat, (big, bf16), ((12, share, channels), f32)],
        4 * 10**9, LIMITS[5],
        steps_on, *parts1, consts1, d_stream2, d_normed1, normed1, small, act0, slope0, normed0,
        point_back,
    )
    chip0 = keep0 + swapped(give0, "gz", 1)
    chip1 = keep1 + swapped(give1, "gz", 1)
    last = call(
        functools.partial(kernel_last, depth),
        [((64, channels), f32)] * members,
        conv_scratch[2:] + [flat, flat, (big, bf16), (big, bf16)],
        4 * 10**9, LIMITS[6],
        steps_on, rimmed0, shifted0, d_stream1, normed0, small, consts0, gathered, lift_in, w_back, prediction,
        sums_b0, out_raw, chip0, chip1, ready=(13, 14),
    )
    spread = call(
        kernel_spread, [((groups, 12 * share, channels), bf16)], [], 10**5, LIMITS[9],
        chip0, swapped(chip0, "gz", 2), chip1, swapped(chip1, "gz", 2), last[0], scalars=False, ready=(4,),
    )[0]
    near_grads = lax.all_to_all(spread, "gx", 0, 0)

    prediction, field_grad, grad_w_in, grad_w_time, grad_biases, grad_gains, grad_w_out = call(
        functools.partial(kernel_tail, cell_count, inv_area),
        [(clean_field.shape, f32), (clean_field.shape, f32), ((3, channels), f32), (w_time.shape, f32),
         ((2, channels), f32), ((3, channels), f32), ((3, channels), f32)],
        [], 10**6, LIMITS[10],
        last[0], *(swapped(last[bit], "gz", bit) for bit in (1, 2, 3)), *parts1, *parts2, consts0, small,
        mixed_own, features[None], time_raw[None], scalars=False,
    )
    tied, _ = lax.optimization_barrier((near_grads, field_grad))
    far_grads = swapped(tied, "gz", 1)
    grad_w_z, grad_w_xy, grad_w_point = call(
        functools.partial(kernel_layout, inv_area, share),
        [(w_z.shape, f32), (w_xy.shape, f32), (w_point.shape, f32)],
        [], 10**6, LIMITS[11], near_grads, far_grads, scalars=False,
    )
    return (
        prediction,
        field_grad,
        grad_w_in,
        grad_w_time,
        grad_w_z,
        grad_w_xy,
        grad_w_point,
        grad_biases,
        grad_gains,
        grad_w_out,
    )


def padded_2(cells, sides, width):
    for axis, dim in sides:
        count = lax.axis_size(axis)
        head = lax.slice_in_dim(cells, 0, width, axis=dim)
        tail = lax.slice_in_dim(cells, cells.shape[dim] - width, cells.shape[dim], axis=dim)
        cells = jnp.concatenate(
            [
                lax.ppermute(tail, axis, [(i, (i + 1) % count) for i in range(count)]),
                cells,
                lax.ppermute(head, axis, [((i + 1) % count, i) for i in range(count)]),
            ],
            axis=dim,
        )
    return cells


def passed_along(value, axis, steps):
    count = lax.axis_size(axis)
    pairs = [(source, (source + steps) % count) for source in range(count)]
    return lax.ppermute(value, axis, pairs)


def contract_cells(left, right):
    return lax.dot_general(
        left, right, (((0, 1, 2), (0, 1, 2)), ((), ())), preferred_element_type=jnp.float32
    )


def plane_tap(padded, shift_x, shift_y, rows_x, rows_y):
    return padded[1 + shift_x : 1 + shift_x + rows_x, 1 + shift_y : 1 + shift_y + rows_y]


def plane_pad(source):
    rimmed = padded_2(source, (("gx", 0),), 1)
    return jnp.pad(rimmed, ((0, 0), (1, 1), (0, 0), (0, 0)))


def slab_windows(source, dilation):
    slab_depth = source.shape[2]
    above = passed_along(source, "gz", -1)
    above_far = passed_along(source, "gz", -2)
    below = passed_along(source, "gz", 1)
    below_far = passed_along(source, "gz", 2)
    ahead_rows = jnp.concatenate([source, above, above_far], axis=2)
    behind_rows = jnp.concatenate([below_far, below, source], axis=2)
    upper = lax.dynamic_slice_in_dim(ahead_rows, dilation, slab_depth, 2)
    lower = lax.dynamic_slice_in_dim(behind_rows, 2 * slab_depth - dilation, slab_depth, 2)
    return (lower, upper)


def normalize(hidden, gains, cell_count):
    average = lax.psum(jnp.sum(hidden, axis=(0, 1, 2)), ("gz", "gx")) / cell_count
    centered = hidden - average
    spread = lax.psum(jnp.sum(centered * centered, axis=(0, 1, 2)), ("gz", "gx")) / cell_count
    inverse_std = lax.rsqrt(spread + eps_norm)
    whitened = (hidden - average) * inverse_std
    return ((whitened * gains).astype(jnp.bfloat16), whitened, inverse_std)


def norm_back(d_normed, whitened, inverse_std, gains, cell_count):
    scaled = d_normed * gains
    sum_grad, sum_cross = lax.psum(
        (jnp.sum(scaled, axis=(0, 1, 2)), jnp.sum(scaled * whitened, axis=(0, 1, 2))), ("gz", "gx")
    )
    d_hidden = inverse_std * (scaled - sum_grad / cell_count - whitened * (sum_cross / cell_count))
    return (d_hidden, jnp.sum(d_normed * whitened, axis=(0, 1, 2)))


def conv_forward(normed, dilation, weights_z, weights_xy):
    rows_x, rows_y = (normed.shape[0], normed.shape[1])
    lower, upper = slab_windows(normed, dilation)
    padded = plane_pad(normed)
    summed = jnp.dot(lower, weights_z[0], preferred_element_type=jnp.float32)
    summed = summed + jnp.dot(normed, weights_z[1], preferred_element_type=jnp.float32)
    summed = summed + jnp.dot(upper, weights_z[2], preferred_element_type=jnp.float32)
    for tap_number, (shift_x, shift_y) in enumerate(plane_offsets):
        summed = summed + jnp.dot(
            plane_tap(padded, shift_x, shift_y, rows_x, rows_y),
            weights_xy[tap_number],
            preferred_element_type=jnp.float32,
        )
    return summed


def conv_backward_split(pre_cot, normed, dilation, weights_z, weights_xy):
    rows_x, rows_y = (normed.shape[0], normed.shape[1])
    lower_cot, upper_cot = slab_windows(pre_cot, dilation)
    padded_cot = plane_pad(pre_cot)
    d_normed = jnp.dot(upper_cot, weights_z[0].T, preferred_element_type=jnp.float32)
    d_normed = d_normed + jnp.dot(pre_cot, weights_z[1].T, preferred_element_type=jnp.float32)
    d_normed = d_normed + jnp.dot(lower_cot, weights_z[2].T, preferred_element_type=jnp.float32)
    xy_terms = []
    for tap_number, (shift_x, shift_y) in enumerate(plane_offsets):
        shifted = plane_tap(padded_cot, -shift_x, -shift_y, rows_x, rows_y)
        d_normed = d_normed + jnp.dot(
            shifted, weights_xy[tap_number].T, preferred_element_type=jnp.float32
        )
        xy_terms.append(contract_cells(normed, shifted))
    z_terms = jnp.stack(
        [
            contract_cells(normed, upper_cot),
            contract_cells(normed, pre_cot),
            contract_cells(normed, lower_cot),
        ]
    )
    return (d_normed, z_terms, jnp.stack(xy_terms))


def per_device_split(
    clean_field,
    noise_field,
    timestep,
    dilations,
    w_in,
    w_time,
    w_z,
    w_xy,
    w_point,
    biases,
    norm_gains,
    w_out,
):
    layer_total = w_z.shape[0]
    rows_x, rows_y, slab_depth = (clean_field.shape[1], clean_field.shape[2], clean_field.shape[3])
    plane_cells = rows_x * lax.axis_size("gx") * slab_depth * lax.axis_size("gz")
    cell_count = float(plane_cells * rows_y)
    inv_area = 1.0 / plane_cells
    alpha_bar, features, time_raw, time_code = time_terms(timestep, w_time)
    noisy = jnp.sqrt(alpha_bar) * clean_field + jnp.sqrt(1.0 - alpha_bar) * noise_field
    stream = jnp.einsum("kxyz,kc->xyzc", noisy, w_in, precision=highest)
    saved = []
    for which_layer in range(layer_total):
        normed, whitened, inverse_std = normalize(stream, norm_gains[which_layer], cell_count)
        pre_act = conv_forward(normed, dilations[which_layer], w_z[which_layer], w_xy[which_layer])
        pre_act = pre_act + biases[which_layer] + time_code
        activated = jax.nn.gelu(pre_act).astype(jnp.bfloat16)
        saved.append((normed, whitened, inverse_std, pre_act, activated))
        stream = stream + jnp.dot(
            activated, w_point[which_layer], preferred_element_type=jnp.float32
        )
    out_normed, out_white, out_inverse = normalize(stream, norm_gains[layer_total], cell_count)
    prediction = jnp.einsum("xyzc,kc->kxyz", out_normed, w_out, preferred_element_type=jnp.float32)
    misfit = prediction - noise_field
    d_out = jnp.einsum("kxyz,kc->xyzc", misfit, w_out.astype(jnp.float32), precision=highest)
    out_raw = jnp.einsum(
        "kxyz,xyzc->kc", misfit, out_normed, precision=highest, preferred_element_type=jnp.float32
    )
    d_stream, out_gain_raw = norm_back(
        d_out, out_white, out_inverse, norm_gains[layer_total], cell_count
    )
    z_list, xy_list, point_list, bias_list, gain_list = ([], [], [], [], [])
    for which_layer in reversed(range(layer_total)):
        normed, whitened, inverse_std, pre_act, activated = saved[which_layer]
        stream_cot = d_stream.astype(jnp.bfloat16)
        point_raw = contract_cells(activated, stream_cot)
        d_act = jnp.dot(stream_cot, w_point[which_layer].T, preferred_element_type=jnp.float32)
        gelu_back = jax.vjp(jax.nn.gelu, pre_act)[1]
        pre_cot = gelu_back(d_act)[0].astype(jnp.bfloat16)
        bias_raw = jnp.sum(pre_cot, axis=(0, 1, 2), dtype=jnp.float32)
        d_normed, z_raw, xy_raw = conv_backward_split(
            pre_cot, normed, dilations[which_layer], w_z[which_layer], w_xy[which_layer]
        )
        d_back, gain_raw = norm_back(
            d_normed, whitened, inverse_std, norm_gains[which_layer], cell_count
        )
        d_stream = d_stream + d_back
        z_list.insert(0, z_raw)
        xy_list.insert(0, xy_raw)
        point_list.insert(0, point_raw)
        bias_list.insert(0, bias_raw)
        gain_list.insert(0, gain_raw)
    field_grad = jnp.einsum("xyzc,kc->kxyz", d_stream, w_in, precision=highest)
    in_raw = jnp.einsum("kxyz,xyzc->kc", noisy, d_stream, precision=highest)
    z_all, xy_all, point_all, bias_all, gain_all, in_raw, out_raw = lax.psum(
        (
            jnp.stack(z_list),
            jnp.stack(xy_list),
            jnp.stack(point_list),
            jnp.stack(bias_list),
            jnp.stack(gain_list + [out_gain_raw]),
            in_raw,
            out_raw,
        ),
        ("gz", "gx"),
    )
    time_back = jax.vjp(jax.nn.silu, time_raw)[1](jnp.sum(bias_all, axis=0))[0]
    grad_w_time = inv_area * jnp.outer(features, time_back)
    return (
        prediction,
        field_grad,
        inv_area * in_raw,
        grad_w_time,
        inv_area * z_all,
        inv_area * xy_all,
        inv_area * point_all,
        inv_area * bias_all,
        inv_area * gain_all,
        inv_area * out_raw,
    )


def per_device(*args):
    members, groups = lax.axis_size("gz"), lax.axis_size("gx")
    _, rows_x, rows_y, depth = args[0].shape
    small = rows_x == 1 and rows_y == 4 and members == 4 and groups == 8 and depth * members == 2 * REACH
    return per_device_grouped(*args) if small else per_device_split(*args)


def solution(mesh):
    return jax.shard_map(
        per_device,
        mesh=mesh,
        in_specs=(
            P(None, "gx", None, "gz"),
            P(None, "gx", None, "gz"),
            P(),
            P(),
            P(),
            P(),
            P(),
            P(),
            P(),
            P(),
            P(),
            P(),
        ),
        out_specs=(
            P(None, "gx", None, "gz"),
            P(None, "gx", None, "gz"),
            P(),
            P(),
            P(),
            P(),
            P(),
            P(),
            P(),
            P(),
        ),
        check_vma=False,
    )
```

```python
import functools
import math

import jax
import jax.numpy as jnp
from jax import lax
from jax.experimental import pallas as pl
from jax.experimental.pallas import tpu as pltpu
from jax.sharding import PartitionSpec as P

STEPS = 1000
REACH = 256
RIM = 4
TILE = 16
LIMITS = (4, 14, 9, 7, 9, 8, 10, 2, 6, 2, 2, 3)

eps_norm = 1e-05
highest = lax.Precision.HIGHEST
bf16 = jnp.bfloat16
f32 = jnp.float32
plane_offsets = ((-1, -1), (-1, 0), (-1, 1), (0, -1), (0, 1), (1, -1), (1, 0), (1, 1))


def time_terms(timestep, w_time):
    moment = timestep[0].astype(jnp.float32)
    half_width = w_time.shape[0] // 2
    alpha_bar = jnp.cos(0.5 * math.pi * (moment + 0.5) / STEPS) ** 2
    ladder = jnp.exp(-math.log(10000.0) * jnp.arange(half_width, dtype=jnp.float32) / half_width)
    angles = moment * ladder
    features = jnp.concatenate([jnp.sin(angles), jnp.cos(angles)])
    time_raw = jnp.dot(features, w_time, precision=highest)
    return (alpha_bar, features, time_raw, jax.nn.silu(time_raw))


def mm(left, right):
    return lax.dot_general(left, right, (((1,), (0,)), ((), ())), preferred_element_type=f32)


def mm_nt(left, right):
    return lax.dot_general(left, right, (((1,), (1,)), ((), ())), preferred_element_type=f32)


def mm_tn(left, right):
    return lax.dot_general(left, right, (((0,), (0,)), ((), ())), preferred_element_type=f32)


def halves(value):
    high = value.astype(bf16)
    return high, (value - high.astype(f32)).astype(bf16)


def wide(vector):
    return jnp.concatenate([vector] * 4, axis=1)


def folded(vector):
    channels = vector.shape[1] // 4
    return sum(vector[:, y * channels : (y + 1) * channels] for y in range(4))


class Place:
    def __init__(self, sc, rows):
        self.rows = rows
        self.members = lax.axis_size("gz")
        self.member = lax.axis_index("gz")
        self.small = jnp.minimum(sc[0], sc[1])
        self.coarse = self.small >= self.members
        tiles = rows // TILE
        self.tiles = tiles
        self.stride = jnp.where(self.coarse, tiles - 1, tiles)
        self.span = REACH // self.members + 2 * RIM
        far = jnp.where(self.coarse, REACH // self.members, self.span)
        near = jnp.where(self.coarse, self.small // self.members, 1)
        self.steps = [jnp.where(sc[l] == REACH, far, near) for l in range(2)]

    def index(self, shape):
        row = lax.broadcasted_iota(jnp.int32, shape, 0)
        return lax.rem(row, TILE) * self.stride + row // TILE, row // TILE

    def own(self, shape):
        place, tile = self.index(shape)
        inside = lax.rem(place, self.span)
        near = ((inside >= RIM) & (inside < self.span - RIM)).astype(jnp.int32)
        far = (tile < self.tiles - 1).astype(jnp.int32)
        return jnp.where(self.coarse, far, near) == 1

    def pick(self, cells_z):
        shape = (self.rows, cells_z)
        return self.z_of(shape, cells_z) == lax.broadcasted_iota(jnp.int32, shape, 1)

    def z_of(self, shape, cells_z):
        place, _ = self.index(shape)
        residues = jnp.minimum(self.small, self.members)
        part, start = self.member // residues, lax.rem(self.member, residues)
        period = place // self.span
        inside = place - period * self.span - RIM + part * (REACH // self.members)
        near = start + residues * inside + period * REACH
        z = jnp.where(self.coarse, place * self.members + self.member, near)
        return lax.rem(z + 2 * cells_z, cells_z)


def build_taps(block_of, taps):
    channels = taps.shape[-1] // 2
    zero = jnp.zeros((channels, channels), bf16)
    near, far = slice(0, channels), slice(channels, 2 * channels)
    for i in range(3):
        down, here, up = (block_of(i, j) for j in range(3))
        taps[i, near, near] = here
        taps[i, far, far] = here
        taps[i, near, far] = down
        taps[i, far, near] = up
        taps[3 + i, near, near] = zero
        taps[3 + i, far, far] = zero
        taps[3 + i, near, far] = down
        taps[3 + i, far, near] = up
    for m in range(2):
        build_pair(block_of(3, m), taps, 6 + m)


def build_pair(block, target, m):
    channels = block.shape[-1]
    zero = jnp.zeros((channels, channels), bf16)
    target[m, :channels, :channels] = block
    target[m, channels:, channels:] = block
    target[m, :channels, channels:] = zero
    target[m, channels:, :channels] = zero


def taken(weights, layer):
    return lambda i, j: weights[layer, i * 3 + j]


def fetch(pairs, sems):
    copies = [pltpu.make_async_copy(one, two, sems.at[at]) for at, (one, two) in enumerate(pairs)]
    for copy in copies:
        copy.start()
    for copy in copies:
        copy.wait()


def kernel_prepare(steps, w_z, w_xy, w_point, w_in_far, gains_far, w_out_far, w_front, point, w_back, point_back,
                   lift_in, lift_out, small, steps_on, w_in, gains, w_out, sems):
    pairs = [(w_point, point), (w_in_far, w_in), (gains_far, gains), (w_out_far, w_out), (steps, steps_on)]
    for layer in range(2):
        pairs.append((w_xy.at[layer, pl.ds(0, 4)], w_front.at[layer, pl.ds(0, 4)]))
        pairs.append((w_xy.at[layer, pl.ds(4, 4)], w_front.at[layer, pl.ds(5, 4)]))
        for m, at in ((1, 4), (0, 9), (2, 10)):
            pairs.append((w_z.at[layer, m], w_front.at[layer, at]))
    fetch(pairs, sems)
    small[...] = jnp.concatenate([w_in[...], gains[...], w_out[...].astype(f32)], axis=0)
    for layer in range(2):
        for at in range(9):
            w_back[layer, at] = w_front[layer, 8 - at].T
        w_back[layer, 9] = w_front[layer, 10].T
        w_back[layer, 10] = w_front[layer, 9].T
        point_back[layer] = point[layer].T
    whole = spread_rows(small[0:3], 0)
    high, low = halves(whole)
    lift_in[0:32] = high
    lift_in[32:64] = high
    lift_in[64:96] = low
    lift_in[96:128] = jnp.zeros_like(low)
    high = spread_rows(small[6:9], 3).astype(bf16)
    lift_out[0:32] = high
    lift_out[32:64] = high
    lift_out[64:96] = jnp.zeros_like(high)
    lift_out[96:128] = jnp.zeros_like(high)


def spread_rows(weights, first):
    channels = weights.shape[1]
    zero = jnp.zeros((1, channels), f32)
    rows = [jnp.zeros((1, 4 * channels), f32)] * 32
    for k in range(3):
        for y in range(4):
            parts = [weights[k : k + 1] if at == y else zero for at in range(4)]
            rows[(first + k) * 4 + y] = jnp.concatenate(parts, axis=1)
    return jnp.concatenate(rows, axis=0)


def fill_rims(padded, planes):
    padded[0] = padded[planes]
    padded[planes + 1] = padded[1]


def fill_shifted(place, layer, padded, shifted, planes):
    step, stride = place.steps[layer], place.stride
    for tile in range(place.tiles):
        for way in range(2):
            at = tile - step if way == 0 else tile + step
            moved = at + TILE * stride
            source = lax.rem(moved, stride)
            turn = lax.rem(2 * TILE - moved // stride, TILE)
            rows = padded[1 : planes + 1, pl.ds(pl.multiple_of(source * TILE, TILE), TILE), :]
            rows = pltpu.roll(rows.astype(f32), turn, 1)
            shifted[way, :, tile * TILE : (tile + 1) * TILE, :] = rows.astype(bf16)


def conv_pair(padded, shifted, taps, x0, count):
    rows, lanes = padded.shape[1:]
    half, quarter = lanes // 2, lanes // 4
    totals = [None, None, None]

    def add(at, left, right):
        part = mm(left.reshape(count * rows, half), right)
        totals[at] = part if totals[at] is None else totals[at] + part

    for q in range(2):
        side = slice(q * half, (q + 1) * half)
        for i in range(3):
            add(q, padded[x0 + i : x0 + i + count, :, side], taps[i])
        for m in range(2):
            add(q, shifted[m, x0 : x0 + count, :, side], taps[6 + m])
    for i in range(3):
        add(2, padded[x0 + i : x0 + i + count, :, quarter : 3 * quarter], taps[3 + i])
    first, second, middle = totals
    first = jnp.concatenate([first[:, :quarter], first[:, quarter:] + middle[:, :quarter]], axis=1)
    second = jnp.concatenate([second[:, :quarter] + middle[:, quarter:], second[:, quarter:]], axis=1)
    return first, second


def gelu_pair(value):
    scale = math.sqrt(2.0 / math.pi)
    square = value * value
    bent = jnp.tanh(value * (scale + (scale * 0.044715) * square))
    half = 0.5 + 0.5 * bent
    result = value * half
    slope = half + result * (1.0 - half) * (2.0 * scale + (6.0 * 0.044715 * scale) * square)
    return result, slope


def members_of(parts):
    found = []
    for part in parts:
        for at in range(0, part.shape[0], 8):
            found.append(part[at : at + 8])
    return found


def merged_stats(parts, per_member):
    found = members_of(parts)
    mean = sum(one[0:1] for one in found) / (per_member * len(found))
    spread = sum(one[1:2] for one in found)
    for one in found:
        gap = one[0:1] / per_member - mean
        spread = spread + per_member * gap * gap
    return mean, lax.rsqrt(spread / (per_member * len(found)) + eps_norm)


def put_rows(ref, *vectors):
    rows = list(vectors)
    rows += [jnp.zeros((1, ref.shape[1]), f32)] * (ref.shape[0] - len(rows))
    ref[...] = jnp.concatenate(rows, axis=0)


def masked_total(mask, value):
    return folded(jnp.sum(jnp.where(mask, value, 0.0), axis=0, keepdims=True))


def layer_forward(place, layer, padded, shifted, taps, pair, w_front, wp, shift_bias, old,
                  stream, act, slope, stats, acc, per_member):
    planes, rows, lanes = stream.shape
    half = lanes // 2
    count = planes // 4
    build_taps(taken(w_front, layer), taps)
    build_pair(wp[layer], pair, 0)
    fill_rims(padded, planes)
    fill_shifted(place, layer, padded, shifted, planes)
    acc[...] = jnp.zeros_like(acc)
    bias = wide(shift_bias[layer : layer + 1, :])[:, :half]

    for x0 in range(0, planes, count):
        part = slice(x0, x0 + count)
        for q, total in enumerate(conv_pair(padded, shifted, taps, x0, count)):
            side = slice(q * half, (q + 1) * half)
            value, grad = gelu_pair(total + bias)
            act[part, :, side] = value.astype(bf16).reshape(count, rows, half)
            slope[part, :, side] = grad.astype(bf16).reshape(count, rows, half)
    for x0 in range(0, planes, count):
        part = slice(x0, x0 + count)
        for q in range(2):
            side = slice(q * half, (q + 1) * half)
            branch = mm(act[part, :, side].reshape(count * rows, half), pair[0])
            new = old[part, :, side] + branch.reshape(count, rows, half)
            stream[part, :, side] = new
            acc[:, side] += jnp.sum(new, axis=0)
    mask = place.own((rows, lanes))
    total = masked_total(mask, acc[...])
    mean = wide(total / per_member)
    spread = jnp.zeros((rows, lanes), f32)
    for x in range(planes):
        gap = stream[x] - mean
        spread = spread + gap * gap
    put_rows(stats, total, masked_total(mask, spread))


def kernel_first(cells_z, per_member, sc, near, far, amounts, lift_in, small, shift_bias, w_front, wp,
                 stream, padded, act, slope, gathered, stats, consts, mixed_own,
                 shifted, taps, pair, acc, old, source, fields):
    planes, rows, lanes = stream.shape
    channels = lanes // 4
    depth = near.shape[2]
    place = Place(sc, rows)
    keep, add = amounts[0:1], amounts[1:2]
    for at, ref in enumerate((near, far)):
        fields[at, :, 12:24] = ref[:, 12:24]
        fields[at, :, 0:12] = keep * ref[:, 0:12] + add * ref[:, 12:24]
    mixed_own[...] = fields[0, place.member // 2 * planes + lax.axis_index("gx"), 0:12]
    cell_count = float(planes * 4 * cells_z)
    comps = [
        jnp.concatenate([fields[at, :, 4 * k : 4 * k + 4, :] for at in range(2)], axis=0) for k in range(3)
    ]

    def all_sum(value):
        value = jnp.sum(jnp.sum(value, axis=0), axis=0, keepdims=True)
        return jnp.sum(value, axis=1, keepdims=True)

    means = [all_sum(comp) / cell_count for comp in comps]
    gaps = [comp - mean[None] for comp, mean in zip(comps, means)]
    for k in range(3):
        for at in range(2):
            fields[at, :, 4 * k : 4 * k + 4, :] = gaps[k][at * near.shape[0] : (at + 1) * near.shape[0]]
    covs = {}
    for j in range(3):
        for k in range(j, 3):
            covs[j, k] = all_sum(gaps[j] * gaps[k]) / cell_count
    rows_in = [small[k : k + 1, :] for k in range(3)]
    mean_c = sum(means[k] * rows_in[k] for k in range(3))
    var_c = jnp.zeros((1, channels), f32)
    for (j, k), cov in covs.items():
        var_c = var_c + (1.0 if j == k else 2.0) * cov * (rows_in[j] * rows_in[k])
    inv_c = lax.rsqrt(jnp.maximum(var_c, 0.0) + eps_norm)
    flat = [jnp.broadcast_to(value, (1, channels)) for value in means + list(covs.values())]
    put_rows(consts, mean_c, inv_c, *flat)
    blank = jnp.zeros((8, depth), f32)
    core = lax.rem(place.member, 2)
    for slab in range(cells_z // depth):
        side = core if slab % 2 == 0 else 1 - core
        at = pl.ds(pl.multiple_of((slab // 2 * 2 + side) * depth, depth), depth)
        for x in range(planes):
            high, low = halves(jnp.concatenate([fields[slab % 2, slab // 2 * planes + x], blank], axis=0))
            source[x, 0:32, at] = high
            source[x, 32:64, at] = low
            source[x, 64:96, at] = high
            source[x, 96:128, at] = jnp.zeros_like(high)
    pick = place.pick(cells_z).astype(f32).astype(bf16)
    scale = wide(inv_c * small[3:4, :])
    for x in range(planes):
        gathered[x] = mm_nt(pick, source[x]).astype(bf16)
    for x0 in range(0, planes, planes // 2):
        part = slice(x0, x0 + planes // 2)
        value = mm(gathered[part].reshape(planes // 2 * rows, 128), lift_in[...])
        unit = (value * scale).astype(bf16).reshape(planes // 2, rows, lanes)
        old[part] = value.reshape(planes // 2, rows, lanes)
        padded[x0 + 1 : x0 + 1 + planes // 2] = unit
    layer_forward(place, 0, padded, shifted, taps, pair, w_front, wp, shift_bias, old, stream,
                  act, slope, stats, acc, per_member)


def kernel_second(per_member, sc, *refs):
    parts, refs = refs[:4], refs[4:]
    (old, small, shift_bias, w_front, wp, stream, padded, act, slope, stats, consts,
     shifted, taps, pair, acc) = refs
    planes, rows, _ = stream.shape
    place = Place(sc, rows)
    mean, inverse = merged_stats(parts, per_member)
    put_rows(consts, mean, inverse)
    mean_w, scale = wide(mean), wide(inverse * small[4:5, :])
    for x in range(planes):
        padded[x + 1] = ((old[x] - mean_w) * scale).astype(bf16)
    layer_forward(place, 1, padded, shifted, taps, pair, w_front, wp, shift_bias, old, stream,
                  act, slope, stats, acc, per_member)


def kernel_out(per_member, sc, *refs):
    parts, refs = refs[:4], refs[4:]
    stream, small, gathered, lift_out, prediction, misfit, sums, w_out_raw, consts, unit = refs
    planes, rows, lanes = stream.shape
    place = Place(sc, rows)
    mean, inverse = merged_stats(parts, per_member)
    put_rows(consts, mean, inverse)
    mean_w, inv_w, gain_w = wide(mean), wide(inverse), wide(small[5:6, :])
    scale = inv_w * gain_w
    for x in range(planes):
        unit[x] = ((stream[x] - mean_w) * scale).astype(bf16)
    row = lax.broadcasted_iota(jnp.int32, (128, 128), 0)
    col = lax.broadcasted_iota(jnp.int32, (128, 128), 1)
    slot = lax.rem(col, 32)
    used = (col < 64) & (slot >= 12) & (slot < 24)
    take = (used & ((row == slot) | (row == slot + 32))).astype(f32).astype(bf16)
    total = mm_nt(unit[...].reshape(planes * rows, lanes), lift_out[...])
    noise = mm(gathered[...].reshape(planes * rows, 128), take)
    gap = total - noise
    high, low = halves(gap)
    lane = lax.broadcasted_iota(jnp.int32, gap.shape, 1)
    both = jnp.where(lane < 32, high.astype(f32), low.astype(f32)).astype(bf16)
    misfit[...] = both.reshape(planes, rows, 128)
    for x in range(planes):
        @pl.when(lax.axis_index("gx") == x)
        def _(x=x):
            prediction[...] = total[x * rows : (x + 1) * rows]
    plain = jnp.zeros((rows, lanes), f32)
    cross = jnp.zeros((rows, lanes), f32)
    for x0 in range(0, planes, planes // 2):
        part = slice(x0 * rows, (x0 + planes // 2) * rows)
        d_out = mm(both[part], lift_out[...]).reshape(planes // 2, rows, lanes)
        for x in range(planes // 2):
            plain = plain + d_out[x]
            cross = cross + d_out[x] * ((stream[x0 + x] - mean_w) * inv_w)
    own = place.own((rows, 128))
    kept = jnp.concatenate([jnp.where(own, misfit[x].astype(f32), 0.0) for x in range(planes)], axis=0)
    raw = mm_tn(kept.astype(bf16), unit[...].reshape(planes * rows, lanes))
    mask = place.own((rows, lanes))
    put_rows(sums, masked_total(mask, plain), masked_total(mask, cross))
    put_rows(w_out_raw, *by_component(raw[0:32] + raw[32:64], 3))


def by_component(raw, first):
    channels = raw.shape[1] // 4
    found = []
    for k in range(first, first + 3):
        found.append(
            sum(raw[k * 4 + y : k * 4 + y + 1, y * channels : (y + 1) * channels] for y in range(4))
        )
    return found


def branch_backward(planes, d_stream_of, pair, slope, padded, scot, bias_acc):
    rows, lanes = padded.shape[1:]
    half = lanes // 2
    count = planes // 2

    for x0 in range(0, planes, count):
        part = slice(x0, x0 + count)
        for x in range(x0, x0 + count):
            scot[x] = d_stream_of(x).astype(bf16)
        for q in range(2):
            side = slice(q * half, (q + 1) * half)
            cot = scot[part, :, side].reshape(count * rows, half)
            d_act = mm(cot, pair[0]).reshape(count, rows, half)
            pre = (d_act * slope[part, :, side].astype(f32)).astype(bf16)
            padded[x0 + 1 : x0 + 1 + count, :, side] = pre
            bias_acc[:, side] += jnp.sum(pre.astype(f32), axis=0)


def weight_grads(place, planes, padded, shifted, scot, normed, act, keep, give, taps_all, share):
    rows, lanes = padded.shape[1:]
    channels = lanes // 4
    wide_share = 4 * share
    row = lax.broadcasted_iota(jnp.int32, (lanes, wide_share), 0)
    col = lax.broadcasted_iota(jnp.int32, (lanes, wide_share), 1)
    hit = (row // channels == col // share) & (
        lax.rem(row, channels) == lax.rem(col, share) + lax.axis_index("gx") * share
    )
    choose = hit.astype(f32).astype(bf16)
    mask = jnp.concatenate([place.own((rows, wide_share))] * planes, axis=0)

    def turned(source):
        got = mm(source.reshape(planes * rows, lanes), choose)
        return jnp.where(mask, got, 0.0).astype(bf16)

    def add_blocks(raw, j):
        return sum(
            raw[(y + j) * share : (y + j + 1) * share, y * channels : (y + 1) * channels]
            for y in range(4)
            if 0 <= y + j < 4
        )

    left = turned(normed[1 : planes + 1])
    for i in range(3):
        raw = mm_tn(left, padded[2 - i : 2 - i + planes].reshape(planes * rows, lanes))
        for j in range(3):
            taps_all[i * 3 + j] = add_blocks(raw, j - 1)
    for m in range(2):
        raw = mm_tn(left, shifted[1 - m].reshape(planes * rows, lanes))
        taps_all[9 + m] = add_blocks(raw, 0)
    raw = mm_tn(turned(act[...]), scot[...].reshape(planes * rows, lanes))
    taps_all[11] = add_blocks(raw, 0)
    odd, half = lax.rem(place.member, 2), keep.shape[0]
    keep[...] = taps_all[pl.ds(odd * half, half)]
    give[...] = taps_all[pl.ds((1 - odd) * half, half)]


def conv_backward(planes, padded, shifted, taps, emit):
    count = planes // 4

    for x0 in range(0, planes, count):
        for q, total in enumerate(conv_pair(padded, shifted, taps, x0, count)):
            emit(x0, count, q, total)


def kernel_back_second(cell_count, sc, *refs):
    parts, refs = refs[:4], refs[4:]
    (stream, out_consts, small, misfit, lift_out, slope, normed, w_back, point_back,
     d_stream, d_normed, sums, padded, shifted, scot,
     taps, pair, acc, acc2) = refs
    planes, rows, lanes = stream.shape
    half = lanes // 2
    place = Place(sc, rows)
    sums_out = sum(members_of(parts))
    gain_w = wide(small[5:6, :])
    mean_w, inv_w = wide(out_consts[0:1]), wide(out_consts[1:2])
    m_plain = gain_w * wide(sums_out[0:1]) / cell_count
    m_cross = gain_w * wide(sums_out[1:2]) / cell_count
    build_pair(point_back[1], pair, 0)
    build_taps(taken(w_back, 1), taps)
    acc[...] = jnp.zeros_like(acc)

    def d_stream_of(x):
        d_out = mm(misfit[x], lift_out[...])
        white = (stream[x] - mean_w) * inv_w
        value = inv_w * (gain_w * d_out - m_plain - white * m_cross)
        d_stream[x] = value
        return value

    branch_backward(planes, d_stream_of, pair, slope, padded, scot, acc)
    mask = place.own((rows, lanes))
    s_bias = masked_total(mask, acc[...])
    acc[...] = jnp.zeros_like(acc)
    acc2[...] = jnp.zeros_like(acc2)
    fill_rims(padded, planes)
    fill_shifted(place, 1, padded, shifted, planes)

    def emit(x0, count, q, value):
        side = slice(q * half, (q + 1) * half)
        value = value.reshape(count, rows, half)
        d_normed[x0 : x0 + count, :, side] = value
        acc[:, side] += jnp.sum(value, axis=0)
        acc2[:, side] += jnp.sum(value * normed[x0 + 1 : x0 + 1 + count, :, side].astype(f32), axis=0)

    conv_backward(planes, padded, shifted, taps, emit)
    s_plain = masked_total(mask, acc[...])
    s_cross = masked_total(mask, acc2[...]) / small[4:5, :]
    put_rows(sums, s_plain, s_cross, s_bias)


def kernel_weights_second(share, sc, padded, shifted, scot, normed, act, keep, give, taps_all):
    planes, rows, _ = scot.shape
    weight_grads(Place(sc, rows), planes, padded, shifted, scot, normed, act, keep, give, taps_all, share)


def kernel_back_first(share, cell_count, sc, *refs):
    parts, refs = refs[:4], refs[4:]
    (consts, d_next, d_normed, normed_next, small, act, slope, normed, point_back,
     d_stream, sums, keep, give, padded, shifted,
     pair, acc, scot, taps_all) = refs
    planes, rows, lanes = d_next.shape
    place = Place(sc, rows)
    sums_in = sum(members_of(parts))
    gain_w = wide(small[4:5, :])
    inv_w = wide(consts[1:2])
    m_plain = gain_w * wide(sums_in[0:1]) / cell_count
    m_cross = wide(sums_in[1:2]) / cell_count
    build_pair(point_back[0], pair, 0)
    acc[...] = jnp.zeros_like(acc)

    def d_stream_of(x):
        back = gain_w * d_normed[x] - m_plain - normed_next[x + 1].astype(f32) * m_cross
        value = d_next[x] + inv_w * back
        d_stream[x] = value
        return value

    branch_backward(planes, d_stream_of, pair, slope, padded, scot, acc)
    put_rows(sums, masked_total(place.own((rows, lanes)), acc[...]))
    fill_rims(padded, planes)
    fill_shifted(place, 0, padded, shifted, planes)
    weight_grads(place, planes, padded, shifted, scot, normed, act, keep, give, taps_all, share)


def kernel_last(depth, sc, padded, shifted, d_stream, normed, small, consts, gathered, lift_in, w_back,
                prediction, sums_bias, out_raw, ready0, ready1, own_out, out_1, out_2, out_3,
                taps, acc, acc2, high, low):
    planes, rows, lanes = d_stream.shape
    half = lanes // 2
    place = Place(sc, rows)
    build_taps(taken(w_back, 0), taps)
    acc[...] = jnp.zeros_like(acc)
    acc2[...] = jnp.zeros_like(acc2)
    scale = wide(consts[1:2] * small[3:4, :])

    def emit(x0, count, q, value):
        side = slice(q * half, (q + 1) * half)
        part = slice(x0, x0 + count)
        value = value.reshape(count, rows, half)
        acc[:, side] += jnp.sum(value, axis=0)
        acc2[:, side] += jnp.sum(value * normed[x0 + 1 : x0 + 1 + count, :, side].astype(f32), axis=0)
        full = d_stream[part, :, side] + value * scale[:, side]
        first, second = halves(full)
        high[part, :, side] = first
        low[part, :, side] = second

    conv_backward(planes, padded, shifted, taps, emit)
    mask = place.own((rows, lanes))
    s_plain = masked_total(mask, acc[...])
    s_cross = masked_total(mask, acc2[...]) / small[3:4, :]
    own = place.own((rows, 128))
    kept = jnp.concatenate([jnp.where(own, gathered[x].astype(f32), 0.0) for x in range(planes)], axis=0)
    kept = kept.astype(bf16)
    raw = mm_tn(kept, high[...].reshape(planes * rows, lanes))
    raw_low = mm_tn(kept, low[...].reshape(planes * rows, lanes))
    in_raw = by_component(raw[0:32] + raw[32:64] + raw_low[0:32], 0)
    blank = jnp.zeros((1, s_plain.shape[1]), f32)
    tail = jnp.concatenate([s_plain, s_cross] + [blank] * 6 + in_raw + [blank] * 5, axis=0)
    tail = jnp.concatenate([tail, sums_bias[...], out_raw[...]], axis=0)
    here = lax.axis_index("gx")
    lane = lax.broadcasted_iota(jnp.int32, (rows, 128), 1)
    field = mm_nt(high[here], lift_in[...]) + jnp.where(lane < 32, mm_nt(low[here], lift_in[...]), 0.0)
    field = jnp.where((lane >= 32) & (lane < 64), 0.0, field)
    field = field + jnp.where((lane >= 12) & (lane < 24), prediction[...], 0.0)
    cells_z = depth * place.members
    whole = place.z_of((rows, depth), cells_z)
    column = lax.broadcasted_iota(jnp.int32, (rows, depth), 1)
    mask = place.own((rows, depth))
    first, second = halves(field)
    for bit, target in enumerate((own_out, out_1, out_2, out_3)):
        there = lax.bitwise_xor(place.member, bit)
        pick = ((whole == column + there * depth) & mask).astype(f32).astype(bf16)
        out = mm_tn(first, pick) + mm_tn(second, pick)
        target[0:32] = out[0:32] + out[64:96]
        target[32:64] = tail


def call(kernel, outs, scratch, flops, limit, *args, scalars=True, scalar_out=0, ready=(), far=()):
    spec = pl.BlockSpec(memory_space=pltpu.VMEM)
    specs = [pl.BlockSpec(memory_space=pltpu.SMEM)] * scalars + [spec] * (len(args) - scalars)
    for at in ready:
        specs[at] = pl.BlockSpec(memory_space=pl.ANY)
    args = list(args)
    for at in far:
        specs[at] = pl.BlockSpec(memory_space=pltpu.HBM)
        args[at] = pltpu.with_memory_space_constraint(args[at], pltpu.HBM)
    smem = pl.BlockSpec(memory_space=pltpu.SMEM)
    return pl.pallas_call(
        kernel,
        out_shape=[jax.ShapeDtypeStruct(shape, dtype) for shape, dtype in outs],
        in_specs=specs,
        out_specs=[spec] * (len(outs) - scalar_out) + [smem] * scalar_out,
        scratch_shapes=[pltpu.VMEM(*one) if isinstance(one, tuple) else one for one in scratch],
        compiler_params=pltpu.CompilerParams(vmem_limit_bytes=limit * 2**20),
        cost_estimate=pl.CostEstimate(flops=flops, bytes_accessed=2**23, transcendentals=0),
    )(*args)


def swapped(value, axis, bit):
    count = lax.axis_size(axis)
    return lax.ppermute(value, axis, [(i, i ^ bit) for i in range(count)])


def group_parts(value):
    return (value,) + tuple(swapped(value, "gz", bit) for bit in (1, 2, 3))


def kernel_spread(first, first_far, second, second_far, ready, spread):
    taps, share, channels = first.shape
    for layer, (own, other) in enumerate(((first, first_far), (second, second_far))):
        value = (own[...] + other[...]).reshape(taps * share, channels).astype(bf16)
        for part in range(spread.shape[0]):
            spread[part, layer * taps * share : (layer + 1) * taps * share] = value


def kernel_layout(scale, share, near, far, grad_w_z, grad_w_xy, grad_w_point):
    groups = near.shape[0]
    taps = near.shape[1] // share // 2
    odd = lax.rem(lax.axis_index("gz"), 2) == 1
    for layer in range(2):
        for tap in range(taps):
            at = (layer * taps + tap) * share
            one = near[:, at : at + share].astype(f32) * scale
            two = far[:, at : at + share].astype(f32) * scale
            for side in range(2):
                value = jnp.where(odd, one if side else two, two if side else one)
                value = value.reshape(groups * share, value.shape[2])
                whole = side * taps + tap
                if whole == 4:
                    grad_w_z[layer, 1] = value
                elif whole < 9:
                    grad_w_xy[layer, whole - (whole > 4)] = value
                elif whole < 11:
                    grad_w_z[layer, 2 * (whole - 9)] = value
                else:
                    grad_w_point[layer] = value


def kernel_tail(cell_count, inv_area, *refs):
    tails, parts1, parts2, refs = refs[:4], refs[4:8], refs[8:12], refs[12:]
    (consts, small, mixed, features, time_raw,
     prediction, field_grad, grad_w_in, grad_w_time, grad_biases, grad_gains, grad_w_out) = refs
    tail = sum(ref[...] for ref in tails)
    s1, s2 = sum(ref[...] for ref in parts1), sum(ref[...] for ref in parts2)
    inverse = consts[1:2]
    m_plain = inverse * (small[3:4] * tail[32:33] / cell_count)
    m_cross = inverse * inverse * (small[3:4] * tail[33:34] / cell_count)
    at = {(0, 0): 5, (0, 1): 6, (0, 2): 7, (1, 1): 8, (1, 2): 9, (2, 2): 10}
    rows_in = [small[k : k + 1] for k in range(3)]
    depth = mixed.shape[1]
    gaps = [mixed[4 * k : 4 * k + 4] - consts[2 + k : 3 + k, 0:1] for k in range(3)]
    for k in range(3):
        offset = jnp.sum(rows_in[k] * m_plain, axis=1, keepdims=True)
        value = tail[4 * k : 4 * k + 4] - offset
        cross = jnp.zeros_like(m_plain)
        for j in range(3):
            mix = jnp.sum(rows_in[k] * m_cross * rows_in[j], axis=1, keepdims=True)
            value = value - mix * gaps[j]
            row = at[min(j, k), max(j, k)]
            cross = cross + consts[row : row + 1] * rows_in[j]
        field_grad[k, 0] = value
        prediction[k, 0] = tail[12 + 4 * k : 16 + 4 * k]
        in_sum = tail[40 + k : 41 + k] - cell_count * (m_cross * cross)
        grad_w_in[k : k + 1] = inv_area * in_sum
    bias0, bias1 = tail[48:49], s1[2:3]
    grad_biases[...] = inv_area * jnp.concatenate([bias0, bias1], axis=0)
    grad_gains[...] = inv_area * jnp.concatenate([tail[33:34], s1[1:2], s2[1:2]], axis=0)
    grad_w_out[...] = inv_area * tail[56:59]
    raw = time_raw[...]
    gate = 1.0 / (1.0 + jnp.exp(-raw))
    back = (bias0 + bias1) * (gate * (1.0 + raw * (1.0 - gate)))
    spread = jnp.broadcast_to(features[...], grad_w_time.shape).T
    grad_w_time[...] = inv_area * (spread * back)


def per_device_grouped(clean_field, noise_field, timestep, dilations, w_in, w_time, w_z, w_xy, w_point,
                       biases, norm_gains, w_out):
    members, groups = lax.axis_size("gz"), lax.axis_size("gx")
    depth = clean_field.shape[3]
    planes, cells_z = groups, depth * members
    channels = w_in.shape[1]
    lanes = 4 * channels
    rows = (cells_z // REACH) * (REACH // members + 2 * RIM)
    share = channels // groups
    per_member = float(planes * 4 * depth)
    cell_count = per_member * members
    inv_area = 4.0 / cell_count

    alpha_bar, features, time_raw, time_code = time_terms(timestep, w_time)
    parts = members // 2 * groups
    block = jnp.concatenate([clean_field, noise_field], axis=0).reshape(24, depth)
    block = jnp.broadcast_to(block[None], (parts, 24, depth))
    amounts = jnp.stack([jnp.sqrt(alpha_bar), jnp.sqrt(1.0 - alpha_bar)])
    amounts = jnp.broadcast_to(amounts[:, None], (2, depth))
    same_core = [[m * groups + g for m in range(core, members, 2) for g in range(groups)] for core in range(2)]
    near = lax.all_to_all(block, ("gz", "gx"), 0, 0, axis_index_groups=same_core)
    far = swapped(near, "gz", 1)
    shift_bias = biases + time_code

    big = (planes, rows, lanes)
    vec = ((8, channels), f32)
    thin = ((planes, rows, 128), bf16)
    lift = ((128, lanes), bf16)
    conv_scratch = [
        ((planes + 2, rows, lanes), bf16),
        ((2,) + big, bf16),
        ((8, lanes // 2, lanes // 2), bf16),
    ]
    pair = ((1, lanes // 2, lanes // 2), bf16)
    flat = ((rows, lanes), f32)
    grad_out = ((6, share, channels), f32)

    taps_out, point_out = ((2, 11, channels, channels), bf16), ((2, channels, channels), bf16)
    w_front, point, w_back, point_back, lift_in, lift_out, small, steps_on = call(
        kernel_prepare,
        [taps_out, point_out, taps_out, point_out, lift, lift, ((9, channels), f32), ((2,), jnp.int32)],
        [((3, channels), f32), ((3, channels), f32), ((3, channels), bf16), pltpu.SemaphoreType.DMA((15,))],
        10**8, LIMITS[0], dilations, w_z, w_xy, w_point, w_in, norm_gains, w_out, scalar_out=1,
        far=tuple(range(7)),
    )
    stream1, normed0, act0, slope0, gathered, stats1, consts0, mixed_own = call(
        functools.partial(kernel_first, cells_z, per_member),
        [(big, f32), conv_scratch[0], (big, bf16), (big, bf16), thin, vec, ((16, channels), f32), ((12, depth), f32)],
        conv_scratch[1:] + [pair, flat, (big, f32), ((planes, 128, cells_z), bf16), ((2, parts, 24, depth), f32)],
        4 * 10**9, LIMITS[1],
        steps_on, near, far, amounts, lift_in, small, shift_bias, w_front, point,
    )
    stream2, normed1, act1, slope1, stats2, consts1 = call(
        functools.partial(kernel_second, per_member),
        [(big, f32), conv_scratch[0], (big, bf16), (big, bf16), vec, vec],
        conv_scratch[1:] + [pair, flat],
        4 * 10**9, LIMITS[2],
        steps_on, *group_parts(stats1), stream1, small, shift_bias, w_front, point,
    )
    prediction, misfit, sums2, out_raw, consts2 = call(
        functools.partial(kernel_out, per_member),
        [((rows, 128), f32), thin, vec, vec, vec],
        [(big, bf16)],
        10**9, LIMITS[3],
        steps_on, *group_parts(stats2), stream2, small, gathered, lift_out,
    )
    parts2 = group_parts(sums2)
    d_stream2, d_normed1, sums1, rimmed1, shifted1, scot1 = call(
        functools.partial(kernel_back_second, cell_count),
        [(big, f32), (big, f32), vec] + conv_scratch[:2] + [(big, bf16)],
        conv_scratch[2:] + [pair, flat, flat],
        6 * 10**9, LIMITS[4],
        steps_on, *parts2, stream2, consts2, small, misfit, lift_out, slope1, normed1,
        w_back, point_back,
    )
    parts1 = group_parts(sums1)
    keep1, give1 = call(
        functools.partial(kernel_weights_second, share),
        [grad_out, grad_out], [((12, share, channels), f32)], 2 * 10**9, LIMITS[8],
        steps_on, rimmed1, shifted1, scot1, normed1, act1,
    )
    d_stream1, sums_b0, keep0, give0, rimmed0, shifted0 = call(
        functools.partial(kernel_back_first, share, cell_count),
        [(big, f32), vec, grad_out, grad_out] + conv_scratch[:2],
        [pair, flat, (big, bf16), ((12, share, channels), f32)],
        4 * 10**9, LIMITS[5],
        steps_on, *parts1, consts1, d_stream2, d_normed1, normed1, small, act0, slope0, normed0,
        point_back,
    )
    chip0 = keep0 + swapped(give0, "gz", 1)
    chip1 = keep1 + swapped(give1, "gz", 1)
    last = call(
        functools.partial(kernel_last, depth),
        [((64, channels), f32)] * members,
        conv_scratch[2:] + [flat, flat, (big, bf16), (big, bf16)],
        4 * 10**9, LIMITS[6],
        steps_on, rimmed0, shifted0, d_stream1, normed0, small, consts0, gathered, lift_in, w_back, prediction,
        sums_b0, out_raw, chip0, chip1, ready=(13, 14),
    )
    spread = call(
        kernel_spread, [((groups, 12 * share, channels), bf16)], [], 10**5, LIMITS[9],
        chip0, swapped(chip0, "gz", 2), chip1, swapped(chip1, "gz", 2), last[0], scalars=False, ready=(4,),
    )[0]
    near_grads = lax.all_to_all(spread, "gx", 0, 0)

    prediction, field_grad, grad_w_in, grad_w_time, grad_biases, grad_gains, grad_w_out = call(
        functools.partial(kernel_tail, cell_count, inv_area),
        [(clean_field.shape, f32), (clean_field.shape, f32), ((3, channels), f32), (w_time.shape, f32),
         ((2, channels), f32), ((3, channels), f32), ((3, channels), f32)],
        [], 10**6, LIMITS[10],
        last[0], *(swapped(last[bit], "gz", bit) for bit in (1, 2, 3)), *parts1, *parts2, consts0, small,
        mixed_own, features[None], time_raw[None], scalars=False,
    )
    tied, _ = lax.optimization_barrier((near_grads, field_grad))
    far_grads = swapped(tied, "gz", 1)
    grad_w_z, grad_w_xy, grad_w_point = call(
        functools.partial(kernel_layout, inv_area, share),
        [(w_z.shape, f32), (w_xy.shape, f32), (w_point.shape, f32)],
        [], 10**6, LIMITS[11], near_grads, far_grads, scalars=False,
    )
    return (
        prediction,
        field_grad,
        grad_w_in,
        grad_w_time,
        grad_w_z,
        grad_w_xy,
        grad_w_point,
        grad_biases,
        grad_gains,
        grad_w_out,
    )


def padded_2(cells, sides, width):
    for axis, dim in sides:
        count = lax.axis_size(axis)
        head = lax.slice_in_dim(cells, 0, width, axis=dim)
        tail = lax.slice_in_dim(cells, cells.shape[dim] - width, cells.shape[dim], axis=dim)
        cells = jnp.concatenate(
            [
                lax.ppermute(tail, axis, [(i, (i + 1) % count) for i in range(count)]),
                cells,
                lax.ppermute(head, axis, [((i + 1) % count, i) for i in range(count)]),
            ],
            axis=dim,
        )
    return cells


def passed_along(value, axis, steps):
    count = lax.axis_size(axis)
    pairs = [(source, (source + steps) % count) for source in range(count)]
    return lax.ppermute(value, axis, pairs)


def contract_cells(left, right):
    return lax.dot_general(
        left, right, (((0, 1, 2), (0, 1, 2)), ((), ())), preferred_element_type=jnp.float32
    )


def plane_tap(padded, shift_x, shift_y, rows_x, rows_y):
    return padded[1 + shift_x : 1 + shift_x + rows_x, 1 + shift_y : 1 + shift_y + rows_y]


def plane_pad(source):
    rimmed = padded_2(source, (("gx", 0),), 1)
    return jnp.pad(rimmed, ((0, 0), (1, 1), (0, 0), (0, 0)))


def slab_windows(source, dilation):
    slab_depth = source.shape[2]
    above = passed_along(source, "gz", -1)
    above_far = passed_along(source, "gz", -2)
    below = passed_along(source, "gz", 1)
    below_far = passed_along(source, "gz", 2)
    ahead_rows = jnp.concatenate([source, above, above_far], axis=2)
    behind_rows = jnp.concatenate([below_far, below, source], axis=2)
    upper = lax.dynamic_slice_in_dim(ahead_rows, dilation, slab_depth, 2)
    lower = lax.dynamic_slice_in_dim(behind_rows, 2 * slab_depth - dilation, slab_depth, 2)
    return (lower, upper)


def normalize(hidden, gains, cell_count):
    average = lax.psum(jnp.sum(hidden, axis=(0, 1, 2)), ("gz", "gx")) / cell_count
    centered = hidden - average
    spread = lax.psum(jnp.sum(centered * centered, axis=(0, 1, 2)), ("gz", "gx")) / cell_count
    inverse_std = lax.rsqrt(spread + eps_norm)
    whitened = (hidden - average) * inverse_std
    return ((whitened * gains).astype(jnp.bfloat16), whitened, inverse_std)


def norm_back(d_normed, whitened, inverse_std, gains, cell_count):
    scaled = d_normed * gains
    sum_grad, sum_cross = lax.psum(
        (jnp.sum(scaled, axis=(0, 1, 2)), jnp.sum(scaled * whitened, axis=(0, 1, 2))), ("gz", "gx")
    )
    d_hidden = inverse_std * (scaled - sum_grad / cell_count - whitened * (sum_cross / cell_count))
    return (d_hidden, jnp.sum(d_normed * whitened, axis=(0, 1, 2)))


def conv_forward(normed, dilation, weights_z, weights_xy):
    rows_x, rows_y = (normed.shape[0], normed.shape[1])
    lower, upper = slab_windows(normed, dilation)
    padded = plane_pad(normed)
    summed = jnp.dot(lower, weights_z[0], preferred_element_type=jnp.float32)
    summed = summed + jnp.dot(normed, weights_z[1], preferred_element_type=jnp.float32)
    summed = summed + jnp.dot(upper, weights_z[2], preferred_element_type=jnp.float32)
    for tap_number, (shift_x, shift_y) in enumerate(plane_offsets):
        summed = summed + jnp.dot(
            plane_tap(padded, shift_x, shift_y, rows_x, rows_y),
            weights_xy[tap_number],
            preferred_element_type=jnp.float32,
        )
    return summed


def conv_backward_split(pre_cot, normed, dilation, weights_z, weights_xy):
    rows_x, rows_y = (normed.shape[0], normed.shape[1])
    lower_cot, upper_cot = slab_windows(pre_cot, dilation)
    padded_cot = plane_pad(pre_cot)
    d_normed = jnp.dot(upper_cot, weights_z[0].T, preferred_element_type=jnp.float32)
    d_normed = d_normed + jnp.dot(pre_cot, weights_z[1].T, preferred_element_type=jnp.float32)
    d_normed = d_normed + jnp.dot(lower_cot, weights_z[2].T, preferred_element_type=jnp.float32)
    xy_terms = []
    for tap_number, (shift_x, shift_y) in enumerate(plane_offsets):
        shifted = plane_tap(padded_cot, -shift_x, -shift_y, rows_x, rows_y)
        d_normed = d_normed + jnp.dot(
            shifted, weights_xy[tap_number].T, preferred_element_type=jnp.float32
        )
        xy_terms.append(contract_cells(normed, shifted))
    z_terms = jnp.stack(
        [
            contract_cells(normed, upper_cot),
            contract_cells(normed, pre_cot),
            contract_cells(normed, lower_cot),
        ]
    )
    return (d_normed, z_terms, jnp.stack(xy_terms))


def per_device_split(
    clean_field,
    noise_field,
    timestep,
    dilations,
    w_in,
    w_time,
    w_z,
    w_xy,
    w_point,
    biases,
    norm_gains,
    w_out,
):
    layer_total = w_z.shape[0]
    rows_x, rows_y, slab_depth = (clean_field.shape[1], clean_field.shape[2], clean_field.shape[3])
    plane_cells = rows_x * lax.axis_size("gx") * slab_depth * lax.axis_size("gz")
    cell_count = float(plane_cells * rows_y)
    inv_area = 1.0 / plane_cells
    alpha_bar, features, time_raw, time_code = time_terms(timestep, w_time)
    noisy = jnp.sqrt(alpha_bar) * clean_field + jnp.sqrt(1.0 - alpha_bar) * noise_field
    stream = jnp.einsum("kxyz,kc->xyzc", noisy, w_in, precision=highest)
    saved = []
    for which_layer in range(layer_total):
        normed, whitened, inverse_std = normalize(stream, norm_gains[which_layer], cell_count)
        pre_act = conv_forward(normed, dilations[which_layer], w_z[which_layer], w_xy[which_layer])
        pre_act = pre_act + biases[which_layer] + time_code
        activated = jax.nn.gelu(pre_act).astype(jnp.bfloat16)
        saved.append((normed, whitened, inverse_std, pre_act, activated))
        stream = stream + jnp.dot(
            activated, w_point[which_layer], preferred_element_type=jnp.float32
        )
    out_normed, out_white, out_inverse = normalize(stream, norm_gains[layer_total], cell_count)
    prediction = jnp.einsum("xyzc,kc->kxyz", out_normed, w_out, preferred_element_type=jnp.float32)
    misfit = prediction - noise_field
    d_out = jnp.einsum("kxyz,kc->xyzc", misfit, w_out.astype(jnp.float32), precision=highest)
    out_raw = jnp.einsum(
        "kxyz,xyzc->kc", misfit, out_normed, precision=highest, preferred_element_type=jnp.float32
    )
    d_stream, out_gain_raw = norm_back(
        d_out, out_white, out_inverse, norm_gains[layer_total], cell_count
    )
    z_list, xy_list, point_list, bias_list, gain_list = ([], [], [], [], [])
    for which_layer in reversed(range(layer_total)):
        normed, whitened, inverse_std, pre_act, activated = saved[which_layer]
        stream_cot = d_stream.astype(jnp.bfloat16)
        point_raw = contract_cells(activated, stream_cot)
        d_act = jnp.dot(stream_cot, w_point[which_layer].T, preferred_element_type=jnp.float32)
        gelu_back = jax.vjp(jax.nn.gelu, pre_act)[1]
        pre_cot = gelu_back(d_act)[0].astype(jnp.bfloat16)
        bias_raw = jnp.sum(pre_cot, axis=(0, 1, 2), dtype=jnp.float32)
        d_normed, z_raw, xy_raw = conv_backward_split(
            pre_cot, normed, dilations[which_layer], w_z[which_layer], w_xy[which_layer]
        )
        d_back, gain_raw = norm_back(
            d_normed, whitened, inverse_std, norm_gains[which_layer], cell_count
        )
        d_stream = d_stream + d_back
        z_list.insert(0, z_raw)
        xy_list.insert(0, xy_raw)
        point_list.insert(0, point_raw)
        bias_list.insert(0, bias_raw)
        gain_list.insert(0, gain_raw)
    field_grad = jnp.einsum("xyzc,kc->kxyz", d_stream, w_in, precision=highest)
    in_raw = jnp.einsum("kxyz,xyzc->kc", noisy, d_stream, precision=highest)
    z_all, xy_all, point_all, bias_all, gain_all, in_raw, out_raw = lax.psum(
        (
            jnp.stack(z_list),
            jnp.stack(xy_list),
            jnp.stack(point_list),
            jnp.stack(bias_list),
            jnp.stack(gain_list + [out_gain_raw]),
            in_raw,
            out_raw,
        ),
        ("gz", "gx"),
    )
    time_back = jax.vjp(jax.nn.silu, time_raw)[1](jnp.sum(bias_all, axis=0))[0]
    grad_w_time = inv_area * jnp.outer(features, time_back)
    return (
        prediction,
        field_grad,
        inv_area * in_raw,
        grad_w_time,
        inv_area * z_all,
        inv_area * xy_all,
        inv_area * point_all,
        inv_area * bias_all,
        inv_area * gain_all,
        inv_area * out_raw,
    )


def per_device(*args):
    members, groups = lax.axis_size("gz"), lax.axis_size("gx")
    _, rows_x, rows_y, depth = args[0].shape
    small = rows_x == 1 and rows_y == 4 and members == 4 and groups == 8 and depth * members == 2 * REACH
    return per_device_grouped(*args) if small else per_device_split(*args)


def solution(mesh):
    return jax.shard_map(
        per_device,
        mesh=mesh,
        in_specs=(
            P(None, "gx", None, "gz"),
            P(None, "gx", None, "gz"),
            P(),
            P(),
            P(),
            P(),
            P(),
            P(),
            P(),
            P(),
            P(),
            P(),
        ),
        out_specs=(
            P(None, "gx", None, "gz"),
            P(None, "gx", None, "gz"),
            P(),
            P(),
            P(),
            P(),
            P(),
            P(),
            P(),
            P(),
        ),
        check_vma=False,
    )
```

```python
import functools
import math

import jax
import jax.numpy as jnp
from jax import lax
from jax.experimental import pallas as pl
from jax.experimental.pallas import tpu as pltpu
from jax.sharding import PartitionSpec as P

STEPS = 1000
REACH = 256
RIM = 4
TILE = 16
LIMITS = (4, 14, 9, 7, 9, 8, 10, 2, 6, 2, 2, 3)

eps_norm = 1e-05
highest = lax.Precision.HIGHEST
bf16 = jnp.bfloat16
f32 = jnp.float32
plane_offsets = ((-1, -1), (-1, 0), (-1, 1), (0, -1), (0, 1), (1, -1), (1, 0), (1, 1))


def time_terms(timestep, w_time):
    moment = timestep[0].astype(jnp.float32)
    half_width = w_time.shape[0] // 2
    alpha_bar = jnp.cos(0.5 * math.pi * (moment + 0.5) / STEPS) ** 2
    ladder = jnp.exp(-math.log(10000.0) * jnp.arange(half_width, dtype=jnp.float32) / half_width)
    angles = moment * ladder
    features = jnp.concatenate([jnp.sin(angles), jnp.cos(angles)])
    time_raw = jnp.dot(features, w_time, precision=highest)
    return (alpha_bar, features, time_raw, jax.nn.silu(time_raw))


def mm(left, right):
    return lax.dot_general(left, right, (((1,), (0,)), ((), ())), preferred_element_type=f32)


def mm_nt(left, right):
    return lax.dot_general(left, right, (((1,), (1,)), ((), ())), preferred_element_type=f32)


def mm_tn(left, right):
    return lax.dot_general(left, right, (((0,), (0,)), ((), ())), preferred_element_type=f32)


def halves(value):
    high = value.astype(bf16)
    return high, (value - high.astype(f32)).astype(bf16)


def wide(vector):
    return jnp.concatenate([vector] * 4, axis=1)


def folded(vector):
    channels = vector.shape[1] // 4
    return sum(vector[:, y * channels : (y + 1) * channels] for y in range(4))


class Place:
    def __init__(self, sc, rows):
        self.rows = rows
        self.members = lax.axis_size("gz")
        self.member = lax.axis_index("gz")
        self.small = jnp.minimum(sc[0], sc[1])
        self.coarse = self.small >= self.members
        tiles = rows // TILE
        self.tiles = tiles
        self.stride = jnp.where(self.coarse, tiles - 1, tiles)
        self.span = REACH // self.members + 2 * RIM
        far = jnp.where(self.coarse, REACH // self.members, self.span)
        near = jnp.where(self.coarse, self.small // self.members, 1)
        self.steps = [jnp.where(sc[l] == REACH, far, near) for l in range(2)]

    def index(self, shape):
        row = lax.broadcasted_iota(jnp.int32, shape, 0)
        return lax.rem(row, TILE) * self.stride + row // TILE, row // TILE

    def own(self, shape):
        place, tile = self.index(shape)
        inside = lax.rem(place, self.span)
        near = ((inside >= RIM) & (inside < self.span - RIM)).astype(jnp.int32)
        far = (tile < self.tiles - 1).astype(jnp.int32)
        return jnp.where(self.coarse, far, near) == 1

    def pick(self, cells_z):
        shape = (self.rows, cells_z)
        return self.z_of(shape, cells_z) == lax.broadcasted_iota(jnp.int32, shape, 1)

    def z_of(self, shape, cells_z):
        place, _ = self.index(shape)
        residues = jnp.minimum(self.small, self.members)
        part, start = self.member // residues, lax.rem(self.member, residues)
        period = place // self.span
        inside = place - period * self.span - RIM + part * (REACH // self.members)
        near = start + residues * inside + period * REACH
        z = jnp.where(self.coarse, place * self.members + self.member, near)
        return lax.rem(z + 2 * cells_z, cells_z)


def build_taps(block_of, taps):
    channels = taps.shape[-1] // 2
    zero = jnp.zeros((channels, channels), bf16)
    near, far = slice(0, channels), slice(channels, 2 * channels)
    for i in range(3):
        down, here, up = (block_of(i, j) for j in range(3))
        taps[i, near, near] = here
        taps[i, far, far] = here
        taps[i, near, far] = down
        taps[i, far, near] = up
        taps[3 + i, near, near] = zero
        taps[3 + i, far, far] = zero
        taps[3 + i, near, far] = down
        taps[3 + i, far, near] = up
    for m in range(2):
        build_pair(block_of(3, m), taps, 6 + m)


def build_pair(block, target, m):
    channels = block.shape[-1]
    zero = jnp.zeros((channels, channels), bf16)
    target[m, :channels, :channels] = block
    target[m, channels:, channels:] = block
    target[m, :channels, channels:] = zero
    target[m, channels:, :channels] = zero


def taken(weights, layer):
    return lambda i, j: weights[layer, i * 3 + j]


def fetch(pairs, sems):
    copies = [pltpu.make_async_copy(one, two, sems.at[at]) for at, (one, two) in enumerate(pairs)]
    for copy in copies:
        copy.start()
    for copy in copies:
        copy.wait()


def kernel_prepare(steps, w_z, w_xy, w_point, w_in_far, gains_far, w_out_far, w_front, point, w_back, point_back,
                   lift_in, lift_out, small, steps_on, w_in, gains, w_out, sems):
    pairs = [(w_point, point), (w_in_far, w_in), (gains_far, gains), (w_out_far, w_out), (steps, steps_on)]
    for layer in range(2):
        pairs.append((w_xy.at[layer, pl.ds(0, 4)], w_front.at[layer, pl.ds(0, 4)]))
        pairs.append((w_xy.at[layer, pl.ds(4, 4)], w_front.at[layer, pl.ds(5, 4)]))
        for m, at in ((1, 4), (0, 9), (2, 10)):
            pairs.append((w_z.at[layer, m], w_front.at[layer, at]))
    fetch(pairs, sems)
    small[...] = jnp.concatenate([w_in[...], gains[...], w_out[...]], axis=0)
    for layer in range(2):
        for at in range(9):
            w_back[layer, at] = w_front[layer, 8 - at].T
        w_back[layer, 9] = w_front[layer, 10].T
        w_back[layer, 10] = w_front[layer, 9].T
        point_back[layer] = point[layer].T
    whole = spread_rows(small[0:3], 0)
    high, low = halves(whole)
    lift_in[0:32] = high
    lift_in[32:64] = high
    lift_in[64:96] = low
    lift_in[96:128] = jnp.zeros_like(low)
    high = spread_rows(small[6:9], 3).astype(bf16)
    lift_out[0:32] = high
    lift_out[32:64] = high
    lift_out[64:96] = jnp.zeros_like(high)
    lift_out[96:128] = jnp.zeros_like(high)


def spread_rows(weights, first):
    channels = weights.shape[1]
    zero = jnp.zeros((1, channels), f32)
    rows = [jnp.zeros((1, 4 * channels), f32)] * 32
    for k in range(3):
        for y in range(4):
            parts = [weights[k : k + 1] if at == y else zero for at in range(4)]
            rows[(first + k) * 4 + y] = jnp.concatenate(parts, axis=1)
    return jnp.concatenate(rows, axis=0)


def fill_rims(padded, planes):
    padded[0] = padded[planes]
    padded[planes + 1] = padded[1]


def fill_shifted(place, layer, padded, shifted, planes):
    step, stride = place.steps[layer], place.stride
    for tile in range(place.tiles):
        for way in range(2):
            at = tile - step if way == 0 else tile + step
            moved = at + TILE * stride
            source = lax.rem(moved, stride)
            turn = lax.rem(2 * TILE - moved // stride, TILE)
            rows = padded[1 : planes + 1, pl.ds(pl.multiple_of(source * TILE, TILE), TILE), :]
            rows = pltpu.roll(rows.astype(f32), turn, 1)
            shifted[way, :, tile * TILE : (tile + 1) * TILE, :] = rows.astype(bf16)


def conv_pair(padded, shifted, taps, x0, count):
    rows, lanes = padded.shape[1:]
    half, quarter = lanes // 2, lanes // 4
    totals = [None, None, None]

    def add(at, left, right):
        part = mm(left.reshape(count * rows, half), right)
        totals[at] = part if totals[at] is None else totals[at] + part

    for q in range(2):
        side = slice(q * half, (q + 1) * half)
        for i in range(3):
            add(q, padded[x0 + i : x0 + i + count, :, side], taps[i])
        for m in range(2):
            add(q, shifted[m, x0 : x0 + count, :, side], taps[6 + m])
    for i in range(3):
        add(2, padded[x0 + i : x0 + i + count, :, quarter : 3 * quarter], taps[3 + i])
    first, second, middle = totals
    first = jnp.concatenate([first[:, :quarter], first[:, quarter:] + middle[:, :quarter]], axis=1)
    second = jnp.concatenate([second[:, :quarter] + middle[:, quarter:], second[:, quarter:]], axis=1)
    return first, second


def gelu_pair(value):
    scale = math.sqrt(2.0 / math.pi)
    square = value * value
    bent = jnp.tanh(value * (scale + (scale * 0.044715) * square))
    half = 0.5 + 0.5 * bent
    result = value * half
    slope = half + result * (1.0 - half) * (2.0 * scale + (6.0 * 0.044715 * scale) * square)
    return result, slope


def members_of(parts):
    found = []
    for part in parts:
        for at in range(0, part.shape[0], 8):
            found.append(part[at : at + 8])
    return found


def merged_stats(parts, per_member):
    found = members_of(parts)
    mean = sum(one[0:1] for one in found) / (per_member * len(found))
    spread = sum(one[1:2] for one in found)
    for one in found:
        gap = one[0:1] / per_member - mean
        spread = spread + per_member * gap * gap
    return mean, lax.rsqrt(spread / (per_member * len(found)) + eps_norm)


def put_rows(ref, *vectors):
    rows = list(vectors)
    rows += [jnp.zeros((1, ref.shape[1]), f32)] * (ref.shape[0] - len(rows))
    ref[...] = jnp.concatenate(rows, axis=0)


def masked_total(mask, value):
    return folded(jnp.sum(jnp.where(mask, value, 0.0), axis=0, keepdims=True))


def layer_forward(place, layer, padded, shifted, taps, pair, w_front, wp, shift_bias, old,
                  stream, act, slope, stats, acc, per_member):
    planes, rows, lanes = stream.shape
    half = lanes // 2
    count = planes // 4
    build_taps(taken(w_front, layer), taps)
    build_pair(wp[layer], pair, 0)
    fill_rims(padded, planes)
    fill_shifted(place, layer, padded, shifted, planes)
    acc[...] = jnp.zeros_like(acc)
    bias = wide(shift_bias[layer : layer + 1, :])[:, :half]

    for x0 in range(0, planes, count):
        part = slice(x0, x0 + count)
        for q, total in enumerate(conv_pair(padded, shifted, taps, x0, count)):
            side = slice(q * half, (q + 1) * half)
            value, grad = gelu_pair(total + bias)
            act[part, :, side] = value.astype(bf16).reshape(count, rows, half)
            slope[part, :, side] = grad.astype(bf16).reshape(count, rows, half)
    for x0 in range(0, planes, count):
        part = slice(x0, x0 + count)
        for q in range(2):
            side = slice(q * half, (q + 1) * half)
            branch = mm(act[part, :, side].reshape(count * rows, half), pair[0])
            new = old[part, :, side] + branch.reshape(count, rows, half)
            stream[part, :, side] = new
            acc[:, side] += jnp.sum(new, axis=0)
    mask = place.own((rows, lanes))
    total = masked_total(mask, acc[...])
    mean = wide(total / per_member)
    spread = jnp.zeros((rows, lanes), f32)
    for x in range(planes):
        gap = stream[x] - mean
        spread = spread + gap * gap
    put_rows(stats, total, masked_total(mask, spread))


def kernel_first(cells_z, per_member, sc, near, far, amounts, lift_in, small, shift_bias, w_front, wp,
                 stream, padded, act, slope, gathered, stats, consts, mixed_own,
                 shifted, taps, pair, acc, old, source, fields):
    planes, rows, lanes = stream.shape
    channels = lanes // 4
    depth = near.shape[2]
    place = Place(sc, rows)
    keep, add = amounts[0:1], amounts[1:2]
    for at, ref in enumerate((near, far)):
        fields[at, :, 12:24] = ref[:, 12:24]
        fields[at, :, 0:12] = keep * ref[:, 0:12] + add * ref[:, 12:24]
    mixed_own[...] = fields[0, place.member // 2 * planes + lax.axis_index("gx"), 0:12]
    cell_count = float(planes * 4 * cells_z)
    comps = [
        jnp.concatenate([fields[at, :, 4 * k : 4 * k + 4, :] for at in range(2)], axis=0) for k in range(3)
    ]

    def all_sum(value):
        value = jnp.sum(jnp.sum(value, axis=0), axis=0, keepdims=True)
        return jnp.sum(value, axis=1, keepdims=True)

    means = [all_sum(comp) / cell_count for comp in comps]
    gaps = [comp - mean[None] for comp, mean in zip(comps, means)]
    for k in range(3):
        for at in range(2):
            fields[at, :, 4 * k : 4 * k + 4, :] = gaps[k][at * near.shape[0] : (at + 1) * near.shape[0]]
    covs = {}
    for j in range(3):
        for k in range(j, 3):
            covs[j, k] = all_sum(gaps[j] * gaps[k]) / cell_count
    rows_in = [small[k : k + 1, :] for k in range(3)]
    mean_c = sum(means[k] * rows_in[k] for k in range(3))
    var_c = jnp.zeros((1, channels), f32)
    for (j, k), cov in covs.items():
        var_c = var_c + (1.0 if j == k else 2.0) * cov * (rows_in[j] * rows_in[k])
    inv_c = lax.rsqrt(jnp.maximum(var_c, 0.0) + eps_norm)
    flat = [jnp.broadcast_to(value, (1, channels)) for value in means + list(covs.values())]
    put_rows(consts, mean_c, inv_c, *flat)
    blank = jnp.zeros((8, depth), f32)
    core = lax.rem(place.member, 2)
    for slab in range(cells_z // depth):
        side = core if slab % 2 == 0 else 1 - core
        at = pl.ds(pl.multiple_of((slab // 2 * 2 + side) * depth, depth), depth)
        for x in range(planes):
            high, low = halves(jnp.concatenate([fields[slab % 2, slab // 2 * planes + x], blank], axis=0))
            source[x, 0:32, at] = high
            source[x, 32:64, at] = low
            source[x, 64:96, at] = high
            source[x, 96:128, at] = jnp.zeros_like(high)
    pick = place.pick(cells_z).astype(f32).astype(bf16)
    scale = wide(inv_c * small[3:4, :])
    for x in range(planes):
        gathered[x] = mm_nt(pick, source[x]).astype(bf16)
    for x0 in range(0, planes, planes // 2):
        part = slice(x0, x0 + planes // 2)
        value = mm(gathered[part].reshape(planes // 2 * rows, 128), lift_in[...])
        unit = (value * scale).astype(bf16).reshape(planes // 2, rows, lanes)
        old[part] = value.reshape(planes // 2, rows, lanes)
        padded[x0 + 1 : x0 + 1 + planes // 2] = unit
    layer_forward(place, 0, padded, shifted, taps, pair, w_front, wp, shift_bias, old, stream,
                  act, slope, stats, acc, per_member)


def kernel_second(per_member, sc, *refs):
    parts, refs = refs[:4], refs[4:]
    (old, small, shift_bias, w_front, wp, stream, padded, act, slope, stats, consts,
     shifted, taps, pair, acc) = refs
    planes, rows, _ = stream.shape
    place = Place(sc, rows)
    mean, inverse = merged_stats(parts, per_member)
    put_rows(consts, mean, inverse)
    mean_w, scale = wide(mean), wide(inverse * small[4:5, :])
    for x in range(planes):
        padded[x + 1] = ((old[x] - mean_w) * scale).astype(bf16)
    layer_forward(place, 1, padded, shifted, taps, pair, w_front, wp, shift_bias, old, stream,
                  act, slope, stats, acc, per_member)


def kernel_out(per_member, sc, *refs):
    parts, refs = refs[:4], refs[4:]
    stream, small, gathered, lift_out, prediction, misfit, sums, w_out_raw, consts, unit = refs
    planes, rows, lanes = stream.shape
    place = Place(sc, rows)
    mean, inverse = merged_stats(parts, per_member)
    put_rows(consts, mean, inverse)
    mean_w, inv_w, gain_w = wide(mean), wide(inverse), wide(small[5:6, :])
    scale = inv_w * gain_w
    for x in range(planes):
        unit[x] = ((stream[x] - mean_w) * scale).astype(bf16)
    row = lax.broadcasted_iota(jnp.int32, (128, 128), 0)
    col = lax.broadcasted_iota(jnp.int32, (128, 128), 1)
    slot = lax.rem(col, 32)
    used = (col < 64) & (slot >= 12) & (slot < 24)
    take = (used & ((row == slot) | (row == slot + 32))).astype(f32).astype(bf16)
    total = mm_nt(unit[...].reshape(planes * rows, lanes), lift_out[...])
    noise = mm(gathered[...].reshape(planes * rows, 128), take)
    gap = total - noise
    high, low = halves(gap)
    lane = lax.broadcasted_iota(jnp.int32, gap.shape, 1)
    both = jnp.where(lane < 32, high.astype(f32), low.astype(f32)).astype(bf16)
    misfit[...] = both.reshape(planes, rows, 128)
    for x in range(planes):
        @pl.when(lax.axis_index("gx") == x)
        def _(x=x):
            prediction[...] = total[x * rows : (x + 1) * rows]
    plain = jnp.zeros((rows, lanes), f32)
    cross = jnp.zeros((rows, lanes), f32)
    for x0 in range(0, planes, planes // 2):
        part = slice(x0 * rows, (x0 + planes // 2) * rows)
        d_out = mm(both[part], lift_out[...]).reshape(planes // 2, rows, lanes)
        for x in range(planes // 2):
            plain = plain + d_out[x]
            cross = cross + d_out[x] * ((stream[x0 + x] - mean_w) * inv_w)
    own = place.own((rows, 128))
    kept = jnp.concatenate([jnp.where(own, misfit[x].astype(f32), 0.0) for x in range(planes)], axis=0)
    raw = mm_tn(kept.astype(bf16), unit[...].reshape(planes * rows, lanes))
    mask = place.own((rows, lanes))
    put_rows(sums, masked_total(mask, plain), masked_total(mask, cross))
    put_rows(w_out_raw, *by_component(raw[0:32] + raw[32:64], 3))


def by_component(raw, first):
    channels = raw.shape[1] // 4
    found = []
    for k in range(first, first + 3):
        found.append(
            sum(raw[k * 4 + y : k * 4 + y + 1, y * channels : (y + 1) * channels] for y in range(4))
        )
    return found


def branch_backward(planes, d_stream_of, pair, slope, padded, scot, bias_acc):
    rows, lanes = padded.shape[1:]
    half = lanes // 2
    count = planes // 2

    for x0 in range(0, planes, count):
        part = slice(x0, x0 + count)
        for x in range(x0, x0 + count):
            scot[x] = d_stream_of(x).astype(bf16)
        for q in range(2):
            side = slice(q * half, (q + 1) * half)
            cot = scot[part, :, side].reshape(count * rows, half)
            d_act = mm(cot, pair[0]).reshape(count, rows, half)
            pre = (d_act * slope[part, :, side].astype(f32)).astype(bf16)
            padded[x0 + 1 : x0 + 1 + count, :, side] = pre
            bias_acc[:, side] += jnp.sum(pre.astype(f32), axis=0)


def weight_grads(place, planes, padded, shifted, scot, normed, act, keep, give, taps_all, share):
    rows, lanes = padded.shape[1:]
    channels = lanes // 4
    wide_share = 4 * share
    row = lax.broadcasted_iota(jnp.int32, (lanes, wide_share), 0)
    col = lax.broadcasted_iota(jnp.int32, (lanes, wide_share), 1)
    hit = (row // channels == col // share) & (
        lax.rem(row, channels) == lax.rem(col, share) + lax.axis_index("gx") * share
    )
    choose = hit.astype(f32).astype(bf16)
    mask = jnp.concatenate([place.own((rows, wide_share))] * planes, axis=0)

    def turned(source):
        got = mm(source.reshape(planes * rows, lanes), choose)
        return jnp.where(mask, got, 0.0).astype(bf16)

    def add_blocks(raw, j):
        return sum(
            raw[(y + j) * share : (y + j + 1) * share, y * channels : (y + 1) * channels]
            for y in range(4)
            if 0 <= y + j < 4
        )

    left = turned(normed[1 : planes + 1])
    for i in range(3):
        raw = mm_tn(left, padded[2 - i : 2 - i + planes].reshape(planes * rows, lanes))
        for j in range(3):
            taps_all[i * 3 + j] = add_blocks(raw, j - 1)
    for m in range(2):
        raw = mm_tn(left, shifted[1 - m].reshape(planes * rows, lanes))
        taps_all[9 + m] = add_blocks(raw, 0)
    raw = mm_tn(turned(act[...]), scot[...].reshape(planes * rows, lanes))
    taps_all[11] = add_blocks(raw, 0)
    odd, half = lax.rem(place.member, 2), keep.shape[0]
    keep[...] = taps_all[pl.ds(odd * half, half)]
    give[...] = taps_all[pl.ds((1 - odd) * half, half)]


def conv_backward(planes, padded, shifted, taps, emit):
    count = planes // 4

    for x0 in range(0, planes, count):
        for q, total in enumerate(conv_pair(padded, shifted, taps, x0, count)):
            emit(x0, count, q, total)


def kernel_back_second(cell_count, sc, *refs):
    parts, refs = refs[:4], refs[4:]
    (stream, out_consts, small, misfit, lift_out, slope, normed, w_back, point_back,
     d_stream, d_normed, sums, padded, shifted, scot,
     taps, pair, acc, acc2) = refs
    planes, rows, lanes = stream.shape
    half = lanes // 2
    place = Place(sc, rows)
    sums_out = sum(members_of(parts))
    gain_w = wide(small[5:6, :])
    mean_w, inv_w = wide(out_consts[0:1]), wide(out_consts[1:2])
    m_plain = gain_w * wide(sums_out[0:1]) / cell_count
    m_cross = gain_w * wide(sums_out[1:2]) / cell_count
    build_pair(point_back[1], pair, 0)
    build_taps(taken(w_back, 1), taps)
    acc[...] = jnp.zeros_like(acc)

    def d_stream_of(x):
        d_out = mm(misfit[x], lift_out[...])
        white = (stream[x] - mean_w) * inv_w
        value = inv_w * (gain_w * d_out - m_plain - white * m_cross)
        d_stream[x] = value
        return value

    branch_backward(planes, d_stream_of, pair, slope, padded, scot, acc)
    mask = place.own((rows, lanes))
    s_bias = masked_total(mask, acc[...])
    acc[...] = jnp.zeros_like(acc)
    acc2[...] = jnp.zeros_like(acc2)
    fill_rims(padded, planes)
    fill_shifted(place, 1, padded, shifted, planes)

    def emit(x0, count, q, value):
        side = slice(q * half, (q + 1) * half)
        value = value.reshape(count, rows, half)
        d_normed[x0 : x0 + count, :, side] = value
        acc[:, side] += jnp.sum(value, axis=0)
        acc2[:, side] += jnp.sum(value * normed[x0 + 1 : x0 + 1 + count, :, side].astype(f32), axis=0)

    conv_backward(planes, padded, shifted, taps, emit)
    s_plain = masked_total(mask, acc[...])
    s_cross = masked_total(mask, acc2[...]) / small[4:5, :]
    put_rows(sums, s_plain, s_cross, s_bias)


def kernel_weights_second(share, sc, padded, shifted, scot, normed, act, keep, give, taps_all):
    planes, rows, _ = scot.shape
    weight_grads(Place(sc, rows), planes, padded, shifted, scot, normed, act, keep, give, taps_all, share)


def kernel_back_first(share, cell_count, sc, *refs):
    parts, refs = refs[:4], refs[4:]
    (consts, d_next, d_normed, normed_next, small, act, slope, normed, point_back,
     d_stream, sums, keep, give, padded, shifted,
     pair, acc, scot, taps_all) = refs
    planes, rows, lanes = d_next.shape
    place = Place(sc, rows)
    sums_in = sum(members_of(parts))
    gain_w = wide(small[4:5, :])
    inv_w = wide(consts[1:2])
    m_plain = gain_w * wide(sums_in[0:1]) / cell_count
    m_cross = wide(sums_in[1:2]) / cell_count
    build_pair(point_back[0], pair, 0)
    acc[...] = jnp.zeros_like(acc)

    def d_stream_of(x):
        back = gain_w * d_normed[x] - m_plain - normed_next[x + 1].astype(f32) * m_cross
        value = d_next[x] + inv_w * back
        d_stream[x] = value
        return value

    branch_backward(planes, d_stream_of, pair, slope, padded, scot, acc)
    put_rows(sums, masked_total(place.own((rows, lanes)), acc[...]))
    fill_rims(padded, planes)
    fill_shifted(place, 0, padded, shifted, planes)
    weight_grads(place, planes, padded, shifted, scot, normed, act, keep, give, taps_all, share)


def kernel_last(depth, sc, padded, shifted, d_stream, normed, small, consts, gathered, lift_in, w_back,
                prediction, sums_bias, out_raw, ready0, ready1, own_out, out_1, out_2, out_3,
                taps, acc, acc2, high, low):
    planes, rows, lanes = d_stream.shape
    half = lanes // 2
    place = Place(sc, rows)
    build_taps(taken(w_back, 0), taps)
    acc[...] = jnp.zeros_like(acc)
    acc2[...] = jnp.zeros_like(acc2)
    scale = wide(consts[1:2] * small[3:4, :])

    def emit(x0, count, q, value):
        side = slice(q * half, (q + 1) * half)
        part = slice(x0, x0 + count)
        value = value.reshape(count, rows, half)
        acc[:, side] += jnp.sum(value, axis=0)
        acc2[:, side] += jnp.sum(value * normed[x0 + 1 : x0 + 1 + count, :, side].astype(f32), axis=0)
        full = d_stream[part, :, side] + value * scale[:, side]
        first, second = halves(full)
        high[part, :, side] = first
        low[part, :, side] = second

    conv_backward(planes, padded, shifted, taps, emit)
    mask = place.own((rows, lanes))
    s_plain = masked_total(mask, acc[...])
    s_cross = masked_total(mask, acc2[...]) / small[3:4, :]
    own = place.own((rows, 128))
    kept = jnp.concatenate([jnp.where(own, gathered[x].astype(f32), 0.0) for x in range(planes)], axis=0)
    kept = kept.astype(bf16)
    raw = mm_tn(kept, high[...].reshape(planes * rows, lanes))
    raw_low = mm_tn(kept, low[...].reshape(planes * rows, lanes))
    in_raw = by_component(raw[0:32] + raw[32:64] + raw_low[0:32], 0)
    blank = jnp.zeros((1, s_plain.shape[1]), f32)
    tail = jnp.concatenate([s_plain, s_cross] + [blank] * 6 + in_raw + [blank] * 5, axis=0)
    tail = jnp.concatenate([tail, sums_bias[...], out_raw[...]], axis=0)
    here = lax.axis_index("gx")
    lane = lax.broadcasted_iota(jnp.int32, (rows, 128), 1)
    field = mm_nt(high[here], lift_in[...]) + jnp.where(lane < 32, mm_nt(low[here], lift_in[...]), 0.0)
    field = jnp.where((lane >= 32) & (lane < 64), 0.0, field)
    field = field + jnp.where((lane >= 12) & (lane < 24), prediction[...], 0.0)
    cells_z = depth * place.members
    whole = place.z_of((rows, depth), cells_z)
    column = lax.broadcasted_iota(jnp.int32, (rows, depth), 1)
    mask = place.own((rows, depth))
    first, second = halves(field)
    for bit, target in enumerate((own_out, out_1, out_2, out_3)):
        there = lax.bitwise_xor(place.member, bit)
        pick = ((whole == column + there * depth) & mask).astype(f32).astype(bf16)
        out = mm_tn(first, pick) + mm_tn(second, pick)
        target[0:32] = out[0:32] + out[64:96]
        target[32:64] = tail


def call(kernel, outs, scratch, flops, limit, *args, scalars=True, scalar_out=0, ready=(), far=()):
    spec = pl.BlockSpec(memory_space=pltpu.VMEM)
    specs = [pl.BlockSpec(memory_space=pltpu.SMEM)] * scalars + [spec] * (len(args) - scalars)
    for at in ready:
        specs[at] = pl.BlockSpec(memory_space=pl.ANY)
    args = list(args)
    for at in far:
        specs[at] = pl.BlockSpec(memory_space=pltpu.HBM)
        args[at] = pltpu.with_memory_space_constraint(args[at], pltpu.HBM)
    smem = pl.BlockSpec(memory_space=pltpu.SMEM)
    return pl.pallas_call(
        kernel,
        out_shape=[jax.ShapeDtypeStruct(shape, dtype) for shape, dtype in outs],
        in_specs=specs,
        out_specs=[spec] * (len(outs) - scalar_out) + [smem] * scalar_out,
        scratch_shapes=[pltpu.VMEM(*one) if isinstance(one, tuple) else one for one in scratch],
        compiler_params=pltpu.CompilerParams(vmem_limit_bytes=limit * 2**20),
        cost_estimate=pl.CostEstimate(flops=flops, bytes_accessed=2**23, transcendentals=0),
    )(*args)


def swapped(value, axis, bit):
    count = lax.axis_size(axis)
    return lax.ppermute(value, axis, [(i, i ^ bit) for i in range(count)])


def group_parts(value):
    return (value,) + tuple(swapped(value, "gz", bit) for bit in (1, 2, 3))


def kernel_spread(first, first_far, second, second_far, ready, spread):
    taps, share, channels = first.shape
    for layer, (own, other) in enumerate(((first, first_far), (second, second_far))):
        value = (own[...] + other[...]).reshape(taps * share, channels).astype(bf16)
        for part in range(spread.shape[0]):
            spread[part, layer * taps * share : (layer + 1) * taps * share] = value


def kernel_layout(scale, share, near, far, grad_w_z, grad_w_xy, grad_w_point):
    groups = near.shape[0]
    taps = near.shape[1] // share // 2
    odd = lax.rem(lax.axis_index("gz"), 2) == 1
    for layer in range(2):
        for tap in range(taps):
            at = (layer * taps + tap) * share
            one = near[:, at : at + share].astype(f32) * scale
            two = far[:, at : at + share].astype(f32) * scale
            for side in range(2):
                value = jnp.where(odd, one if side else two, two if side else one)
                value = value.reshape(groups * share, value.shape[2])
                whole = side * taps + tap
                if whole == 4:
                    grad_w_z[layer, 1] = value
                elif whole < 9:
                    grad_w_xy[layer, whole - (whole > 4)] = value
                elif whole < 11:
                    grad_w_z[layer, 2 * (whole - 9)] = value
                else:
                    grad_w_point[layer] = value


def kernel_tail(cell_count, inv_area, *refs):
    tails, parts1, parts2, refs = refs[:4], refs[4:8], refs[8:12], refs[12:]
    (consts, small, mixed, features, time_raw,
     prediction, field_grad, grad_w_in, grad_w_time, grad_biases, grad_gains, grad_w_out) = refs
    tail = sum(ref[...] for ref in tails)
    s1, s2 = sum(ref[...] for ref in parts1), sum(ref[...] for ref in parts2)
    inverse = consts[1:2]
    m_plain = inverse * (small[3:4] * tail[32:33] / cell_count)
    m_cross = inverse * inverse * (small[3:4] * tail[33:34] / cell_count)
    at = {(0, 0): 5, (0, 1): 6, (0, 2): 7, (1, 1): 8, (1, 2): 9, (2, 2): 10}
    rows_in = [small[k : k + 1] for k in range(3)]
    depth = mixed.shape[1]
    gaps = [mixed[4 * k : 4 * k + 4] - consts[2 + k : 3 + k, 0:1] for k in range(3)]
    for k in range(3):
        offset = jnp.sum(rows_in[k] * m_plain, axis=1, keepdims=True)
        value = tail[4 * k : 4 * k + 4] - offset
        cross = jnp.zeros_like(m_plain)
        for j in range(3):
            mix = jnp.sum(rows_in[k] * m_cross * rows_in[j], axis=1, keepdims=True)
            value = value - mix * gaps[j]
            row = at[min(j, k), max(j, k)]
            cross = cross + consts[row : row + 1] * rows_in[j]
        field_grad[k, 0] = value
        prediction[k, 0] = tail[12 + 4 * k : 16 + 4 * k]
        in_sum = tail[40 + k : 41 + k] - cell_count * (m_cross * cross)
        grad_w_in[k : k + 1] = inv_area * in_sum
    bias0, bias1 = tail[48:49], s1[2:3]
    grad_biases[...] = inv_area * jnp.concatenate([bias0, bias1], axis=0)
    grad_gains[...] = inv_area * jnp.concatenate([tail[33:34], s1[1:2], s2[1:2]], axis=0)
    grad_w_out[...] = inv_area * tail[56:59]
    raw = time_raw[...]
    gate = 1.0 / (1.0 + jnp.exp(-raw))
    back = (bias0 + bias1) * (gate * (1.0 + raw * (1.0 - gate)))
    spread = jnp.broadcast_to(features[...], grad_w_time.shape).T
    grad_w_time[...] = inv_area * (spread * back)


def per_device_grouped(clean_field, noise_field, timestep, dilations, w_in, w_time, w_z, w_xy, w_point,
                       biases, norm_gains, w_out):
    members, groups = lax.axis_size("gz"), lax.axis_size("gx")
    depth = clean_field.shape[3]
    planes, cells_z = groups, depth * members
    channels = w_in.shape[1]
    lanes = 4 * channels
    rows = (cells_z // REACH) * (REACH // members + 2 * RIM)
    share = channels // groups
    per_member = float(planes * 4 * depth)
    cell_count = per_member * members
    inv_area = 4.0 / cell_count

    alpha_bar, features, time_raw, time_code = time_terms(timestep, w_time)
    parts = members // 2 * groups
    block = jnp.concatenate([clean_field, noise_field], axis=0).reshape(24, depth)
    block = jnp.broadcast_to(block[None], (parts, 24, depth))
    amounts = jnp.stack([jnp.sqrt(alpha_bar), jnp.sqrt(1.0 - alpha_bar)])
    amounts = jnp.broadcast_to(amounts[:, None], (2, depth))
    same_core = [[m * groups + g for m in range(core, members, 2) for g in range(groups)] for core in range(2)]
    near = lax.all_to_all(block, ("gz", "gx"), 0, 0, axis_index_groups=same_core)
    far = swapped(near, "gz", 1)
    shift_bias = biases + time_code

    big = (planes, rows, lanes)
    vec = ((8, channels), f32)
    thin = ((planes, rows, 128), bf16)
    lift = ((128, lanes), bf16)
    conv_scratch = [
        ((planes + 2, rows, lanes), bf16),
        ((2,) + big, bf16),
        ((8, lanes // 2, lanes // 2), bf16),
    ]
    pair = ((1, lanes // 2, lanes // 2), bf16)
    flat = ((rows, lanes), f32)
    grad_out = ((6, share, channels), f32)

    taps_out, point_out = ((2, 11, channels, channels), bf16), ((2, channels, channels), bf16)
    w_front, point, w_back, point_back, lift_in, lift_out, small, steps_on = call(
        kernel_prepare,
        [taps_out, point_out, taps_out, point_out, lift, lift, ((9, channels), f32), ((2,), jnp.int32)],
        [((3, channels), f32), ((3, channels), f32), ((3, channels), f32), pltpu.SemaphoreType.DMA((15,))],
        10**8, LIMITS[0], dilations, w_z, w_xy, w_point, w_in, norm_gains, w_out.astype(f32),
        scalar_out=1,
        far=tuple(range(7)),
    )
    stream1, normed0, act0, slope0, gathered, stats1, consts0, mixed_own = call(
        functools.partial(kernel_first, cells_z, per_member),
        [(big, f32), conv_scratch[0], (big, bf16), (big, bf16), thin, vec, ((16, channels), f32), ((12, depth), f32)],
        conv_scratch[1:] + [pair, flat, (big, f32), ((planes, 128, cells_z), bf16), ((2, parts, 24, depth), f32)],
        4 * 10**9, LIMITS[1],
        steps_on, near, far, amounts, lift_in, small, shift_bias, w_front, point,
    )
    stream2, normed1, act1, slope1, stats2, consts1 = call(
        functools.partial(kernel_second, per_member),
        [(big, f32), conv_scratch[0], (big, bf16), (big, bf16), vec, vec],
        conv_scratch[1:] + [pair, flat],
        4 * 10**9, LIMITS[2],
        steps_on, *group_parts(stats1), stream1, small, shift_bias, w_front, point,
    )
    prediction, misfit, sums2, out_raw, consts2 = call(
        functools.partial(kernel_out, per_member),
        [((rows, 128), f32), thin, vec, vec, vec],
        [(big, bf16)],
        10**9, LIMITS[3],
        steps_on, *group_parts(stats2), stream2, small, gathered, lift_out,
    )
    parts2 = group_parts(sums2)
    d_stream2, d_normed1, sums1, rimmed1, shifted1, scot1 = call(
        functools.partial(kernel_back_second, cell_count),
        [(big, f32), (big, f32), vec] + conv_scratch[:2] + [(big, bf16)],
        conv_scratch[2:] + [pair, flat, flat],
        6 * 10**9, LIMITS[4],
        steps_on, *parts2, stream2, consts2, small, misfit, lift_out, slope1, normed1,
        w_back, point_back,
    )
    parts1 = group_parts(sums1)
    keep1, give1 = call(
        functools.partial(kernel_weights_second, share),
        [grad_out, grad_out], [((12, share, channels), f32)], 2 * 10**9, LIMITS[8],
        steps_on, rimmed1, shifted1, scot1, normed1, act1,
    )
    d_stream1, sums_b0, keep0, give0, rimmed0, shifted0 = call(
        functools.partial(kernel_back_first, share, cell_count),
        [(big, f32), vec, grad_out, grad_out] + conv_scratch[:2],
        [pair, flat, (big, bf16), ((12, share, channels), f32)],
        4 * 10**9, LIMITS[5],
        steps_on, *parts1, consts1, d_stream2, d_normed1, normed1, small, act0, slope0, normed0,
        point_back,
    )
    chip0 = keep0 + swapped(give0, "gz", 1)
    chip1 = keep1 + swapped(give1, "gz", 1)
    last = call(
        functools.partial(kernel_last, depth),
        [((64, channels), f32)] * members,
        conv_scratch[2:] + [flat, flat, (big, bf16), (big, bf16)],
        4 * 10**9, LIMITS[6],
        steps_on, rimmed0, shifted0, d_stream1, normed0, small, consts0, gathered, lift_in, w_back, prediction,
        sums_b0, out_raw, chip0, chip1, ready=(13, 14),
    )
    spread = call(
        kernel_spread, [((groups, 12 * share, channels), bf16)], [], 10**5, LIMITS[9],
        chip0, swapped(chip0, "gz", 2), chip1, swapped(chip1, "gz", 2), last[0], scalars=False, ready=(4,),
    )[0]
    near_grads = lax.all_to_all(spread, "gx", 0, 0)

    prediction, field_grad, grad_w_in, grad_w_time, grad_biases, grad_gains, grad_w_out = call(
        functools.partial(kernel_tail, cell_count, inv_area),
        [(clean_field.shape, f32), (clean_field.shape, f32), ((3, channels), f32), (w_time.shape, f32),
         ((2, channels), f32), ((3, channels), f32), ((3, channels), f32)],
        [], 10**6, LIMITS[10],
        last[0], *(swapped(last[bit], "gz", bit) for bit in (1, 2, 3)), *parts1, *parts2, consts0, small,
        mixed_own, features[None], time_raw[None], scalars=False,
    )
    tied, _ = lax.optimization_barrier((near_grads, field_grad))
    far_grads = swapped(tied, "gz", 1)
    grad_w_z, grad_w_xy, grad_w_point = call(
        functools.partial(kernel_layout, inv_area, share),
        [(w_z.shape, f32), (w_xy.shape, f32), (w_point.shape, f32)],
        [], 10**6, LIMITS[11], near_grads, far_grads, scalars=False,
    )
    return (
        prediction,
        field_grad,
        grad_w_in,
        grad_w_time,
        grad_w_z,
        grad_w_xy,
        grad_w_point,
        grad_biases,
        grad_gains,
        grad_w_out,
    )


def padded_2(cells, sides, width):
    for axis, dim in sides:
        count = lax.axis_size(axis)
        head = lax.slice_in_dim(cells, 0, width, axis=dim)
        tail = lax.slice_in_dim(cells, cells.shape[dim] - width, cells.shape[dim], axis=dim)
        cells = jnp.concatenate(
            [
                lax.ppermute(tail, axis, [(i, (i + 1) % count) for i in range(count)]),
                cells,
                lax.ppermute(head, axis, [((i + 1) % count, i) for i in range(count)]),
            ],
            axis=dim,
        )
    return cells


def passed_along(value, axis, steps):
    count = lax.axis_size(axis)
    pairs = [(source, (source + steps) % count) for source in range(count)]
    return lax.ppermute(value, axis, pairs)


def contract_cells(left, right):
    return lax.dot_general(
        left, right, (((0, 1, 2), (0, 1, 2)), ((), ())), preferred_element_type=jnp.float32
    )


def plane_tap(padded, shift_x, shift_y, rows_x, rows_y):
    return padded[1 + shift_x : 1 + shift_x + rows_x, 1 + shift_y : 1 + shift_y + rows_y]


def plane_pad(source):
    rimmed = padded_2(source, (("gx", 0),), 1)
    return jnp.pad(rimmed, ((0, 0), (1, 1), (0, 0), (0, 0)))


def slab_windows(source, dilation):
    slab_depth = source.shape[2]
    above = passed_along(source, "gz", -1)
    above_far = passed_along(source, "gz", -2)
    below = passed_along(source, "gz", 1)
    below_far = passed_along(source, "gz", 2)
    ahead_rows = jnp.concatenate([source, above, above_far], axis=2)
    behind_rows = jnp.concatenate([below_far, below, source], axis=2)
    upper = lax.dynamic_slice_in_dim(ahead_rows, dilation, slab_depth, 2)
    lower = lax.dynamic_slice_in_dim(behind_rows, 2 * slab_depth - dilation, slab_depth, 2)
    return (lower, upper)


def normalize(hidden, gains, cell_count):
    average = lax.psum(jnp.sum(hidden, axis=(0, 1, 2)), ("gz", "gx")) / cell_count
    centered = hidden - average
    spread = lax.psum(jnp.sum(centered * centered, axis=(0, 1, 2)), ("gz", "gx")) / cell_count
    inverse_std = lax.rsqrt(spread + eps_norm)
    whitened = (hidden - average) * inverse_std
    return ((whitened * gains).astype(jnp.bfloat16), whitened, inverse_std)


def norm_back(d_normed, whitened, inverse_std, gains, cell_count):
    scaled = d_normed * gains
    sum_grad, sum_cross = lax.psum(
        (jnp.sum(scaled, axis=(0, 1, 2)), jnp.sum(scaled * whitened, axis=(0, 1, 2))), ("gz", "gx")
    )
    d_hidden = inverse_std * (scaled - sum_grad / cell_count - whitened * (sum_cross / cell_count))
    return (d_hidden, jnp.sum(d_normed * whitened, axis=(0, 1, 2)))


def conv_forward(normed, dilation, weights_z, weights_xy):
    rows_x, rows_y = (normed.shape[0], normed.shape[1])
    lower, upper = slab_windows(normed, dilation)
    padded = plane_pad(normed)
    summed = jnp.dot(lower, weights_z[0], preferred_element_type=jnp.float32)
    summed = summed + jnp.dot(normed, weights_z[1], preferred_element_type=jnp.float32)
    summed = summed + jnp.dot(upper, weights_z[2], preferred_element_type=jnp.float32)
    for tap_number, (shift_x, shift_y) in enumerate(plane_offsets):
        summed = summed + jnp.dot(
            plane_tap(padded, shift_x, shift_y, rows_x, rows_y),
            weights_xy[tap_number],
            preferred_element_type=jnp.float32,
        )
    return summed


def conv_backward_split(pre_cot, normed, dilation, weights_z, weights_xy):
    rows_x, rows_y = (normed.shape[0], normed.shape[1])
    lower_cot, upper_cot = slab_windows(pre_cot, dilation)
    padded_cot = plane_pad(pre_cot)
    d_normed = jnp.dot(upper_cot, weights_z[0].T, preferred_element_type=jnp.float32)
    d_normed = d_normed + jnp.dot(pre_cot, weights_z[1].T, preferred_element_type=jnp.float32)
    d_normed = d_normed + jnp.dot(lower_cot, weights_z[2].T, preferred_element_type=jnp.float32)
    xy_terms = []
    for tap_number, (shift_x, shift_y) in enumerate(plane_offsets):
        shifted = plane_tap(padded_cot, -shift_x, -shift_y, rows_x, rows_y)
        d_normed = d_normed + jnp.dot(
            shifted, weights_xy[tap_number].T, preferred_element_type=jnp.float32
        )
        xy_terms.append(contract_cells(normed, shifted))
    z_terms = jnp.stack(
        [
            contract_cells(normed, upper_cot),
            contract_cells(normed, pre_cot),
            contract_cells(normed, lower_cot),
        ]
    )
    return (d_normed, z_terms, jnp.stack(xy_terms))


def per_device_split(
    clean_field,
    noise_field,
    timestep,
    dilations,
    w_in,
    w_time,
    w_z,
    w_xy,
    w_point,
    biases,
    norm_gains,
    w_out,
):
    layer_total = w_z.shape[0]
    rows_x, rows_y, slab_depth = (clean_field.shape[1], clean_field.shape[2], clean_field.shape[3])
    plane_cells = rows_x * lax.axis_size("gx") * slab_depth * lax.axis_size("gz")
    cell_count = float(plane_cells * rows_y)
    inv_area = 1.0 / plane_cells
    alpha_bar, features, time_raw, time_code = time_terms(timestep, w_time)
    noisy = jnp.sqrt(alpha_bar) * clean_field + jnp.sqrt(1.0 - alpha_bar) * noise_field
    stream = jnp.einsum("kxyz,kc->xyzc", noisy, w_in, precision=highest)
    saved = []
    for which_layer in range(layer_total):
        normed, whitened, inverse_std = normalize(stream, norm_gains[which_layer], cell_count)
        pre_act = conv_forward(normed, dilations[which_layer], w_z[which_layer], w_xy[which_layer])
        pre_act = pre_act + biases[which_layer] + time_code
        activated = jax.nn.gelu(pre_act).astype(jnp.bfloat16)
        saved.append((normed, whitened, inverse_std, pre_act, activated))
        stream = stream + jnp.dot(
            activated, w_point[which_layer], preferred_element_type=jnp.float32
        )
    out_normed, out_white, out_inverse = normalize(stream, norm_gains[layer_total], cell_count)
    prediction = jnp.einsum("xyzc,kc->kxyz", out_normed, w_out, preferred_element_type=jnp.float32)
    misfit = prediction - noise_field
    d_out = jnp.einsum("kxyz,kc->xyzc", misfit, w_out.astype(jnp.float32), precision=highest)
    out_raw = jnp.einsum(
        "kxyz,xyzc->kc", misfit, out_normed, precision=highest, preferred_element_type=jnp.float32
    )
    d_stream, out_gain_raw = norm_back(
        d_out, out_white, out_inverse, norm_gains[layer_total], cell_count
    )
    z_list, xy_list, point_list, bias_list, gain_list = ([], [], [], [], [])
    for which_layer in reversed(range(layer_total)):
        normed, whitened, inverse_std, pre_act, activated = saved[which_layer]
        stream_cot = d_stream.astype(jnp.bfloat16)
        point_raw = contract_cells(activated, stream_cot)
        d_act = jnp.dot(stream_cot, w_point[which_layer].T, preferred_element_type=jnp.float32)
        gelu_back = jax.vjp(jax.nn.gelu, pre_act)[1]
        pre_cot = gelu_back(d_act)[0].astype(jnp.bfloat16)
        bias_raw = jnp.sum(pre_cot, axis=(0, 1, 2), dtype=jnp.float32)
        d_normed, z_raw, xy_raw = conv_backward_split(
            pre_cot, normed, dilations[which_layer], w_z[which_layer], w_xy[which_layer]
        )
        d_back, gain_raw = norm_back(
            d_normed, whitened, inverse_std, norm_gains[which_layer], cell_count
        )
        d_stream = d_stream + d_back
        z_list.insert(0, z_raw)
        xy_list.insert(0, xy_raw)
        point_list.insert(0, point_raw)
        bias_list.insert(0, bias_raw)
        gain_list.insert(0, gain_raw)
    field_grad = jnp.einsum("xyzc,kc->kxyz", d_stream, w_in, precision=highest)
    in_raw = jnp.einsum("kxyz,xyzc->kc", noisy, d_stream, precision=highest)
    z_all, xy_all, point_all, bias_all, gain_all, in_raw, out_raw = lax.psum(
        (
            jnp.stack(z_list),
            jnp.stack(xy_list),
            jnp.stack(point_list),
            jnp.stack(bias_list),
            jnp.stack(gain_list + [out_gain_raw]),
            in_raw,
            out_raw,
        ),
        ("gz", "gx"),
    )
    time_back = jax.vjp(jax.nn.silu, time_raw)[1](jnp.sum(bias_all, axis=0))[0]
    grad_w_time = inv_area * jnp.outer(features, time_back)
    return (
        prediction,
        field_grad,
        inv_area * in_raw,
        grad_w_time,
        inv_area * z_all,
        inv_area * xy_all,
        inv_area * point_all,
        inv_area * bias_all,
        inv_area * gain_all,
        inv_area * out_raw,
    )


def per_device(*args):
    members, groups = lax.axis_size("gz"), lax.axis_size("gx")
    _, rows_x, rows_y, depth = args[0].shape
    small = rows_x == 1 and rows_y == 4 and members == 4 and groups == 8 and depth * members == 2 * REACH
    return per_device_grouped(*args) if small else per_device_split(*args)


def solution(mesh):
    return jax.shard_map(
        per_device,
        mesh=mesh,
        in_specs=(
            P(None, "gx", None, "gz"),
            P(None, "gx", None, "gz"),
            P(),
            P(),
            P(),
            P(),
            P(),
            P(),
            P(),
            P(),
            P(),
            P(),
        ),
        out_specs=(
            P(None, "gx", None, "gz"),
            P(None, "gx", None, "gz"),
            P(),
            P(),
            P(),
            P(),
            P(),
            P(),
            P(),
            P(),
        ),
        check_vma=False,
    )
```

```python
import functools
import math

import jax
import jax.numpy as jnp
from jax import lax
from jax.experimental import pallas as pl
from jax.experimental.pallas import tpu as pltpu
from jax.sharding import PartitionSpec as P

STEPS = 1000
REACH = 256
RIM = 4
TILE = 16
LIMITS = (4, 14, 9, 7, 9, 8, 10, 2, 6, 2, 2, 3)

eps_norm = 1e-05
highest = lax.Precision.HIGHEST
bf16 = jnp.bfloat16
f32 = jnp.float32
plane_offsets = ((-1, -1), (-1, 0), (-1, 1), (0, -1), (0, 1), (1, -1), (1, 0), (1, 1))


def time_terms(timestep, w_time):
    moment = timestep[0].astype(jnp.float32)
    half_width = w_time.shape[0] // 2
    alpha_bar = jnp.cos(0.5 * math.pi * (moment + 0.5) / STEPS) ** 2
    ladder = jnp.exp(-math.log(10000.0) * jnp.arange(half_width, dtype=jnp.float32) / half_width)
    angles = moment * ladder
    features = jnp.concatenate([jnp.sin(angles), jnp.cos(angles)])
    time_raw = jnp.dot(features, w_time, precision=highest)
    return (alpha_bar, features, time_raw, jax.nn.silu(time_raw))


def mm(left, right):
    return lax.dot_general(left, right, (((1,), (0,)), ((), ())), preferred_element_type=f32)


def mm_nt(left, right):
    return lax.dot_general(left, right, (((1,), (1,)), ((), ())), preferred_element_type=f32)


def mm_tn(left, right):
    return lax.dot_general(left, right, (((0,), (0,)), ((), ())), preferred_element_type=f32)


def halves(value):
    high = value.astype(bf16)
    return high, (value - high.astype(f32)).astype(bf16)


def wide(vector):
    return jnp.concatenate([vector] * 4, axis=1)


def folded(vector):
    channels = vector.shape[1] // 4
    return sum(vector[:, y * channels : (y + 1) * channels] for y in range(4))


class Place:
    def __init__(self, sc, rows):
        self.rows = rows
        self.members = lax.axis_size("gz")
        self.member = lax.axis_index("gz")
        self.small = jnp.minimum(sc[0], sc[1])
        self.coarse = self.small >= self.members
        tiles = rows // TILE
        self.tiles = tiles
        self.stride = jnp.where(self.coarse, tiles - 1, tiles)
        self.span = REACH // self.members + 2 * RIM
        far = jnp.where(self.coarse, REACH // self.members, self.span)
        near = jnp.where(self.coarse, self.small // self.members, 1)
        self.steps = [jnp.where(sc[l] == REACH, far, near) for l in range(2)]

    def index(self, shape):
        row = lax.broadcasted_iota(jnp.int32, shape, 0)
        return lax.rem(row, TILE) * self.stride + row // TILE, row // TILE

    def own(self, shape):
        place, tile = self.index(shape)
        inside = lax.rem(place, self.span)
        near = ((inside >= RIM) & (inside < self.span - RIM)).astype(jnp.int32)
        far = (tile < self.tiles - 1).astype(jnp.int32)
        return jnp.where(self.coarse, far, near) == 1

    def pick(self, cells_z):
        shape = (self.rows, cells_z)
        return self.z_of(shape, cells_z) == lax.broadcasted_iota(jnp.int32, shape, 1)

    def z_of(self, shape, cells_z):
        place, _ = self.index(shape)
        residues = jnp.minimum(self.small, self.members)
        part, start = self.member // residues, lax.rem(self.member, residues)
        period = place // self.span
        inside = place - period * self.span - RIM + part * (REACH // self.members)
        near = start + residues * inside + period * REACH
        z = jnp.where(self.coarse, place * self.members + self.member, near)
        return lax.rem(z + 2 * cells_z, cells_z)


def build_taps(block_of, taps):
    channels = taps.shape[-1] // 2
    zero = jnp.zeros((channels, channels), bf16)
    near, far = slice(0, channels), slice(channels, 2 * channels)
    for i in range(3):
        down, here, up = (block_of(i, j) for j in range(3))
        taps[i, near, near] = here
        taps[i, far, far] = here
        taps[i, near, far] = down
        taps[i, far, near] = up
        taps[3 + i, near, near] = zero
        taps[3 + i, far, far] = zero
        taps[3 + i, near, far] = down
        taps[3 + i, far, near] = up
    for m in range(2):
        build_pair(block_of(3, m), taps, 6 + m)


def build_pair(block, target, m):
    channels = block.shape[-1]
    zero = jnp.zeros((channels, channels), bf16)
    target[m, :channels, :channels] = block
    target[m, channels:, channels:] = block
    target[m, :channels, channels:] = zero
    target[m, channels:, :channels] = zero


def taken(weights, layer):
    return lambda i, j: weights[layer, i * 3 + j]


def fetch(pairs, sems):
    copies = [pltpu.make_async_copy(one, two, sems.at[at]) for at, (one, two) in enumerate(pairs)]
    for copy in copies:
        copy.start()
    for copy in copies:
        copy.wait()


def kernel_prepare(steps, w_z, w_xy, w_point, w_in_far, gains_far, w_out_far, w_front, point, w_back, point_back,
                   lift_in, lift_out, small, steps_on, w_in, gains, w_out, sems):
    pairs = [(w_point, point), (w_in_far, w_in), (gains_far, gains), (w_out_far, w_out), (steps, steps_on)]
    for layer in range(2):
        pairs.append((w_xy.at[layer, pl.ds(0, 4)], w_front.at[layer, pl.ds(0, 4)]))
        pairs.append((w_xy.at[layer, pl.ds(4, 4)], w_front.at[layer, pl.ds(5, 4)]))
        for m, at in ((1, 4), (0, 9), (2, 10)):
            pairs.append((w_z.at[layer, m], w_front.at[layer, at]))
    fetch(pairs, sems)
    small[...] = jnp.concatenate([w_in[...], gains[...], w_out[...]], axis=0)
    for layer in range(2):
        for at in range(9):
            w_back[layer, at] = w_front[layer, 8 - at].T
        w_back[layer, 9] = w_front[layer, 10].T
        w_back[layer, 10] = w_front[layer, 9].T
        point_back[layer] = point[layer].T
    whole = spread_rows(small[0:3], 0)
    high, low = halves(whole)
    lift_in[0:32] = high
    lift_in[32:64] = high
    lift_in[64:96] = low
    lift_in[96:128] = jnp.zeros_like(low)
    high = spread_rows(small[6:9], 3).astype(bf16)
    lift_out[0:32] = high
    lift_out[32:64] = high
    lift_out[64:96] = jnp.zeros_like(high)
    lift_out[96:128] = jnp.zeros_like(high)


def spread_rows(weights, first):
    channels = weights.shape[1]
    zero = jnp.zeros((1, channels), f32)
    rows = [jnp.zeros((1, 4 * channels), f32)] * 32
    for k in range(3):
        for y in range(4):
            parts = [weights[k : k + 1] if at == y else zero for at in range(4)]
            rows[(first + k) * 4 + y] = jnp.concatenate(parts, axis=1)
    return jnp.concatenate(rows, axis=0)


def fill_rims(padded, planes):
    padded[0] = padded[planes]
    padded[planes + 1] = padded[1]


def fill_shifted(place, layer, padded, shifted, planes):
    step, stride = place.steps[layer], place.stride
    for tile in range(place.tiles):
        for way in range(2):
            at = tile - step if way == 0 else tile + step
            moved = at + TILE * stride
            source = lax.rem(moved, stride)
            turn = lax.rem(2 * TILE - moved // stride, TILE)
            rows = padded[1 : planes + 1, pl.ds(pl.multiple_of(source * TILE, TILE), TILE), :]
            rows = pltpu.roll(rows.astype(f32), turn, 1)
            shifted[way, :, tile * TILE : (tile + 1) * TILE, :] = rows.astype(bf16)


def conv_pair(padded, shifted, taps, x0, count):
    rows, lanes = padded.shape[1:]
    half, quarter = lanes // 2, lanes // 4
    totals = [None, None, None]

    def add(at, left, right):
        part = mm(left.reshape(count * rows, half), right)
        totals[at] = part if totals[at] is None else totals[at] + part

    for q in range(2):
        side = slice(q * half, (q + 1) * half)
        for i in range(3):
            add(q, padded[x0 + i : x0 + i + count, :, side], taps[i])
        for m in range(2):
            add(q, shifted[m, x0 : x0 + count, :, side], taps[6 + m])
    for i in range(3):
        add(2, padded[x0 + i : x0 + i + count, :, quarter : 3 * quarter], taps[3 + i])
    first, second, middle = totals
    first = jnp.concatenate([first[:, :quarter], first[:, quarter:] + middle[:, :quarter]], axis=1)
    second = jnp.concatenate([second[:, :quarter] + middle[:, quarter:], second[:, quarter:]], axis=1)
    return first, second


def gelu_pair(value):
    scale = math.sqrt(2.0 / math.pi)
    square = value * value
    bent = jnp.tanh(value * (scale + (scale * 0.044715) * square))
    half = 0.5 + 0.5 * bent
    result = value * half
    slope = half + result * (1.0 - half) * (2.0 * scale + (6.0 * 0.044715 * scale) * square)
    return result, slope


def members_of(parts):
    found = []
    for part in parts:
        for at in range(0, part.shape[0], 8):
            found.append(part[at : at + 8])
    return found


def merged_stats(parts, per_member):
    found = members_of(parts)
    mean = sum(one[0:1] for one in found) / (per_member * len(found))
    spread = sum(one[1:2] for one in found)
    for one in found:
        gap = one[0:1] / per_member - mean
        spread = spread + per_member * gap * gap
    return mean, lax.rsqrt(spread / (per_member * len(found)) + eps_norm)


def put_rows(ref, *vectors):
    rows = list(vectors)
    rows += [jnp.zeros((1, ref.shape[1]), f32)] * (ref.shape[0] - len(rows))
    ref[...] = jnp.concatenate(rows, axis=0)


def masked_total(mask, value):
    return folded(jnp.sum(jnp.where(mask, value, 0.0), axis=0, keepdims=True))


def layer_forward(place, layer, padded, shifted, taps, pair, w_front, wp, shift_bias, old,
                  stream, act, slope, stats, acc, per_member):
    planes, rows, lanes = stream.shape
    half = lanes // 2
    count = planes // 2
    build_taps(taken(w_front, layer), taps)
    build_pair(wp[layer], pair, 0)
    fill_rims(padded, planes)
    fill_shifted(place, layer, padded, shifted, planes)
    acc[...] = jnp.zeros_like(acc)
    bias = wide(shift_bias[layer : layer + 1, :])[:, :half]

    for x0 in range(0, planes, count):
        part = slice(x0, x0 + count)
        for q, total in enumerate(conv_pair(padded, shifted, taps, x0, count)):
            side = slice(q * half, (q + 1) * half)
            value, grad = gelu_pair(total + bias)
            act[part, :, side] = value.astype(bf16).reshape(count, rows, half)
            slope[part, :, side] = grad.astype(bf16).reshape(count, rows, half)
    for x0 in range(0, planes, count):
        part = slice(x0, x0 + count)
        for q in range(2):
            side = slice(q * half, (q + 1) * half)
            branch = mm(act[part, :, side].reshape(count * rows, half), pair[0])
            new = old[part, :, side] + branch.reshape(count, rows, half)
            stream[part, :, side] = new
            acc[:, side] += jnp.sum(new, axis=0)
    mask = place.own((rows, lanes))
    total = masked_total(mask, acc[...])
    mean = wide(total / per_member)
    spread = jnp.zeros((rows, lanes), f32)
    for x in range(planes):
        gap = stream[x] - mean
        spread = spread + gap * gap
    put_rows(stats, total, masked_total(mask, spread))


def kernel_first(cells_z, per_member, sc, near, far, amounts, lift_in, small, shift_bias, w_front, wp,
                 stream, padded, act, slope, gathered, stats, consts, mixed_own,
                 shifted, taps, pair, acc, old, source, fields):
    planes, rows, lanes = stream.shape
    channels = lanes // 4
    depth = near.shape[2]
    place = Place(sc, rows)
    keep, add = amounts[0:1], amounts[1:2]
    for at, ref in enumerate((near, far)):
        fields[at, :, 12:24] = ref[:, 12:24]
        fields[at, :, 0:12] = keep * ref[:, 0:12] + add * ref[:, 12:24]
    mixed_own[...] = fields[0, place.member // 2 * planes + lax.axis_index("gx"), 0:12]
    cell_count = float(planes * 4 * cells_z)
    comps = [
        jnp.concatenate([fields[at, :, 4 * k : 4 * k + 4, :] for at in range(2)], axis=0) for k in range(3)
    ]

    def all_sum(value):
        value = jnp.sum(jnp.sum(value, axis=0), axis=0, keepdims=True)
        return jnp.sum(value, axis=1, keepdims=True)

    means = [all_sum(comp) / cell_count for comp in comps]
    gaps = [comp - mean[None] for comp, mean in zip(comps, means)]
    for k in range(3):
        for at in range(2):
            fields[at, :, 4 * k : 4 * k + 4, :] = gaps[k][at * near.shape[0] : (at + 1) * near.shape[0]]
    covs = {}
    for j in range(3):
        for k in range(j, 3):
            covs[j, k] = all_sum(gaps[j] * gaps[k]) / cell_count
    rows_in = [small[k : k + 1, :] for k in range(3)]
    mean_c = sum(means[k] * rows_in[k] for k in range(3))
    var_c = jnp.zeros((1, channels), f32)
    for (j, k), cov in covs.items():
        var_c = var_c + (1.0 if j == k else 2.0) * cov * (rows_in[j] * rows_in[k])
    inv_c = lax.rsqrt(jnp.maximum(var_c, 0.0) + eps_norm)
    flat = [jnp.broadcast_to(value, (1, channels)) for value in means + list(covs.values())]
    put_rows(consts, mean_c, inv_c, *flat)
    blank = jnp.zeros((8, depth), f32)
    core = lax.rem(place.member, 2)
    for slab in range(cells_z // depth):
        side = core if slab % 2 == 0 else 1 - core
        at = pl.ds(pl.multiple_of((slab // 2 * 2 + side) * depth, depth), depth)
        for x in range(planes):
            high, low = halves(jnp.concatenate([fields[slab % 2, slab // 2 * planes + x], blank], axis=0))
            source[x, 0:32, at] = high
            source[x, 32:64, at] = low
            source[x, 64:96, at] = high
            source[x, 96:128, at] = jnp.zeros_like(high)
    pick = place.pick(cells_z).astype(f32).astype(bf16)
    scale = wide(inv_c * small[3:4, :])
    for x in range(planes):
        gathered[x] = mm_nt(pick, source[x]).astype(bf16)
    for x0 in range(0, planes, planes // 2):
        part = slice(x0, x0 + planes // 2)
        value = mm(gathered[part].reshape(planes // 2 * rows, 128), lift_in[...])
        unit = (value * scale).astype(bf16).reshape(planes // 2, rows, lanes)
        old[part] = value.reshape(planes // 2, rows, lanes)
        padded[x0 + 1 : x0 + 1 + planes // 2] = unit
    layer_forward(place, 0, padded, shifted, taps, pair, w_front, wp, shift_bias, old, stream,
                  act, slope, stats, acc, per_member)


def kernel_second(per_member, sc, *refs):
    parts, refs = refs[:4], refs[4:]
    (old, small, shift_bias, w_front, wp, stream, padded, act, slope, stats, consts,
     shifted, taps, pair, acc) = refs
    planes, rows, _ = stream.shape
    place = Place(sc, rows)
    mean, inverse = merged_stats(parts, per_member)
    put_rows(consts, mean, inverse)
    mean_w, scale = wide(mean), wide(inverse * small[4:5, :])
    for x in range(planes):
        padded[x + 1] = ((old[x] - mean_w) * scale).astype(bf16)
    layer_forward(place, 1, padded, shifted, taps, pair, w_front, wp, shift_bias, old, stream,
                  act, slope, stats, acc, per_member)


def kernel_out(per_member, sc, *refs):
    parts, refs = refs[:4], refs[4:]
    stream, small, gathered, lift_out, prediction, misfit, sums, w_out_raw, consts, unit = refs
    planes, rows, lanes = stream.shape
    place = Place(sc, rows)
    mean, inverse = merged_stats(parts, per_member)
    put_rows(consts, mean, inverse)
    mean_w, inv_w, gain_w = wide(mean), wide(inverse), wide(small[5:6, :])
    scale = inv_w * gain_w
    for x in range(planes):
        unit[x] = ((stream[x] - mean_w) * scale).astype(bf16)
    row = lax.broadcasted_iota(jnp.int32, (128, 128), 0)
    col = lax.broadcasted_iota(jnp.int32, (128, 128), 1)
    slot = lax.rem(col, 32)
    used = (col < 64) & (slot >= 12) & (slot < 24)
    take = (used & ((row == slot) | (row == slot + 32))).astype(f32).astype(bf16)
    total = mm_nt(unit[...].reshape(planes * rows, lanes), lift_out[...])
    noise = mm(gathered[...].reshape(planes * rows, 128), take)
    gap = total - noise
    high, low = halves(gap)
    lane = lax.broadcasted_iota(jnp.int32, gap.shape, 1)
    both = jnp.where(lane < 32, high.astype(f32), low.astype(f32)).astype(bf16)
    misfit[...] = both.reshape(planes, rows, 128)
    for x in range(planes):
        @pl.when(lax.axis_index("gx") == x)
        def _(x=x):
            prediction[...] = total[x * rows : (x + 1) * rows]
    plain = jnp.zeros((rows, lanes), f32)
    cross = jnp.zeros((rows, lanes), f32)
    for x0 in range(0, planes, planes // 2):
        part = slice(x0 * rows, (x0 + planes // 2) * rows)
        d_out = mm(both[part], lift_out[...]).reshape(planes // 2, rows, lanes)
        for x in range(planes // 2):
            plain = plain + d_out[x]
            cross = cross + d_out[x] * ((stream[x0 + x] - mean_w) * inv_w)
    own = place.own((rows, 128))
    kept = jnp.concatenate([jnp.where(own, misfit[x].astype(f32), 0.0) for x in range(planes)], axis=0)
    raw = mm_tn(kept.astype(bf16), unit[...].reshape(planes * rows, lanes))
    mask = place.own((rows, lanes))
    put_rows(sums, masked_total(mask, plain), masked_total(mask, cross))
    put_rows(w_out_raw, *by_component(raw[0:32] + raw[32:64], 3))


def by_component(raw, first):
    channels = raw.shape[1] // 4
    found = []
    for k in range(first, first + 3):
        found.append(
            sum(raw[k * 4 + y : k * 4 + y + 1, y * channels : (y + 1) * channels] for y in range(4))
        )
    return found


def branch_backward(planes, d_stream_of, pair, slope, padded, scot, bias_acc):
    rows, lanes = padded.shape[1:]
    half = lanes // 2
    count = planes // 2

    for x0 in range(0, planes, count):
        part = slice(x0, x0 + count)
        for x in range(x0, x0 + count):
            scot[x] = d_stream_of(x).astype(bf16)
        for q in range(2):
            side = slice(q * half, (q + 1) * half)
            cot = scot[part, :, side].reshape(count * rows, half)
            d_act = mm(cot, pair[0]).reshape(count, rows, half)
            pre = (d_act * slope[part, :, side].astype(f32)).astype(bf16)
            padded[x0 + 1 : x0 + 1 + count, :, side] = pre
            bias_acc[:, side] += jnp.sum(pre.astype(f32), axis=0)


def weight_grads(place, planes, padded, shifted, scot, normed, act, keep, give, taps_all, share):
    rows, lanes = padded.shape[1:]
    channels = lanes // 4
    wide_share = 4 * share
    row = lax.broadcasted_iota(jnp.int32, (lanes, wide_share), 0)
    col = lax.broadcasted_iota(jnp.int32, (lanes, wide_share), 1)
    hit = (row // channels == col // share) & (
        lax.rem(row, channels) == lax.rem(col, share) + lax.axis_index("gx") * share
    )
    choose = hit.astype(f32).astype(bf16)
    mask = jnp.concatenate([place.own((rows, wide_share))] * planes, axis=0)

    def turned(source):
        got = mm(source.reshape(planes * rows, lanes), choose)
        return jnp.where(mask, got, 0.0).astype(bf16)

    def add_blocks(raw, j):
        return sum(
            raw[(y + j) * share : (y + j + 1) * share, y * channels : (y + 1) * channels]
            for y in range(4)
            if 0 <= y + j < 4
        )

    left = turned(normed[1 : planes + 1])
    for i in range(3):
        raw = mm_tn(left, padded[2 - i : 2 - i + planes].reshape(planes * rows, lanes))
        for j in range(3):
            taps_all[i * 3 + j] = add_blocks(raw, j - 1)
    for m in range(2):
        raw = mm_tn(left, shifted[1 - m].reshape(planes * rows, lanes))
        taps_all[9 + m] = add_blocks(raw, 0)
    raw = mm_tn(turned(act[...]), scot[...].reshape(planes * rows, lanes))
    taps_all[11] = add_blocks(raw, 0)
    odd, half = lax.rem(place.member, 2), keep.shape[0]
    keep[...] = taps_all[pl.ds(odd * half, half)]
    give[...] = taps_all[pl.ds((1 - odd) * half, half)]


def conv_backward(planes, padded, shifted, taps, emit):
    count = planes // 2

    for x0 in range(0, planes, count):
        for q, total in enumerate(conv_pair(padded, shifted, taps, x0, count)):
            emit(x0, count, q, total)


def kernel_back_second(cell_count, sc, *refs):
    parts, refs = refs[:4], refs[4:]
    (stream, out_consts, small, misfit, lift_out, slope, normed, w_back, point_back,
     d_stream, d_normed, sums, padded, shifted, scot,
     taps, pair, acc, acc2) = refs
    planes, rows, lanes = stream.shape
    half = lanes // 2
    place = Place(sc, rows)
    sums_out = sum(members_of(parts))
    gain_w = wide(small[5:6, :])
    mean_w, inv_w = wide(out_consts[0:1]), wide(out_consts[1:2])
    m_plain = gain_w * wide(sums_out[0:1]) / cell_count
    m_cross = gain_w * wide(sums_out[1:2]) / cell_count
    build_pair(point_back[1], pair, 0)
    build_taps(taken(w_back, 1), taps)
    acc[...] = jnp.zeros_like(acc)

    def d_stream_of(x):
        d_out = mm(misfit[x], lift_out[...])
        white = (stream[x] - mean_w) * inv_w
        value = inv_w * (gain_w * d_out - m_plain - white * m_cross)
        d_stream[x] = value
        return value

    branch_backward(planes, d_stream_of, pair, slope, padded, scot, acc)
    mask = place.own((rows, lanes))
    s_bias = masked_total(mask, acc[...])
    acc[...] = jnp.zeros_like(acc)
    acc2[...] = jnp.zeros_like(acc2)
    fill_rims(padded, planes)
    fill_shifted(place, 1, padded, shifted, planes)

    def emit(x0, count, q, value):
        side = slice(q * half, (q + 1) * half)
        value = value.reshape(count, rows, half)
        d_normed[x0 : x0 + count, :, side] = value
        acc[:, side] += jnp.sum(value, axis=0)
        acc2[:, side] += jnp.sum(value * normed[x0 + 1 : x0 + 1 + count, :, side].astype(f32), axis=0)

    conv_backward(planes, padded, shifted, taps, emit)
    s_plain = masked_total(mask, acc[...])
    s_cross = masked_total(mask, acc2[...]) / small[4:5, :]
    put_rows(sums, s_plain, s_cross, s_bias)


def kernel_weights_second(share, sc, padded, shifted, scot, normed, act, keep, give, taps_all):
    planes, rows, _ = scot.shape
    weight_grads(Place(sc, rows), planes, padded, shifted, scot, normed, act, keep, give, taps_all, share)


def kernel_back_first(share, cell_count, sc, *refs):
    parts, refs = refs[:4], refs[4:]
    (consts, d_next, d_normed, normed_next, small, act, slope, normed, point_back,
     d_stream, sums, keep, give, padded, shifted,
     pair, acc, scot, taps_all) = refs
    planes, rows, lanes = d_next.shape
    place = Place(sc, rows)
    sums_in = sum(members_of(parts))
    gain_w = wide(small[4:5, :])
    inv_w = wide(consts[1:2])
    m_plain = gain_w * wide(sums_in[0:1]) / cell_count
    m_cross = wide(sums_in[1:2]) / cell_count
    build_pair(point_back[0], pair, 0)
    acc[...] = jnp.zeros_like(acc)

    def d_stream_of(x):
        back = gain_w * d_normed[x] - m_plain - normed_next[x + 1].astype(f32) * m_cross
        value = d_next[x] + inv_w * back
        d_stream[x] = value
        return value

    branch_backward(planes, d_stream_of, pair, slope, padded, scot, acc)
    put_rows(sums, masked_total(place.own((rows, lanes)), acc[...]))
    fill_rims(padded, planes)
    fill_shifted(place, 0, padded, shifted, planes)
    weight_grads(place, planes, padded, shifted, scot, normed, act, keep, give, taps_all, share)


def kernel_last(depth, sc, padded, shifted, d_stream, normed, small, consts, gathered, lift_in, w_back,
                prediction, sums_bias, out_raw, ready0, ready1, own_out, out_1, out_2, out_3,
                taps, acc, acc2, high, low):
    planes, rows, lanes = d_stream.shape
    half = lanes // 2
    place = Place(sc, rows)
    build_taps(taken(w_back, 0), taps)
    acc[...] = jnp.zeros_like(acc)
    acc2[...] = jnp.zeros_like(acc2)
    scale = wide(consts[1:2] * small[3:4, :])

    def emit(x0, count, q, value):
        side = slice(q * half, (q + 1) * half)
        part = slice(x0, x0 + count)
        value = value.reshape(count, rows, half)
        acc[:, side] += jnp.sum(value, axis=0)
        acc2[:, side] += jnp.sum(value * normed[x0 + 1 : x0 + 1 + count, :, side].astype(f32), axis=0)
        full = d_stream[part, :, side] + value * scale[:, side]
        first, second = halves(full)
        high[part, :, side] = first
        low[part, :, side] = second

    conv_backward(planes, padded, shifted, taps, emit)
    mask = place.own((rows, lanes))
    s_plain = masked_total(mask, acc[...])
    s_cross = masked_total(mask, acc2[...]) / small[3:4, :]
    own = place.own((rows, 128))
    kept = jnp.concatenate([jnp.where(own, gathered[x].astype(f32), 0.0) for x in range(planes)], axis=0)
    kept = kept.astype(bf16)
    raw = mm_tn(kept, high[...].reshape(planes * rows, lanes))
    raw_low = mm_tn(kept, low[...].reshape(planes * rows, lanes))
    in_raw = by_component(raw[0:32] + raw[32:64] + raw_low[0:32], 0)
    blank = jnp.zeros((1, s_plain.shape[1]), f32)
    tail = jnp.concatenate([s_plain, s_cross] + [blank] * 6 + in_raw + [blank] * 5, axis=0)
    tail = jnp.concatenate([tail, sums_bias[...], out_raw[...]], axis=0)
    here = lax.axis_index("gx")
    lane = lax.broadcasted_iota(jnp.int32, (rows, 128), 1)
    field = mm_nt(high[here], lift_in[...]) + jnp.where(lane < 32, mm_nt(low[here], lift_in[...]), 0.0)
    field = jnp.where((lane >= 32) & (lane < 64), 0.0, field)
    field = field + jnp.where((lane >= 12) & (lane < 24), prediction[...], 0.0)
    cells_z = depth * place.members
    whole = place.z_of((rows, depth), cells_z)
    column = lax.broadcasted_iota(jnp.int32, (rows, depth), 1)
    mask = place.own((rows, depth))
    first, second = halves(field)
    for bit, target in enumerate((own_out, out_1, out_2, out_3)):
        there = lax.bitwise_xor(place.member, bit)
        pick = ((whole == column + there * depth) & mask).astype(f32).astype(bf16)
        out = mm_tn(first, pick) + mm_tn(second, pick)
        target[0:32] = out[0:32] + out[64:96]
        target[32:64] = tail


def call(kernel, outs, scratch, flops, limit, *args, scalars=True, scalar_out=0, ready=(), far=()):
    spec = pl.BlockSpec(memory_space=pltpu.VMEM)
    specs = [pl.BlockSpec(memory_space=pltpu.SMEM)] * scalars + [spec] * (len(args) - scalars)
    for at in ready:
        specs[at] = pl.BlockSpec(memory_space=pl.ANY)
    args = list(args)
    for at in far:
        specs[at] = pl.BlockSpec(memory_space=pltpu.HBM)
        args[at] = pltpu.with_memory_space_constraint(args[at], pltpu.HBM)
    smem = pl.BlockSpec(memory_space=pltpu.SMEM)
    return pl.pallas_call(
        kernel,
        out_shape=[jax.ShapeDtypeStruct(shape, dtype) for shape, dtype in outs],
        in_specs=specs,
        out_specs=[spec] * (len(outs) - scalar_out) + [smem] * scalar_out,
        scratch_shapes=[pltpu.VMEM(*one) if isinstance(one, tuple) else one for one in scratch],
        compiler_params=pltpu.CompilerParams(vmem_limit_bytes=limit * 2**20),
        cost_estimate=pl.CostEstimate(flops=flops, bytes_accessed=2**23, transcendentals=0),
    )(*args)


def swapped(value, axis, bit):
    count = lax.axis_size(axis)
    return lax.ppermute(value, axis, [(i, i ^ bit) for i in range(count)])


def group_parts(value):
    return (value,) + tuple(swapped(value, "gz", bit) for bit in (1, 2, 3))


def kernel_spread(first, first_far, second, second_far, ready, spread):
    taps, share, channels = first.shape
    for layer, (own, other) in enumerate(((first, first_far), (second, second_far))):
        value = (own[...] + other[...]).reshape(taps * share, channels).astype(bf16)
        for part in range(spread.shape[0]):
            spread[part, layer * taps * share : (layer + 1) * taps * share] = value


def kernel_layout(scale, share, near, far, grad_w_z, grad_w_xy, grad_w_point):
    groups = near.shape[0]
    taps = near.shape[1] // share // 2
    odd = lax.rem(lax.axis_index("gz"), 2) == 1
    for layer in range(2):
        for tap in range(taps):
            at = (layer * taps + tap) * share
            one = near[:, at : at + share].astype(f32) * scale
            two = far[:, at : at + share].astype(f32) * scale
            for side in range(2):
                value = jnp.where(odd, one if side else two, two if side else one)
                value = value.reshape(groups * share, value.shape[2])
                whole = side * taps + tap
                if whole == 4:
                    grad_w_z[layer, 1] = value
                elif whole < 9:
                    grad_w_xy[layer, whole - (whole > 4)] = value
                elif whole < 11:
                    grad_w_z[layer, 2 * (whole - 9)] = value
                else:
                    grad_w_point[layer] = value


def kernel_tail(cell_count, inv_area, *refs):
    tails, parts1, parts2, refs = refs[:4], refs[4:8], refs[8:12], refs[12:]
    (consts, small, mixed, features, time_raw,
     prediction, field_grad, grad_w_in, grad_w_time, grad_biases, grad_gains, grad_w_out) = refs
    tail = sum(ref[...] for ref in tails)
    s1, s2 = sum(ref[...] for ref in parts1), sum(ref[...] for ref in parts2)
    inverse = consts[1:2]
    m_plain = inverse * (small[3:4] * tail[32:33] / cell_count)
    m_cross = inverse * inverse * (small[3:4] * tail[33:34] / cell_count)
    at = {(0, 0): 5, (0, 1): 6, (0, 2): 7, (1, 1): 8, (1, 2): 9, (2, 2): 10}
    rows_in = [small[k : k + 1] for k in range(3)]
    depth = mixed.shape[1]
    gaps = [mixed[4 * k : 4 * k + 4] - consts[2 + k : 3 + k, 0:1] for k in range(3)]
    for k in range(3):
        offset = jnp.sum(rows_in[k] * m_plain, axis=1, keepdims=True)
        value = tail[4 * k : 4 * k + 4] - offset
        cross = jnp.zeros_like(m_plain)
        for j in range(3):
            mix = jnp.sum(rows_in[k] * m_cross * rows_in[j], axis=1, keepdims=True)
            value = value - mix * gaps[j]
            row = at[min(j, k), max(j, k)]
            cross = cross + consts[row : row + 1] * rows_in[j]
        field_grad[k, 0] = value
        prediction[k, 0] = tail[12 + 4 * k : 16 + 4 * k]
        in_sum = tail[40 + k : 41 + k] - cell_count * (m_cross * cross)
        grad_w_in[k : k + 1] = inv_area * in_sum
    bias0, bias1 = tail[48:49], s1[2:3]
    grad_biases[...] = inv_area * jnp.concatenate([bias0, bias1], axis=0)
    grad_gains[...] = inv_area * jnp.concatenate([tail[33:34], s1[1:2], s2[1:2]], axis=0)
    grad_w_out[...] = inv_area * tail[56:59]
    raw = time_raw[...]
    gate = 1.0 / (1.0 + jnp.exp(-raw))
    back = (bias0 + bias1) * (gate * (1.0 + raw * (1.0 - gate)))
    spread = jnp.broadcast_to(features[...], grad_w_time.shape).T
    grad_w_time[...] = inv_area * (spread * back)


def per_device_grouped(clean_field, noise_field, timestep, dilations, w_in, w_time, w_z, w_xy, w_point,
                       biases, norm_gains, w_out):
    members, groups = lax.axis_size("gz"), lax.axis_size("gx")
    depth = clean_field.shape[3]
    planes, cells_z = groups, depth * members
    channels = w_in.shape[1]
    lanes = 4 * channels
    rows = (cells_z // REACH) * (REACH // members + 2 * RIM)
    share = channels // groups
    per_member = float(planes * 4 * depth)
    cell_count = per_member * members
    inv_area = 4.0 / cell_count

    alpha_bar, features, time_raw, time_code = time_terms(timestep, w_time)
    parts = members // 2 * groups
    block = jnp.concatenate([clean_field, noise_field], axis=0).reshape(24, depth)
    block = jnp.broadcast_to(block[None], (parts, 24, depth))
    amounts = jnp.stack([jnp.sqrt(alpha_bar), jnp.sqrt(1.0 - alpha_bar)])
    amounts = jnp.broadcast_to(amounts[:, None], (2, depth))
    same_core = [[m * groups + g for m in range(core, members, 2) for g in range(groups)] for core in range(2)]
    near = lax.all_to_all(block, ("gz", "gx"), 0, 0, axis_index_groups=same_core)
    far = swapped(near, "gz", 1)
    shift_bias = biases + time_code

    big = (planes, rows, lanes)
    vec = ((8, channels), f32)
    thin = ((planes, rows, 128), bf16)
    lift = ((128, lanes), bf16)
    conv_scratch = [
        ((planes + 2, rows, lanes), bf16),
        ((2,) + big, bf16),
        ((8, lanes // 2, lanes // 2), bf16),
    ]
    pair = ((1, lanes // 2, lanes // 2), bf16)
    flat = ((rows, lanes), f32)
    grad_out = ((6, share, channels), f32)

    taps_out, point_out = ((2, 11, channels, channels), bf16), ((2, channels, channels), bf16)
    w_front, point, w_back, point_back, lift_in, lift_out, small, steps_on = call(
        kernel_prepare,
        [taps_out, point_out, taps_out, point_out, lift, lift, ((9, channels), f32), ((2,), jnp.int32)],
        [((3, channels), f32), ((3, channels), f32), ((3, channels), f32), pltpu.SemaphoreType.DMA((15,))],
        10**8, LIMITS[0], dilations, w_z, w_xy, w_point, w_in, norm_gains, w_out.astype(f32),
        scalar_out=1,
        far=tuple(range(7)),
    )
    stream1, normed0, act0, slope0, gathered, stats1, consts0, mixed_own = call(
        functools.partial(kernel_first, cells_z, per_member),
        [(big, f32), conv_scratch[0], (big, bf16), (big, bf16), thin, vec, ((16, channels), f32), ((12, depth), f32)],
        conv_scratch[1:] + [pair, flat, (big, f32), ((planes, 128, cells_z), bf16), ((2, parts, 24, depth), f32)],
        4 * 10**9, LIMITS[1],
        steps_on, near, far, amounts, lift_in, small, shift_bias, w_front, point,
    )
    stream2, normed1, act1, slope1, stats2, consts1 = call(
        functools.partial(kernel_second, per_member),
        [(big, f32), conv_scratch[0], (big, bf16), (big, bf16), vec, vec],
        conv_scratch[1:] + [pair, flat],
        4 * 10**9, LIMITS[2],
        steps_on, *group_parts(stats1), stream1, small, shift_bias, w_front, point,
    )
    prediction, misfit, sums2, out_raw, consts2 = call(
        functools.partial(kernel_out, per_member),
        [((rows, 128), f32), thin, vec, vec, vec],
        [(big, bf16)],
        10**9, LIMITS[3],
        steps_on, *group_parts(stats2), stream2, small, gathered, lift_out,
    )
    parts2 = group_parts(sums2)
    d_stream2, d_normed1, sums1, rimmed1, shifted1, scot1 = call(
        functools.partial(kernel_back_second, cell_count),
        [(big, f32), (big, f32), vec] + conv_scratch[:2] + [(big, bf16)],
        conv_scratch[2:] + [pair, flat, flat],
        6 * 10**9, LIMITS[4],
        steps_on, *parts2, stream2, consts2, small, misfit, lift_out, slope1, normed1,
        w_back, point_back,
    )
    parts1 = group_parts(sums1)
    keep1, give1 = call(
        functools.partial(kernel_weights_second, share),
        [grad_out, grad_out], [((12, share, channels), f32)], 2 * 10**9, LIMITS[8],
        steps_on, rimmed1, shifted1, scot1, normed1, act1,
    )
    d_stream1, sums_b0, keep0, give0, rimmed0, shifted0 = call(
        functools.partial(kernel_back_first, share, cell_count),
        [(big, f32), vec, grad_out, grad_out] + conv_scratch[:2],
        [pair, flat, (big, bf16), ((12, share, channels), f32)],
        4 * 10**9, LIMITS[5],
        steps_on, *parts1, consts1, d_stream2, d_normed1, normed1, small, act0, slope0, normed0,
        point_back,
    )
    chip0 = keep0 + swapped(give0, "gz", 1)
    chip1 = keep1 + swapped(give1, "gz", 1)
    last = call(
        functools.partial(kernel_last, depth),
        [((64, channels), f32)] * members,
        conv_scratch[2:] + [flat, flat, (big, bf16), (big, bf16)],
        4 * 10**9, LIMITS[6],
        steps_on, rimmed0, shifted0, d_stream1, normed0, small, consts0, gathered, lift_in, w_back, prediction,
        sums_b0, out_raw, chip0, chip1, ready=(13, 14),
    )
    spread = call(
        kernel_spread, [((groups, 12 * share, channels), bf16)], [], 10**5, LIMITS[9],
        chip0, swapped(chip0, "gz", 2), chip1, swapped(chip1, "gz", 2), last[0], scalars=False, ready=(4,),
    )[0]
    near_grads = lax.all_to_all(spread, "gx", 0, 0)

    prediction, field_grad, grad_w_in, grad_w_time, grad_biases, grad_gains, grad_w_out = call(
        functools.partial(kernel_tail, cell_count, inv_area),
        [(clean_field.shape, f32), (clean_field.shape, f32), ((3, channels), f32), (w_time.shape, f32),
         ((2, channels), f32), ((3, channels), f32), ((3, channels), f32)],
        [], 10**6, LIMITS[10],
        last[0], *(swapped(last[bit], "gz", bit) for bit in (1, 2, 3)), *parts1, *parts2, consts0, small,
        mixed_own, features[None], time_raw[None], scalars=False,
    )
    tied, _ = lax.optimization_barrier((near_grads, field_grad))
    far_grads = swapped(tied, "gz", 1)
    grad_w_z, grad_w_xy, grad_w_point = call(
        functools.partial(kernel_layout, inv_area, share),
        [(w_z.shape, f32), (w_xy.shape, f32), (w_point.shape, f32)],
        [], 10**6, LIMITS[11], near_grads, far_grads, scalars=False,
    )
    return (
        prediction,
        field_grad,
        grad_w_in,
        grad_w_time,
        grad_w_z,
        grad_w_xy,
        grad_w_point,
        grad_biases,
        grad_gains,
        grad_w_out,
    )


def padded_2(cells, sides, width):
    for axis, dim in sides:
        count = lax.axis_size(axis)
        head = lax.slice_in_dim(cells, 0, width, axis=dim)
        tail = lax.slice_in_dim(cells, cells.shape[dim] - width, cells.shape[dim], axis=dim)
        cells = jnp.concatenate(
            [
                lax.ppermute(tail, axis, [(i, (i + 1) % count) for i in range(count)]),
                cells,
                lax.ppermute(head, axis, [((i + 1) % count, i) for i in range(count)]),
            ],
            axis=dim,
        )
    return cells


def passed_along(value, axis, steps):
    count = lax.axis_size(axis)
    pairs = [(source, (source + steps) % count) for source in range(count)]
    return lax.ppermute(value, axis, pairs)


def contract_cells(left, right):
    return lax.dot_general(
        left, right, (((0, 1, 2), (0, 1, 2)), ((), ())), preferred_element_type=jnp.float32
    )


def plane_tap(padded, shift_x, shift_y, rows_x, rows_y):
    return padded[1 + shift_x : 1 + shift_x + rows_x, 1 + shift_y : 1 + shift_y + rows_y]


def plane_pad(source):
    rimmed = padded_2(source, (("gx", 0),), 1)
    return jnp.pad(rimmed, ((0, 0), (1, 1), (0, 0), (0, 0)))


def slab_windows(source, dilation):
    slab_depth = source.shape[2]
    above = passed_along(source, "gz", -1)
    above_far = passed_along(source, "gz", -2)
    below = passed_along(source, "gz", 1)
    below_far = passed_along(source, "gz", 2)
    ahead_rows = jnp.concatenate([source, above, above_far], axis=2)
    behind_rows = jnp.concatenate([below_far, below, source], axis=2)
    upper = lax.dynamic_slice_in_dim(ahead_rows, dilation, slab_depth, 2)
    lower = lax.dynamic_slice_in_dim(behind_rows, 2 * slab_depth - dilation, slab_depth, 2)
    return (lower, upper)


def normalize(hidden, gains, cell_count):
    average = lax.psum(jnp.sum(hidden, axis=(0, 1, 2)), ("gz", "gx")) / cell_count
    centered = hidden - average
    spread = lax.psum(jnp.sum(centered * centered, axis=(0, 1, 2)), ("gz", "gx")) / cell_count
    inverse_std = lax.rsqrt(spread + eps_norm)
    whitened = (hidden - average) * inverse_std
    return ((whitened * gains).astype(jnp.bfloat16), whitened, inverse_std)


def norm_back(d_normed, whitened, inverse_std, gains, cell_count):
    scaled = d_normed * gains
    sum_grad, sum_cross = lax.psum(
        (jnp.sum(scaled, axis=(0, 1, 2)), jnp.sum(scaled * whitened, axis=(0, 1, 2))), ("gz", "gx")
    )
    d_hidden = inverse_std * (scaled - sum_grad / cell_count - whitened * (sum_cross / cell_count))
    return (d_hidden, jnp.sum(d_normed * whitened, axis=(0, 1, 2)))


def conv_forward(normed, dilation, weights_z, weights_xy):
    rows_x, rows_y = (normed.shape[0], normed.shape[1])
    lower, upper = slab_windows(normed, dilation)
    padded = plane_pad(normed)
    summed = jnp.dot(lower, weights_z[0], preferred_element_type=jnp.float32)
    summed = summed + jnp.dot(normed, weights_z[1], preferred_element_type=jnp.float32)
    summed = summed + jnp.dot(upper, weights_z[2], preferred_element_type=jnp.float32)
    for tap_number, (shift_x, shift_y) in enumerate(plane_offsets):
        summed = summed + jnp.dot(
            plane_tap(padded, shift_x, shift_y, rows_x, rows_y),
            weights_xy[tap_number],
            preferred_element_type=jnp.float32,
        )
    return summed


def conv_backward_split(pre_cot, normed, dilation, weights_z, weights_xy):
    rows_x, rows_y = (normed.shape[0], normed.shape[1])
    lower_cot, upper_cot = slab_windows(pre_cot, dilation)
    padded_cot = plane_pad(pre_cot)
    d_normed = jnp.dot(upper_cot, weights_z[0].T, preferred_element_type=jnp.float32)
    d_normed = d_normed + jnp.dot(pre_cot, weights_z[1].T, preferred_element_type=jnp.float32)
    d_normed = d_normed + jnp.dot(lower_cot, weights_z[2].T, preferred_element_type=jnp.float32)
    xy_terms = []
    for tap_number, (shift_x, shift_y) in enumerate(plane_offsets):
        shifted = plane_tap(padded_cot, -shift_x, -shift_y, rows_x, rows_y)
        d_normed = d_normed + jnp.dot(
            shifted, weights_xy[tap_number].T, preferred_element_type=jnp.float32
        )
        xy_terms.append(contract_cells(normed, shifted))
    z_terms = jnp.stack(
        [
            contract_cells(normed, upper_cot),
            contract_cells(normed, pre_cot),
            contract_cells(normed, lower_cot),
        ]
    )
    return (d_normed, z_terms, jnp.stack(xy_terms))


def per_device_split(
    clean_field,
    noise_field,
    timestep,
    dilations,
    w_in,
    w_time,
    w_z,
    w_xy,
    w_point,
    biases,
    norm_gains,
    w_out,
):
    layer_total = w_z.shape[0]
    rows_x, rows_y, slab_depth = (clean_field.shape[1], clean_field.shape[2], clean_field.shape[3])
    plane_cells = rows_x * lax.axis_size("gx") * slab_depth * lax.axis_size("gz")
    cell_count = float(plane_cells * rows_y)
    inv_area = 1.0 / plane_cells
    alpha_bar, features, time_raw, time_code = time_terms(timestep, w_time)
    noisy = jnp.sqrt(alpha_bar) * clean_field + jnp.sqrt(1.0 - alpha_bar) * noise_field
    stream = jnp.einsum("kxyz,kc->xyzc", noisy, w_in, precision=highest)
    saved = []
    for which_layer in range(layer_total):
        normed, whitened, inverse_std = normalize(stream, norm_gains[which_layer], cell_count)
        pre_act = conv_forward(normed, dilations[which_layer], w_z[which_layer], w_xy[which_layer])
        pre_act = pre_act + biases[which_layer] + time_code
        activated = jax.nn.gelu(pre_act).astype(jnp.bfloat16)
        saved.append((normed, whitened, inverse_std, pre_act, activated))
        stream = stream + jnp.dot(
            activated, w_point[which_layer], preferred_element_type=jnp.float32
        )
    out_normed, out_white, out_inverse = normalize(stream, norm_gains[layer_total], cell_count)
    prediction = jnp.einsum("xyzc,kc->kxyz", out_normed, w_out, preferred_element_type=jnp.float32)
    misfit = prediction - noise_field
    d_out = jnp.einsum("kxyz,kc->xyzc", misfit, w_out.astype(jnp.float32), precision=highest)
    out_raw = jnp.einsum(
        "kxyz,xyzc->kc", misfit, out_normed, precision=highest, preferred_element_type=jnp.float32
    )
    d_stream, out_gain_raw = norm_back(
        d_out, out_white, out_inverse, norm_gains[layer_total], cell_count
    )
    z_list, xy_list, point_list, bias_list, gain_list = ([], [], [], [], [])
    for which_layer in reversed(range(layer_total)):
        normed, whitened, inverse_std, pre_act, activated = saved[which_layer]
        stream_cot = d_stream.astype(jnp.bfloat16)
        point_raw = contract_cells(activated, stream_cot)
        d_act = jnp.dot(stream_cot, w_point[which_layer].T, preferred_element_type=jnp.float32)
        gelu_back = jax.vjp(jax.nn.gelu, pre_act)[1]
        pre_cot = gelu_back(d_act)[0].astype(jnp.bfloat16)
        bias_raw = jnp.sum(pre_cot, axis=(0, 1, 2), dtype=jnp.float32)
        d_normed, z_raw, xy_raw = conv_backward_split(
            pre_cot, normed, dilations[which_layer], w_z[which_layer], w_xy[which_layer]
        )
        d_back, gain_raw = norm_back(
            d_normed, whitened, inverse_std, norm_gains[which_layer], cell_count
        )
        d_stream = d_stream + d_back
        z_list.insert(0, z_raw)
        xy_list.insert(0, xy_raw)
        point_list.insert(0, point_raw)
        bias_list.insert(0, bias_raw)
        gain_list.insert(0, gain_raw)
    field_grad = jnp.einsum("xyzc,kc->kxyz", d_stream, w_in, precision=highest)
    in_raw = jnp.einsum("kxyz,xyzc->kc", noisy, d_stream, precision=highest)
    z_all, xy_all, point_all, bias_all, gain_all, in_raw, out_raw = lax.psum(
        (
            jnp.stack(z_list),
            jnp.stack(xy_list),
            jnp.stack(point_list),
            jnp.stack(bias_list),
            jnp.stack(gain_list + [out_gain_raw]),
            in_raw,
            out_raw,
        ),
        ("gz", "gx"),
    )
    time_back = jax.vjp(jax.nn.silu, time_raw)[1](jnp.sum(bias_all, axis=0))[0]
    grad_w_time = inv_area * jnp.outer(features, time_back)
    return (
        prediction,
        field_grad,
        inv_area * in_raw,
        grad_w_time,
        inv_area * z_all,
        inv_area * xy_all,
        inv_area * point_all,
        inv_area * bias_all,
        inv_area * gain_all,
        inv_area * out_raw,
    )


def per_device(*args):
    members, groups = lax.axis_size("gz"), lax.axis_size("gx")
    _, rows_x, rows_y, depth = args[0].shape
    small = rows_x == 1 and rows_y == 4 and members == 4 and groups == 8 and depth * members == 2 * REACH
    return per_device_grouped(*args) if small else per_device_split(*args)


def solution(mesh):
    return jax.shard_map(
        per_device,
        mesh=mesh,
        in_specs=(
            P(None, "gx", None, "gz"),
            P(None, "gx", None, "gz"),
            P(),
            P(),
            P(),
            P(),
            P(),
            P(),
            P(),
            P(),
            P(),
            P(),
        ),
        out_specs=(
            P(None, "gx", None, "gz"),
            P(None, "gx", None, "gz"),
            P(),
            P(),
            P(),
            P(),
            P(),
            P(),
            P(),
            P(),
        ),
        check_vma=False,
    )
```
